32 devices in a mesh: grp: 1, row: 16 (over z, y, x), col: 2 (over core).
Axes of the slice: x: 2, y: 2, z: 4, core: 2. Of those that a mesh axis runs over, the one named last changes fastest.
Arguments:
- pair: bfloat16 [192, 192, 128], P(('grp', 'row'), 'col'), may hold values from -6 to 6
- tile_mask: int32 [2, 2], P('grp'), may hold values 0 or 1
- chain_ids: int32 [192], P('grp'), may hold values from 0 to 5, never falling along the last dimension, each value on 1 to 64 neighbouring positions
- gain_in: float32 [128], replicated, may hold values from 0.1 to 1.9
- w_proj: bfloat16 [128, 640], replicated, may hold values from -0.5 to 0.5
- gain_mid: float32 [128], replicated, may hold values from 0.1 to 1.9
- w_out: bfloat16 [128, 128], replicated, may hold values from -0.5 to 0.5
Outputs:
- update: bfloat16 [192, 192, 128], P(('grp', 'row'), 'col')
The draws below stay inside these ranges and needn't reach their ends.
Inputs may be any that keep to these rules, and one draw needn't show every extreme that they name: `chain_ids`: chains are runs of consecutive tokens with never falling ids, each at most 64 tokens long; one chain has exactly that many.
All inputs are finite; a program needn't handle non-finite values.
Results may differ from the reference program's by a relative error of at most 0.0079.
Values may be sent and summed in bfloat16 or wider, within the bound.
No kernel may reach another device: no remote copies, remote signals or barrier semaphores. Data moves between devices by JAX's collectives and lax.ppermute only.
A program may use at most 128 MiB of HBM per device.

```python
import math
import jax
import jax.numpy as jnp
import numpy as np
from jax import lax

PAIR = 128
HIDDEN_SIZE = 128
TILE = 96
CHAINS = 6
N = 192
TILES = 2


def set_ends(array, stream_key, smallest, high):
    spot = [jax.random.randint(jax.random.fold_in(stream_key, axis), (), 0, length) for axis, length in enumerate(array.shape)]
    longest = array.shape.index(max(array.shape))
    neighbour = spot[:longest] + [(spot[longest] + 1) % array.shape[longest]] + spot[longest + 1:]
    return array.at[tuple(spot)].set(smallest).at[tuple(neighbour)].set(high)


def steps_of(own_key, extent, pieces, smallest, top_value):
    level, own = 1.0, jax.random.fold_in(own_key, 6)
    for axis_at, parts in pieces:
        steps = jnp.exp(jax.random.uniform(jax.random.fold_in(own, axis_at), (parts,), jnp.float32, smallest / len(pieces), top_value / len(pieces)))
        level = level * jnp.repeat(steps, extent[axis_at] // parts).reshape([-1 if axis == axis_at else 1 for axis in range(len(extent))])
    return level


def length_profile(count, total, most, slope):
    loads = [(1 << 20) // math.isqrt(standing ** slope) + 1 for standing in range(2, count + 1)]
    surplus, counts = total - most - (count - 1), [1] * (count - 1)
    while surplus > 0:
        movable = [i for i in range(count - 1) if counts[i] < most]
        whole, remaining = sum([loads[i] for i in movable]), surplus
        for i in movable:
            extra = min(most - counts[i], max(1, remaining * loads[i] // whole), surplus)
            counts[i] = counts[i] + extra
            surplus = surplus - extra
    return np.array([most] + counts)


def ragged(key, count, total, bound, slope):
    if count == 2:
        one = jax.random.randint(key, (), max(1, total - bound), min(bound, total - 1) + 1)
        return jnp.stack([one, total - one])
    lengths = jnp.asarray(length_profile(count, total, bound, slope), jnp.int32)
    couples = (count - 1) // 2
    source_of, sink = lengths[1:1 + 2 * couples:2], lengths[2:2 + 2 * couples:2]
    margin = jnp.minimum(source_of - 1, bound - sink)
    passed = jax.random.randint(jax.random.fold_in(key, 1), (couples,), 0, 1 << 20) % (margin + 1)
    lengths = lengths.at[1:1 + 2 * couples:2].set(source_of - passed).at[2:2 + 2 * couples:2].set(sink + passed)
    return lengths[jax.random.permutation(jax.random.fold_in(key, 2), count)]


def noise(stream_key, dims, deviation, limit, pieces=(), dtype=jnp.bfloat16):
    entries = jax.random.normal(stream_key, dims, jnp.float32) * deviation
    if len(pieces) > 0:
        entries = steps_of(stream_key, dims, pieces, -0.22, 0.18) * entries
    return jnp.clip(entries, min=-limit, max=limit).astype(dtype)


def setup_inputs(seed: int = 0, part: int = 0) -> dict:
    seeds = jax.random.split(jax.random.key(seed), 8)
    part_splits = jax.random.split(jax.random.fold_in(seeds[7], part), 8)
    pair = noise(part_splits[0], (N, N, PAIR), 1.0, 6.0, ((0, 16), (1, 2)))
    tile_mask = set_ends((jax.random.randint(part_splits[1], (TILES, TILES), 0, 2) < 1).astype(jnp.int32), jax.random.fold_in(part_splits[1], 1), 0, 1)
    chain_ids = jnp.searchsorted(jnp.cumsum(ragged(part_splits[2], CHAINS, N, N // 3, 0)), jnp.arange(N), side="right").astype(jnp.int32)
    gain_in = jnp.clip(1.0 + 0.18 * jax.random.normal(seeds[3], (PAIR,), jnp.float32), 0.1, 1.9)
    w_proj = noise(seeds[4], (PAIR, 4 * HIDDEN_SIZE + PAIR), PAIR ** -0.5, 0.5)
    gain_mid = jnp.clip(1.0 + 0.18 * jax.random.normal(seeds[5], (HIDDEN_SIZE,), jnp.float32), 0.1, 1.9)
    w_out = noise(seeds[6], (HIDDEN_SIZE, PAIR), HIDDEN_SIZE ** -0.5, 0.5)
    return {"pair": pair, "tile_mask": tile_mask, "chain_ids": chain_ids, "gain_in": gain_in, "w_proj": w_proj, "gain_mid": gain_mid, "w_out": w_out}


def layer_norm(values, gain):
    center = values - lax.optimization_barrier(jnp.mean(values, axis=-1, keepdims=True))
    spread = lax.optimization_barrier(jnp.mean(center * center, axis=-1, keepdims=True))
    return center * lax.rsqrt(spread + 1e-05) * gain

def reference(pair, tile_mask, chain_ids, gain_in, w_proj, gain_mid, w_out):
    tile_of = (jnp.arange(N) // TILE).astype(jnp.int32)
    tile_vals = tile_mask[tile_of][:, tile_of].astype(jnp.float32)
    same_chain = chain_ids[:, None] == chain_ids[None, :]
    keep_mask = jnp.where(same_chain, jnp.float32(1.0), tile_vals).astype(jnp.float32)[..., None]
    normed = layer_norm(pair.astype(jnp.float32), gain_in).astype(jnp.bfloat16)
    projected = jnp.dot(normed.reshape(N * N, PAIR), w_proj, preferred_element_type=jnp.float32)
    projected = projected.reshape(N, N, 4 * HIDDEN_SIZE + PAIR)
    left_terms = jax.nn.sigmoid(projected[..., HIDDEN_SIZE:2 * HIDDEN_SIZE]) * projected[..., :HIDDEN_SIZE] * keep_mask
    right_terms = jax.nn.sigmoid(projected[..., 3 * HIDDEN_SIZE:4 * HIDDEN_SIZE]) * projected[..., 2 * HIDDEN_SIZE:3 * HIDDEN_SIZE] * keep_mask
    left_terms = left_terms.astype(jnp.bfloat16)
    right_terms = right_terms.astype(jnp.bfloat16)
    mixed_sum = jnp.einsum('kic,kjc->ijc', left_terms.astype(jnp.float32), right_terms.astype(jnp.float32))
    mixed_norm = layer_norm(mixed_sum, gain_mid).astype(jnp.bfloat16)
    projected_out = jnp.dot(mixed_norm.reshape(N * N, HIDDEN_SIZE), w_out, preferred_element_type=jnp.float32)
    projected_out = projected_out.reshape(N, N, PAIR)
    return (jax.nn.sigmoid(projected[..., 4 * HIDDEN_SIZE:]) * projected_out).astype(jnp.bfloat16)
```

```python
import functools
import math

import jax
import jax.numpy as jnp
from jax import lax
from jax.experimental import pallas as pl
from jax.experimental.pallas import tpu as pltpu
from jax.sharding import PartitionSpec as P

TILE = 96
LANES = 128
EPS = 1e-05
VMEM = pl.BlockSpec(memory_space=pltpu.VMEM)
SMEM = pl.BlockSpec(memory_space=pltpu.SMEM)


def steps(at, width, count):
    total = jnp.zeros_like(at)
    for edge in range(1, count):
        total += (at >= edge * width).astype(jnp.int32)
    return total


def sigmoid(values):
    return 0.5 * jnp.tanh(0.5 * values) + 0.5


def keep_of(tile_ref, chain_ref, rows, cols):
    tokens = chain_ref.shape[1]
    tiles = tile_ref.shape[1]
    positions = rows * cols
    at = lax.broadcasted_iota(jnp.int32, (1, positions), 1)
    row = steps(at, cols, rows)
    k = lax.axis_index("row") * rows + row
    i = lax.axis_index("col") * cols + at - row * cols
    token = lax.broadcasted_iota(jnp.int32, (tokens, positions), 0)
    pick = (token == k).astype(jnp.float32) - (token == i).astype(jnp.float32)
    chains = jnp.broadcast_to(chain_ref[...].astype(jnp.bfloat16), (8, tokens))
    apart = jnp.dot(chains, pick.astype(jnp.bfloat16), preferred_element_type=jnp.float32)[:1]
    k_tile = steps(k, TILE, tiles)
    i_tile = steps(i, TILE, tiles)
    tile_vals = jnp.zeros((1, positions), jnp.float32)
    for a in range(tiles):
        for b in range(tiles):
            here = (k_tile == a) & (i_tile == b)
            tile_vals = jnp.where(here, tile_ref[a, b].astype(jnp.float32), tile_vals)
    return jnp.where(apart == 0.0, 1.0, tile_vals)


def project_kernel(
    rows, cols, shares, tile_ref, chain_ref, pair_ref, gain_ref, w_ref, left_ref, right_ref, gate_ref,
    w_t, left_f32, right_f32,
):
    hidden = (w_ref.shape[1] - w_ref.shape[0]) // 4
    own = hidden // shares
    keep = keep_of(tile_ref, chain_ref, rows, cols)
    w_t[...] = w_ref[...].T
    gain = gain_ref[...]
    for group in range(rows * cols // LANES):
        block = pair_ref[group * LANES : (group + 1) * LANES, :].astype(jnp.float32).T
        center = block - jnp.mean(block, axis=0, keepdims=True)
        spread = jnp.mean(center * center, axis=0, keepdims=True)
        normed = (center * lax.rsqrt(spread + EPS) * gain).astype(jnp.bfloat16)
        projected = jnp.dot(w_t[...], normed, preferred_element_type=jnp.float32)
        kept = keep[:, group * LANES : (group + 1) * LANES]
        left = sigmoid(projected[hidden : 2 * hidden]) * projected[:hidden] * kept
        right = sigmoid(projected[3 * hidden : 4 * hidden]) * projected[2 * hidden : 3 * hidden] * kept
        left_f32[:, group * own : (group + 1) * own, :] = left.reshape(shares, own, LANES)
        right_f32[:, group * own : (group + 1) * own, :] = right.reshape(shares, own, LANES)
        gate_ref[group] = sigmoid(projected[4 * hidden :])
    left_ref[...] = left_f32[...].astype(jnp.bfloat16)
    right_ref[...] = right_f32[...].astype(jnp.bfloat16)


def take_channel(ref, channel, own, cols):
    cycle = math.lcm(cols, LANES)
    groups, tokens = cycle // LANES, cycle // cols
    count = ref.shape[0] // (own * groups)
    lanes = [
        ref[pl.ds(group * own + channel, count, stride=own * groups), :] for group in range(groups)
    ]
    found = []
    for token in range(tokens):
        start, pieces = token * cols, []
        while start < (token + 1) * cols:
            group = start // LANES
            end = min((group + 1) * LANES, (token + 1) * cols)
            pieces.append(lanes[group][:, start - group * LANES : end - group * LANES])
            start = end
        found.append(jnp.concatenate(pieces, axis=1).astype(jnp.bfloat16))
    return jnp.concatenate(found, axis=0)


def put_channel(ref, first, held, channel, own, cols):
    cycle = math.lcm(cols, LANES)
    groups, tokens = cycle // LANES, cycle // cols
    count = cols // tokens
    lines = [
        jnp.concatenate(
            [held[piece, pl.ds(token, count, stride=tokens), :] for piece in range(held.shape[0])], axis=1
        )
        for token in range(tokens)
    ]
    for group in range(groups):
        start, pieces = group * LANES, []
        while start < (group + 1) * LANES:
            token = start // cols
            end = min((token + 1) * cols, (group + 1) * LANES)
            pieces.append(lines[token][:, start - token * cols : end - token * cols])
            start = end
        ref[pl.ds(first + group * own + channel, count, stride=own * groups), :] = jnp.concatenate(
            pieces, axis=1
        )


def triangle_kernel(own, cols, left_ref, other_ref, right_ref, mixed_ref, lefts, rights, held, mixed):
    lines = rights.shape[0]
    at = lax.axis_index("col")
    lefts[at] = left_ref[...].astype(jnp.float32).reshape(lines, LANES)
    lefts[1 - at] = other_ref[...].astype(jnp.float32).reshape(lines, LANES)
    rights[...] = right_ref[...].astype(jnp.float32).reshape(lines, LANES)
    for channel in range(own):
        right = take_channel(rights, channel, own, cols)
        for half in range(2):
            left = take_channel(lefts.at[half], channel, own, cols)
            total = lax.dot_general(
                left, right, (((0,), (0,)), ((), ())), preferred_element_type=jnp.float32
            )
            for start in range(0, cols, LANES):
                width = min(LANES, cols - start)
                held[half, start // LANES, :, :width] = total[:, start : start + width]
            put_channel(mixed, half * (lines // 2), held.at[half], channel, own, cols)
    mixed_ref[...] = mixed[...].astype(jnp.bfloat16).reshape(mixed_ref.shape)


def output_kernel(own, mixed_ref, gate_ref, gain_ref, w_ref, update_ref, mixed):
    shares = mixed_ref.shape[0]
    mixed[...] = mixed_ref[...].astype(jnp.float32)
    w_t = w_ref[...].T
    gain = gain_ref[...]
    for group in range(gate_ref.shape[0]):
        block = mixed[:, group * own : (group + 1) * own, :].reshape(shares * own, LANES)
        center = block - jnp.mean(block, axis=0, keepdims=True)
        spread = jnp.mean(center * center, axis=0, keepdims=True)
        normed = (center * lax.rsqrt(spread + EPS) * gain).astype(jnp.bfloat16)
        projected = jnp.dot(w_t, normed, preferred_element_type=jnp.float32)
        update = (gate_ref[group] * projected).T
        update_ref[group * LANES : (group + 1) * LANES, :] = update.astype(jnp.bfloat16)


def on_device(shares, pair, tile_mask, chain_ids, gain_in, w_proj, gain_mid, w_out):
    rows, cols, width = pair.shape
    hidden = w_out.shape[0]
    own = hidden // shares
    positions = rows * cols
    groups = positions // LANES
    lines = groups * own
    message = jax.ShapeDtypeStruct((shares, lines, LANES), jnp.bfloat16)
    params = pltpu.CompilerParams(vmem_limit_bytes=32 * 1024 * 1024)
    left, right, gate = pl.pallas_call(
        functools.partial(project_kernel, rows, cols, shares),
        out_shape=(message, message, jax.ShapeDtypeStruct((groups, width, LANES), jnp.float32)),
        in_specs=[SMEM, VMEM, VMEM, VMEM, VMEM],
        out_specs=(VMEM, VMEM, VMEM),
        scratch_shapes=[
            pltpu.VMEM((w_proj.shape[1], width), jnp.bfloat16),
            pltpu.VMEM((shares, lines, LANES), jnp.float32),
            pltpu.VMEM((shares, lines, LANES), jnp.float32),
        ],
        compiler_params=params,
        name="project",
    )(tile_mask, chain_ids[None, :], pair.reshape(positions, width), gain_in[:, None], w_proj)
    left = lax.all_to_all(left, "row", split_axis=0, concat_axis=0, tiled=True)
    other = lax.ppermute(left, "col", [(0, 1), (1, 0)])
    right = lax.all_to_all(right, "row", split_axis=0, concat_axis=0, tiled=True)
    mixed = pl.pallas_call(
        functools.partial(triangle_kernel, own, cols),
        out_shape=message,
        in_specs=[VMEM, VMEM, VMEM],
        out_specs=VMEM,
        scratch_shapes=[
            pltpu.VMEM((2, shares * lines, LANES), jnp.float32),
            pltpu.VMEM((shares * lines, LANES), jnp.float32),
            pltpu.VMEM((2, pl.cdiv(cols, LANES), cols, LANES), jnp.float32),
            pltpu.VMEM((shares * lines, LANES), jnp.float32),
        ],
        compiler_params=params,
        name="triangle",
    )(left, other, right)
    mixed = lax.all_to_all(mixed, "row", split_axis=0, concat_axis=0, tiled=True)
    update = pl.pallas_call(
        functools.partial(output_kernel, own),
        out_shape=jax.ShapeDtypeStruct((positions, width), jnp.bfloat16),
        in_specs=[VMEM, VMEM, VMEM, VMEM],
        out_specs=VMEM,
        scratch_shapes=[pltpu.VMEM((shares, lines, LANES), jnp.float32)],
        compiler_params=params,
        name="output",
    )(mixed, gate, gain_mid[:, None], w_out)
    return update.reshape(rows, cols, width)


def solution(mesh):
    in_specs = (P(("grp", "row"), "col", None), P("grp", None), P("grp"), P(), P(), P(), P())
    out_specs = P(("grp", "row"), "col", None)
    return jax.shard_map(
        functools.partial(on_device, mesh.shape["row"]),
        mesh=mesh,
        in_specs=in_specs,
        out_specs=out_specs,
        check_vma=False,
    )
```

```python
import functools
import math

import jax
import jax.numpy as jnp
from jax import lax
from jax.experimental import pallas as pl
from jax.experimental.pallas import tpu as pltpu
from jax.sharding import PartitionSpec as P

TILE = 96
LANES = 128
EPS = 1e-05
VMEM = pl.BlockSpec(memory_space=pltpu.VMEM)
HBM = pl.BlockSpec(memory_space=pltpu.HBM)
SMEM = pl.BlockSpec(memory_space=pltpu.SMEM)


def steps(at, width, count):
    total = jnp.zeros_like(at)
    for edge in range(1, count):
        total += (at >= edge * width).astype(jnp.int32)
    return total


def sigmoid(values):
    return 0.5 * jnp.tanh(0.5 * values) + 0.5


def keep_of(tile_ref, chain_ref, rows, cols):
    tokens = chain_ref.shape[1]
    tiles = tile_ref.shape[1]
    positions = rows * cols
    at = lax.broadcasted_iota(jnp.int32, (1, positions), 1)
    row = steps(at, cols, rows)
    k = lax.axis_index("row") * rows + row
    i = lax.axis_index("col") * cols + at - row * cols
    token = lax.broadcasted_iota(jnp.int32, (tokens, positions), 0)
    pick = (token == k).astype(jnp.float32) - (token == i).astype(jnp.float32)
    chains = jnp.broadcast_to(chain_ref[...].astype(jnp.bfloat16), (8, tokens))
    apart = jnp.dot(chains, pick.astype(jnp.bfloat16), preferred_element_type=jnp.float32)[:1]
    k_tile = steps(k, TILE, tiles)
    i_tile = steps(i, TILE, tiles)
    tile_vals = jnp.zeros((1, positions), jnp.float32)
    for a in range(tiles):
        for b in range(tiles):
            here = (k_tile == a) & (i_tile == b)
            tile_vals = jnp.where(here, tile_ref[a, b].astype(jnp.float32), tile_vals)
    return jnp.where(apart == 0.0, 1.0, tile_vals)


def column(row):
    return jnp.broadcast_to(row, (8, row.shape[1])).T[:, :1]


def project_kernel(rows, cols, shares, *refs):
    tile_ref, chain_ref, pair_hbm, gain_hbm, w_hbm = refs[:5]
    left_refs, right_refs = refs[5 : 5 + shares], refs[5 + shares : 5 + 2 * shares]
    gate_ref, pair_ref, gain_ref, w_ref, w_t, left_f32, right_f32, sems = refs[5 + 2 * shares :]
    copies = [
        pltpu.make_async_copy(src, dst, sems.at[at])
        for at, (src, dst) in enumerate(((w_hbm, w_ref), (gain_hbm, gain_ref), (pair_hbm, pair_ref)))
    ]
    for copy in copies:
        copy.start()
    hidden = (w_ref.shape[1] - w_ref.shape[0]) // 4
    own = hidden // shares
    keep = keep_of(tile_ref, chain_ref, rows, cols)
    for copy in copies:
        copy.wait()
    w_t[...] = w_ref[...].T
    gain = column(gain_ref[...])
    for group in range(rows * cols // LANES):
        block = pair_ref[group * LANES : (group + 1) * LANES, :].astype(jnp.float32).T
        center = block - jnp.mean(block, axis=0, keepdims=True)
        spread = jnp.mean(center * center, axis=0, keepdims=True)
        normed = (center * lax.rsqrt(spread + EPS) * gain).astype(jnp.bfloat16)
        projected = jnp.dot(w_t[...], normed, preferred_element_type=jnp.float32)
        kept = keep[:, group * LANES : (group + 1) * LANES]
        left = sigmoid(projected[hidden : 2 * hidden]) * projected[:hidden] * kept
        right = sigmoid(projected[3 * hidden : 4 * hidden]) * projected[2 * hidden : 3 * hidden] * kept
        left_f32[:, group * own : (group + 1) * own, :] = left.reshape(shares, own, LANES)
        right_f32[:, group * own : (group + 1) * own, :] = right.reshape(shares, own, LANES)
        gate_ref[group] = sigmoid(projected[4 * hidden :])
    at = lax.axis_index("row")
    for step in range(shares):
        left_refs[step][...] = left_f32[at ^ step].astype(jnp.bfloat16)
        right_refs[step][...] = right_f32[at ^ step].astype(jnp.bfloat16)


def take_channel(ref, channel, own, cols):
    cycle = math.lcm(cols, LANES)
    groups, tokens = cycle // LANES, cycle // cols
    count = ref.shape[0] // (own * groups)
    lanes = [
        ref[pl.ds(group * own + channel, count, stride=own * groups), :] for group in range(groups)
    ]
    found = []
    for token in range(tokens):
        start, pieces = token * cols, []
        while start < (token + 1) * cols:
            group = start // LANES
            end = min((group + 1) * LANES, (token + 1) * cols)
            pieces.append(lanes[group][:, start - group * LANES : end - group * LANES])
            start = end
        found.append(jnp.concatenate(pieces, axis=1).astype(jnp.bfloat16))
    return jnp.concatenate(found, axis=0)


def put_channel(ref, first, held, channel, own, cols):
    cycle = math.lcm(cols, LANES)
    groups, tokens = cycle // LANES, cycle // cols
    count = cols // tokens
    lines = [
        jnp.concatenate(
            [held[piece, pl.ds(token, count, stride=tokens), :] for piece in range(held.shape[0])], axis=1
        )
        for token in range(tokens)
    ]
    for group in range(groups):
        start, pieces = group * LANES, []
        while start < (group + 1) * LANES:
            token = start // cols
            end = min((token + 1) * cols, (group + 1) * LANES)
            pieces.append(lines[token][:, start - token * cols : end - token * cols])
            start = end
        ref[pl.ds(first + group * own + channel, count, stride=own * groups), :] = jnp.concatenate(
            pieces, axis=1
        )


def collect_kernel(*refs):
    for step, ref in enumerate(refs[:-1]):
        refs[-1][step] = ref[...]


def triangle_kernel(own, cols, shares, left_ref, other_ref, *refs):
    right_refs, mixed_refs = refs[:shares], refs[shares : 2 * shares]
    lefts, rights, held, mixed = refs[2 * shares :]
    lines = rights.shape[0]
    at = lax.axis_index("col")
    lefts[at] = left_ref[...].astype(jnp.float32).reshape(lines, LANES)
    lefts[1 - at] = other_ref[...].astype(jnp.float32).reshape(lines, LANES)
    each = lines // shares
    for step in range(shares):
        rights[step * each : (step + 1) * each, :] = right_refs[step][...].astype(jnp.float32)
    for channel in range(own):
        right = take_channel(rights, channel, own, cols)
        for half in range(2):
            left = take_channel(lefts.at[half], channel, own, cols)
            total = lax.dot_general(
                left, right, (((0,), (0,)), ((), ())), preferred_element_type=jnp.float32
            )
            for start in range(0, cols, LANES):
                width = min(LANES, cols - start)
                held[half, start // LANES, :, :width] = total[:, start : start + width]
            put_channel(mixed, half * (lines // 2), held.at[half], channel, own, cols)
    at = lax.axis_index("row")
    for step in range(shares):
        first = pl.multiple_of((at ^ step) * each, 8)
        mixed_refs[step][...] = mixed[pl.ds(first, each), :].astype(jnp.bfloat16)


def output_kernel(own, shares, *refs):
    gate_ref, gain_ref, w_ref, update_ref, mixed = refs[shares:]
    at = lax.axis_index("row")
    for step in range(shares):
        mixed[at ^ step] = refs[step][...].astype(jnp.float32)
    w_t = w_ref[...].T
    gain = column(gain_ref[...])
    for group in range(gate_ref.shape[0]):
        block = mixed[:, group * own : (group + 1) * own, :].reshape(shares * own, LANES)
        center = block - jnp.mean(block, axis=0, keepdims=True)
        spread = jnp.mean(center * center, axis=0, keepdims=True)
        normed = (center * lax.rsqrt(spread + EPS) * gain).astype(jnp.bfloat16)
        projected = jnp.dot(w_t, normed, preferred_element_type=jnp.float32)
        update = (gate_ref[group] * projected).T
        update_ref[group * LANES : (group + 1) * LANES, :] = update.astype(jnp.bfloat16)


def exchange(blocks):
    shares = len(blocks)
    return [blocks[0]] + [
        lax.ppermute(blocks[step], "row", [(src, src ^ step) for src in range(shares)])
        for step in range(1, shares)
    ]


def on_device(shares, pair, tile_mask, chain_ids, gain_in, w_proj, gain_mid, w_out):
    rows, cols, width = pair.shape
    hidden = w_out.shape[0]
    own = hidden // shares
    positions = rows * cols
    groups = positions // LANES
    lines = groups * own
    message = jax.ShapeDtypeStruct((lines, LANES), jnp.bfloat16)
    params = pltpu.CompilerParams(vmem_limit_bytes=32 * 1024 * 1024)
    outs = pl.pallas_call(
        functools.partial(project_kernel, rows, cols, shares),
        out_shape=[message] * (2 * shares)
        + [jax.ShapeDtypeStruct((groups, width, LANES), jnp.float32)],
        in_specs=[SMEM, VMEM, HBM, HBM, HBM],
        out_specs=[VMEM] * (2 * shares + 1),
        scratch_shapes=[
            pltpu.VMEM((positions, width), jnp.bfloat16),
            pltpu.VMEM((1, width), jnp.float32),
            pltpu.VMEM(w_proj.shape, jnp.bfloat16),
            pltpu.VMEM((w_proj.shape[1], width), jnp.bfloat16),
            pltpu.VMEM((shares, lines, LANES), jnp.float32),
            pltpu.VMEM((shares, lines, LANES), jnp.float32),
            pltpu.SemaphoreType.DMA((3,)),
        ],
        compiler_params=params,
        name="project",
    )(tile_mask, chain_ids[None, :], pair.reshape(positions, width), gain_in[None, :], w_proj)
    lefts, rights, gate = outs[:shares], outs[shares : 2 * shares], outs[2 * shares]
    lefts, rights = exchange(lefts), exchange(rights)
    left = pl.pallas_call(
        collect_kernel,
        out_shape=jax.ShapeDtypeStruct((shares, lines, LANES), jnp.bfloat16),
        in_specs=[VMEM] * shares,
        out_specs=VMEM,
        compiler_params=params,
        name="collect",
    )(*lefts)
    other = lax.ppermute(left, "col", [(0, 1), (1, 0)])
    mixed = pl.pallas_call(
        functools.partial(triangle_kernel, own, cols, shares),
        out_shape=[message] * shares,
        in_specs=[VMEM] * (2 + shares),
        out_specs=[VMEM] * shares,
        scratch_shapes=[
            pltpu.VMEM((2, shares * lines, LANES), jnp.float32),
            pltpu.VMEM((shares * lines, LANES), jnp.float32),
            pltpu.VMEM((2, pl.cdiv(cols, LANES), cols, LANES), jnp.float32),
            pltpu.VMEM((shares * lines, LANES), jnp.float32),
        ],
        compiler_params=params,
        name="triangle",
    )(left, other, *rights)
    mixed = exchange(mixed)
    update = pl.pallas_call(
        functools.partial(output_kernel, own, shares),
        out_shape=jax.ShapeDtypeStruct((positions, width), jnp.bfloat16),
        in_specs=[VMEM] * (shares + 3),
        out_specs=VMEM,
        scratch_shapes=[pltpu.VMEM((shares, lines, LANES), jnp.float32)],
        compiler_params=params,
        name="output",
    )(*mixed, gate, gain_mid[None, :], w_out)
    return update.reshape(rows, cols, width)


def solution(mesh):
    in_specs = (P(("grp", "row"), "col", None), P("grp", None), P("grp"), P(), P(), P(), P())
    out_specs = P(("grp", "row"), "col", None)
    return jax.shard_map(
        functools.partial(on_device, mesh.shape["row"]),
        mesh=mesh,
        in_specs=in_specs,
        out_specs=out_specs,
        check_vma=False,
    )
```

```python
import functools
import math

import jax
import jax.numpy as jnp
from jax import lax
from jax.experimental import pallas as pl
from jax.experimental.pallas import tpu as pltpu
from jax.sharding import PartitionSpec as P

TILE = 96
LANES = 128
EPS = 1e-05
VMEM_BYTES = 32 * 1024 * 1024
WHOLE_VMEM_BYTES = 64 * 1024 * 1024
VMEM = pl.BlockSpec(memory_space=pltpu.VMEM)
HBM = pl.BlockSpec(memory_space=pltpu.HBM)
SMEM = pl.BlockSpec(memory_space=pltpu.SMEM)


def column(row):
    return jnp.broadcast_to(row, (8, row.shape[1])).T[:, :1]


def steps(at, width, count):
    total = jnp.zeros_like(at)
    for edge in range(1, count):
        total += (at >= edge * width).astype(jnp.int32)
    return total


def sigmoid(values):
    return 0.5 * jnp.tanh(0.5 * values) + 0.5


def keep_of(tile_ref, chain_ref, rows, cols):
    tokens = chain_ref.shape[1]
    tiles = tile_ref.shape[1]
    positions = rows * cols
    at = lax.broadcasted_iota(jnp.int32, (1, positions), 1)
    row = steps(at, cols, rows)
    k = lax.axis_index("row") * rows + row
    i = lax.axis_index("col") * cols + at - row * cols
    token = lax.broadcasted_iota(jnp.int32, (tokens, positions), 0)
    pick = (token == k).astype(jnp.float32) - (token == i).astype(jnp.float32)
    chains = jnp.broadcast_to(chain_ref[...].astype(jnp.bfloat16), (8, tokens))
    apart = jnp.dot(chains, pick.astype(jnp.bfloat16), preferred_element_type=jnp.float32)[:1]
    k_tile = steps(k, TILE, tiles)
    i_tile = steps(i, TILE, tiles)
    tile_vals = jnp.zeros((1, positions), jnp.float32)
    for a in range(tiles):
        for b in range(tiles):
            here = (k_tile == a) & (i_tile == b)
            tile_vals = jnp.where(here, tile_ref[a, b].astype(jnp.float32), tile_vals)
    return jnp.where(apart == 0.0, 1.0, tile_vals)


def cycle_of(cols):
    cycle = math.lcm(cols, LANES)
    return cycle // cols, cycle // LANES


def fetch(sems, *pairs):
    copies = [pltpu.make_async_copy(src, dst, sems.at[at]) for at, (src, dst) in enumerate(pairs)]
    for copy in copies:
        copy.start()
    for copy in copies:
        copy.wait()


def project_kernel(
    rows, cols, shares, tile_hbm, chain_hbm, pair_hbm, gain_hbm, w_hbm, message_ref, gate_ref,
    tile_ref, chain_ref, pair_ref, gain_ref, w_ref, message, sems,
):
    fetch(
        sems,
        (w_hbm, w_ref),
        (pair_hbm, pair_ref),
        (gain_hbm, gain_ref),
        (chain_hbm, chain_ref),
        (tile_hbm, tile_ref),
    )
    hidden = (w_ref.shape[1] - w_ref.shape[0]) // 4
    own = hidden // shares
    groups = cycle_of(cols)[1]
    keep = keep_of(tile_ref, chain_ref, rows, cols)
    w_t = w_ref[...].T
    gain = column(gain_ref[...])
    for group in range(rows * cols // LANES):
        block = pair_ref[group * LANES : (group + 1) * LANES, :].astype(jnp.float32).T
        center = block - jnp.mean(block, axis=0, keepdims=True)
        spread = jnp.mean(center * center, axis=0, keepdims=True)
        normed = (center * lax.rsqrt(spread + EPS) * gain).astype(jnp.bfloat16)
        projected = jnp.dot(w_t, normed, preferred_element_type=jnp.float32)
        kept = keep[:, group * LANES : (group + 1) * LANES]
        for side in range(2):
            value = projected[2 * side * hidden : (2 * side + 1) * hidden]
            gate = projected[(2 * side + 1) * hidden : (2 * side + 2) * hidden]
            line = (group // groups * 2 + side) * groups + group % groups
            message[:, line * own : (line + 1) * own, :] = (sigmoid(gate) * value * kept).reshape(
                shares, own, LANES
            )
        gate_ref[group] = sigmoid(projected[4 * hidden :])
    message_ref[...] = message[...].astype(jnp.bfloat16)


def take_channel(ref, side, channel, own, cols):
    tokens, groups = cycle_of(cols)
    count = ref.shape[0] // (own * groups * 2)
    lanes = [
        ref[pl.ds((side * groups + group) * own + channel, count, stride=own * groups * 2), :]
        for group in range(groups)
    ]
    found = []
    for token in range(tokens):
        start, pieces = token * cols, []
        while start < (token + 1) * cols:
            group = start // LANES
            end = min((group + 1) * LANES, (token + 1) * cols)
            pieces.append(lanes[group][:, start - group * LANES : end - group * LANES])
            start = end
        found.append(jnp.concatenate(pieces, axis=1).astype(jnp.bfloat16))
    return jnp.concatenate(found, axis=0)


def put_channel(ref, held, channel, own, cols):
    tokens, groups = cycle_of(cols)
    count = cols // tokens
    lines = [
        jnp.concatenate(
            [held[piece, pl.ds(token, count, stride=tokens), :] for piece in range(held.shape[0])], axis=1
        )
        for token in range(tokens)
    ]
    for group in range(groups):
        start, pieces = group * LANES, []
        while start < (group + 1) * LANES:
            token = start // cols
            end = min((token + 1) * cols, (group + 1) * LANES)
            pieces.append(lines[token][:, start - token * cols : end - token * cols])
            start = end
        ref[pl.ds(group * own + channel, count, stride=own * groups), :] = jnp.concatenate(pieces, axis=1)


def triangle(own, cols, lefts, rights, held, mixed):
    for channel in range(own):
        right = take_channel(rights, 1, channel, own, cols)
        left = take_channel(lefts, 0, channel, own, cols)
        total = lax.dot_general(left, right, (((0,), (0,)), ((), ())), preferred_element_type=jnp.float32)
        at = channel % 2
        for start in range(0, cols, LANES):
            width = min(LANES, cols - start)
            held[at, start // LANES, :, :width] = total[:, start : start + width]
        put_channel(mixed, held.at[at], channel, own, cols)


def first_kernel(own, cols, own_ref, mixed_ref, ours, held, mixed):
    ours[...] = own_ref[...].astype(jnp.float32).reshape(ours.shape)
    triangle(own, cols, ours, ours, held, mixed)
    mixed_ref[...] = mixed[...].astype(jnp.bfloat16).reshape(mixed_ref.shape)


def second_kernel(own, cols, own_ref, other_ref, first_ref, mixed_ref, ours, others, held, mixed):
    half = first_ref.shape[0]
    at = lax.axis_index("col")
    ours[...] = own_ref[...].astype(jnp.float32).reshape(ours.shape)
    others[...] = other_ref[...].astype(jnp.float32).reshape(others.shape)
    mixed_ref[pl.ds(at * half, half)] = first_ref[...]
    triangle(own, cols, others, ours, held, mixed)
    mixed_ref[pl.ds((1 - at) * half, half)] = mixed[...].astype(jnp.bfloat16).reshape(first_ref.shape)


def output_kernel(own, mixed_ref, gate_ref, gain_ref, w_ref, update_ref, mixed):
    shares = mixed_ref.shape[0]
    mixed[...] = mixed_ref[...].astype(jnp.float32)
    w_t = w_ref[...].T
    gain = column(gain_ref[...])
    for group in range(gate_ref.shape[0]):
        block = mixed[:, group * own : (group + 1) * own, :].reshape(shares * own, LANES)
        center = block - jnp.mean(block, axis=0, keepdims=True)
        spread = jnp.mean(center * center, axis=0, keepdims=True)
        normed = (center * lax.rsqrt(spread + EPS) * gain).astype(jnp.bfloat16)
        projected = jnp.dot(w_t, normed, preferred_element_type=jnp.float32)
        update = (gate_ref[group] * projected).T
        update_ref[group * LANES : (group + 1) * LANES, :] = update.astype(jnp.bfloat16)


def on_device(shares, pair, tile_mask, chain_ids, gain_in, w_proj, gain_mid, w_out):
    rows, cols, width = pair.shape
    hidden = w_out.shape[0]
    own = hidden // shares
    positions = rows * cols
    lines = positions // LANES * own
    half = shares // 2
    params = pltpu.CompilerParams(vmem_limit_bytes=VMEM_BYTES)
    tokens = chain_ids.shape[0]
    message, gate = pl.pallas_call(
        functools.partial(project_kernel, rows, cols, shares),
        out_shape=(
            jax.ShapeDtypeStruct((shares, 2 * lines, LANES), jnp.bfloat16),
            jax.ShapeDtypeStruct((positions // LANES, width, LANES), jnp.float32),
        ),
        in_specs=[HBM] * 5,
        out_specs=(VMEM, VMEM),
        scratch_shapes=[
            pltpu.SMEM(tile_mask.shape, jnp.int32),
            pltpu.VMEM((1, tokens), jnp.int32),
            pltpu.VMEM((positions, width), jnp.bfloat16),
            pltpu.VMEM((1, width), jnp.float32),
            pltpu.VMEM(w_proj.shape, jnp.bfloat16),
            pltpu.VMEM((shares, 2 * lines, LANES), jnp.float32),
            pltpu.SemaphoreType.DMA((5,)),
        ],
        compiler_params=pltpu.CompilerParams(vmem_limit_bytes=WHOLE_VMEM_BYTES),
        name="project",
    )(tile_mask, chain_ids[None, :], pair.reshape(positions, width), gain_in[None, :], w_proj)
    message = lax.all_to_all(message, "row", split_axis=0, concat_axis=0, tiled=True)
    other = lax.ppermute(message, "col", [(0, 1), (1, 0)])
    blocks = pltpu.VMEM((shares * 2 * lines, LANES), jnp.float32)
    held = pltpu.VMEM((2, pl.cdiv(cols, LANES), cols, LANES), jnp.float32)
    out = pltpu.VMEM((half * lines, LANES), jnp.float32)
    first = pl.pallas_call(
        functools.partial(first_kernel, own, cols),
        out_shape=jax.ShapeDtypeStruct((half, lines, LANES), jnp.bfloat16),
        in_specs=[VMEM],
        out_specs=VMEM,
        scratch_shapes=[blocks, held, out],
        compiler_params=params,
        cost_estimate=pl.CostEstimate(
            flops=2 * own * cols * cols * tokens, bytes_accessed=8 * shares * lines * LANES, transcendentals=0
        ),
        name="first",
    )(message)
    mixed = pl.pallas_call(
        functools.partial(second_kernel, own, cols),
        out_shape=jax.ShapeDtypeStruct((shares, lines, LANES), jnp.bfloat16),
        in_specs=[VMEM, VMEM, VMEM],
        out_specs=VMEM,
        scratch_shapes=[blocks, blocks, held, out],
        compiler_params=params,
        name="second",
    )(message, other, first)
    mixed = lax.all_to_all(mixed, "row", split_axis=0, concat_axis=0, tiled=True)
    update = pl.pallas_call(
        functools.partial(output_kernel, own),
        out_shape=jax.ShapeDtypeStruct((positions, width), jnp.bfloat16),
        in_specs=[VMEM, VMEM, VMEM, VMEM],
        out_specs=VMEM,
        scratch_shapes=[pltpu.VMEM((shares, lines, LANES), jnp.float32)],
        compiler_params=params,
        name="output",
    )(mixed, gate, gain_mid[None, :], w_out)
    return update.reshape(rows, cols, width)


def solution(mesh):
    in_specs = (P(("grp", "row"), "col", None), P("grp", None), P("grp"), P(), P(), P(), P())
    out_specs = P(("grp", "row"), "col", None)
    return jax.shard_map(
        functools.partial(on_device, mesh.shape["row"]),
        mesh=mesh,
        in_specs=in_specs,
        out_specs=out_specs,
        check_vma=False,
    )
```

```python
import functools
import math

import jax
import jax.numpy as jnp
from jax import lax
from jax.experimental import pallas as pl
from jax.experimental.pallas import tpu as pltpu
from jax.sharding import PartitionSpec as P

TILE = 96
LANES = 128
EPS = 1e-05
PARTS = 2
VMEM_BYTES = 32 * 1024 * 1024
WHOLE_VMEM_BYTES = 64 * 1024 * 1024
VMEM = pl.BlockSpec(memory_space=pltpu.VMEM)
HBM = pl.BlockSpec(memory_space=pltpu.HBM)
SMEM = pl.BlockSpec(memory_space=pltpu.SMEM)


def column(row):
    return jnp.broadcast_to(row, (8, row.shape[1])).T[:, :1]


def steps(at, width, count):
    total = jnp.zeros_like(at)
    for edge in range(1, count):
        total += (at >= edge * width).astype(jnp.int32)
    return total


def sigmoid(values):
    return 0.5 * jnp.tanh(0.5 * values) + 0.5


def keep_of(tile_ref, chain_ref, rows, cols):
    tokens = chain_ref.shape[1]
    tiles = tile_ref.shape[1]
    positions = rows * cols
    at = lax.broadcasted_iota(jnp.int32, (1, positions), 1)
    row = steps(at, cols, rows)
    k = lax.axis_index("row") * rows + row
    i = lax.axis_index("col") * cols + at - row * cols
    token = lax.broadcasted_iota(jnp.int32, (tokens, positions), 0)
    pick = (token == k).astype(jnp.float32) - (token == i).astype(jnp.float32)
    chains = jnp.broadcast_to(chain_ref[...].astype(jnp.bfloat16), (8, tokens))
    apart = jnp.dot(chains, pick.astype(jnp.bfloat16), preferred_element_type=jnp.float32)[:1]
    k_tile = steps(k, TILE, tiles)
    i_tile = steps(i, TILE, tiles)
    tile_vals = jnp.zeros((1, positions), jnp.float32)
    for a in range(tiles):
        for b in range(tiles):
            here = (k_tile == a) & (i_tile == b)
            tile_vals = jnp.where(here, tile_ref[a, b].astype(jnp.float32), tile_vals)
    return jnp.where(apart == 0.0, 1.0, tile_vals)


def cycle_of(cols):
    cycle = math.lcm(cols, LANES)
    return cycle // cols, cycle // LANES


def fetch(sems, *pairs):
    copies = [pltpu.make_async_copy(src, dst, sems.at[at]) for at, (src, dst) in enumerate(pairs)]
    for copy in copies:
        copy.start()
    for copy in copies:
        copy.wait()


def project_kernel(
    rows, cols, peers, tile_hbm, chain_hbm, pair_hbm, gain_hbm, w_hbm, message_ref, normed_ref,
    tile_ref, chain_ref, pair_ref, gain_ref, w_ref, sems,
):
    fetch(
        sems,
        (w_hbm, w_ref),
        (pair_hbm, pair_ref),
        (gain_hbm, gain_ref),
        (chain_hbm, chain_ref),
        (tile_hbm, tile_ref),
    )
    hidden = (w_ref.shape[1] - w_ref.shape[0]) // 4
    own = hidden // peers
    groups = cycle_of(cols)[1]
    keep = keep_of(tile_ref, chain_ref, rows, cols)
    w_t = w_ref[:, : 4 * hidden].T
    gain = column(gain_ref[...])
    positions = rows * cols
    for start in range(0, positions, 2 * LANES):
        end = min(start + 2 * LANES, positions)
        block = pair_ref[start:end, :].astype(jnp.float32).T
        center = block - jnp.mean(block, axis=0, keepdims=True)
        spread = jnp.mean(center * center, axis=0, keepdims=True)
        normed = (center * lax.rsqrt(spread + EPS) * gain).astype(jnp.bfloat16)
        normed_ref[:, start:end] = normed
        projected = jnp.dot(w_t, normed, preferred_element_type=jnp.float32)
        kept = keep[:, start:end]
        for side in range(2):
            value = projected[2 * side * hidden : (2 * side + 1) * hidden]
            gate = projected[(2 * side + 1) * hidden : (2 * side + 2) * hidden]
            sent = (sigmoid(gate) * value * kept).astype(jnp.bfloat16)
            for group in range(start // LANES, end // LANES):
                line = (group // groups * 2 + side) * groups + group % groups
                at = group * LANES - start
                message_ref[:, line * own : (line + 1) * own, :] = sent[:, at : at + LANES].reshape(
                    peers, own, LANES
                )


def gate_kernel(normed_ref, w_hbm, gain_hbm, w_out_hbm, gate_ref, w_out_ref, gain_ref, w, w_out, gain, sems):
    width = w_hbm.shape[0]
    last = w_hbm.shape[1] - width
    fetch(sems, (w_hbm, w), (w_out_hbm, w_out), (gain_hbm, gain))
    gate_ref[...] = sigmoid(
        jnp.dot(w[:, last:].T, normed_ref[...], preferred_element_type=jnp.float32)
    )
    w_out_ref[...] = w_out[...].T
    gain_ref[...] = jnp.broadcast_to(column(gain[...]), gain_ref.shape)


def take_channel(ref, side, channel, own, cols):
    tokens, groups = cycle_of(cols)
    count = ref.shape[0] // (own * groups * 2)
    lanes = [
        ref[pl.ds((side * groups + group) * own + channel, count, stride=own * groups * 2), :]
        for group in range(groups)
    ]
    found = []
    for token in range(tokens):
        start, pieces = token * cols, []
        while start < (token + 1) * cols:
            group = start // LANES
            end = min((group + 1) * LANES, (token + 1) * cols)
            pieces.append(lanes[group][:, start - group * LANES : end - group * LANES])
            start = end
        found.append(jnp.concatenate(pieces, axis=1))
    return jnp.concatenate(found, axis=0).astype(jnp.bfloat16)


def put_channel(ref, held, channel, own, cols):
    tokens, groups = cycle_of(cols)
    count = cols // tokens
    lines = [
        jnp.concatenate(
            [held[piece, pl.ds(token, count, stride=tokens), :] for piece in range(held.shape[0])], axis=1
        )
        for token in range(tokens)
    ]
    for group in range(groups):
        start, pieces = group * LANES, []
        while start < (group + 1) * LANES:
            token = start // cols
            end = min((token + 1) * cols, (group + 1) * LANES)
            pieces.append(lines[token][:, start - token * cols : end - token * cols])
            start = end
        ref[pl.ds(group * own + channel, count, stride=own * groups), :] = jnp.concatenate(pieces, axis=1)


def triangle(own, cols, lefts, rights, held, mixed):
    for channel in range(own):
        right = take_channel(rights, 1, channel, own, cols)
        left = take_channel(lefts, 0, channel, own, cols)
        total = lax.dot_general(left, right, (((0,), (0,)), ((), ())), preferred_element_type=jnp.float32)
        at = channel % 2
        for start in range(0, cols, LANES):
            width = min(LANES, cols - start)
            held[at, start // LANES, :, :width] = total[:, start : start + width]
        put_channel(mixed, held.at[at], channel, own, cols)


def first_kernel(own, cols, own_ref, mixed_ref, ours, held, mixed):
    ours[...] = own_ref[...].astype(jnp.float32).reshape(ours.shape)
    triangle(own, cols, ours, ours, held, mixed)
    mixed_ref[...] = mixed[...].astype(jnp.bfloat16).reshape(mixed_ref.shape)


def second_kernel(own, cols, own_ref, other_ref, first_ref, mixed_ref, ours, others, held, mixed):
    half = first_ref.shape[0]
    at = lax.axis_index("col")
    ours[...] = own_ref[...].astype(jnp.float32).reshape(ours.shape)
    others[...] = other_ref[...].astype(jnp.float32).reshape(others.shape)
    mixed_ref[pl.ds(at * half, half)] = first_ref[...]
    triangle(own, cols, others, ours, held, mixed)
    mixed_ref[pl.ds((1 - at) * half, half)] = mixed[...].astype(jnp.bfloat16).reshape(first_ref.shape)


def output_kernel(own, mixed_ref, gate_ref, gain_ref, w_t_ref, update_ref):
    shares, hidden = mixed_ref.shape[0], w_t_ref.shape[1]
    peers = hidden // own
    for group in range(gate_ref.shape[1] // LANES):
        block = jnp.zeros((hidden, LANES), jnp.float32)
        for part in range(shares // peers):
            sums = mixed_ref[part * peers : (part + 1) * peers, group * own : (group + 1) * own, :]
            block += sums.astype(jnp.float32).reshape(hidden, LANES)
        center = block - jnp.mean(block, axis=0, keepdims=True)
        spread = jnp.mean(center * center, axis=0, keepdims=True)
        normed = (center * lax.rsqrt(spread + EPS) * gain_ref[...]).astype(jnp.bfloat16)
        projected = jnp.dot(w_t_ref[...], normed, preferred_element_type=jnp.float32)
        lanes = slice(group * LANES, (group + 1) * LANES)
        update_ref[lanes, :] = (gate_ref[:, lanes] * projected).T.astype(jnp.bfloat16)


def on_device(shares, pair, tile_mask, chain_ids, gain_in, w_proj, gain_mid, w_out):
    rows, cols, width = pair.shape
    hidden = w_out.shape[0]
    peers = shares // PARTS
    own = hidden // peers
    positions = rows * cols
    lines = positions // LANES * own
    half = shares // 2
    params = pltpu.CompilerParams(vmem_limit_bytes=VMEM_BYTES)
    tokens = chain_ids.shape[0]
    message, normed = pl.pallas_call(
        functools.partial(project_kernel, rows, cols, peers),
        out_shape=(
            jax.ShapeDtypeStruct((peers, 2 * lines, LANES), jnp.bfloat16),
            jax.ShapeDtypeStruct((width, positions), jnp.bfloat16),
        ),
        in_specs=[HBM] * 5,
        out_specs=(VMEM, VMEM),
        scratch_shapes=[
            pltpu.SMEM(tile_mask.shape, jnp.int32),
            pltpu.VMEM((1, tokens), jnp.int32),
            pltpu.VMEM((positions, width), jnp.bfloat16),
            pltpu.VMEM((1, width), jnp.float32),
            pltpu.VMEM(w_proj.shape, jnp.bfloat16),
            pltpu.SemaphoreType.DMA((5,)),
        ],
        compiler_params=pltpu.CompilerParams(vmem_limit_bytes=WHOLE_VMEM_BYTES),
        name="project",
    )(tile_mask, chain_ids[None, :], pair.reshape(positions, width), gain_in[None, :], w_proj)
    message = lax.all_to_all(
        message,
        "row",
        split_axis=0,
        concat_axis=0,
        axis_index_groups=[list(range(part * peers, (part + 1) * peers)) for part in range(PARTS)],
        tiled=True,
    )
    gate, w_out_t, gain = pl.pallas_call(
        gate_kernel,
        out_shape=(
            jax.ShapeDtypeStruct((width, positions), jnp.float32),
            jax.ShapeDtypeStruct(w_out.shape[::-1], jnp.bfloat16),
            jax.ShapeDtypeStruct((hidden, LANES), jnp.float32),
        ),
        in_specs=[VMEM] + [HBM] * 3,
        out_specs=(VMEM, VMEM, VMEM),
        scratch_shapes=[
            pltpu.VMEM(w_proj.shape, jnp.bfloat16),
            pltpu.VMEM(w_out.shape, jnp.bfloat16),
            pltpu.VMEM((1, hidden), jnp.float32),
            pltpu.SemaphoreType.DMA((3,)),
        ],
        compiler_params=params,
        cost_estimate=pl.CostEstimate(
            flops=2 * width * width * positions, bytes_accessed=4 * width * positions, transcendentals=0
        ),
        name="gate",
    )(normed, w_proj, gain_mid[None, :], w_out)
    other = lax.ppermute(message, "col", [(0, 1), (1, 0)])
    blocks = pltpu.VMEM((peers * 2 * lines, LANES), jnp.float32)
    held = pltpu.VMEM((2, pl.cdiv(cols, LANES), cols, LANES), jnp.float32)
    out = pltpu.VMEM((half * lines, LANES), jnp.float32)
    first = pl.pallas_call(
        functools.partial(first_kernel, own, cols),
        out_shape=jax.ShapeDtypeStruct((half, lines, LANES), jnp.bfloat16),
        in_specs=[VMEM],
        out_specs=VMEM,
        scratch_shapes=[blocks, held, out],
        compiler_params=params,
        cost_estimate=pl.CostEstimate(
            flops=2 * own * cols * cols * tokens, bytes_accessed=8 * shares * lines * LANES, transcendentals=0
        ),
        name="first",
    )(message)
    mixed = pl.pallas_call(
        functools.partial(second_kernel, own, cols),
        out_shape=jax.ShapeDtypeStruct((shares, lines, LANES), jnp.bfloat16),
        in_specs=[VMEM, VMEM, VMEM],
        out_specs=VMEM,
        scratch_shapes=[blocks, blocks, held, out],
        compiler_params=params,
        name="second",
    )(message, other, first)
    mixed = lax.all_to_all(mixed, "row", split_axis=0, concat_axis=0, tiled=True)
    update = pl.pallas_call(
        functools.partial(output_kernel, own),
        out_shape=jax.ShapeDtypeStruct((positions, width), jnp.bfloat16),
        in_specs=[VMEM] * 4,
        out_specs=VMEM,
        compiler_params=params,
        name="output",
    )(mixed, gate, gain, w_out_t)
    return update.reshape(rows, cols, width)


def solution(mesh):
    in_specs = (P(("grp", "row"), "col", None), P("grp", None), P("grp"), P(), P(), P(), P())
    out_specs = P(("grp", "row"), "col", None)
    return jax.shard_map(
        functools.partial(on_device, mesh.shape["row"]),
        mesh=mesh,
        in_specs=in_specs,
        out_specs=out_specs,
        check_vma=False,
    )
```

```python
import functools
import math

import jax
import jax.numpy as jnp
from jax import lax
from jax.experimental import pallas as pl
from jax.experimental.pallas import tpu as pltpu
from jax.sharding import PartitionSpec as P

TILE = 96
LANES = 128
EPS = 1e-05
PARTS = 2
VMEM_BYTES = 32 * 1024 * 1024
WHOLE_VMEM_BYTES = 64 * 1024 * 1024
VMEM = pl.BlockSpec(memory_space=pltpu.VMEM)
HBM = pl.BlockSpec(memory_space=pltpu.HBM)
SMEM = pl.BlockSpec(memory_space=pltpu.SMEM)


def column(row):
    return jnp.broadcast_to(row, (8, row.shape[1])).T[:, :1]


def steps(at, width, count):
    total = jnp.zeros_like(at)
    for edge in range(1, count):
        total += (at >= edge * width).astype(jnp.int32)
    return total


def sigmoid(values):
    return 0.5 * jnp.tanh(0.5 * values) + 0.5


def keep_of(tile_ref, chain_ref, rows, cols):
    tokens = chain_ref.shape[1]
    tiles = tile_ref.shape[1]
    positions = rows * cols
    at = lax.broadcasted_iota(jnp.int32, (1, positions), 1)
    row = steps(at, cols, rows)
    k = lax.axis_index("row") * rows + row
    i = lax.axis_index("col") * cols + at - row * cols
    token = lax.broadcasted_iota(jnp.int32, (tokens, positions), 0)
    pick = (token == k).astype(jnp.float32) - (token == i).astype(jnp.float32)
    chains = jnp.broadcast_to(chain_ref[...].astype(jnp.bfloat16), (8, tokens))
    apart = jnp.dot(chains, pick.astype(jnp.bfloat16), preferred_element_type=jnp.float32)[:1]
    k_tile = steps(k, TILE, tiles)
    i_tile = steps(i, TILE, tiles)
    tile_vals = jnp.zeros((1, positions), jnp.float32)
    for a in range(tiles):
        for b in range(tiles):
            here = (k_tile == a) & (i_tile == b)
            tile_vals = jnp.where(here, tile_ref[a, b].astype(jnp.float32), tile_vals)
    return jnp.where(apart == 0.0, 1.0, tile_vals)


def cycle_of(cols):
    cycle = math.lcm(cols, LANES)
    return cycle // cols, cycle // LANES


def fetch(sems, *pairs):
    copies = [pltpu.make_async_copy(src, dst, sems.at[at]) for at, (src, dst) in enumerate(pairs)]
    for copy in copies:
        copy.start()
    for copy in copies:
        copy.wait()


def project_kernel(
    rows, cols, peers, tile_hbm, chain_hbm, pair_hbm, gain_hbm, w_hbm, message_ref, normed_ref,
    tile_ref, chain_ref, pair_ref, gain_ref, w_ref, sems,
):
    fetch(
        sems,
        (w_hbm, w_ref),
        (pair_hbm, pair_ref),
        (gain_hbm, gain_ref),
        (chain_hbm, chain_ref),
        (tile_hbm, tile_ref),
    )
    hidden = (w_ref.shape[1] - w_ref.shape[0]) // 4
    own = hidden // peers
    groups = cycle_of(cols)[1]
    keep = keep_of(tile_ref, chain_ref, rows, cols)
    w_t = w_ref[:, : 4 * hidden].T
    gain = column(gain_ref[...])
    positions = rows * cols
    for start in range(0, positions, 2 * LANES):
        end = min(start + 2 * LANES, positions)
        block = pair_ref[start:end, :].astype(jnp.float32).T
        center = block - jnp.mean(block, axis=0, keepdims=True)
        spread = jnp.mean(center * center, axis=0, keepdims=True)
        normed = (center * lax.rsqrt(spread + EPS) * gain).astype(jnp.bfloat16)
        normed_ref[:, start:end] = normed
        projected = jnp.dot(w_t, normed, preferred_element_type=jnp.float32)
        kept = keep[:, start:end]
        for side in range(2):
            value = projected[2 * side * hidden : (2 * side + 1) * hidden]
            gate = projected[(2 * side + 1) * hidden : (2 * side + 2) * hidden]
            sent = (sigmoid(gate) * value * kept).astype(jnp.bfloat16)
            for group in range(start // LANES, end // LANES):
                line = (group // groups * 2 + side) * groups + group % groups
                at = group * LANES - start
                message_ref[:, line * own : (line + 1) * own, :] = sent[:, at : at + LANES].reshape(
                    peers, own, LANES
                )


def gate_kernel(normed_ref, w_hbm, gain_hbm, w_out_hbm, gate_ref, w_out_ref, gain_ref, w, w_out, gain, sems):
    width = w_hbm.shape[0]
    last = w_hbm.shape[1] - width
    fetch(sems, (w_hbm, w), (w_out_hbm, w_out), (gain_hbm, gain))
    gate_ref[...] = sigmoid(
        jnp.dot(w[:, last:].T, normed_ref[...], preferred_element_type=jnp.float32)
    )
    w_out_ref[...] = w_out[...].T
    gain_ref[...] = jnp.broadcast_to(column(gain[...]), gain_ref.shape)


def unpack(message_ref, side, spread_ref, own, cols):
    tokens, groups = cycle_of(cols)
    lane = lax.broadcasted_iota(jnp.int32, (own, LANES), 1)
    peers, lines, _ = message_ref.shape
    cycles = lines // (2 * groups * own)
    for peer in range(peers):
        for cycle in range(cycles):
            base = (cycle * 2 + side) * groups * own
            held = [
                message_ref[peer, base + group * own : base + (group + 1) * own, :].astype(jnp.float32)
                for group in range(groups)
            ]
            for token in range(tokens):
                k = (peer * cycles + cycle) * tokens + token
                for chunk in range(spread_ref.shape[0]):
                    group, off = divmod(token * cols + chunk * LANES, LANES)
                    value = held[group]
                    if off and group + 1 < groups:
                        value = jnp.where(lane >= off, value, held[group + 1])
                    if off:
                        value = pltpu.roll(value, LANES - off, axis=1)
                    spread_ref[chunk, k * own : (k + 1) * own, :] = value


def pack(spread_ref, mixed_ref, first, own, cols):
    tokens, groups = cycle_of(cols)
    lane = lax.broadcasted_iota(jnp.int32, (own, LANES), 1)
    cycles = mixed_ref.shape[1] // (groups * own)
    for at in range(cols // tokens):
        peer, cycle = divmod(at, cycles)
        rolled = {}
        lines = []
        for group in range(groups):
            value, here = None, 0
            while here < LANES:
                token, col = divmod(group * LANES + here, cols)
                chunk, there = divmod(col, LANES)
                shift = (here - there) % LANES
                if (token, chunk, shift) not in rolled:
                    line = (at * tokens + token) * own
                    piece = spread_ref[chunk, line : line + own, :]
                    rolled[token, chunk, shift] = pltpu.roll(piece, shift, axis=1) if shift else piece
                piece = rolled[token, chunk, shift]
                value = piece if value is None else jnp.where(lane >= here, piece, value)
                here += min(LANES - here, LANES - there, cols - col)
            lines.append(value)
        base = cycle * groups * own
        mixed_ref[first + peer, base : base + groups * own, :] = jnp.concatenate(lines, axis=0).astype(
            jnp.bfloat16
        )


def channel_of(spread_ref, channel, own):
    count = spread_ref.shape[1] // own
    return jnp.concatenate(
        [spread_ref[chunk, pl.ds(channel, count, stride=own), :] for chunk in range(spread_ref.shape[0])],
        axis=1,
    ).astype(jnp.bfloat16)


def multiply(lefts, rights, mixed, own, cols):
    width = lefts.shape[0] * LANES
    one = lax.broadcasted_iota(jnp.int32, (cols, width), 0) == lax.broadcasted_iota(jnp.int32, (cols, width), 1)
    one = one.astype(jnp.bfloat16)
    for channel in range(own):
        left = channel_of(lefts, channel, own)
        left_t = lax.dot_general(one, left, (((1,), (1,)), ((), ())), preferred_element_type=jnp.float32)
        total = jnp.dot(left_t.astype(jnp.bfloat16), rights[channel], preferred_element_type=jnp.float32)
        for chunk in range(mixed.shape[0]):
            mixed[chunk, pl.ds(channel, cols, stride=own), :] = total[:, chunk * LANES : (chunk + 1) * LANES]


def first_kernel(own, cols, message_ref, mixed_ref, right_ref, lefts, rights, mixed):
    unpack(message_ref, 0, lefts, own, cols)
    unpack(message_ref, 1, rights, own, cols)
    for channel in range(own):
        right_ref[channel] = channel_of(rights, channel, own)
    multiply(lefts, right_ref, mixed, own, cols)
    pack(mixed, mixed_ref, 0, own, cols)


def second_kernel(own, cols, other_ref, right_ref, first_ref, mixed_ref, lefts, mixed):
    half = first_ref.shape[0]
    at = lax.axis_index("col")
    mixed_ref[pl.ds(at * half, half)] = first_ref[...]
    unpack(other_ref, 0, lefts, own, cols)
    multiply(lefts, right_ref, mixed, own, cols)
    pack(mixed, mixed_ref, (1 - at) * half, own, cols)


def output_kernel(own, mixed_ref, gate_ref, gain_ref, w_t_ref, update_ref):
    shares, hidden = mixed_ref.shape[0], w_t_ref.shape[1]
    peers = hidden // own
    for group in range(gate_ref.shape[1] // LANES):
        block = jnp.zeros((hidden, LANES), jnp.float32)
        for part in range(shares // peers):
            sums = mixed_ref[part * peers : (part + 1) * peers, group * own : (group + 1) * own, :]
            block += sums.astype(jnp.float32).reshape(hidden, LANES)
        center = block - jnp.mean(block, axis=0, keepdims=True)
        spread = jnp.mean(center * center, axis=0, keepdims=True)
        normed = (center * lax.rsqrt(spread + EPS) * gain_ref[...]).astype(jnp.bfloat16)
        projected = jnp.dot(w_t_ref[...], normed, preferred_element_type=jnp.float32)
        lanes = slice(group * LANES, (group + 1) * LANES)
        update_ref[lanes, :] = (gate_ref[:, lanes] * projected).T.astype(jnp.bfloat16)


def on_device(shares, pair, tile_mask, chain_ids, gain_in, w_proj, gain_mid, w_out):
    rows, cols, width = pair.shape
    hidden = w_out.shape[0]
    peers = shares // PARTS
    own = hidden // peers
    positions = rows * cols
    lines = positions // LANES * own
    half = shares // 2
    params = pltpu.CompilerParams(vmem_limit_bytes=VMEM_BYTES)
    tokens = chain_ids.shape[0]
    message, normed = pl.pallas_call(
        functools.partial(project_kernel, rows, cols, peers),
        out_shape=(
            jax.ShapeDtypeStruct((peers, 2 * lines, LANES), jnp.bfloat16),
            jax.ShapeDtypeStruct((width, positions), jnp.bfloat16),
        ),
        in_specs=[HBM] * 5,
        out_specs=(VMEM, VMEM),
        scratch_shapes=[
            pltpu.SMEM(tile_mask.shape, jnp.int32),
            pltpu.VMEM((1, tokens), jnp.int32),
            pltpu.VMEM((positions, width), jnp.bfloat16),
            pltpu.VMEM((1, width), jnp.float32),
            pltpu.VMEM(w_proj.shape, jnp.bfloat16),
            pltpu.SemaphoreType.DMA((5,)),
        ],
        compiler_params=pltpu.CompilerParams(vmem_limit_bytes=WHOLE_VMEM_BYTES),
        name="project",
    )(tile_mask, chain_ids[None, :], pair.reshape(positions, width), gain_in[None, :], w_proj)
    message = lax.all_to_all(
        message,
        "row",
        split_axis=0,
        concat_axis=0,
        axis_index_groups=[list(range(part * peers, (part + 1) * peers)) for part in range(PARTS)],
        tiled=True,
    )
    gate, w_out_t, gain = pl.pallas_call(
        gate_kernel,
        out_shape=(
            jax.ShapeDtypeStruct((width, positions), jnp.float32),
            jax.ShapeDtypeStruct(w_out.shape[::-1], jnp.bfloat16),
            jax.ShapeDtypeStruct((hidden, LANES), jnp.float32),
        ),
        in_specs=[VMEM] + [HBM] * 3,
        out_specs=(VMEM, VMEM, VMEM),
        scratch_shapes=[
            pltpu.VMEM(w_proj.shape, jnp.bfloat16),
            pltpu.VMEM(w_out.shape, jnp.bfloat16),
            pltpu.VMEM((1, hidden), jnp.float32),
            pltpu.SemaphoreType.DMA((3,)),
        ],
        compiler_params=params,
        cost_estimate=pl.CostEstimate(
            flops=2 * width * width * positions, bytes_accessed=4 * width * positions, transcendentals=0
        ),
        name="gate",
    )(normed, w_proj, gain_mid[None, :], w_out)
    other = lax.ppermute(message, "col", [(0, 1), (1, 0)])
    chunks = pl.cdiv(cols, LANES)
    depth = peers * rows
    spread = pltpu.VMEM((chunks, depth * own, LANES), jnp.float32)
    held = pltpu.VMEM((chunks, cols * own, LANES), jnp.float32)
    first, right = pl.pallas_call(
        functools.partial(first_kernel, own, cols),
        out_shape=(
            jax.ShapeDtypeStruct((half, lines, LANES), jnp.bfloat16),
            jax.ShapeDtypeStruct((own, depth, chunks * LANES), jnp.bfloat16),
        ),
        in_specs=[VMEM],
        out_specs=(VMEM, VMEM),
        scratch_shapes=[spread, spread, held],
        compiler_params=params,
        cost_estimate=pl.CostEstimate(
            flops=4 * own * cols * cols * depth, bytes_accessed=8 * shares * lines * LANES, transcendentals=0
        ),
        name="first",
    )(message)
    mixed = pl.pallas_call(
        functools.partial(second_kernel, own, cols),
        out_shape=jax.ShapeDtypeStruct((shares, lines, LANES), jnp.bfloat16),
        in_specs=[VMEM, VMEM, VMEM],
        out_specs=VMEM,
        scratch_shapes=[spread, held],
        compiler_params=params,
        name="second",
    )(other, right, first)
    mixed = lax.all_to_all(mixed, "row", split_axis=0, concat_axis=0, tiled=True)
    update = pl.pallas_call(
        functools.partial(output_kernel, own),
        out_shape=jax.ShapeDtypeStruct((positions, width), jnp.bfloat16),
        in_specs=[VMEM] * 4,
        out_specs=VMEM,
        compiler_params=params,
        name="output",
    )(mixed, gate, gain, w_out_t)
    return update.reshape(rows, cols, width)


def solution(mesh):
    in_specs = (P(("grp", "row"), "col", None), P("grp", None), P("grp"), P(), P(), P(), P())
    out_specs = P(("grp", "row"), "col", None)
    return jax.shard_map(
        functools.partial(on_device, mesh.shape["row"]),
        mesh=mesh,
        in_specs=in_specs,
        out_specs=out_specs,
        check_vma=False,
    )
```

```python
import functools
import math

import jax
import jax.numpy as jnp
from jax import lax
from jax.experimental import pallas as pl
from jax.experimental.pallas import tpu as pltpu
from jax.sharding import PartitionSpec as P

TILE = 96
LANES = 128
EPS = 1e-05
PARTS = 2
VMEM_BYTES = 32 * 1024 * 1024
WHOLE_VMEM_BYTES = 64 * 1024 * 1024
VMEM = pl.BlockSpec(memory_space=pltpu.VMEM)
ANY = pl.BlockSpec(memory_space=pl.ANY)
HBM = pl.BlockSpec(memory_space=pltpu.HBM)
SMEM = pl.BlockSpec(memory_space=pltpu.SMEM)


def column(row):
    return jnp.broadcast_to(row, (8, row.shape[1])).T[:, :1]


def steps(at, width, count):
    total = jnp.zeros_like(at)
    for edge in range(1, count):
        total += (at >= edge * width).astype(jnp.int32)
    return total


def sigmoid(values):
    return 0.5 * jnp.tanh(0.5 * values) + 0.5


def keep_of(tile_ref, chain_ref, rows, cols):
    tokens = chain_ref.shape[1]
    tiles = tile_ref.shape[1]
    positions = rows * cols
    at = lax.broadcasted_iota(jnp.int32, (1, positions), 1)
    row = steps(at, cols, rows)
    k = lax.axis_index("row") * rows + row
    i = lax.axis_index("col") * cols + at - row * cols
    token = lax.broadcasted_iota(jnp.int32, (tokens, positions), 0)
    pick = (token == k).astype(jnp.float32) - (token == i).astype(jnp.float32)
    chains = jnp.broadcast_to(chain_ref[...].astype(jnp.bfloat16), (8, tokens))
    apart = jnp.dot(chains, pick.astype(jnp.bfloat16), preferred_element_type=jnp.float32)[:1]
    k_tile = steps(k, TILE, tiles)
    i_tile = steps(i, TILE, tiles)
    tile_vals = jnp.zeros((1, positions), jnp.float32)
    for a in range(tiles):
        for b in range(tiles):
            here = (k_tile == a) & (i_tile == b)
            tile_vals = jnp.where(here, tile_ref[a, b].astype(jnp.float32), tile_vals)
    return jnp.where(apart == 0.0, 1.0, tile_vals)


def cycle_of(cols):
    cycle = math.lcm(cols, LANES)
    return cycle // cols, cycle // LANES


def fetch(sems, *pairs):
    copies = [pltpu.make_async_copy(src, dst, sems.at[at]) for at, (src, dst) in enumerate(pairs)]
    for copy in copies:
        copy.start()
    for copy in copies:
        copy.wait()


def project_kernel(
    rows, cols, peers, tile_hbm, chain_hbm, pair_hbm, gain_hbm, w_hbm, message_ref, normed_ref,
    tile_ref, chain_ref, pair_ref, gain_ref, w_ref, sems,
):
    fetch(
        sems,
        (w_hbm, w_ref),
        (pair_hbm, pair_ref),
        (gain_hbm, gain_ref),
        (chain_hbm, chain_ref),
        (tile_hbm, tile_ref),
    )
    hidden = (w_ref.shape[1] - w_ref.shape[0]) // 4
    own = hidden // peers
    groups = cycle_of(cols)[1]
    keep = keep_of(tile_ref, chain_ref, rows, cols)
    w_t = w_ref[:, : 4 * hidden].T
    gain = column(gain_ref[...])
    positions = rows * cols
    for start in range(0, positions, 2 * LANES):
        end = min(start + 2 * LANES, positions)
        block = pair_ref[start:end, :].astype(jnp.float32).T
        center = block - jnp.mean(block, axis=0, keepdims=True)
        spread = jnp.mean(center * center, axis=0, keepdims=True)
        normed = (center * lax.rsqrt(spread + EPS) * gain).astype(jnp.bfloat16)
        normed_ref[:, start:end] = normed
        projected = jnp.dot(w_t, normed, preferred_element_type=jnp.float32)
        kept = keep[:, start:end]
        for side in range(2):
            value = projected[2 * side * hidden : (2 * side + 1) * hidden]
            gate = projected[(2 * side + 1) * hidden : (2 * side + 2) * hidden]
            sent = (sigmoid(gate) * value * kept).astype(jnp.bfloat16)
            for group in range(start // LANES, end // LANES):
                line = (group // groups * 2 + side) * groups + group % groups
                at = group * LANES - start
                message_ref[:, line * own : (line + 1) * own, :] = sent[:, at : at + LANES].reshape(
                    peers, own, LANES
                )


def gate_kernel(normed_ref, w_hbm, gate_ref, done_ref, w, sems):
    last = w_hbm.shape[1] - w_hbm.shape[0]
    fetch(sems, (w_hbm, w))
    gate_ref[...] = sigmoid(
        jnp.dot(w[:, last:].T, normed_ref[...], preferred_element_type=jnp.float32)
    )
    done_ref[...] = jnp.zeros_like(done_ref)


def weights_kernel(_, gain_hbm, w_out_hbm, w_out_ref, gain_ref, w_out, gain, sems):
    fetch(sems, (w_out_hbm, w_out), (gain_hbm, gain))
    w_out_ref[...] = w_out[...].T
    gain_ref[...] = jnp.broadcast_to(column(gain[...]), gain_ref.shape)


def unpack(message_ref, side, spread_ref, own, cols):
    tokens, groups = cycle_of(cols)
    lane = lax.broadcasted_iota(jnp.int32, (own, LANES), 1)
    peers, lines, _ = message_ref.shape
    cycles = lines // (2 * groups * own)
    for peer in range(peers):
        for cycle in range(cycles):
            base = (cycle * 2 + side) * groups * own
            held = [
                message_ref[peer, base + group * own : base + (group + 1) * own, :].astype(jnp.float32)
                for group in range(groups)
            ]
            for token in range(tokens):
                k = (peer * cycles + cycle) * tokens + token
                for chunk in range(spread_ref.shape[0]):
                    group, off = divmod(token * cols + chunk * LANES, LANES)
                    value = held[group]
                    if off and group + 1 < groups:
                        value = jnp.where(lane >= off, value, held[group + 1])
                    if off:
                        value = pltpu.roll(value, LANES - off, axis=1)
                    spread_ref[chunk, k * own : (k + 1) * own, :] = value


def pack(spread_ref, mixed_ref, first, own, cols):
    tokens, groups = cycle_of(cols)
    lane = lax.broadcasted_iota(jnp.int32, (own, LANES), 1)
    cycles = mixed_ref.shape[1] // (groups * own)
    for at in range(cols // tokens):
        peer, cycle = divmod(at, cycles)
        rolled = {}
        lines = []
        for group in range(groups):
            value, here = None, 0
            while here < LANES:
                token, col = divmod(group * LANES + here, cols)
                chunk, there = divmod(col, LANES)
                shift = (here - there) % LANES
                if (token, chunk, shift) not in rolled:
                    line = (at * tokens + token) * own
                    piece = spread_ref[chunk, line : line + own, :]
                    rolled[token, chunk, shift] = pltpu.roll(piece, shift, axis=1) if shift else piece
                piece = rolled[token, chunk, shift]
                value = piece if value is None else jnp.where(lane >= here, piece, value)
                here += min(LANES - here, LANES - there, cols - col)
            lines.append(value)
        base = cycle * groups * own
        mixed_ref[first + peer, base : base + groups * own, :] = jnp.concatenate(lines, axis=0).astype(
            jnp.bfloat16
        )


def channel_of(spread_ref, channel, own):
    count = spread_ref.shape[1] // own
    return jnp.concatenate(
        [spread_ref[chunk, pl.ds(channel, count, stride=own), :] for chunk in range(spread_ref.shape[0])],
        axis=1,
    ).astype(jnp.bfloat16)


def multiply(lefts, rights, left, left_t, mixed, own, cols):
    _, deep, width = rights.shape
    depth = lefts.shape[1] // own
    one = lax.broadcasted_iota(jnp.int32, (cols, width), 0) == lax.broadcasted_iota(jnp.int32, (cols, width), 1)
    one = one.astype(jnp.bfloat16)
    if depth < deep:
        left[:, depth:, :] = jnp.zeros((own, deep - depth, width), jnp.bfloat16)
    for channel in range(own):
        left[channel, :depth, :] = channel_of(lefts, channel, own)
    for pair in range(0, own, 2):
        both = lax.dot_general(
            one,
            left[pair : pair + 2].reshape(2 * deep, width),
            (((1,), (1,)), ((), ())),
            preferred_element_type=jnp.float32,
        ).astype(jnp.bfloat16)
        left_t[pair] = both[:, :deep]
        left_t[pair + 1] = both[:, deep:]
    for pair in range(0, own, 2):
        both = jnp.dot(
            left_t[pair : pair + 2].reshape(2 * cols, deep),
            jnp.concatenate([rights[pair], rights[pair + 1]], axis=1),
            preferred_element_type=jnp.float32,
        )
        for at in range(2):
            for chunk in range(mixed.shape[0]):
                start = at * width + chunk * LANES
                mixed[chunk, pl.ds(pair + at, cols, stride=own), :] = both[
                    at * cols : (at + 1) * cols, start : start + LANES
                ]


def first_kernel(own, cols, message_ref, _, mixed_ref, right_ref, lefts, rights, left, left_t, mixed):
    unpack(message_ref, 1, rights, own, cols)
    depth = rights.shape[1] // own
    if depth < right_ref.shape[1]:
        right_ref[:, depth:, :] = jnp.zeros((own, right_ref.shape[1] - depth, right_ref.shape[2]), jnp.bfloat16)
    for channel in range(own):
        right_ref[channel, :depth, :] = channel_of(rights, channel, own)
    unpack(message_ref, 0, lefts, own, cols)
    multiply(lefts, right_ref, left, left_t, mixed, own, cols)
    pack(mixed, mixed_ref, 0, own, cols)


def second_kernel(own, cols, other_ref, right_ref, first_ref, mixed_ref, lefts, left, left_t, mixed):
    half = first_ref.shape[0]
    at = lax.axis_index("col")
    mixed_ref[pl.ds(at * half, half)] = first_ref[...]
    unpack(other_ref, 0, lefts, own, cols)
    multiply(lefts, right_ref, left, left_t, mixed, own, cols)
    pack(mixed, mixed_ref, (1 - at) * half, own, cols)


def output_kernel(own, mixed_ref, gate_ref, gain_ref, w_t_ref, update_ref):
    shares, hidden = mixed_ref.shape[0], w_t_ref.shape[1]
    peers = hidden // own
    for group in range(gate_ref.shape[1] // LANES):
        block = jnp.zeros((hidden, LANES), jnp.float32)
        for part in range(shares // peers):
            sums = mixed_ref[part * peers : (part + 1) * peers, group * own : (group + 1) * own, :]
            block += sums.astype(jnp.float32).reshape(hidden, LANES)
        center = block - jnp.mean(block, axis=0, keepdims=True)
        spread = jnp.mean(center * center, axis=0, keepdims=True)
        normed = (center * lax.rsqrt(spread + EPS) * gain_ref[...]).astype(jnp.bfloat16)
        projected = jnp.dot(w_t_ref[...], normed, preferred_element_type=jnp.float32)
        lanes = slice(group * LANES, (group + 1) * LANES)
        update_ref[lanes, :] = (gate_ref[:, lanes] * projected).T.astype(jnp.bfloat16)


def on_device(shares, pair, tile_mask, chain_ids, gain_in, w_proj, gain_mid, w_out):
    rows, cols, width = pair.shape
    hidden = w_out.shape[0]
    peers = shares // PARTS
    own = hidden // peers
    positions = rows * cols
    lines = positions // LANES * own
    half = shares // 2
    params = pltpu.CompilerParams(vmem_limit_bytes=VMEM_BYTES)
    tokens = chain_ids.shape[0]
    message, normed = pl.pallas_call(
        functools.partial(project_kernel, rows, cols, peers),
        out_shape=(
            jax.ShapeDtypeStruct((peers, 2 * lines, LANES), jnp.bfloat16),
            jax.ShapeDtypeStruct((width, positions), jnp.bfloat16),
        ),
        in_specs=[HBM] * 5,
        out_specs=(VMEM, VMEM),
        scratch_shapes=[
            pltpu.SMEM(tile_mask.shape, jnp.int32),
            pltpu.VMEM((1, tokens), jnp.int32),
            pltpu.VMEM((positions, width), jnp.bfloat16),
            pltpu.VMEM((1, width), jnp.float32),
            pltpu.VMEM(w_proj.shape, jnp.bfloat16),
            pltpu.SemaphoreType.DMA((5,)),
        ],
        compiler_params=pltpu.CompilerParams(vmem_limit_bytes=WHOLE_VMEM_BYTES),
        name="project",
    )(tile_mask, chain_ids[None, :], pair.reshape(positions, width), gain_in[None, :], w_proj)
    message = lax.all_to_all(
        message,
        "row",
        split_axis=0,
        concat_axis=0,
        axis_index_groups=[list(range(part * peers, (part + 1) * peers)) for part in range(PARTS)],
        tiled=True,
    )
    gate, done = pl.pallas_call(
        gate_kernel,
        out_shape=(
            jax.ShapeDtypeStruct((width, positions), jnp.float32),
            jax.ShapeDtypeStruct((8, LANES), jnp.float32),
        ),
        in_specs=[VMEM, HBM],
        out_specs=(VMEM, VMEM),
        scratch_shapes=[pltpu.VMEM(w_proj.shape, jnp.bfloat16), pltpu.SemaphoreType.DMA((1,))],
        compiler_params=params,
        cost_estimate=pl.CostEstimate(
            flops=2 * width * width * positions, bytes_accessed=4 * width * positions, transcendentals=0
        ),
        name="gate",
    )(normed, w_proj)
    message, done = lax.optimization_barrier((message, done))
    other = lax.ppermute(message, "col", [(0, 1), (1, 0)])
    chunks = pl.cdiv(cols, LANES)
    depth = peers * rows
    deep = pl.cdiv(depth, LANES) * LANES
    spread = pltpu.VMEM((chunks, depth * own, LANES), jnp.float32)
    held = [
        pltpu.VMEM((own, deep, chunks * LANES), jnp.bfloat16),
        pltpu.VMEM((own, cols, deep), jnp.bfloat16),
        pltpu.VMEM((chunks, cols * own, LANES), jnp.float32),
    ]
    cost = pl.CostEstimate(
        flops=4 * own * cols * cols * depth, bytes_accessed=8 * shares * lines * LANES, transcendentals=0
    )
    first, right = pl.pallas_call(
        functools.partial(first_kernel, own, cols),
        out_shape=(
            jax.ShapeDtypeStruct((half, lines, LANES), jnp.bfloat16),
            jax.ShapeDtypeStruct((own, deep, chunks * LANES), jnp.bfloat16),
        ),
        in_specs=[VMEM, VMEM],
        out_specs=(VMEM, VMEM),
        scratch_shapes=[spread, spread, *held],
        compiler_params=params,
        cost_estimate=cost,
        name="first",
    )(message, done)
    mixed = pl.pallas_call(
        functools.partial(second_kernel, own, cols),
        out_shape=jax.ShapeDtypeStruct((shares, lines, LANES), jnp.bfloat16),
        in_specs=[VMEM, VMEM, VMEM],
        out_specs=VMEM,
        scratch_shapes=[spread, *held],
        compiler_params=params,
        cost_estimate=cost,
        name="second",
    )(other, right, first)
    w_out_t, gain = pl.pallas_call(
        weights_kernel,
        out_shape=(
            jax.ShapeDtypeStruct(w_out.shape[::-1], jnp.bfloat16),
            jax.ShapeDtypeStruct((hidden, LANES), jnp.float32),
        ),
        in_specs=[ANY, HBM, HBM],
        out_specs=(VMEM, VMEM),
        scratch_shapes=[
            pltpu.VMEM(w_out.shape, jnp.bfloat16),
            pltpu.VMEM((1, hidden), jnp.float32),
            pltpu.SemaphoreType.DMA((2,)),
        ],
        compiler_params=params,
        cost_estimate=pl.CostEstimate(flops=hidden * width, bytes_accessed=8 * hidden * width, transcendentals=0),
        name="weights",
    )(right, gain_mid[None, :], w_out)
    mixed = lax.all_to_all(mixed, "row", split_axis=0, concat_axis=0, tiled=True)
    update = pl.pallas_call(
        functools.partial(output_kernel, own),
        out_shape=jax.ShapeDtypeStruct((positions, width), jnp.bfloat16),
        in_specs=[VMEM] * 4,
        out_specs=VMEM,
        compiler_params=params,
        name="output",
    )(mixed, gate, gain, w_out_t)
    return update.reshape(rows, cols, width)


def solution(mesh):
    in_specs = (P(("grp", "row"), "col", None), P("grp", None), P("grp"), P(), P(), P(), P())
    out_specs = P(("grp", "row"), "col", None)
    return jax.shard_map(
        functools.partial(on_device, mesh.shape["row"]),
        mesh=mesh,
        in_specs=in_specs,
        out_specs=out_specs,
        check_vma=False,
    )
```

```python
import functools
import math

import jax
import jax.numpy as jnp
from jax import lax
from jax.experimental import pallas as pl
from jax.experimental.pallas import tpu as pltpu
from jax.sharding import PartitionSpec as P

TILE = 96
LANES = 128
EPS = 1e-05
PARTS = 2
VMEM_BYTES = 32 * 1024 * 1024
WHOLE_VMEM_BYTES = 64 * 1024 * 1024
VMEM = pl.BlockSpec(memory_space=pltpu.VMEM)
ANY = pl.BlockSpec(memory_space=pl.ANY)
HBM = pl.BlockSpec(memory_space=pltpu.HBM)
SMEM = pl.BlockSpec(memory_space=pltpu.SMEM)


def column(row):
    return jnp.broadcast_to(row, (8, row.shape[1])).T[:, :1]


def steps(at, width, count):
    total = jnp.zeros_like(at)
    for edge in range(1, count):
        total += (at >= edge * width).astype(jnp.int32)
    return total


def sigmoid(values):
    return 0.5 * jnp.tanh(0.5 * values) + 0.5


def keep_of(tile_ref, chain_ref, rows, cols):
    tokens = chain_ref.shape[1]
    tiles = tile_ref.shape[1]
    positions = rows * cols
    at = lax.broadcasted_iota(jnp.int32, (1, positions), 1)
    row = steps(at, cols, rows)
    k = lax.axis_index("row") * rows + row
    i = lax.axis_index("col") * cols + at - row * cols
    token = lax.broadcasted_iota(jnp.int32, (tokens, positions), 0)
    pick = (token == k).astype(jnp.float32) - (token == i).astype(jnp.float32)
    chains = jnp.broadcast_to(chain_ref[...].astype(jnp.bfloat16), (8, tokens))
    apart = jnp.dot(chains, pick.astype(jnp.bfloat16), preferred_element_type=jnp.float32)[:1]
    k_tile = steps(k, TILE, tiles)
    i_tile = steps(i, TILE, tiles)
    tile_vals = jnp.zeros((1, positions), jnp.float32)
    for a in range(tiles):
        for b in range(tiles):
            here = (k_tile == a) & (i_tile == b)
            tile_vals = jnp.where(here, tile_ref[a, b].astype(jnp.float32), tile_vals)
    return jnp.where(apart == 0.0, 1.0, tile_vals)


def cycle_of(cols):
    cycle = math.lcm(cols, LANES)
    return cycle // cols, cycle // LANES


def start_copies(sems, *pairs):
    copies = [pltpu.make_async_copy(src, dst, sems.at[at]) for at, (src, dst) in enumerate(pairs)]
    for copy in copies:
        copy.start()
    return copies


def fetch(sems, *pairs):
    for copy in start_copies(sems, *pairs):
        copy.wait()


def project_kernel(
    rows, cols, tile_hbm, chain_hbm, pair_hbm, gain_hbm, w_hbm, message_hbm, normed_hbm,
    tile_ref, chain_ref, pair_ref, gain_ref, w_ref, message_ref, normed_ref, sems, out_sems,
):
    *small, last = start_copies(
        sems,
        (w_hbm, w_ref),
        (gain_hbm, gain_ref),
        (chain_hbm, chain_ref),
        (tile_hbm, tile_ref),
        (pair_hbm, pair_ref),
    )
    hidden = (w_ref.shape[1] - w_ref.shape[0]) // 4
    peers = message_ref.shape[0]
    own = hidden // peers
    groups = cycle_of(cols)[1]
    for copy in small:
        copy.wait()
    keep = keep_of(tile_ref, chain_ref, rows, cols)
    w_t = w_ref[:, : 4 * hidden].T
    gain = column(gain_ref[...])
    last.wait()
    leaving = []
    for cycle in range(rows * cols // (groups * LANES)):
        lanes = slice(cycle * groups * LANES, (cycle + 1) * groups * LANES)
        block = pair_ref[lanes, :].astype(jnp.float32).T
        center = block - jnp.mean(block, axis=0, keepdims=True)
        spread = jnp.mean(center * center, axis=0, keepdims=True)
        normed = (center * lax.rsqrt(spread + EPS) * gain).astype(jnp.bfloat16)
        normed_ref[:, lanes] = normed
        projected = jnp.dot(w_t, normed, preferred_element_type=jnp.float32)
        sides = []
        for side in range(2):
            value = projected[2 * side * hidden : (2 * side + 1) * hidden]
            gate = projected[(2 * side + 1) * hidden : (2 * side + 2) * hidden]
            sides.append((sigmoid(gate) * value * keep[:, lanes]).reshape(peers, own, groups * LANES))
        both = jnp.concatenate(sides, axis=1).astype(jnp.bfloat16)
        for group in range(groups):
            line = (cycle * groups + group) * 2 * own
            message_ref[:, line : line + 2 * own, :] = both[:, :, group * LANES : (group + 1) * LANES]
        lines = slice(cycle * groups * 2 * own, (cycle + 1) * groups * 2 * own)
        leaving += start_copies(
            out_sems.at[cycle],
            (message_ref.at[:, lines, :], message_hbm.at[:, lines, :]),
            (normed_ref.at[:, lanes], normed_hbm.at[:, lanes]),
        )
    for copy in leaving:
        copy.wait()


def gate_kernel(normed_ref, w_hbm, gate_ref, w, sems):
    last = w_hbm.shape[1] - w_hbm.shape[0]
    fetch(sems, (w_hbm, w))
    gate_ref[...] = sigmoid(
        jnp.dot(w[:, last:].T, normed_ref[...], preferred_element_type=jnp.float32)
    )


def weights_kernel(_, gain_hbm, w_out_hbm, w_out_ref, gain_ref, w_out, gain, sems):
    fetch(sems, (w_out_hbm, w_out), (gain_hbm, gain))
    w_out_ref[...] = w_out[...].T
    gain_ref[...] = jnp.broadcast_to(column(gain[...]), gain_ref.shape)


def unpack(message_ref, spread_ref, own, cols):
    tokens, groups = cycle_of(cols)
    peers, lines, _ = message_ref.shape
    lane = lax.broadcasted_iota(jnp.int32, (2 * own, LANES), 1)
    cycles = lines // (2 * groups * own)
    for peer in range(peers):
        for cycle in range(cycles):
            base = cycle * groups
            held = [
                message_ref[peer, (base + group) * 2 * own : (base + group + 1) * 2 * own, :].astype(jnp.float32)
                for group in range(groups)
            ]
            for token in range(tokens):
                k = (peer * cycles + cycle) * tokens + token
                for chunk in range(spread_ref.shape[0]):
                    group, off = divmod(token * cols + chunk * LANES, LANES)
                    value = held[group]
                    if off and group + 1 < groups:
                        value = jnp.where(lane >= off, value, held[group + 1])
                    if off:
                        value = pltpu.roll(value, LANES - off, axis=1)
                    spread_ref[chunk, k * 2 * own : (k + 1) * 2 * own, :] = value


def pack(spread_ref, mixed_ref, first, own, cols):
    tokens, groups = cycle_of(cols)
    lane = lax.broadcasted_iota(jnp.int32, (own, LANES), 1)
    batch = 16 // math.gcd(groups * own, 16)
    for start in range(0, cols // tokens, batch):
        lines = []
        for at in range(start, start + batch):
            rolled = {}
            for group in range(groups):
                value, here = None, 0
                while here < LANES:
                    token, col = divmod(group * LANES + here, cols)
                    chunk, there = divmod(col, LANES)
                    shift = (here - there) % LANES
                    if (token, chunk, shift) not in rolled:
                        line = (at * tokens + token) * own
                        piece = spread_ref[chunk, line : line + own, :]
                        rolled[token, chunk, shift] = pltpu.roll(piece, shift, axis=1) if shift else piece
                    piece = rolled[token, chunk, shift]
                    value = piece if value is None else jnp.where(lane >= here, piece, value)
                    here += min(LANES - here, LANES - there, cols - col)
                lines.append(value)
        at = first + start * groups * own
        mixed_ref[at : at + batch * groups * own, :] = jnp.concatenate(lines, axis=0).astype(jnp.bfloat16)


def channel_of(spread_ref, line, stride):
    count = spread_ref.shape[1] // stride
    return jnp.concatenate(
        [spread_ref[chunk, pl.ds(line, count, stride=stride), :] for chunk in range(spread_ref.shape[0])],
        axis=1,
    ).astype(jnp.bfloat16)


def triangle_kernel(own, cols, shares, message_ref, mixed_hbm, done_ref, spread, left, left_t, right, mixed, out, sems):
    halves, chunks = spread.shape[:2]
    width = chunks * LANES
    deep = right.shape[1]
    depth = spread.shape[2] // (2 * own)
    done_ref[...] = jnp.zeros_like(done_ref)
    one = lax.broadcasted_iota(jnp.int32, (cols, width), 0) == lax.broadcasted_iota(jnp.int32, (cols, width), 1)
    one = one.astype(jnp.bfloat16)
    if depth < deep:
        right[:, depth:, :] = jnp.zeros((own, deep - depth, halves * width), jnp.bfloat16)
    peers = message_ref.shape[0] // halves
    for half in range(halves):
        unpack(message_ref.at[half * peers : (half + 1) * peers], spread.at[half], own, cols)
        if depth < deep:
            left[:, half * deep + depth : (half + 1) * deep, :] = jnp.zeros((own, deep - depth, width), jnp.bfloat16)
        for channel in range(own):
            left[channel, half * deep : half * deep + depth, :] = channel_of(spread.at[half], channel, 2 * own)
            right[channel, :depth, half * width : (half + 1) * width] = channel_of(
                spread.at[half], own + channel, 2 * own
            )
    for channel in range(own):
        both = lax.dot_general(
            one, left[channel], (((1,), (1,)), ((), ())), preferred_element_type=jnp.float32
        ).astype(jnp.bfloat16)
        for half in range(halves):
            left_t[channel, half * cols : (half + 1) * cols, :] = both[:, half * deep : (half + 1) * deep]
    for channel in range(own):
        total = jnp.dot(left_t[channel], right[channel], preferred_element_type=jnp.float32)
        for i_half in range(halves):
            for j_half in range(halves):
                for chunk in range(chunks):
                    start = j_half * width + chunk * LANES
                    mixed[i_half, j_half, chunk, pl.ds(channel, cols, stride=own), :] = total[
                        i_half * cols : (i_half + 1) * cols, start : start + LANES
                    ]
    each = out.shape[0] // (halves * halves)
    leaving = []
    for j_half in range(halves):
        for i_half in range(halves):
            at = j_half * halves + i_half
            pack(mixed.at[i_half, j_half], out, at * each, own, cols)
            lines = slice(at * each, (at + 1) * each)
            leaving += start_copies(sems.at[at], (out.at[lines, :], mixed_hbm.at[lines, :]))
    for copy in leaving:
        copy.wait()


def output_kernel(own, shares, halves, mixed_ref, gate_ref, gain_ref, w_t_ref, update_ref, mixed):
    lines = mixed.shape[1]
    peers = shares // PARTS
    mixed[...] = mixed_ref[...].astype(jnp.float32).reshape(mixed.shape)
    for group in range(lines // own):
        blocks = []
        for half in range(halves):
            first = half * shares
            block = mixed[first : first + peers, group * own : (group + 1) * own, :]
            for part in range(1, PARTS):
                start = first + part * peers
                block += mixed[start : start + peers, group * own : (group + 1) * own, :]
            blocks.append(block.reshape(peers * own, LANES))
        block = jnp.concatenate(blocks, axis=0)
        center = block - jnp.mean(block, axis=0, keepdims=True)
        spread = jnp.mean(center * center, axis=0, keepdims=True)
        normed = (center * lax.rsqrt(spread + EPS) * gain_ref[...]).astype(jnp.bfloat16)
        projected = jnp.dot(w_t_ref[...], normed, preferred_element_type=jnp.float32)
        lanes = slice(group * LANES, (group + 1) * LANES)
        update_ref[lanes, :] = (gate_ref[:, lanes] * projected).T.astype(jnp.bfloat16)


def on_device(shares, halves, pair, tile_mask, chain_ids, gain_in, w_proj, gain_mid, w_out):
    rows, cols, width = pair.shape
    hidden = w_out.shape[0]
    peers = shares // PARTS
    own = hidden // (peers * halves)
    positions = rows * cols
    groups = positions // LANES
    lines = groups * own
    cycles = groups // cycle_of(cols)[1]
    params = pltpu.CompilerParams(vmem_limit_bytes=VMEM_BYTES)
    whole_params = pltpu.CompilerParams(vmem_limit_bytes=WHOLE_VMEM_BYTES)
    tokens = chain_ids.shape[0]
    message = jax.ShapeDtypeStruct((peers * halves, 2 * lines, LANES), jnp.bfloat16)
    message, normed = pl.pallas_call(
        functools.partial(project_kernel, rows, cols),
        out_shape=(message, jax.ShapeDtypeStruct((width, positions), jnp.bfloat16)),
        in_specs=[HBM] * 5,
        out_specs=(HBM, HBM),
        scratch_shapes=[
            pltpu.SMEM(tile_mask.shape, jnp.int32),
            pltpu.VMEM((1, tokens), jnp.int32),
            pltpu.VMEM((positions, width), jnp.bfloat16),
            pltpu.VMEM((1, width), jnp.float32),
            pltpu.VMEM(w_proj.shape, jnp.bfloat16),
            pltpu.VMEM(message.shape, jnp.bfloat16),
            pltpu.VMEM((width, positions), jnp.bfloat16),
            pltpu.SemaphoreType.DMA((5,)),
            pltpu.SemaphoreType.DMA((cycles, 2)),
        ],
        compiler_params=whole_params,
        name="project",
    )(tile_mask, chain_ids[None, :], pair.reshape(positions, width), gain_in[None, :], w_proj)
    message = lax.all_to_all(
        message,
        ("col", "row"),
        split_axis=0,
        concat_axis=0,
        axis_index_groups=[
            [half * shares + part * peers + at for half in range(halves) for at in range(peers)]
            for part in range(PARTS)
        ],
        tiled=True,
    )
    gate = pl.pallas_call(
        gate_kernel,
        out_shape=jax.ShapeDtypeStruct((width, positions), jnp.float32),
        in_specs=[VMEM, HBM],
        out_specs=VMEM,
        scratch_shapes=[pltpu.VMEM(w_proj.shape, jnp.bfloat16), pltpu.SemaphoreType.DMA((1,))],
        compiler_params=params,
        cost_estimate=pl.CostEstimate(
            flops=2 * width * width * positions, bytes_accessed=4 * width * positions, transcendentals=0
        ),
        name="gate",
    )(normed, w_proj)
    chunks = pl.cdiv(cols, LANES)
    depth = peers * rows
    deep = pl.cdiv(depth, LANES) * LANES
    mixed, done = pl.pallas_call(
        functools.partial(triangle_kernel, own, cols, shares),
        out_shape=(
            jax.ShapeDtypeStruct((halves * shares * lines, LANES), jnp.bfloat16),
            jax.ShapeDtypeStruct((8, LANES), jnp.float32),
        ),
        in_specs=[VMEM],
        out_specs=(HBM, VMEM),
        scratch_shapes=[
            pltpu.VMEM((halves, chunks, depth * 2 * own, LANES), jnp.float32),
            pltpu.VMEM((own, halves * deep, chunks * LANES), jnp.bfloat16),
            pltpu.VMEM((own, halves * cols, deep), jnp.bfloat16),
            pltpu.VMEM((own, deep, halves * chunks * LANES), jnp.bfloat16),
            pltpu.VMEM((halves, halves, chunks, cols * own, LANES), jnp.float32),
            pltpu.VMEM((halves * shares * lines, LANES), jnp.bfloat16),
            pltpu.SemaphoreType.DMA((halves * halves, 1)),
        ],
        compiler_params=params,
        name="triangle",
    )(message)
    mixed = lax.all_to_all(
        mixed.reshape(halves * shares, lines, LANES),
        ("col", "row"),
        split_axis=0,
        concat_axis=0,
        tiled=True,
    ).reshape(halves * shares * lines, LANES)
    w_out_t, gain = pl.pallas_call(
        weights_kernel,
        out_shape=(
            jax.ShapeDtypeStruct(w_out.shape[::-1], jnp.bfloat16),
            jax.ShapeDtypeStruct((hidden, LANES), jnp.float32),
        ),
        in_specs=[ANY, HBM, HBM],
        out_specs=(VMEM, VMEM),
        scratch_shapes=[
            pltpu.VMEM(w_out.shape, jnp.bfloat16),
            pltpu.VMEM((1, hidden), jnp.float32),
            pltpu.SemaphoreType.DMA((2,)),
        ],
        compiler_params=params,
        cost_estimate=pl.CostEstimate(flops=hidden * width, bytes_accessed=8 * hidden * width, transcendentals=0),
        name="weights",
    )(done, gain_mid[None, :], w_out)
    update = pl.pallas_call(
        functools.partial(output_kernel, own, shares, halves),
        out_shape=jax.ShapeDtypeStruct((positions, width), jnp.bfloat16),
        in_specs=[VMEM] * 4,
        out_specs=VMEM,
        scratch_shapes=[pltpu.VMEM((halves * shares, lines, LANES), jnp.float32)],
        compiler_params=params,
        name="output",
    )(mixed, gate, gain, w_out_t)
    return update.reshape(rows, cols, width)


def solution(mesh):
    in_specs = (P(("grp", "row"), "col", None), P("grp", None), P("grp"), P(), P(), P(), P())
    out_specs = P(("grp", "row"), "col", None)
    return jax.shard_map(
        functools.partial(on_device, mesh.shape["row"], mesh.shape["col"]),
        mesh=mesh,
        in_specs=in_specs,
        out_specs=out_specs,
        check_vma=False,
    )
```

```python
import functools
import math

import jax
import jax.numpy as jnp
from jax import lax
from jax.experimental import pallas as pl
from jax.experimental.pallas import tpu as pltpu
from jax.sharding import PartitionSpec as P

TILE = 96
LANES = 128
EPS = 1e-05
PARTS = 2
VMEM_BYTES = 32 * 1024 * 1024
WHOLE_VMEM_BYTES = 64 * 1024 * 1024
VMEM = pl.BlockSpec(memory_space=pltpu.VMEM)
ANY = pl.BlockSpec(memory_space=pl.ANY)
HBM = pl.BlockSpec(memory_space=pltpu.HBM)
SMEM = pl.BlockSpec(memory_space=pltpu.SMEM)


def column(row):
    return jnp.broadcast_to(row, (8, row.shape[1])).T[:, :1]


def steps(at, width, count):
    total = jnp.zeros_like(at)
    for edge in range(1, count):
        total += (at >= edge * width).astype(jnp.int32)
    return total


def sigmoid(values):
    return 0.5 * jnp.tanh(0.5 * values) + 0.5


def keep_of(tile_ref, chain_ref, rows, cols):
    tokens = chain_ref.shape[1]
    tiles = tile_ref.shape[1]
    positions = rows * cols
    at = lax.broadcasted_iota(jnp.int32, (1, positions), 1)
    row = steps(at, cols, rows)
    k = lax.axis_index("row") * rows + row
    i = lax.axis_index("col") * cols + at - row * cols
    token = lax.broadcasted_iota(jnp.int32, (tokens, positions), 0)
    pick = (token == k).astype(jnp.float32) - (token == i).astype(jnp.float32)
    chains = jnp.broadcast_to(chain_ref[...].astype(jnp.bfloat16), (8, tokens))
    apart = jnp.dot(chains, pick.astype(jnp.bfloat16), preferred_element_type=jnp.float32)[:1]
    k_tile = steps(k, TILE, tiles)
    i_tile = steps(i, TILE, tiles)
    tile_vals = jnp.zeros((1, positions), jnp.float32)
    for a in range(tiles):
        for b in range(tiles):
            here = (k_tile == a) & (i_tile == b)
            tile_vals = jnp.where(here, tile_ref[a, b].astype(jnp.float32), tile_vals)
    return jnp.where(apart == 0.0, 1.0, tile_vals)


def cycle_of(cols):
    cycle = math.lcm(cols, LANES)
    return cycle // cols, cycle // LANES


def start_copies(sems, *pairs):
    copies = [pltpu.make_async_copy(src, dst, sems.at[at]) for at, (src, dst) in enumerate(pairs)]
    for copy in copies:
        copy.start()
    return copies


def fetch(sems, *pairs):
    for copy in start_copies(sems, *pairs):
        copy.wait()


def project_kernel(
    rows, cols, tile_hbm, chain_hbm, pair_hbm, gain_hbm, w_hbm, message_hbm, normed_hbm,
    tile_ref, chain_ref, pair_ref, gain_ref, w_ref, message_ref, normed_ref, sems, out_sems,
):
    hidden = (w_ref.shape[1] - w_ref.shape[0]) // 4
    peers = message_ref.shape[0]
    own = hidden // peers
    groups = cycle_of(cols)[1]
    size = groups * LANES
    copies = start_copies(
        sems,
        (w_hbm, w_ref),
        (gain_hbm, gain_ref),
        (chain_hbm, chain_ref),
        (tile_hbm, tile_ref),
        *[
            (pair_hbm.at[start : start + size, :], pair_ref.at[start : start + size, :])
            for start in range(0, rows * cols, size)
        ],
    )
    for copy in copies[:4]:
        copy.wait()
    keep = keep_of(tile_ref, chain_ref, rows, cols)
    w_t = w_ref[:, : 4 * hidden].T
    gain = column(gain_ref[...])
    leaving = []
    for cycle in range(rows * cols // size):
        lanes = slice(cycle * size, (cycle + 1) * size)
        copies[4 + cycle].wait()
        block = pair_ref[lanes, :].T.astype(jnp.float32)
        center = block - jnp.mean(block, axis=0, keepdims=True)
        spread = jnp.mean(center * center, axis=0, keepdims=True)
        normed = (center * lax.rsqrt(spread + EPS) * gain).astype(jnp.bfloat16)
        normed_ref[:, lanes] = normed
        projected = jnp.dot(w_t, normed, preferred_element_type=jnp.float32)
        sides = []
        for side in range(2):
            value = projected[2 * side * hidden : (2 * side + 1) * hidden]
            gate = projected[(2 * side + 1) * hidden : (2 * side + 2) * hidden]
            sides.append((sigmoid(gate) * value * keep[:, lanes]).reshape(peers, own, size))
        both = jnp.concatenate(sides, axis=1).astype(jnp.bfloat16)
        for group in range(groups):
            line = (cycle * groups + group) * 2 * own
            message_ref[:, line : line + 2 * own, :] = both[:, :, group * LANES : (group + 1) * LANES]
        lines = slice(cycle * groups * 2 * own, (cycle + 1) * groups * 2 * own)
        leaving += start_copies(
            out_sems.at[cycle],
            (message_ref.at[:, lines, :], message_hbm.at[:, lines, :]),
            (normed_ref.at[:, lanes], normed_hbm.at[:, lanes]),
        )
    for copy in leaving:
        copy.wait()


def gate_kernel(normed_ref, w_hbm, gain_hbm, w_out_hbm, gate_ref, w_out_ref, gain_ref, done_ref, w, w_out, gain, sems):
    fetch(sems, (w_hbm, w), (w_out_hbm, w_out), (gain_hbm, gain))
    last = w_hbm.shape[1] - w_hbm.shape[0]
    gate_ref[...] = sigmoid(
        jnp.dot(w[:, last:].T, normed_ref[...], preferred_element_type=jnp.float32)
    )
    w_out_ref[...] = w_out[...].T
    gain_ref[...] = jnp.broadcast_to(column(gain[...]), gain_ref.shape)
    done_ref[...] = jnp.zeros_like(done_ref)


def unpack(message_ref, spread_ref, own, cols):
    tokens, groups = cycle_of(cols)
    peers, lines, _ = message_ref.shape
    lane = lax.broadcasted_iota(jnp.int32, (2 * own, LANES), 1)
    cycles = lines // (2 * groups * own)
    for peer in range(peers):
        for cycle in range(cycles):
            base = cycle * groups
            held = [
                message_ref[peer, (base + group) * 2 * own : (base + group + 1) * 2 * own, :].astype(jnp.float32)
                for group in range(groups)
            ]
            for token in range(tokens):
                k = (peer * cycles + cycle) * tokens + token
                for chunk in range(spread_ref.shape[0]):
                    group, off = divmod(token * cols + chunk * LANES, LANES)
                    value = held[group]
                    if off and group + 1 < groups:
                        value = jnp.where(lane >= off, value, held[group + 1])
                    if off:
                        value = pltpu.roll(value, LANES - off, axis=1)
                    spread_ref[chunk, k * 2 * own : (k + 1) * 2 * own, :] = value


def pack(spread_ref, mixed_ref, first, own, cols):
    tokens, groups = cycle_of(cols)
    lane = lax.broadcasted_iota(jnp.int32, (own, LANES), 1)
    batch = 16 // math.gcd(groups * own, 16)
    for start in range(0, cols // tokens, batch):
        lines = []
        for at in range(start, start + batch):
            rolled = {}
            for group in range(groups):
                value, here = None, 0
                while here < LANES:
                    token, col = divmod(group * LANES + here, cols)
                    chunk, there = divmod(col, LANES)
                    shift = (here - there) % LANES
                    if (token, chunk, shift) not in rolled:
                        line = (at * tokens + token) * own
                        piece = spread_ref[chunk, line : line + own, :]
                        rolled[token, chunk, shift] = pltpu.roll(piece, shift, axis=1) if shift else piece
                    piece = rolled[token, chunk, shift]
                    value = piece if value is None else jnp.where(lane >= here, piece, value)
                    here += min(LANES - here, LANES - there, cols - col)
                lines.append(value)
        at = first + start * groups * own
        mixed_ref[at : at + batch * groups * own, :] = jnp.concatenate(lines, axis=0).astype(jnp.bfloat16)


def channel_of(spread_ref, line, stride):
    count = spread_ref.shape[1] // stride
    return jnp.concatenate(
        [spread_ref[chunk, pl.ds(line, count, stride=stride), :] for chunk in range(spread_ref.shape[0])],
        axis=1,
    ).astype(jnp.bfloat16)


def triangle_kernel(own, cols, message_ref, _, mixed_ref, spread, left, left_t, right, mixed):
    halves, chunks = spread.shape[:2]
    width = chunks * LANES
    deep = right.shape[1]
    depth = spread.shape[2] // (2 * own)
    one = lax.broadcasted_iota(jnp.int32, (cols, width), 0) == lax.broadcasted_iota(jnp.int32, (cols, width), 1)
    one = one.astype(jnp.bfloat16)
    if depth < deep:
        right[:, depth:, :] = jnp.zeros((own, deep - depth, halves * width), jnp.bfloat16)
    peers = message_ref.shape[0] // halves
    for half in range(halves):
        unpack(message_ref.at[half * peers : (half + 1) * peers], spread.at[half], own, cols)
        if depth < deep:
            left[:, half * deep + depth : (half + 1) * deep, :] = jnp.zeros((own, deep - depth, width), jnp.bfloat16)
        for channel in range(own):
            left[channel, half * deep : half * deep + depth, :] = channel_of(spread.at[half], channel, 2 * own)
            right[channel, :depth, half * width : (half + 1) * width] = channel_of(
                spread.at[half], own + channel, 2 * own
            )
    for channel in range(own):
        both = lax.dot_general(
            one, left[channel], (((1,), (1,)), ((), ())), preferred_element_type=jnp.float32
        ).astype(jnp.bfloat16)
        for half in range(halves):
            left_t[channel, half * cols : (half + 1) * cols, :] = both[:, half * deep : (half + 1) * deep]
    for channel in range(own):
        total = jnp.dot(left_t[channel], right[channel], preferred_element_type=jnp.float32)
        for i_half in range(halves):
            for j_half in range(halves):
                for chunk in range(chunks):
                    start = j_half * width + chunk * LANES
                    mixed[i_half, j_half, chunk, pl.ds(channel, cols, stride=own), :] = total[
                        i_half * cols : (i_half + 1) * cols, start : start + LANES
                    ]
    each = mixed_ref.shape[0] // (halves * halves)
    for j_half in range(halves):
        for i_half in range(halves):
            at = j_half * halves + i_half
            pack(mixed.at[i_half, j_half], mixed_ref, at * each, own, cols)


def output_kernel(own, shares, halves, mixed_ref, gate_ref, gain_ref, w_t_ref, update_ref, mixed):
    lines = mixed.shape[1]
    peers = shares // PARTS
    mixed[...] = mixed_ref[...].astype(jnp.float32).reshape(mixed.shape)
    for group in range(lines // own):
        blocks = []
        for half in range(halves):
            first = half * shares
            block = mixed[first : first + peers, group * own : (group + 1) * own, :]
            for part in range(1, PARTS):
                start = first + part * peers
                block += mixed[start : start + peers, group * own : (group + 1) * own, :]
            blocks.append(block.reshape(peers * own, LANES))
        block = jnp.concatenate(blocks, axis=0)
        center = block - jnp.mean(block, axis=0, keepdims=True)
        spread = jnp.mean(center * center, axis=0, keepdims=True)
        normed = (center * lax.rsqrt(spread + EPS) * gain_ref[...]).astype(jnp.bfloat16)
        projected = jnp.dot(w_t_ref[...], normed, preferred_element_type=jnp.float32)
        lanes = slice(group * LANES, (group + 1) * LANES)
        update_ref[lanes, :] = (gate_ref[:, lanes] * projected).astype(jnp.bfloat16).T


def on_device(shares, halves, pair, tile_mask, chain_ids, gain_in, w_proj, gain_mid, w_out):
    rows, cols, width = pair.shape
    hidden = w_out.shape[0]
    peers = shares // PARTS
    own = hidden // (peers * halves)
    positions = rows * cols
    groups = positions // LANES
    lines = groups * own
    cycles = groups // cycle_of(cols)[1]
    params = pltpu.CompilerParams(vmem_limit_bytes=VMEM_BYTES)
    whole_params = pltpu.CompilerParams(vmem_limit_bytes=WHOLE_VMEM_BYTES)
    tokens = chain_ids.shape[0]
    message = jax.ShapeDtypeStruct((peers * halves, 2 * lines, LANES), jnp.bfloat16)
    message, normed = pl.pallas_call(
        functools.partial(project_kernel, rows, cols),
        out_shape=(message, jax.ShapeDtypeStruct((width, positions), jnp.bfloat16)),
        in_specs=[HBM] * 5,
        out_specs=(HBM, HBM),
        scratch_shapes=[
            pltpu.SMEM(tile_mask.shape, jnp.int32),
            pltpu.VMEM((1, tokens), jnp.int32),
            pltpu.VMEM((positions, width), jnp.bfloat16),
            pltpu.VMEM((1, width), jnp.float32),
            pltpu.VMEM(w_proj.shape, jnp.bfloat16),
            pltpu.VMEM(message.shape, jnp.bfloat16),
            pltpu.VMEM((width, positions), jnp.bfloat16),
            pltpu.SemaphoreType.DMA((4 + cycles,)),
            pltpu.SemaphoreType.DMA((cycles, 2)),
        ],
        compiler_params=whole_params,
        name="project",
    )(tile_mask, chain_ids[None, :], pair.reshape(positions, width), gain_in[None, :], w_proj)
    message = lax.all_to_all(
        message,
        ("col", "row"),
        split_axis=0,
        concat_axis=0,
        axis_index_groups=[
            [half * shares + part * peers + at for half in range(halves) for at in range(peers)]
            for part in range(PARTS)
        ],
        tiled=True,
    )
    gate, w_out_t, gain, done = pl.pallas_call(
        gate_kernel,
        out_shape=(
            jax.ShapeDtypeStruct((width, positions), jnp.float32),
            jax.ShapeDtypeStruct(w_out.shape[::-1], jnp.bfloat16),
            jax.ShapeDtypeStruct((hidden, LANES), jnp.float32),
            jax.ShapeDtypeStruct((8, LANES), jnp.float32),
        ),
        in_specs=[VMEM, HBM, HBM, HBM],
        out_specs=(VMEM, VMEM, VMEM, VMEM),
        scratch_shapes=[
            pltpu.VMEM(w_proj.shape, jnp.bfloat16),
            pltpu.VMEM(w_out.shape, jnp.bfloat16),
            pltpu.VMEM((1, hidden), jnp.float32),
            pltpu.SemaphoreType.DMA((3,)),
        ],
        compiler_params=params,
        cost_estimate=pl.CostEstimate(
            flops=2 * width * width * positions, bytes_accessed=4 * width * positions, transcendentals=0
        ),
        name="gate",
    )(normed, w_proj, gain_mid[None, :], w_out)
    message, done = lax.optimization_barrier((message, done))
    chunks = pl.cdiv(cols, LANES)
    depth = peers * rows
    deep = pl.cdiv(depth, LANES) * LANES
    mixed = pl.pallas_call(
        functools.partial(triangle_kernel, own, cols),
        out_shape=jax.ShapeDtypeStruct((halves * shares * lines, LANES), jnp.bfloat16),
        in_specs=[VMEM, ANY],
        out_specs=VMEM,
        scratch_shapes=[
            pltpu.VMEM((halves, chunks, depth * 2 * own, LANES), jnp.float32),
            pltpu.VMEM((own, halves * deep, chunks * LANES), jnp.bfloat16),
            pltpu.VMEM((own, halves * cols, deep), jnp.bfloat16),
            pltpu.VMEM((own, deep, halves * chunks * LANES), jnp.bfloat16),
            pltpu.VMEM((halves, halves, chunks, cols * own, LANES), jnp.float32),
        ],
        compiler_params=params,
        name="triangle",
    )(message, done)
    mixed = lax.all_to_all(
        mixed.reshape(halves * shares, lines, LANES),
        ("col", "row"),
        split_axis=0,
        concat_axis=0,
        tiled=True,
    ).reshape(halves * shares * lines, LANES)
    update = pl.pallas_call(
        functools.partial(output_kernel, own, shares, halves),
        out_shape=jax.ShapeDtypeStruct((positions, width), jnp.bfloat16),
        in_specs=[VMEM] * 4,
        out_specs=VMEM,
        scratch_shapes=[pltpu.VMEM((halves * shares, lines, LANES), jnp.float32)],
        compiler_params=params,
        name="output",
    )(mixed, gate, gain, w_out_t)
    return update.reshape(rows, cols, width)


def solution(mesh):
    in_specs = (P(("grp", "row"), "col", None), P("grp", None), P("grp"), P(), P(), P(), P())
    out_specs = P(("grp", "row"), "col", None)
    return jax.shard_map(
        functools.partial(on_device, mesh.shape["row"], mesh.shape["col"]),
        mesh=mesh,
        in_specs=in_specs,
        out_specs=out_specs,
        check_vma=False,
    )
```

```python
import functools
import math

import jax
import jax.numpy as jnp
from jax import lax
from jax.experimental import pallas as pl
from jax.experimental.pallas import tpu as pltpu
from jax.sharding import PartitionSpec as P

TILE = 96
LANES = 128
EPS = 1e-05
PARTS = 2
VMEM_BYTES = 32 * 1024 * 1024
WHOLE_VMEM_BYTES = 64 * 1024 * 1024
VMEM = pl.BlockSpec(memory_space=pltpu.VMEM)
ANY = pl.BlockSpec(memory_space=pl.ANY)
HBM = pl.BlockSpec(memory_space=pltpu.HBM)
SMEM = pl.BlockSpec(memory_space=pltpu.SMEM)


def column(row):
    return jnp.broadcast_to(row, (8, row.shape[1])).T[:, :1]


def steps(at, width, count):
    total = jnp.zeros_like(at)
    for edge in range(1, count):
        total += (at >= edge * width).astype(jnp.int32)
    return total


def identity(rows, cols):
    same = lax.broadcasted_iota(jnp.int32, (rows, cols), 0) == lax.broadcasted_iota(jnp.int32, (rows, cols), 1)
    return same.astype(jnp.bfloat16)


def transpose(block):
    return lax.dot_general(
        identity(block.shape[1], block.shape[1]),
        block,
        (((1,), (1,)), ((), ())),
        preferred_element_type=jnp.float32,
    )


def sigmoid(values):
    return 0.5 * jnp.tanh(0.5 * values) + 0.5


def keep_of(tile_ref, chain_ref, rows, cols):
    tokens = chain_ref.shape[1]
    tiles = tile_ref.shape[1]
    positions = rows * cols
    at = lax.broadcasted_iota(jnp.int32, (1, positions), 1)
    row = steps(at, cols, rows)
    k = lax.axis_index("row") * rows + row
    i = lax.axis_index("col") * cols + at - row * cols
    token = lax.broadcasted_iota(jnp.int32, (tokens, positions), 0)
    pick = (token == k).astype(jnp.float32) - (token == i).astype(jnp.float32)
    chains = jnp.broadcast_to(chain_ref[...].astype(jnp.bfloat16), (8, tokens))
    apart = jnp.dot(chains, pick.astype(jnp.bfloat16), preferred_element_type=jnp.float32)[:1]
    k_tile = steps(k, TILE, tiles)
    i_tile = steps(i, TILE, tiles)
    tile_vals = jnp.zeros((1, positions), jnp.float32)
    for a in range(tiles):
        for b in range(tiles):
            here = (k_tile == a) & (i_tile == b)
            tile_vals = jnp.where(here, tile_ref[a, b].astype(jnp.float32), tile_vals)
    return jnp.where(apart == 0.0, 1.0, tile_vals)


def cycle_of(cols):
    cycle = math.lcm(cols, LANES)
    return cycle // cols, cycle // LANES


def start_copies(sems, *pairs):
    copies = [pltpu.make_async_copy(src, dst, sems.at[at]) for at, (src, dst) in enumerate(pairs)]
    for copy in copies:
        copy.start()
    return copies


def fetch(sems, *pairs):
    for copy in start_copies(sems, *pairs):
        copy.wait()


def project_kernel(
    rows, cols, tile_hbm, chain_hbm, pair_hbm, gain_hbm, w_hbm, message_hbm, normed_hbm,
    tile_ref, chain_ref, pair_ref, gain_ref, w_ref, message_ref, normed_ref, sems, out_sems,
):
    hidden = (w_ref.shape[1] - w_ref.shape[0]) // 4
    peers = message_ref.shape[0]
    own = hidden // peers
    groups = cycle_of(cols)[1]
    size = groups * LANES
    copies = start_copies(
        sems,
        (w_hbm, w_ref),
        (gain_hbm, gain_ref),
        (chain_hbm, chain_ref),
        (tile_hbm, tile_ref),
        (pair_hbm, pair_ref),
    )
    for copy in copies[:4]:
        copy.wait()
    keep = keep_of(tile_ref, chain_ref, rows, cols)
    w_t = w_ref[:, : 4 * hidden].T
    gain = column(gain_ref[...])
    copies[4].wait()
    cycles = [slice(start, start + size) for start in range(0, rows * cols, size)]
    for lanes in cycles:
        block = transpose(pair_ref[lanes, :])
        center = block - jnp.mean(block, axis=0, keepdims=True)
        spread = jnp.mean(center * center, axis=0, keepdims=True)
        normed_ref[:, lanes] = (center * lax.rsqrt(spread + EPS) * gain).astype(jnp.bfloat16)
    leaving = []
    for cycle, lanes in enumerate(cycles):
        projected = jnp.dot(w_t, normed_ref[:, lanes], preferred_element_type=jnp.float32)
        sides = []
        for side in range(2):
            value = projected[2 * side * hidden : (2 * side + 1) * hidden]
            gate = projected[(2 * side + 1) * hidden : (2 * side + 2) * hidden]
            sides.append((sigmoid(gate) * value * keep[:, lanes]).reshape(peers, own, size))
        both = jnp.concatenate(sides, axis=1).astype(jnp.bfloat16)
        for group in range(groups):
            line = (cycle * groups + group) * 2 * own
            message_ref[:, line : line + 2 * own, :] = both[:, :, group * LANES : (group + 1) * LANES]
        lines = slice(cycle * groups * 2 * own, (cycle + 1) * groups * 2 * own)
        leaving += start_copies(
            out_sems.at[cycle],
            (message_ref.at[:, lines, :], message_hbm.at[:, lines, :]),
            (normed_ref.at[:, lanes], normed_hbm.at[:, lanes]),
        )
    for copy in leaving:
        copy.wait()


def gate_kernel(normed_ref, w_hbm, gain_hbm, w_out_hbm, gate_ref, w_out_ref, gain_ref, done_ref, w, w_out, gain, sems):
    fetch(sems, (w_hbm, w), (w_out_hbm, w_out), (gain_hbm, gain))
    last = w_hbm.shape[1] - w_hbm.shape[0]
    gate_ref[...] = sigmoid(
        jnp.dot(w[:, last:].T, normed_ref[...], preferred_element_type=jnp.float32)
    )
    w_out_ref[...] = w_out[...].T
    gain_ref[...] = jnp.broadcast_to(column(gain[...]), gain_ref.shape)
    done_ref[...] = jnp.zeros_like(done_ref)


def unpack(message_ref, spread_ref, own, cols):
    tokens, groups = cycle_of(cols)
    peers, lines, _ = message_ref.shape
    lane = lax.broadcasted_iota(jnp.int32, (2 * own, LANES), 1)
    cycles = lines // (2 * groups * own)
    for peer in range(peers):
        for cycle in range(cycles):
            base = cycle * groups
            held = [
                message_ref[peer, (base + group) * 2 * own : (base + group + 1) * 2 * own, :].astype(jnp.float32)
                for group in range(groups)
            ]
            for token in range(tokens):
                k = (peer * cycles + cycle) * tokens + token
                for chunk in range(spread_ref.shape[0]):
                    group, off = divmod(token * cols + chunk * LANES, LANES)
                    value = held[group]
                    if off and group + 1 < groups:
                        value = jnp.where(lane >= off, value, held[group + 1])
                    if off:
                        value = pltpu.roll(value, LANES - off, axis=1)
                    spread_ref[chunk, k * 2 * own : (k + 1) * 2 * own, :] = value


def pack(spread_ref, mixed_ref, first, own, cols):
    tokens, groups = cycle_of(cols)
    lane = lax.broadcasted_iota(jnp.int32, (own, LANES), 1)
    batch = 16 // math.gcd(groups * own, 16)
    for start in range(0, cols // tokens, batch):
        lines = []
        for at in range(start, start + batch):
            rolled = {}
            for group in range(groups):
                value, here = None, 0
                while here < LANES:
                    token, col = divmod(group * LANES + here, cols)
                    chunk, there = divmod(col, LANES)
                    shift = (here - there) % LANES
                    if (token, chunk, shift) not in rolled:
                        line = (at * tokens + token) * own
                        piece = spread_ref[chunk, line : line + own, :]
                        rolled[token, chunk, shift] = pltpu.roll(piece, shift, axis=1) if shift else piece
                    piece = rolled[token, chunk, shift]
                    value = piece if value is None else jnp.where(lane >= here, piece, value)
                    here += min(LANES - here, LANES - there, cols - col)
                lines.append(value)
        at = first + start * groups * own
        mixed_ref[at : at + batch * groups * own, :] = jnp.concatenate(lines, axis=0).astype(jnp.bfloat16)


def channel_of(spread_ref, line, stride):
    count = spread_ref.shape[1] // stride
    return jnp.concatenate(
        [spread_ref[chunk, pl.ds(line, count, stride=stride), :] for chunk in range(spread_ref.shape[0])],
        axis=1,
    ).astype(jnp.bfloat16)


def triangle_kernel(own, cols, message_ref, _, mixed_ref, spread, left, left_t, right, mixed):
    halves, chunks = spread.shape[:2]
    width = chunks * LANES
    deep = right.shape[1]
    depth = spread.shape[2] // (2 * own)
    one = identity(cols, width)
    if depth < deep:
        right[:, depth:, :] = jnp.zeros((own, deep - depth, halves * width), jnp.bfloat16)
    peers = message_ref.shape[0] // halves
    for half in range(halves):
        unpack(message_ref.at[half * peers : (half + 1) * peers], spread.at[half], own, cols)
        if depth < deep:
            left[:, half * deep + depth : (half + 1) * deep, :] = jnp.zeros((own, deep - depth, width), jnp.bfloat16)
        for channel in range(own):
            left[channel, half * deep : half * deep + depth, :] = channel_of(spread.at[half], channel, 2 * own)
            right[channel, :depth, half * width : (half + 1) * width] = channel_of(
                spread.at[half], own + channel, 2 * own
            )
    for channel in range(own):
        both = lax.dot_general(
            one, left[channel], (((1,), (1,)), ((), ())), preferred_element_type=jnp.float32
        ).astype(jnp.bfloat16)
        for half in range(halves):
            left_t[channel, half * cols : (half + 1) * cols, :] = both[:, half * deep : (half + 1) * deep]
    for channel in range(own):
        total = jnp.dot(left_t[channel], right[channel], preferred_element_type=jnp.float32)
        for i_half in range(halves):
            for j_half in range(halves):
                for chunk in range(chunks):
                    start = j_half * width + chunk * LANES
                    mixed[i_half, j_half, chunk, pl.ds(channel, cols, stride=own), :] = total[
                        i_half * cols : (i_half + 1) * cols, start : start + LANES
                    ]
    each = mixed_ref.shape[0] // (halves * halves)
    for j_half in range(halves):
        for i_half in range(halves):
            at = j_half * halves + i_half
            pack(mixed.at[i_half, j_half], mixed_ref, at * each, own, cols)


def output_kernel(own, shares, halves, mixed_ref, gate_ref, gain_ref, w_t_ref, update_ref, mixed, normed):
    lines = mixed.shape[1]
    peers = shares // PARTS
    mixed[...] = mixed_ref[...].astype(jnp.float32).reshape(mixed.shape)
    for group in range(lines // own):
        blocks = []
        for half in range(halves):
            first = half * shares
            block = mixed[first : first + peers, group * own : (group + 1) * own, :]
            for part in range(1, PARTS):
                start = first + part * peers
                block += mixed[start : start + peers, group * own : (group + 1) * own, :]
            blocks.append(block.reshape(peers * own, LANES))
        block = jnp.concatenate(blocks, axis=0)
        center = block - jnp.mean(block, axis=0, keepdims=True)
        spread = jnp.mean(center * center, axis=0, keepdims=True)
        normed[:, group * LANES : (group + 1) * LANES] = (
            center * lax.rsqrt(spread + EPS) * gain_ref[...]
        ).astype(jnp.bfloat16)
    projected = jnp.dot(w_t_ref[...], normed[...], preferred_element_type=jnp.float32)
    update = (gate_ref[...] * projected).astype(jnp.bfloat16)
    for group in range(lines // own):
        lanes = slice(group * LANES, (group + 1) * LANES)
        update_ref[lanes, :] = transpose(update[:, lanes]).astype(jnp.bfloat16)


def on_device(shares, halves, pair, tile_mask, chain_ids, gain_in, w_proj, gain_mid, w_out):
    rows, cols, width = pair.shape
    hidden = w_out.shape[0]
    peers = shares // PARTS
    own = hidden // (peers * halves)
    positions = rows * cols
    groups = positions // LANES
    lines = groups * own
    cycles = groups // cycle_of(cols)[1]
    params = pltpu.CompilerParams(vmem_limit_bytes=VMEM_BYTES)
    whole_params = pltpu.CompilerParams(vmem_limit_bytes=WHOLE_VMEM_BYTES)
    tokens = chain_ids.shape[0]
    message = jax.ShapeDtypeStruct((peers * halves, 2 * lines, LANES), jnp.bfloat16)
    message, normed = pl.pallas_call(
        functools.partial(project_kernel, rows, cols),
        out_shape=(message, jax.ShapeDtypeStruct((width, positions), jnp.bfloat16)),
        in_specs=[HBM] * 5,
        out_specs=(HBM, HBM),
        scratch_shapes=[
            pltpu.SMEM(tile_mask.shape, jnp.int32),
            pltpu.VMEM((1, tokens), jnp.int32),
            pltpu.VMEM((positions, width), jnp.bfloat16),
            pltpu.VMEM((1, width), jnp.float32),
            pltpu.VMEM(w_proj.shape, jnp.bfloat16),
            pltpu.VMEM(message.shape, jnp.bfloat16),
            pltpu.VMEM((width, positions), jnp.bfloat16),
            pltpu.SemaphoreType.DMA((5,)),
            pltpu.SemaphoreType.DMA((cycles, 2)),
        ],
        compiler_params=whole_params,
        name="project",
    )(tile_mask, chain_ids[None, :], pair.reshape(positions, width), gain_in[None, :], w_proj)
    message = lax.all_to_all(
        message,
        ("col", "row"),
        split_axis=0,
        concat_axis=0,
        axis_index_groups=[
            [half * shares + part * peers + at for half in range(halves) for at in range(peers)]
            for part in range(PARTS)
        ],
        tiled=True,
    )
    gate, w_out_t, gain, done = pl.pallas_call(
        gate_kernel,
        out_shape=(
            jax.ShapeDtypeStruct((width, positions), jnp.float32),
            jax.ShapeDtypeStruct(w_out.shape[::-1], jnp.bfloat16),
            jax.ShapeDtypeStruct((hidden, LANES), jnp.float32),
            jax.ShapeDtypeStruct((8, LANES), jnp.float32),
        ),
        in_specs=[VMEM, HBM, HBM, HBM],
        out_specs=(VMEM, VMEM, VMEM, VMEM),
        scratch_shapes=[
            pltpu.VMEM(w_proj.shape, jnp.bfloat16),
            pltpu.VMEM(w_out.shape, jnp.bfloat16),
            pltpu.VMEM((1, hidden), jnp.float32),
            pltpu.SemaphoreType.DMA((3,)),
        ],
        compiler_params=params,
        cost_estimate=pl.CostEstimate(
            flops=2 * width * width * positions, bytes_accessed=4 * width * positions, transcendentals=0
        ),
        name="gate",
    )(normed, w_proj, gain_mid[None, :], w_out)
    message, done = lax.optimization_barrier((message, done))
    chunks = pl.cdiv(cols, LANES)
    depth = peers * rows
    deep = pl.cdiv(depth, LANES) * LANES
    mixed = pl.pallas_call(
        functools.partial(triangle_kernel, own, cols),
        out_shape=jax.ShapeDtypeStruct((halves * shares * lines, LANES), jnp.bfloat16),
        in_specs=[VMEM, ANY],
        out_specs=VMEM,
        scratch_shapes=[
            pltpu.VMEM((halves, chunks, depth * 2 * own, LANES), jnp.float32),
            pltpu.VMEM((own, halves * deep, chunks * LANES), jnp.bfloat16),
            pltpu.VMEM((own, halves * cols, deep), jnp.bfloat16),
            pltpu.VMEM((own, deep, halves * chunks * LANES), jnp.bfloat16),
            pltpu.VMEM((halves, halves, chunks, cols * own, LANES), jnp.float32),
        ],
        compiler_params=params,
        name="triangle",
    )(message, done)
    mixed = lax.all_to_all(
        mixed.reshape(halves * shares, lines, LANES),
        ("col", "row"),
        split_axis=0,
        concat_axis=0,
        tiled=True,
    ).reshape(halves * shares * lines, LANES)
    update = pl.pallas_call(
        functools.partial(output_kernel, own, shares, halves),
        out_shape=jax.ShapeDtypeStruct((positions, width), jnp.bfloat16),
        in_specs=[VMEM] * 4,
        out_specs=VMEM,
        scratch_shapes=[
            pltpu.VMEM((halves * shares, lines, LANES), jnp.float32),
            pltpu.VMEM((hidden, positions), jnp.bfloat16),
        ],
        compiler_params=params,
        name="output",
    )(mixed, gate, gain, w_out_t)
    return update.reshape(rows, cols, width)


def solution(mesh):
    in_specs = (P(("grp", "row"), "col", None), P("grp", None), P("grp"), P(), P(), P(), P())
    out_specs = P(("grp", "row"), "col", None)
    return jax.shard_map(
        functools.partial(on_device, mesh.shape["row"], mesh.shape["col"]),
        mesh=mesh,
        in_specs=in_specs,
        out_specs=out_specs,
        check_vma=False,
    )
```

```python
import functools
import math

import jax
import jax.numpy as jnp
from jax import lax
from jax.experimental import pallas as pl
from jax.experimental.pallas import tpu as pltpu
from jax.sharding import PartitionSpec as P

TILE = 96
LANES = 128
EPS = 1e-05
PARTS = 2
VMEM_BYTES = 32 * 1024 * 1024
WHOLE_VMEM_BYTES = 64 * 1024 * 1024
VMEM = pl.BlockSpec(memory_space=pltpu.VMEM)
ANY = pl.BlockSpec(memory_space=pl.ANY)
HBM = pl.BlockSpec(memory_space=pltpu.HBM)
SMEM = pl.BlockSpec(memory_space=pltpu.SMEM)


def column(row):
    return jnp.broadcast_to(row, (8, row.shape[1])).T[:, :1]


def steps(at, width, count):
    total = jnp.zeros_like(at)
    for edge in range(1, count):
        total += (at >= edge * width).astype(jnp.int32)
    return total


def identity(rows, cols):
    same = lax.broadcasted_iota(jnp.int32, (rows, cols), 0) == lax.broadcasted_iota(jnp.int32, (rows, cols), 1)
    return same.astype(jnp.bfloat16)


def transpose(block):
    return lax.dot_general(
        identity(block.shape[1], block.shape[1]),
        block,
        (((1,), (1,)), ((), ())),
        preferred_element_type=jnp.float32,
    )


def sigmoid(values):
    return 0.5 * jnp.tanh(0.5 * values) + 0.5


def keep_of(tile_ref, chain_ref, rows, cols):
    tokens = chain_ref.shape[1]
    tiles = tile_ref.shape[1]
    positions = rows * cols
    at = lax.broadcasted_iota(jnp.int32, (1, positions), 1)
    row = steps(at, cols, rows)
    k = lax.axis_index("row") * rows + row
    i = lax.axis_index("col") * cols + at - row * cols
    token = lax.broadcasted_iota(jnp.int32, (tokens, positions), 0)
    pick = (token == k).astype(jnp.float32) - (token == i).astype(jnp.float32)
    chains = jnp.broadcast_to(chain_ref[...].astype(jnp.bfloat16), (8, tokens))
    apart = jnp.dot(chains, pick.astype(jnp.bfloat16), preferred_element_type=jnp.float32)[:1]
    k_tile = steps(k, TILE, tiles)
    i_tile = steps(i, TILE, tiles)
    tile_vals = jnp.zeros((1, positions), jnp.float32)
    for a in range(tiles):
        for b in range(tiles):
            here = (k_tile == a) & (i_tile == b)
            tile_vals = jnp.where(here, tile_ref[a, b].astype(jnp.float32), tile_vals)
    return jnp.where(apart == 0.0, 1.0, tile_vals)


def cycle_of(cols):
    cycle = math.lcm(cols, LANES)
    return cycle // cols, cycle // LANES


def start_copies(sems, *pairs):
    copies = [pltpu.make_async_copy(src, dst, sems.at[at]) for at, (src, dst) in enumerate(pairs)]
    for copy in copies:
        copy.start()
    return copies


def fetch(sems, *pairs):
    for copy in start_copies(sems, *pairs):
        copy.wait()


def project_kernel(
    rows, cols, tile_hbm, chain_hbm, pair_hbm, gain_hbm, w_hbm, message_hbm, normed_hbm,
    tile_ref, chain_ref, pair_ref, gain_ref, w_ref, message_ref, normed_ref, sems, out_sems,
):
    hidden = (w_ref.shape[1] - w_ref.shape[0]) // 4
    peers = message_ref.shape[0]
    own = hidden // peers
    groups = cycle_of(cols)[1]
    size = groups * LANES
    copies = start_copies(
        sems,
        (w_hbm, w_ref),
        (gain_hbm, gain_ref),
        (chain_hbm, chain_ref),
        (tile_hbm, tile_ref),
        (pair_hbm, pair_ref),
    )
    for copy in copies[:4]:
        copy.wait()
    keep = keep_of(tile_ref, chain_ref, rows, cols)
    w_t = w_ref[:, : 4 * hidden].T
    gain = column(gain_ref[...])
    copies[4].wait()
    cycles = [slice(start, start + size) for start in range(0, rows * cols, size)]
    for lanes in cycles:
        block = transpose(pair_ref[lanes, :])
        center = block - jnp.mean(block, axis=0, keepdims=True)
        spread = jnp.mean(center * center, axis=0, keepdims=True)
        normed_ref[:, lanes] = (center * lax.rsqrt(spread + EPS) * gain).astype(jnp.bfloat16)
    leaving = []
    for cycle, lanes in enumerate(cycles):
        projected = jnp.dot(w_t, normed_ref[:, lanes], preferred_element_type=jnp.float32)
        sides = []
        for side in range(2):
            value = projected[2 * side * hidden : (2 * side + 1) * hidden]
            gate = projected[(2 * side + 1) * hidden : (2 * side + 2) * hidden]
            sides.append((sigmoid(gate) * value * keep[:, lanes]).reshape(peers, own, size))
        both = jnp.concatenate(sides, axis=1).astype(jnp.bfloat16)
        for group in range(groups):
            line = (cycle * groups + group) * 2 * own
            message_ref[:, line : line + 2 * own, :] = both[:, :, group * LANES : (group + 1) * LANES]
        lines = slice(cycle * groups * 2 * own, (cycle + 1) * groups * 2 * own)
        leaving += start_copies(
            out_sems.at[cycle],
            (message_ref.at[:, lines, :], message_hbm.at[:, lines, :]),
            (normed_ref.at[:, lanes], normed_hbm.at[:, lanes]),
        )
    for copy in leaving:
        copy.wait()


def gate_kernel(normed_ref, w_hbm, gain_hbm, w_out_hbm, gate_ref, w_out_ref, gain_ref, done_ref, w, w_out, gain, sems):
    fetch(sems, (w_hbm, w), (w_out_hbm, w_out), (gain_hbm, gain))
    last = w_hbm.shape[1] - w_hbm.shape[0]
    gate_ref[...] = sigmoid(
        jnp.dot(w[:, last:].T, normed_ref[...], preferred_element_type=jnp.float32)
    )
    w_out_ref[...] = w_out[...].T
    gain_ref[...] = jnp.broadcast_to(column(gain[...]), gain_ref.shape)
    done_ref[...] = jnp.zeros_like(done_ref)


def unpack(message_ref, half, halves, spread_ref, own, cols):
    tokens, groups = cycle_of(cols)
    members, lines, _ = message_ref.shape
    peers = members // halves
    lane = lax.broadcasted_iota(jnp.int32, (2 * own, LANES), 1)
    cycles = lines // (2 * groups * own)
    for peer in range(peers):
        for cycle in range(cycles):
            base = cycle * groups
            held = [
                message_ref[
                    peer * halves + half, (base + group) * 2 * own : (base + group + 1) * 2 * own, :
                ].astype(jnp.float32)
                for group in range(groups)
            ]
            for token in range(tokens):
                k = (peer * cycles + cycle) * tokens + token
                for chunk in range(spread_ref.shape[0]):
                    group, off = divmod(token * cols + chunk * LANES, LANES)
                    value = held[group]
                    if off and group + 1 < groups:
                        value = jnp.where(lane >= off, value, held[group + 1])
                    if off:
                        value = pltpu.roll(value, LANES - off, axis=1)
                    spread_ref[chunk, k * 2 * own : (k + 1) * 2 * own, :] = value


def pack(spread_ref, at, own, cols):
    tokens, groups = cycle_of(cols)
    lane = lax.broadcasted_iota(jnp.int32, (own, LANES), 1)
    rolled, lines = {}, []
    for group in range(groups):
        value, here = None, 0
        while here < LANES:
            token, col = divmod(group * LANES + here, cols)
            chunk, there = divmod(col, LANES)
            shift = (here - there) % LANES
            if (token, chunk, shift) not in rolled:
                line = (at * tokens + token) * own
                piece = spread_ref[chunk, line : line + own, :]
                rolled[token, chunk, shift] = pltpu.roll(piece, shift, axis=1) if shift else piece
            piece = rolled[token, chunk, shift]
            value = piece if value is None else jnp.where(lane >= here, piece, value)
            here += min(LANES - here, LANES - there, cols - col)
        lines.append(value)
    return lines


def channel_of(spread_ref, line, stride):
    count = spread_ref.shape[1] // stride
    return jnp.concatenate(
        [spread_ref[chunk, pl.ds(line, count, stride=stride), :] for chunk in range(spread_ref.shape[0])],
        axis=1,
    ).astype(jnp.bfloat16)


def triangle_kernel(own, cols, shares, message_ref, _, mixed_ref, spread, left, left_t, right, mixed):
    halves, chunks = spread.shape[:2]
    width = chunks * LANES
    deep = right.shape[1]
    depth = spread.shape[2] // (2 * own)
    one = identity(cols, width)
    if depth < deep:
        right[:, depth:, :] = jnp.zeros((own, deep - depth, halves * width), jnp.bfloat16)
    for half in range(halves):
        unpack(message_ref, half, halves, spread.at[half], own, cols)
        if depth < deep:
            left[:, half * deep + depth : (half + 1) * deep, :] = jnp.zeros((own, deep - depth, width), jnp.bfloat16)
        for channel in range(own):
            left[channel, half * deep : half * deep + depth, :] = channel_of(spread.at[half], channel, 2 * own)
            right[channel, :depth, half * width : (half + 1) * width] = channel_of(
                spread.at[half], own + channel, 2 * own
            )
    for channel in range(own):
        both = lax.dot_general(
            one, left[channel], (((1,), (1,)), ((), ())), preferred_element_type=jnp.float32
        ).astype(jnp.bfloat16)
        for half in range(halves):
            left_t[channel, half * cols : (half + 1) * cols, :] = both[:, half * deep : (half + 1) * deep]
    for channel in range(own):
        total = jnp.dot(left_t[channel], right[channel], preferred_element_type=jnp.float32)
        for i_half in range(halves):
            for j_half in range(halves):
                for chunk in range(chunks):
                    start = j_half * width + chunk * LANES
                    mixed[i_half, j_half, chunk, pl.ds(channel, cols, stride=own), :] = total[
                        i_half * cols : (i_half + 1) * cols, start : start + LANES
                    ]
    groups = cycle_of(cols)[1]
    each = mixed_ref.shape[0] // shares
    cycles = each // (halves * groups * own)
    for share in range(shares):
        i_half, peer = divmod(share, shares // halves)
        lines = []
        for j_half in range(halves):
            for cycle in range(cycles):
                lines += pack(mixed.at[i_half, j_half], peer * cycles + cycle, own, cols)
        mixed_ref[share * each : (share + 1) * each, :] = jnp.concatenate(lines, axis=0).astype(jnp.bfloat16)


def output_kernel(own, parts, mixed_ref, gate_ref, gain_ref, w_t_ref, update_hbm, mixed, update, sems):
    members, lines, _ = mixed.shape
    members = members // parts
    mixed[...] = mixed_ref[...].astype(jnp.float32).reshape(mixed.shape)
    groups = lines // own
    steps = math.gcd(groups, 3)
    leaving = []
    for group in range(groups):
        sums = mixed[:members, group * own : (group + 1) * own, :]
        for part in range(1, parts):
            sums += mixed[part * members : (part + 1) * members, group * own : (group + 1) * own, :]
        block = sums.reshape(members * own, LANES)
        center = block - jnp.mean(block, axis=0, keepdims=True)
        spread = jnp.mean(center * center, axis=0, keepdims=True)
        normed = (center * lax.rsqrt(spread + EPS) * gain_ref[...]).astype(jnp.bfloat16)
        projected = jnp.dot(w_t_ref[...], normed, preferred_element_type=jnp.float32)
        lanes = slice(group * LANES, (group + 1) * LANES)
        update[lanes, :] = (gate_ref[:, lanes] * projected).T.astype(jnp.bfloat16)
        step, last = divmod((group + 1) * steps, groups)
        if last == 0:
            done = slice((step - 1) * (groups // steps) * LANES, (group + 1) * LANES)
            leaving += start_copies(sems.at[step - 1], (update.at[done, :], update_hbm.at[done, :]))
    for copy in leaving:
        copy.wait()


def on_device(shares, halves, pair, tile_mask, chain_ids, gain_in, w_proj, gain_mid, w_out):
    rows, cols, width = pair.shape
    hidden = w_out.shape[0]
    peers = shares // PARTS
    own = hidden // (peers * halves)
    positions = rows * cols
    groups = positions // LANES
    lines = groups * own
    cycles = groups // cycle_of(cols)[1]
    params = pltpu.CompilerParams(vmem_limit_bytes=VMEM_BYTES)
    whole_params = pltpu.CompilerParams(vmem_limit_bytes=WHOLE_VMEM_BYTES)
    tokens = chain_ids.shape[0]
    message = jax.ShapeDtypeStruct((peers * halves, 2 * lines, LANES), jnp.bfloat16)
    message, normed = pl.pallas_call(
        functools.partial(project_kernel, rows, cols),
        out_shape=(message, jax.ShapeDtypeStruct((width, positions), jnp.bfloat16)),
        in_specs=[HBM] * 5,
        out_specs=(HBM, HBM),
        scratch_shapes=[
            pltpu.SMEM(tile_mask.shape, jnp.int32),
            pltpu.VMEM((1, tokens), jnp.int32),
            pltpu.VMEM((positions, width), jnp.bfloat16),
            pltpu.VMEM((1, width), jnp.float32),
            pltpu.VMEM(w_proj.shape, jnp.bfloat16),
            pltpu.VMEM(message.shape, jnp.bfloat16),
            pltpu.VMEM((width, positions), jnp.bfloat16),
            pltpu.SemaphoreType.DMA((5,)),
            pltpu.SemaphoreType.DMA((cycles, 2)),
        ],
        compiler_params=whole_params,
        name="project",
    )(tile_mask, chain_ids[None, :], pair.reshape(positions, width), gain_in[None, :], w_proj)
    message = lax.all_to_all(
        message,
        ("row", "col"),
        split_axis=0,
        concat_axis=0,
        axis_index_groups=[
            list(range(part * peers * halves, (part + 1) * peers * halves))
            for part in range(PARTS)
        ],
        tiled=True,
    )
    gate, w_out_t, gain, done = pl.pallas_call(
        gate_kernel,
        out_shape=(
            jax.ShapeDtypeStruct((width, positions), jnp.float32),
            jax.ShapeDtypeStruct(w_out.shape[::-1], jnp.bfloat16),
            jax.ShapeDtypeStruct((hidden, LANES), jnp.float32),
            jax.ShapeDtypeStruct((8, LANES), jnp.float32),
        ),
        in_specs=[VMEM, HBM, HBM, HBM],
        out_specs=(VMEM, VMEM, VMEM, VMEM),
        scratch_shapes=[
            pltpu.VMEM(w_proj.shape, jnp.bfloat16),
            pltpu.VMEM(w_out.shape, jnp.bfloat16),
            pltpu.VMEM((1, hidden), jnp.float32),
            pltpu.SemaphoreType.DMA((3,)),
        ],
        compiler_params=params,
        cost_estimate=pl.CostEstimate(
            flops=2 * width * width * positions, bytes_accessed=4 * width * positions, transcendentals=0
        ),
        name="gate",
    )(normed, w_proj, gain_mid[None, :], w_out)
    message, done = lax.optimization_barrier((message, done))
    chunks = pl.cdiv(cols, LANES)
    depth = peers * rows
    deep = pl.cdiv(depth, LANES) * LANES
    mixed = pl.pallas_call(
        functools.partial(triangle_kernel, own, cols, shares),
        out_shape=jax.ShapeDtypeStruct((halves * shares * lines, LANES), jnp.bfloat16),
        in_specs=[VMEM, ANY],
        out_specs=VMEM,
        scratch_shapes=[
            pltpu.VMEM((halves, chunks, depth * 2 * own, LANES), jnp.float32),
            pltpu.VMEM((own, halves * deep, chunks * LANES), jnp.bfloat16),
            pltpu.VMEM((own, halves * cols, deep), jnp.bfloat16),
            pltpu.VMEM((own, deep, halves * chunks * LANES), jnp.bfloat16),
            pltpu.VMEM((halves, halves, chunks, cols * own, LANES), jnp.float32),
        ],
        compiler_params=params,
        name="triangle",
    )(message, done)
    mixed = lax.all_to_all(
        mixed.reshape(halves * shares, lines, LANES),
        ("row", "col"),
        split_axis=0,
        concat_axis=0,
        tiled=True,
    ).reshape(halves * shares * lines, LANES)
    update = pl.pallas_call(
        functools.partial(output_kernel, own, PARTS),
        out_shape=jax.ShapeDtypeStruct((positions, width), jnp.bfloat16),
        in_specs=[VMEM] * 4,
        out_specs=HBM,
        scratch_shapes=[
            pltpu.VMEM((shares * halves, lines, LANES), jnp.float32),
            pltpu.VMEM((positions, width), jnp.bfloat16),
            pltpu.SemaphoreType.DMA((math.gcd(groups, 3), 1)),
        ],
        compiler_params=params,
        name="output",
    )(mixed, gate, gain, w_out_t)
    return update.reshape(rows, cols, width)


def solution(mesh):
    in_specs = (P(("grp", "row"), "col", None), P("grp", None), P("grp"), P(), P(), P(), P())
    out_specs = P(("grp", "row"), "col", None)
    return jax.shard_map(
        functools.partial(on_device, mesh.shape["row"], mesh.shape["col"]),
        mesh=mesh,
        in_specs=in_specs,
        out_specs=out_specs,
        check_vma=False,
    )
```

```python
import functools
import math

import jax
import jax.numpy as jnp
from jax import lax
from jax.experimental import pallas as pl
from jax.experimental.pallas import tpu as pltpu
from jax.sharding import PartitionSpec as P

TILE = 96
LANES = 128
EPS = 1e-05
PARTS = 2
VMEM_BYTES = 32 * 1024 * 1024
WHOLE_VMEM_BYTES = 64 * 1024 * 1024
VMEM = pl.BlockSpec(memory_space=pltpu.VMEM)
ANY = pl.BlockSpec(memory_space=pl.ANY)
HBM = pl.BlockSpec(memory_space=pltpu.HBM)
SMEM = pl.BlockSpec(memory_space=pltpu.SMEM)


def forward_order(peers, halves):
    bits = (peers - 1).bit_length()
    turned = sorted(range(peers), key=lambda at: sum((at >> bit & 1) << (bits - 1 - bit) for bit in range(bits)))
    return [(at, half) for half in range(halves) for at in turned]


def return_order(peers, halves, parts):
    return [(part, at, half) for at in range(peers) for half in range(halves) for part in range(parts)]


def column(row):
    return jnp.broadcast_to(row, (8, row.shape[1])).T[:, :1]


def steps(at, width, count):
    total = jnp.zeros_like(at)
    for edge in range(1, count):
        total += (at >= edge * width).astype(jnp.int32)
    return total


def identity(rows, cols):
    same = lax.broadcasted_iota(jnp.int32, (rows, cols), 0) == lax.broadcasted_iota(jnp.int32, (rows, cols), 1)
    return same.astype(jnp.bfloat16)


def transpose(block):
    return lax.dot_general(
        identity(block.shape[1], block.shape[1]),
        block,
        (((1,), (1,)), ((), ())),
        preferred_element_type=jnp.float32,
    )


def sigmoid(values):
    return 0.5 * jnp.tanh(0.5 * values) + 0.5


def keep_of(tile_ref, chain_ref, rows, cols):
    tokens = chain_ref.shape[1]
    tiles = tile_ref.shape[1]
    positions = rows * cols
    at = lax.broadcasted_iota(jnp.int32, (1, positions), 1)
    row = steps(at, cols, rows)
    k = lax.axis_index("row") * rows + row
    i = lax.axis_index("col") * cols + at - row * cols
    token = lax.broadcasted_iota(jnp.int32, (tokens, positions), 0)
    pick = (token == k).astype(jnp.float32) - (token == i).astype(jnp.float32)
    chains = jnp.broadcast_to(chain_ref[...].astype(jnp.bfloat16), (8, tokens))
    apart = jnp.dot(chains, pick.astype(jnp.bfloat16), preferred_element_type=jnp.float32)[:1]
    k_tile = steps(k, TILE, tiles)
    i_tile = steps(i, TILE, tiles)
    tile_vals = jnp.zeros((1, positions), jnp.float32)
    for a in range(tiles):
        for b in range(tiles):
            here = (k_tile == a) & (i_tile == b)
            tile_vals = jnp.where(here, tile_ref[a, b].astype(jnp.float32), tile_vals)
    return jnp.where(apart == 0.0, 1.0, tile_vals)


def cycle_of(cols):
    cycle = math.lcm(cols, LANES)
    return cycle // cols, cycle // LANES


def start_copies(sems, *pairs):
    copies = [pltpu.make_async_copy(src, dst, sems.at[at]) for at, (src, dst) in enumerate(pairs)]
    for copy in copies:
        copy.start()
    return copies


def fetch(sems, *pairs):
    for copy in start_copies(sems, *pairs):
        copy.wait()


def project_kernel(
    rows, cols, tile_hbm, chain_hbm, pair_hbm, gain_hbm, w_hbm, message_hbm, normed_hbm,
    tile_ref, chain_ref, pair_ref, gain_ref, w_ref, message_ref, normed_ref, sems, out_sems,
):
    hidden = (w_ref.shape[1] - w_ref.shape[0]) // 4
    peers = message_ref.shape[0]
    own = hidden // peers
    groups = cycle_of(cols)[1]
    size = groups * LANES
    copies = start_copies(
        sems,
        (w_hbm, w_ref),
        (gain_hbm, gain_ref),
        (chain_hbm, chain_ref),
        (tile_hbm, tile_ref),
        (pair_hbm, pair_ref),
    )
    for copy in copies[:4]:
        copy.wait()
    keep = keep_of(tile_ref, chain_ref, rows, cols)
    w_t = w_ref[:, : 4 * hidden].T
    gain = column(gain_ref[...])
    copies[4].wait()
    cycles = [slice(start, start + size) for start in range(0, rows * cols, size)]
    for lanes in cycles:
        block = transpose(pair_ref[lanes, :])
        center = block - jnp.mean(block, axis=0, keepdims=True)
        spread = jnp.mean(center * center, axis=0, keepdims=True)
        normed_ref[:, lanes] = (center * lax.rsqrt(spread + EPS) * gain).astype(jnp.bfloat16)
    leaving = []
    for cycle, lanes in enumerate(cycles):
        projected = jnp.dot(w_t, normed_ref[:, lanes], preferred_element_type=jnp.float32)
        sides = []
        for side in range(2):
            value = projected[2 * side * hidden : (2 * side + 1) * hidden]
            gate = projected[(2 * side + 1) * hidden : (2 * side + 2) * hidden]
            sides.append((sigmoid(gate) * value * keep[:, lanes]).reshape(peers, own, size))
        both = jnp.concatenate(sides, axis=1).astype(jnp.bfloat16)
        for group in range(groups):
            line = (cycle * groups + group) * 2 * own
            message_ref[:, line : line + 2 * own, :] = both[:, :, group * LANES : (group + 1) * LANES]
        lines = slice(cycle * groups * 2 * own, (cycle + 1) * groups * 2 * own)
        leaving += start_copies(
            out_sems.at[cycle],
            (message_ref.at[:, lines, :], message_hbm.at[:, lines, :]),
            (normed_ref.at[:, lanes], normed_hbm.at[:, lanes]),
        )
    for copy in leaving:
        copy.wait()


def gate_kernel(normed_ref, w_hbm, gain_hbm, w_out_hbm, gate_ref, w_out_ref, gain_ref, done_ref, w, w_out, gain, sems):
    fetch(sems, (w_hbm, w), (w_out_hbm, w_out), (gain_hbm, gain))
    last = w_hbm.shape[1] - w_hbm.shape[0]
    gate_ref[...] = sigmoid(
        jnp.dot(w[:, last:].T, normed_ref[...], preferred_element_type=jnp.float32)
    )
    w_out_ref[...] = w_out[...].T
    gain_ref[...] = jnp.broadcast_to(column(gain[...]), gain_ref.shape)
    done_ref[...] = jnp.zeros_like(done_ref)


def unpack(message_ref, half, halves, spread_ref, own, cols):
    tokens, groups = cycle_of(cols)
    members, lines, _ = message_ref.shape
    peers = members // halves
    order = forward_order(peers, halves)
    lane = lax.broadcasted_iota(jnp.int32, (2 * own, LANES), 1)
    cycles = lines // (2 * groups * own)
    for peer in range(peers):
        member = order.index((peer, half))
        for cycle in range(cycles):
            base = cycle * groups
            held = [
                message_ref[
                    member, (base + group) * 2 * own : (base + group + 1) * 2 * own, :
                ].astype(jnp.float32)
                for group in range(groups)
            ]
            for token in range(tokens):
                k = (peer * cycles + cycle) * tokens + token
                for chunk in range(spread_ref.shape[0]):
                    group, off = divmod(token * cols + chunk * LANES, LANES)
                    value = held[group]
                    if off and group + 1 < groups:
                        value = jnp.where(lane >= off, value, held[group + 1])
                    if off:
                        value = pltpu.roll(value, LANES - off, axis=1)
                    spread_ref[chunk, k * 2 * own : (k + 1) * 2 * own, :] = value


def pack(spread_ref, at, own, cols):
    tokens, groups = cycle_of(cols)
    lane = lax.broadcasted_iota(jnp.int32, (own, LANES), 1)
    rolled, lines = {}, []
    for group in range(groups):
        value, here = None, 0
        while here < LANES:
            token, col = divmod(group * LANES + here, cols)
            chunk, there = divmod(col, LANES)
            shift = (here - there) % LANES
            if (token, chunk, shift) not in rolled:
                line = (at * tokens + token) * own
                piece = spread_ref[chunk, line : line + own, :]
                rolled[token, chunk, shift] = pltpu.roll(piece, shift, axis=1) if shift else piece
            piece = rolled[token, chunk, shift]
            value = piece if value is None else jnp.where(lane >= here, piece, value)
            here += min(LANES - here, LANES - there, cols - col)
        lines.append(value)
    return lines


def channel_of(spread_ref, line, stride):
    count = spread_ref.shape[1] // stride
    return jnp.concatenate(
        [spread_ref[chunk, pl.ds(line, count, stride=stride), :] for chunk in range(spread_ref.shape[0])],
        axis=1,
    ).astype(jnp.bfloat16)


def triangle_kernel(own, cols, shares, parts, message_ref, _, mixed_ref, spread, left, left_t, right, mixed):
    halves, chunks = spread.shape[:2]
    width = chunks * LANES
    deep = right.shape[1]
    depth = spread.shape[2] // (2 * own)
    one = identity(cols, width)
    if depth < deep:
        right[:, depth:, :] = jnp.zeros((own, deep - depth, halves * width), jnp.bfloat16)
    for half in range(halves):
        unpack(message_ref, half, halves, spread.at[half], own, cols)
        if depth < deep:
            left[:, half * deep + depth : (half + 1) * deep, :] = jnp.zeros((own, deep - depth, width), jnp.bfloat16)
        for channel in range(own):
            left[channel, half * deep : half * deep + depth, :] = channel_of(spread.at[half], channel, 2 * own)
            right[channel, :depth, half * width : (half + 1) * width] = channel_of(
                spread.at[half], own + channel, 2 * own
            )
    for channel in range(own):
        both = lax.dot_general(
            one, left[channel], (((1,), (1,)), ((), ())), preferred_element_type=jnp.float32
        ).astype(jnp.bfloat16)
        for half in range(halves):
            left_t[channel, half * cols : (half + 1) * cols, :] = both[:, half * deep : (half + 1) * deep]
    for channel in range(own):
        total = jnp.dot(left_t[channel], right[channel], preferred_element_type=jnp.float32)
        for i_half in range(halves):
            for j_half in range(halves):
                for chunk in range(chunks):
                    start = j_half * width + chunk * LANES
                    mixed[i_half, j_half, chunk, pl.ds(channel, cols, stride=own), :] = total[
                        i_half * cols : (i_half + 1) * cols, start : start + LANES
                    ]
    groups = cycle_of(cols)[1]
    peers = shares // parts
    order = return_order(peers, halves, parts)
    each = mixed_ref.shape[0] // len(order)
    cycles = each // (groups * own)
    batch = 16 // math.gcd(each, 16)
    for start in range(0, len(order), batch):
        lines = []
        for part, at, j_half in order[start : start + batch]:
            i_half, peer = divmod(part * peers + at, shares // halves)
            for cycle in range(cycles):
                lines += pack(mixed.at[i_half, j_half], peer * cycles + cycle, own, cols)
        mixed_ref[start * each : (start + batch) * each, :] = jnp.concatenate(lines, axis=0).astype(jnp.bfloat16)


def output_kernel(own, halves, parts, mixed_ref, gate_ref, gain_ref, w_t_ref, update_hbm, mixed, update, sems):
    members, lines, _ = mixed.shape
    peers = members // (halves * parts)
    order = return_order(peers, halves, parts)
    mixed[...] = mixed_ref[...].astype(jnp.float32).reshape(mixed.shape)
    groups = lines // own
    steps = math.gcd(groups, 3)
    leaving = []
    for group in range(groups):
        blocks = []
        for at, half in forward_order(peers, halves):
            pieces = [
                mixed[order.index((part, at, half)), group * own : (group + 1) * own, :] for part in range(parts)
            ]
            blocks.append(functools.reduce(jnp.add, pieces))
        block = jnp.concatenate(blocks, axis=0)
        center = block - jnp.mean(block, axis=0, keepdims=True)
        spread = jnp.mean(center * center, axis=0, keepdims=True)
        normed = (center * lax.rsqrt(spread + EPS) * gain_ref[...]).astype(jnp.bfloat16)
        projected = jnp.dot(w_t_ref[...], normed, preferred_element_type=jnp.float32)
        lanes = slice(group * LANES, (group + 1) * LANES)
        update[lanes, :] = (gate_ref[:, lanes] * projected).T.astype(jnp.bfloat16)
        step, last = divmod((group + 1) * steps, groups)
        if last == 0:
            done = slice((step - 1) * (groups // steps) * LANES, (group + 1) * LANES)
            leaving += start_copies(sems.at[step - 1], (update.at[done, :], update_hbm.at[done, :]))
    for copy in leaving:
        copy.wait()


def on_device(shares, halves, pair, tile_mask, chain_ids, gain_in, w_proj, gain_mid, w_out):
    rows, cols, width = pair.shape
    hidden = w_out.shape[0]
    peers = shares // PARTS
    own = hidden // (peers * halves)
    positions = rows * cols
    groups = positions // LANES
    lines = groups * own
    cycles = groups // cycle_of(cols)[1]
    params = pltpu.CompilerParams(vmem_limit_bytes=VMEM_BYTES)
    whole_params = pltpu.CompilerParams(vmem_limit_bytes=WHOLE_VMEM_BYTES)
    tokens = chain_ids.shape[0]
    message = jax.ShapeDtypeStruct((peers * halves, 2 * lines, LANES), jnp.bfloat16)
    message, normed = pl.pallas_call(
        functools.partial(project_kernel, rows, cols),
        out_shape=(message, jax.ShapeDtypeStruct((width, positions), jnp.bfloat16)),
        in_specs=[HBM] * 5,
        out_specs=(HBM, HBM),
        scratch_shapes=[
            pltpu.SMEM(tile_mask.shape, jnp.int32),
            pltpu.VMEM((1, tokens), jnp.int32),
            pltpu.VMEM((positions, width), jnp.bfloat16),
            pltpu.VMEM((1, width), jnp.float32),
            pltpu.VMEM(w_proj.shape, jnp.bfloat16),
            pltpu.VMEM(message.shape, jnp.bfloat16),
            pltpu.VMEM((width, positions), jnp.bfloat16),
            pltpu.SemaphoreType.DMA((5,)),
            pltpu.SemaphoreType.DMA((cycles, 2)),
        ],
        compiler_params=whole_params,
        name="project",
    )(tile_mask, chain_ids[None, :], pair.reshape(positions, width), gain_in[None, :], w_proj)
    message = lax.all_to_all(
        message,
        ("row", "col"),
        split_axis=0,
        concat_axis=0,
        axis_index_groups=[
            [(part * peers + at) * halves + half for at, half in forward_order(peers, halves)]
            for part in range(PARTS)
        ],
        tiled=True,
    )
    gate, w_out_t, gain, done = pl.pallas_call(
        gate_kernel,
        out_shape=(
            jax.ShapeDtypeStruct((width, positions), jnp.float32),
            jax.ShapeDtypeStruct(w_out.shape[::-1], jnp.bfloat16),
            jax.ShapeDtypeStruct((hidden, LANES), jnp.float32),
            jax.ShapeDtypeStruct((8, LANES), jnp.float32),
        ),
        in_specs=[VMEM, HBM, HBM, HBM],
        out_specs=(VMEM, VMEM, VMEM, VMEM),
        scratch_shapes=[
            pltpu.VMEM(w_proj.shape, jnp.bfloat16),
            pltpu.VMEM(w_out.shape, jnp.bfloat16),
            pltpu.VMEM((1, hidden), jnp.float32),
            pltpu.SemaphoreType.DMA((3,)),
        ],
        compiler_params=params,
        cost_estimate=pl.CostEstimate(
            flops=2 * width * width * positions, bytes_accessed=4 * width * positions, transcendentals=0
        ),
        name="gate",
    )(normed, w_proj, gain_mid[None, :], w_out)
    message, done = lax.optimization_barrier((message, done))
    chunks = pl.cdiv(cols, LANES)
    depth = peers * rows
    deep = pl.cdiv(depth, LANES) * LANES
    mixed = pl.pallas_call(
        functools.partial(triangle_kernel, own, cols, shares, PARTS),
        out_shape=jax.ShapeDtypeStruct((halves * shares * lines, LANES), jnp.bfloat16),
        in_specs=[VMEM, ANY],
        out_specs=VMEM,
        scratch_shapes=[
            pltpu.VMEM((halves, chunks, depth * 2 * own, LANES), jnp.float32),
            pltpu.VMEM((own, halves * deep, chunks * LANES), jnp.bfloat16),
            pltpu.VMEM((own, halves * cols, deep), jnp.bfloat16),
            pltpu.VMEM((own, deep, halves * chunks * LANES), jnp.bfloat16),
            pltpu.VMEM((halves, halves, chunks, cols * own, LANES), jnp.float32),
        ],
        compiler_params=params,
        name="triangle",
    )(message, done)
    mixed = lax.all_to_all(
        mixed.reshape(halves * shares, lines, LANES),
        ("row", "col"),
        split_axis=0,
        concat_axis=0,
        axis_index_groups=[
            [(part * peers + at) * halves + half for part, at, half in return_order(peers, halves, PARTS)]
        ],
        tiled=True,
    ).reshape(halves * shares * lines, LANES)
    update = pl.pallas_call(
        functools.partial(output_kernel, own, halves, PARTS),
        out_shape=jax.ShapeDtypeStruct((positions, width), jnp.bfloat16),
        in_specs=[VMEM] * 4,
        out_specs=HBM,
        scratch_shapes=[
            pltpu.VMEM((shares * halves, lines, LANES), jnp.float32),
            pltpu.VMEM((positions, width), jnp.bfloat16),
            pltpu.SemaphoreType.DMA((math.gcd(groups, 3), 1)),
        ],
        compiler_params=params,
        name="output",
    )(mixed, gate, gain, w_out_t)
    return update.reshape(rows, cols, width)


def solution(mesh):
    in_specs = (P(("grp", "row"), "col", None), P("grp", None), P("grp"), P(), P(), P(), P())
    out_specs = P(("grp", "row"), "col", None)
    return jax.shard_map(
        functools.partial(on_device, mesh.shape["row"], mesh.shape["col"]),
        mesh=mesh,
        in_specs=in_specs,
        out_specs=out_specs,
        check_vma=False,
    )
```

```python
import functools
import math

import jax
import jax.numpy as jnp
from jax import lax
from jax.experimental import pallas as pl
from jax.experimental.pallas import tpu as pltpu
from jax.sharding import PartitionSpec as P

TILE = 96
LANES = 128
EPS = 1e-05
OWN = 4
VMEM_BYTES = 32 * 1024 * 1024
WHOLE_VMEM_BYTES = 64 * 1024 * 1024
ROWS = 8
VMEM = pl.BlockSpec(memory_space=pltpu.VMEM)
ANY = pl.BlockSpec(memory_space=pl.ANY)
HBM = pl.BlockSpec(memory_space=pltpu.HBM)
SMEM = pl.BlockSpec(memory_space=pltpu.SMEM)


def column(row):
    return jnp.broadcast_to(row, (8, row.shape[1])).T[:, :1]


def steps(at, width, count):
    total = jnp.zeros_like(at)
    for edge in range(1, count):
        total += (at >= edge * width).astype(jnp.int32)
    return total


def identity(rows, cols):
    same = lax.broadcasted_iota(jnp.int32, (rows, cols), 0) == lax.broadcasted_iota(jnp.int32, (rows, cols), 1)
    return same.astype(jnp.bfloat16)


def transpose(block):
    return lax.dot_general(
        identity(block.shape[1], block.shape[1]),
        block,
        (((1,), (1,)), ((), ())),
        preferred_element_type=jnp.float32,
    )


def sigmoid(values):
    return 0.5 * jnp.tanh(0.5 * values) + 0.5


def keep_of(tile_ref, chain_ref, rows, cols):
    tokens = chain_ref.shape[1]
    tiles = tile_ref.shape[1]
    positions = rows * cols
    at = lax.broadcasted_iota(jnp.int32, (1, positions), 1)
    row = steps(at, cols, rows)
    k = lax.axis_index("row") * rows + row
    i = lax.axis_index("col") * cols + at - row * cols
    token = lax.broadcasted_iota(jnp.int32, (tokens, positions), 0)
    pick = (token == k).astype(jnp.float32) - (token == i).astype(jnp.float32)
    chains = jnp.broadcast_to(chain_ref[...].astype(jnp.bfloat16), (8, tokens))
    apart = jnp.dot(chains, pick.astype(jnp.bfloat16), preferred_element_type=jnp.float32)[:1]
    k_tile = steps(k, TILE, tiles)
    i_tile = steps(i, TILE, tiles)
    tile_vals = jnp.zeros((1, positions), jnp.float32)
    for a in range(tiles):
        for b in range(tiles):
            here = (k_tile == a) & (i_tile == b)
            tile_vals = jnp.where(here, tile_ref[a, b].astype(jnp.float32), tile_vals)
    return jnp.where(apart == 0.0, 1.0, tile_vals)


def cycle_of(cols):
    cycle = math.lcm(cols, LANES)
    return cycle // cols, cycle // LANES


def start_copies(sems, *pairs):
    copies = [pltpu.make_async_copy(src, dst, sems.at[at]) for at, (src, dst) in enumerate(pairs)]
    for copy in copies:
        copy.start()
    return copies


def fetch(sems, *pairs):
    for copy in start_copies(sems, *pairs):
        copy.wait()


def turn_pairs(first, second):
    axis = first.ndim - 2
    upper = lax.broadcasted_iota(jnp.int32, first.shape, axis) < OWN
    return (
        jnp.where(upper, first, pltpu.roll(second, OWN, axis=axis)),
        jnp.where(upper, pltpu.roll(first, OWN, axis=axis), second),
    )


def sides_by_member(left, right):
    lines, width = left.shape
    pairs = turn_pairs(left.reshape(-1, ROWS, width), right.reshape(-1, ROWS, width))
    return jnp.stack(pairs, axis=1).reshape(2 * lines, width).astype(jnp.bfloat16)


def project_kernel(
    rows, cols, tile_hbm, chain_hbm, pair_hbm, gain_hbm, w_hbm, message_hbm, normed_hbm,
    tile_ref, chain_ref, pair_ref, gain_ref, w_ref, held, message_ref, normed_ref, sems, out_sems,
):
    hidden = (w_ref.shape[1] - w_ref.shape[0]) // 4
    members = held.shape[0]
    size = cycle_of(cols)[1] * LANES
    copies = start_copies(
        sems,
        (w_hbm, w_ref),
        (gain_hbm, gain_ref),
        (chain_hbm, chain_ref),
        (tile_hbm, tile_ref),
        (pair_hbm, pair_ref),
    )
    for copy in copies[:4]:
        copy.wait()
    keep = keep_of(tile_ref, chain_ref, rows, cols)
    w_t = w_ref[:, : 4 * hidden].astype(jnp.float32).T
    w_value = sides_by_member(w_t[:hidden], w_t[2 * hidden : 3 * hidden])
    w_gate = sides_by_member(w_t[hidden : 2 * hidden], w_t[3 * hidden :])
    gain = column(gain_ref[...])
    copies[4].wait()
    cycles = [slice(start, start + size) for start in range(0, rows * cols, size)]
    for lanes in cycles:
        block = transpose(pair_ref[lanes, :])
        center = block - jnp.mean(block, axis=0, keepdims=True)
        spread = jnp.mean(center * center, axis=0, keepdims=True)
        normed_ref[:, lanes] = (center * lax.rsqrt(spread + EPS) * gain).astype(jnp.bfloat16)
    leaving = start_copies(out_sems.at[0], (normed_ref, normed_hbm))
    for lanes in cycles:
        normed = normed_ref[:, lanes]
        value = jnp.dot(w_value, normed, preferred_element_type=jnp.float32)
        gate = jnp.dot(w_gate, normed, preferred_element_type=jnp.float32)
        sent = (sigmoid(gate) * value * keep[:, lanes]).reshape(members, ROWS, size)
        for start in range(0, size, LANES):
            line = (lanes.start + start) // LANES * ROWS
            held[:, line : line + ROWS, :] = sent[:, :, start : start + LANES]
    steps = out_sems.shape[0] - 1
    some = members // steps
    for step in range(steps):
        lines = slice(step * some * held.shape[1], (step + 1) * some * held.shape[1])
        message_ref[lines, :] = (
            held[step * some : (step + 1) * some].reshape(-1, LANES).astype(jnp.bfloat16)
        )
        leaving += start_copies(out_sems.at[step + 1], (message_ref.at[lines, :], message_hbm.at[lines, :]))
    for copy in leaving:
        copy.wait()


def gate_kernel(normed_ref, w_hbm, gain_hbm, w_out_hbm, gate_ref, w_out_ref, gain_ref, done_ref, w, w_out, gain, sems):
    fetch(sems, (w_hbm, w), (w_out_hbm, w_out), (gain_hbm, gain))
    last = w_hbm.shape[1] - w_hbm.shape[0]
    gate_ref[...] = sigmoid(
        jnp.dot(w[:, last:].T, normed_ref[...], preferred_element_type=jnp.float32)
    )
    w_out_ref[...] = w_out[...].T
    gain_ref[...] = jnp.broadcast_to(column(gain[...]), gain_ref.shape)
    done_ref[...] = jnp.zeros_like(done_ref)


def unpack(message, half, halves, spread_ref, cols):
    tokens, groups = cycle_of(cols)
    members, lines, _ = message.shape
    lane = lax.broadcasted_iota(jnp.int32, (ROWS, LANES), 1)
    cycles = lines // (ROWS * groups)
    for peer in range(members // halves):
        for cycle in range(cycles):
            base = cycle * groups * ROWS
            held = [
                message[peer * halves + half, base + group * ROWS : base + (group + 1) * ROWS, :]
                for group in range(groups)
            ]
            for token in range(tokens):
                k = (peer * cycles + cycle) * tokens + token
                for chunk in range(spread_ref.shape[0]):
                    group, off = divmod(token * cols + chunk * LANES, LANES)
                    value = held[group]
                    if off and group + 1 < groups:
                        value = jnp.where(lane >= off, value, held[group + 1])
                    if off:
                        value = pltpu.roll(value, LANES - off, axis=1)
                    spread_ref[chunk, k * ROWS : (k + 1) * ROWS, :] = value


def pack(spread_ref, at, cols):
    tokens, groups = cycle_of(cols)
    lane = lax.broadcasted_iota(jnp.int32, (ROWS, LANES), 1)
    rolled, lines = {}, []
    for group in range(groups):
        value, here = None, 0
        while here < LANES:
            token, col = divmod(group * LANES + here, cols)
            chunk, there = divmod(col, LANES)
            shift = (here - there) % LANES
            if (token, chunk, shift) not in rolled:
                line = (at * tokens + token) * ROWS
                piece = spread_ref[chunk, line : line + ROWS, :]
                rolled[token, chunk, shift] = pltpu.roll(piece, shift, axis=1) if shift else piece
            piece = rolled[token, chunk, shift]
            value = piece if value is None else jnp.where(lane >= here, piece, value)
            here += min(LANES - here, LANES - there, cols - col)
        lines.append(value)
    return lines


def channel_of(spread_ref, line, stride):
    count = spread_ref.shape[1] // stride
    return jnp.concatenate(
        [spread_ref[chunk, pl.ds(line, count, stride=stride), :] for chunk in range(spread_ref.shape[0])],
        axis=1,
    ).astype(jnp.bfloat16)


def triangle_kernel(cols, shares, message_ref, _, mixed_ref, message, spread, left, left_t, right, mixed):
    halves, chunks = spread.shape[:2]
    width = chunks * LANES
    deep = right.shape[1]
    depth = spread.shape[2] // ROWS
    one = identity(cols, width)
    message[...] = message_ref[...].astype(jnp.float32).reshape(message.shape)
    if depth < deep:
        right[:, depth:, :] = jnp.zeros((OWN, deep - depth, halves * width), jnp.bfloat16)
    for half in range(halves):
        unpack(message, half, halves, spread.at[half], cols)
        if depth < deep:
            left[:, half * deep + depth : (half + 1) * deep, :] = jnp.zeros((OWN, deep - depth, width), jnp.bfloat16)
        for channel in range(OWN):
            left[channel, half * deep : half * deep + depth, :] = channel_of(spread.at[half], channel, ROWS)
            right[channel, :depth, half * width : (half + 1) * width] = channel_of(
                spread.at[half], OWN + channel, ROWS
            )
    for channel in range(OWN):
        both = lax.dot_general(
            one, left[channel], (((1,), (1,)), ((), ())), preferred_element_type=jnp.float32
        ).astype(jnp.bfloat16)
        for half in range(halves):
            left_t[channel, half * cols : (half + 1) * cols, :] = both[:, half * deep : (half + 1) * deep]
    for channel in range(OWN):
        total = jnp.dot(left_t[channel], right[channel], preferred_element_type=jnp.float32)
        for i_half in range(halves):
            for j_half in range(halves):
                for chunk in range(chunks):
                    start = j_half * width + chunk * LANES
                    mixed[i_half, chunk, pl.ds(j_half * OWN + channel, cols, stride=ROWS), :] = total[
                        i_half * cols : (i_half + 1) * cols, start : start + LANES
                    ]
    each = mixed_ref.shape[0] // shares
    cycles = message.shape[1] // (ROWS * cycle_of(cols)[1])
    for share in range(shares):
        i_half, peer = divmod(share, shares // halves)
        lines = []
        for cycle in range(cycles):
            lines += pack(mixed.at[i_half], peer * cycles + cycle, cols)
        lines += lines[-1:] * (len(lines) % 2)
        turned = [turn_pairs(lines[at], lines[at + 1]) for at in range(0, len(lines), 2)]
        lines = [pair[j_half] for j_half in range(halves) for pair in turned]
        mixed_ref[share * each : (share + 1) * each, :] = jnp.concatenate(lines, axis=0).astype(jnp.bfloat16)


def output_kernel(parts, mixed_ref, gate_ref, gain_ref, w_t_ref, update_hbm, mixed, update, sems):
    members = mixed.shape[0] // parts
    mixed[...] = mixed_ref[...].astype(jnp.float32).reshape(mixed.shape)
    groups = update.shape[0] // LANES
    steps = math.gcd(groups, 3)
    leaving = []
    for group in range(groups):
        if group % 2 == 0:
            lines = slice(group // 2 * ROWS, (group // 2 + 1) * ROWS)
            sums = mixed[:members, lines, :]
            for part in range(1, parts):
                sums += mixed[part * members : (part + 1) * members, lines, :]
            sums = sums.reshape(members // 2, 2, ROWS, LANES)
            blocks = turn_pairs(sums[:, 0], sums[:, 1])
        block = blocks[group % 2].reshape(members * OWN, LANES)
        center = block - jnp.mean(block, axis=0, keepdims=True)
        spread = jnp.mean(center * center, axis=0, keepdims=True)
        normed = (center * lax.rsqrt(spread + EPS) * gain_ref[...]).astype(jnp.bfloat16)
        projected = jnp.dot(w_t_ref[...], normed, preferred_element_type=jnp.float32)
        lanes = slice(group * LANES, (group + 1) * LANES)
        update[lanes, :] = (gate_ref[:, lanes] * projected).T.astype(jnp.bfloat16)
        step, last = divmod((group + 1) * steps, groups)
        if last == 0:
            done = slice((step - 1) * (groups // steps) * LANES, (group + 1) * LANES)
            leaving += start_copies(sems.at[step - 1], (update.at[done, :], update_hbm.at[done, :]))
    for copy in leaving:
        copy.wait()


def on_device(shares, halves, pair, tile_mask, chain_ids, gain_in, w_proj, gain_mid, w_out):
    rows, cols, width = pair.shape
    hidden = w_out.shape[0]
    devices = shares * halves
    members = hidden // OWN
    parts = devices // members
    positions = rows * cols
    groups = positions // LANES
    sent, back = groups * ROWS, pl.cdiv(groups, 2) * ROWS
    params = pltpu.CompilerParams(vmem_limit_bytes=VMEM_BYTES)
    whole_params = pltpu.CompilerParams(vmem_limit_bytes=WHOLE_VMEM_BYTES)
    tokens = chain_ids.shape[0]
    message, normed = pl.pallas_call(
        functools.partial(project_kernel, rows, cols),
        out_shape=(
            jax.ShapeDtypeStruct((members * sent, LANES), jnp.bfloat16),
            jax.ShapeDtypeStruct((width, positions), jnp.bfloat16),
        ),
        in_specs=[HBM] * 5,
        out_specs=(HBM, HBM),
        scratch_shapes=[
            pltpu.SMEM(tile_mask.shape, jnp.int32),
            pltpu.VMEM((1, tokens), jnp.int32),
            pltpu.VMEM((positions, width), jnp.bfloat16),
            pltpu.VMEM((1, width), jnp.float32),
            pltpu.VMEM(w_proj.shape, jnp.bfloat16),
            pltpu.VMEM((members, sent, LANES), jnp.float32),
            pltpu.VMEM((members * sent, LANES), jnp.bfloat16),
            pltpu.VMEM((width, positions), jnp.bfloat16),
            pltpu.SemaphoreType.DMA((5,)),
            pltpu.SemaphoreType.DMA((5, 1)),
        ],
        compiler_params=whole_params,
        name="project",
    )(tile_mask, chain_ids[None, :], pair.reshape(positions, width), gain_in[None, :], w_proj)
    message = lax.all_to_all(
        message.reshape(members, sent, LANES),
        ("row", "col"),
        split_axis=0,
        concat_axis=0,
        axis_index_groups=[list(range(part * members, (part + 1) * members)) for part in range(parts)],
        tiled=True,
    ).reshape(members * sent, LANES)
    gate, w_out_t, gain, done = pl.pallas_call(
        gate_kernel,
        out_shape=(
            jax.ShapeDtypeStruct((width, positions), jnp.float32),
            jax.ShapeDtypeStruct(w_out.shape[::-1], jnp.bfloat16),
            jax.ShapeDtypeStruct((hidden, LANES), jnp.float32),
            jax.ShapeDtypeStruct((8, LANES), jnp.float32),
        ),
        in_specs=[VMEM, HBM, HBM, HBM],
        out_specs=(VMEM, VMEM, VMEM, VMEM),
        scratch_shapes=[
            pltpu.VMEM(w_proj.shape, jnp.bfloat16),
            pltpu.VMEM(w_out.shape, jnp.bfloat16),
            pltpu.VMEM((1, hidden), jnp.float32),
            pltpu.SemaphoreType.DMA((3,)),
        ],
        compiler_params=params,
        cost_estimate=pl.CostEstimate(
            flops=2 * width * width * positions, bytes_accessed=4 * width * positions, transcendentals=0
        ),
        name="gate",
    )(normed, w_proj, gain_mid[None, :], w_out)
    message, done = lax.optimization_barrier((message, done))
    chunks = pl.cdiv(cols, LANES)
    depth = members // halves * rows
    deep = pl.cdiv(depth, LANES) * LANES
    mixed = pl.pallas_call(
        functools.partial(triangle_kernel, cols, shares),
        out_shape=jax.ShapeDtypeStruct((devices * back, LANES), jnp.bfloat16),
        in_specs=[VMEM, ANY],
        out_specs=VMEM,
        scratch_shapes=[
            pltpu.VMEM((members, sent, LANES), jnp.float32),
            pltpu.VMEM((halves, chunks, depth * ROWS, LANES), jnp.float32),
            pltpu.VMEM((OWN, halves * deep, chunks * LANES), jnp.bfloat16),
            pltpu.VMEM((OWN, halves * cols, deep), jnp.bfloat16),
            pltpu.VMEM((OWN, deep, halves * chunks * LANES), jnp.bfloat16),
            pltpu.VMEM((halves, chunks, cols * ROWS, LANES), jnp.float32),
        ],
        compiler_params=params,
        name="triangle",
    )(message, done)
    mixed = lax.all_to_all(
        mixed.reshape(devices, back, LANES), ("row", "col"), split_axis=0, concat_axis=0, tiled=True
    ).reshape(devices * back, LANES)
    update = pl.pallas_call(
        functools.partial(output_kernel, parts),
        out_shape=jax.ShapeDtypeStruct((positions, width), jnp.bfloat16),
        in_specs=[VMEM] * 4,
        out_specs=HBM,
        scratch_shapes=[
            pltpu.VMEM((devices, back, LANES), jnp.float32),
            pltpu.VMEM((positions, width), jnp.bfloat16),
            pltpu.SemaphoreType.DMA((math.gcd(groups, 3), 1)),
        ],
        compiler_params=params,
        name="output",
    )(mixed, gate, gain, w_out_t)
    return update.reshape(rows, cols, width)


def solution(mesh):
    in_specs = (P(("grp", "row"), "col", None), P("grp", None), P("grp"), P(), P(), P(), P())
    out_specs = P(("grp", "row"), "col", None)
    return jax.shard_map(
        functools.partial(on_device, mesh.shape["row"], mesh.shape["col"]),
        mesh=mesh,
        in_specs=in_specs,
        out_specs=out_specs,
        check_vma=False,
    )
```

```python
import functools
import math

import jax
import jax.numpy as jnp
from jax import lax
from jax.experimental import pallas as pl
from jax.experimental.pallas import tpu as pltpu
from jax.sharding import PartitionSpec as P

TILE = 96
LANES = 128
EPS = 1e-05
PARTS = 2
VMEM_BYTES = 32 * 1024 * 1024
WHOLE_VMEM_BYTES = 64 * 1024 * 1024
VMEM = pl.BlockSpec(memory_space=pltpu.VMEM)
ANY = pl.BlockSpec(memory_space=pl.ANY)
HBM = pl.BlockSpec(memory_space=pltpu.HBM)
SMEM = pl.BlockSpec(memory_space=pltpu.SMEM)


def forward_order(peers, halves):
    return [(at, half) for at in reversed(range(peers)) for half in reversed(range(halves))]


def return_order(peers, halves, parts):
    order = [(part, at, half) for part in range(parts) for at in range(peers) for half in range(halves)]
    start = peers * halves // 2
    return order[start:] + order[:start]


def column(row):
    return jnp.broadcast_to(row, (8, row.shape[1])).T[:, :1]


def steps(at, width, count):
    total = jnp.zeros_like(at)
    for edge in range(1, count):
        total += (at >= edge * width).astype(jnp.int32)
    return total


def identity(rows, cols):
    same = lax.broadcasted_iota(jnp.int32, (rows, cols), 0) == lax.broadcasted_iota(jnp.int32, (rows, cols), 1)
    return same.astype(jnp.bfloat16)


def transpose(block):
    return lax.dot_general(
        identity(block.shape[1], block.shape[1]),
        block,
        (((1,), (1,)), ((), ())),
        preferred_element_type=jnp.float32,
    )


def sigmoid(values):
    return 0.5 * jnp.tanh(0.5 * values) + 0.5


def keep_of(tile_ref, chain_ref, rows, cols):
    tokens = chain_ref.shape[1]
    tiles = tile_ref.shape[1]
    positions = rows * cols
    at = lax.broadcasted_iota(jnp.int32, (1, positions), 1)
    row = steps(at, cols, rows)
    k = lax.axis_index("row") * rows + row
    i = lax.axis_index("col") * cols + at - row * cols
    token = lax.broadcasted_iota(jnp.int32, (tokens, positions), 0)
    pick = (token == k).astype(jnp.float32) - (token == i).astype(jnp.float32)
    chains = jnp.broadcast_to(chain_ref[...].astype(jnp.bfloat16), (8, tokens))
    apart = jnp.dot(chains, pick.astype(jnp.bfloat16), preferred_element_type=jnp.float32)[:1]
    k_tile = steps(k, TILE, tiles)
    i_tile = steps(i, TILE, tiles)
    tile_vals = jnp.zeros((1, positions), jnp.float32)
    for a in range(tiles):
        for b in range(tiles):
            here = (k_tile == a) & (i_tile == b)
            tile_vals = jnp.where(here, tile_ref[a, b].astype(jnp.float32), tile_vals)
    return jnp.where(apart == 0.0, 1.0, tile_vals)


def cycle_of(cols):
    cycle = math.lcm(cols, LANES)
    return cycle // cols, cycle // LANES


def start_copies(sems, *pairs):
    copies = [pltpu.make_async_copy(src, dst, sems.at[at]) for at, (src, dst) in enumerate(pairs)]
    for copy in copies:
        copy.start()
    return copies


def fetch(sems, *pairs):
    for copy in start_copies(sems, *pairs):
        copy.wait()


def project_kernel(
    rows, cols, tile_hbm, chain_hbm, pair_hbm, gain_hbm, w_hbm, message_hbm, normed_hbm,
    tile_ref, chain_ref, pair_ref, gain_ref, w_ref, message_ref, normed_ref, sems, out_sems,
):
    hidden = (w_ref.shape[1] - w_ref.shape[0]) // 4
    peers = message_ref.shape[0]
    own = hidden // peers
    groups = cycle_of(cols)[1]
    size = groups * LANES
    copies = start_copies(
        sems,
        (w_hbm, w_ref),
        (gain_hbm, gain_ref),
        (chain_hbm, chain_ref),
        (tile_hbm, tile_ref),
        (pair_hbm, pair_ref),
    )
    for copy in copies[:4]:
        copy.wait()
    keep = keep_of(tile_ref, chain_ref, rows, cols)
    w_t = w_ref[:, : 4 * hidden].T
    gain = column(gain_ref[...])
    copies[4].wait()
    cycles = [slice(start, start + size) for start in range(0, rows * cols, size)]
    for lanes in cycles:
        block = transpose(pair_ref[lanes, :])
        center = block - jnp.mean(block, axis=0, keepdims=True)
        spread = jnp.mean(center * center, axis=0, keepdims=True)
        normed_ref[:, lanes] = (center * lax.rsqrt(spread + EPS) * gain).astype(jnp.bfloat16)
    leaving = []
    for cycle, lanes in enumerate(cycles):
        projected = jnp.dot(w_t, normed_ref[:, lanes], preferred_element_type=jnp.float32)
        sides = []
        for side in range(2):
            value = projected[2 * side * hidden : (2 * side + 1) * hidden]
            gate = projected[(2 * side + 1) * hidden : (2 * side + 2) * hidden]
            sides.append((sigmoid(gate) * value * keep[:, lanes]).reshape(peers, own, size))
        both = jnp.concatenate(sides, axis=1).astype(jnp.bfloat16)
        for group in range(groups):
            line = (cycle * groups + group) * 2 * own
            message_ref[:, line : line + 2 * own, :] = both[:, :, group * LANES : (group + 1) * LANES]
        lines = slice(cycle * groups * 2 * own, (cycle + 1) * groups * 2 * own)
        leaving += start_copies(
            out_sems.at[cycle],
            (message_ref.at[:, lines, :], message_hbm.at[:, lines, :]),
            (normed_ref.at[:, lanes], normed_hbm.at[:, lanes]),
        )
    for copy in leaving:
        copy.wait()


def gate_kernel(normed_ref, w_hbm, gain_hbm, w_out_hbm, gate_ref, w_out_ref, gain_ref, done_ref, w, w_out, gain, sems):
    fetch(sems, (w_hbm, w), (w_out_hbm, w_out), (gain_hbm, gain))
    last = w_hbm.shape[1] - w_hbm.shape[0]
    gate_ref[...] = sigmoid(
        jnp.dot(w[:, last:].T, normed_ref[...], preferred_element_type=jnp.float32)
    )
    w_out_ref[...] = w_out[...].T
    gain_ref[...] = jnp.broadcast_to(column(gain[...]), gain_ref.shape)
    done_ref[...] = jnp.zeros_like(done_ref)


def unpack(message_ref, half, halves, spread_ref, own, cols):
    tokens, groups = cycle_of(cols)
    members, lines, _ = message_ref.shape
    peers = members // halves
    order = forward_order(peers, halves)
    lane = lax.broadcasted_iota(jnp.int32, (2 * own, LANES), 1)
    cycles = lines // (2 * groups * own)
    for peer in range(peers):
        member = order.index((peer, half))
        for cycle in range(cycles):
            base = cycle * groups
            held = [
                message_ref[
                    member, (base + group) * 2 * own : (base + group + 1) * 2 * own, :
                ].astype(jnp.float32)
                for group in range(groups)
            ]
            for token in range(tokens):
                k = (peer * cycles + cycle) * tokens + token
                for chunk in range(spread_ref.shape[0]):
                    group, off = divmod(token * cols + chunk * LANES, LANES)
                    value = held[group]
                    if off and group + 1 < groups:
                        value = jnp.where(lane >= off, value, held[group + 1])
                    if off:
                        value = pltpu.roll(value, LANES - off, axis=1)
                    spread_ref[chunk, k * 2 * own : (k + 1) * 2 * own, :] = value


def pack(spread_ref, at, own, cols):
    tokens, groups = cycle_of(cols)
    lane = lax.broadcasted_iota(jnp.int32, (own, LANES), 1)
    rolled, lines = {}, []
    for group in range(groups):
        value, here = None, 0
        while here < LANES:
            token, col = divmod(group * LANES + here, cols)
            chunk, there = divmod(col, LANES)
            shift = (here - there) % LANES
            if (token, chunk, shift) not in rolled:
                line = (at * tokens + token) * own
                piece = spread_ref[chunk, line : line + own, :]
                rolled[token, chunk, shift] = pltpu.roll(piece, shift, axis=1) if shift else piece
            piece = rolled[token, chunk, shift]
            value = piece if value is None else jnp.where(lane >= here, piece, value)
            here += min(LANES - here, LANES - there, cols - col)
        lines.append(value)
    return lines


def channel_of(spread_ref, line, stride):
    count = spread_ref.shape[1] // stride
    return jnp.concatenate(
        [spread_ref[chunk, pl.ds(line, count, stride=stride), :] for chunk in range(spread_ref.shape[0])],
        axis=1,
    ).astype(jnp.bfloat16)


def triangle_kernel(own, cols, shares, parts, message_ref, _, mixed_ref, spread, left, left_t, right, mixed):
    halves, chunks = spread.shape[:2]
    width = chunks * LANES
    deep = right.shape[1]
    depth = spread.shape[2] // (2 * own)
    one = identity(cols, width)
    if depth < deep:
        right[:, depth:, :] = jnp.zeros((own, deep - depth, halves * width), jnp.bfloat16)
    for half in range(halves):
        unpack(message_ref, half, halves, spread.at[half], own, cols)
        if depth < deep:
            left[:, half * deep + depth : (half + 1) * deep, :] = jnp.zeros((own, deep - depth, width), jnp.bfloat16)
        for channel in range(own):
            left[channel, half * deep : half * deep + depth, :] = channel_of(spread.at[half], channel, 2 * own)
            right[channel, :depth, half * width : (half + 1) * width] = channel_of(
                spread.at[half], own + channel, 2 * own
            )
    for channel in range(own):
        both = lax.dot_general(
            one, left[channel], (((1,), (1,)), ((), ())), preferred_element_type=jnp.float32
        ).astype(jnp.bfloat16)
        for half in range(halves):
            left_t[channel, half * cols : (half + 1) * cols, :] = both[:, half * deep : (half + 1) * deep]
    for channel in range(own):
        total = jnp.dot(left_t[channel], right[channel], preferred_element_type=jnp.float32)
        for i_half in range(halves):
            for j_half in range(halves):
                for chunk in range(chunks):
                    start = j_half * width + chunk * LANES
                    mixed[i_half, j_half, chunk, pl.ds(channel, cols, stride=own), :] = total[
                        i_half * cols : (i_half + 1) * cols, start : start + LANES
                    ]
    groups = cycle_of(cols)[1]
    peers = shares // parts
    order = return_order(peers, halves, parts)
    each = mixed_ref.shape[0] // len(order)
    cycles = each // (groups * own)
    batch = 16 // math.gcd(each, 16)
    for start in range(0, len(order), batch):
        lines = []
        for part, at, j_half in order[start : start + batch]:
            i_half, peer = divmod(part * peers + at, shares // halves)
            for cycle in range(cycles):
                lines += pack(mixed.at[i_half, j_half], peer * cycles + cycle, own, cols)
        mixed_ref[start * each : (start + batch) * each, :] = jnp.concatenate(lines, axis=0).astype(jnp.bfloat16)


def output_kernel(own, halves, parts, mixed_ref, gate_ref, gain_ref, w_t_ref, update_hbm, mixed, update, sems):
    members, lines, _ = mixed.shape
    peers = members // (halves * parts)
    order = return_order(peers, halves, parts)
    mixed[...] = mixed_ref[...].astype(jnp.float32).reshape(mixed.shape)
    groups = lines // own
    steps = math.gcd(groups, 3)
    leaving = []
    for group in range(groups):
        blocks = []
        for at, half in forward_order(peers, halves):
            pieces = [
                mixed[order.index((part, at, half)), group * own : (group + 1) * own, :] for part in range(parts)
            ]
            blocks.append(functools.reduce(jnp.add, pieces))
        block = jnp.concatenate(blocks, axis=0)
        center = block - jnp.mean(block, axis=0, keepdims=True)
        spread = jnp.mean(center * center, axis=0, keepdims=True)
        normed = (center * lax.rsqrt(spread + EPS) * gain_ref[...]).astype(jnp.bfloat16)
        projected = jnp.dot(w_t_ref[...], normed, preferred_element_type=jnp.float32)
        lanes = slice(group * LANES, (group + 1) * LANES)
        update[lanes, :] = (gate_ref[:, lanes] * projected).T.astype(jnp.bfloat16)
        step, last = divmod((group + 1) * steps, groups)
        if last == 0:
            done = slice((step - 1) * (groups // steps) * LANES, (group + 1) * LANES)
            leaving += start_copies(sems.at[step - 1], (update.at[done, :], update_hbm.at[done, :]))
    for copy in leaving:
        copy.wait()


def on_device(shares, halves, pair, tile_mask, chain_ids, gain_in, w_proj, gain_mid, w_out):
    rows, cols, width = pair.shape
    hidden = w_out.shape[0]
    peers = shares // PARTS
    own = hidden // (peers * halves)
    positions = rows * cols
    groups = positions // LANES
    lines = groups * own
    cycles = groups // cycle_of(cols)[1]
    params = pltpu.CompilerParams(vmem_limit_bytes=VMEM_BYTES)
    whole_params = pltpu.CompilerParams(vmem_limit_bytes=WHOLE_VMEM_BYTES)
    tokens = chain_ids.shape[0]
    message = jax.ShapeDtypeStruct((peers * halves, 2 * lines, LANES), jnp.bfloat16)
    message, normed = pl.pallas_call(
        functools.partial(project_kernel, rows, cols),
        out_shape=(message, jax.ShapeDtypeStruct((width, positions), jnp.bfloat16)),
        in_specs=[HBM] * 5,
        out_specs=(HBM, HBM),
        scratch_shapes=[
            pltpu.SMEM(tile_mask.shape, jnp.int32),
            pltpu.VMEM((1, tokens), jnp.int32),
            pltpu.VMEM((positions, width), jnp.bfloat16),
            pltpu.VMEM((1, width), jnp.float32),
            pltpu.VMEM(w_proj.shape, jnp.bfloat16),
            pltpu.VMEM(message.shape, jnp.bfloat16),
            pltpu.VMEM((width, positions), jnp.bfloat16),
            pltpu.SemaphoreType.DMA((5,)),
            pltpu.SemaphoreType.DMA((cycles, 2)),
        ],
        compiler_params=whole_params,
        name="project",
    )(tile_mask, chain_ids[None, :], pair.reshape(positions, width), gain_in[None, :], w_proj)
    message = lax.all_to_all(
        message,
        ("row", "col"),
        split_axis=0,
        concat_axis=0,
        axis_index_groups=[
            [(part * peers + at) * halves + half for at, half in forward_order(peers, halves)]
            for part in range(PARTS)
        ],
        tiled=True,
    )
    gate, w_out_t, gain, done = pl.pallas_call(
        gate_kernel,
        out_shape=(
            jax.ShapeDtypeStruct((width, positions), jnp.float32),
            jax.ShapeDtypeStruct(w_out.shape[::-1], jnp.bfloat16),
            jax.ShapeDtypeStruct((hidden, LANES), jnp.float32),
            jax.ShapeDtypeStruct((8, LANES), jnp.float32),
        ),
        in_specs=[VMEM, HBM, HBM, HBM],
        out_specs=(VMEM, VMEM, VMEM, VMEM),
        scratch_shapes=[
            pltpu.VMEM(w_proj.shape, jnp.bfloat16),
            pltpu.VMEM(w_out.shape, jnp.bfloat16),
            pltpu.VMEM((1, hidden), jnp.float32),
            pltpu.SemaphoreType.DMA((3,)),
        ],
        compiler_params=params,
        cost_estimate=pl.CostEstimate(
            flops=2 * width * width * positions, bytes_accessed=4 * width * positions, transcendentals=0
        ),
        name="gate",
    )(normed, w_proj, gain_mid[None, :], w_out)
    message, done = lax.optimization_barrier((message, done))
    chunks = pl.cdiv(cols, LANES)
    depth = peers * rows
    deep = pl.cdiv(depth, LANES) * LANES
    mixed = pl.pallas_call(
        functools.partial(triangle_kernel, own, cols, shares, PARTS),
        out_shape=jax.ShapeDtypeStruct((halves * shares * lines, LANES), jnp.bfloat16),
        in_specs=[VMEM, ANY],
        out_specs=VMEM,
        scratch_shapes=[
            pltpu.VMEM((halves, chunks, depth * 2 * own, LANES), jnp.float32),
            pltpu.VMEM((own, halves * deep, chunks * LANES), jnp.bfloat16),
            pltpu.VMEM((own, halves * cols, deep), jnp.bfloat16),
            pltpu.VMEM((own, deep, halves * chunks * LANES), jnp.bfloat16),
            pltpu.VMEM((halves, halves, chunks, cols * own, LANES), jnp.float32),
        ],
        compiler_params=params,
        name="triangle",
    )(message, done)
    mixed = lax.all_to_all(
        mixed.reshape(halves * shares, lines, LANES),
        ("row", "col"),
        split_axis=0,
        concat_axis=0,
        axis_index_groups=[
            [(part * peers + at) * halves + half for part, at, half in return_order(peers, halves, PARTS)]
        ],
        tiled=True,
    ).reshape(halves * shares * lines, LANES)
    update = pl.pallas_call(
        functools.partial(output_kernel, own, halves, PARTS),
        out_shape=jax.ShapeDtypeStruct((positions, width), jnp.bfloat16),
        in_specs=[VMEM] * 4,
        out_specs=HBM,
        scratch_shapes=[
            pltpu.VMEM((shares * halves, lines, LANES), jnp.float32),
            pltpu.VMEM((positions, width), jnp.bfloat16),
            pltpu.SemaphoreType.DMA((math.gcd(groups, 3), 1)),
        ],
        compiler_params=params,
        name="output",
    )(mixed, gate, gain, w_out_t)
    return update.reshape(rows, cols, width)


def solution(mesh):
    in_specs = (P(("grp", "row"), "col", None), P("grp", None), P("grp"), P(), P(), P(), P())
    out_specs = P(("grp", "row"), "col", None)
    return jax.shard_map(
        functools.partial(on_device, mesh.shape["row"], mesh.shape["col"]),
        mesh=mesh,
        in_specs=in_specs,
        out_specs=out_specs,
        check_vma=False,
    )
```

```python
import functools
import math

import jax
import jax.numpy as jnp
from jax import lax
from jax.experimental import pallas as pl
from jax.experimental.pallas import tpu as pltpu
from jax.sharding import Mesh
from jax.sharding import PartitionSpec as P

TILE = 96
LANES = 128
EPS = 1e-05
PARTS = 2
VMEM_BYTES = 32 * 1024 * 1024
WHOLE_VMEM_BYTES = 64 * 1024 * 1024
VMEM = pl.BlockSpec(memory_space=pltpu.VMEM)
ANY = pl.BlockSpec(memory_space=pl.ANY)
HBM = pl.BlockSpec(memory_space=pltpu.HBM)
SMEM = pl.BlockSpec(memory_space=pltpu.SMEM)


def column(row):
    return jnp.broadcast_to(row, (8, row.shape[1])).T[:, :1]


def steps(at, width, count):
    total = jnp.zeros_like(at)
    for edge in range(1, count):
        total += (at >= edge * width).astype(jnp.int32)
    return total


def identity(rows, cols):
    same = lax.broadcasted_iota(jnp.int32, (rows, cols), 0) == lax.broadcasted_iota(jnp.int32, (rows, cols), 1)
    return same.astype(jnp.bfloat16)


def transpose(block):
    return lax.dot_general(
        identity(block.shape[1], block.shape[1]),
        block,
        (((1,), (1,)), ((), ())),
        preferred_element_type=jnp.float32,
    )


def sigmoid(values):
    return 0.5 * jnp.tanh(0.5 * values) + 0.5


def keep_of(tile_ref, chain_ref, rows, cols):
    tokens = chain_ref.shape[1]
    tiles = tile_ref.shape[1]
    positions = rows * cols
    at = lax.broadcasted_iota(jnp.int32, (1, positions), 1)
    row = steps(at, cols, rows)
    k = (lax.axis_index("part") * lax.axis_size("row") + lax.axis_index("row")) * rows + row
    i = lax.axis_index("col") * cols + at - row * cols
    token = lax.broadcasted_iota(jnp.int32, (tokens, positions), 0)
    pick = (token == k).astype(jnp.float32) - (token == i).astype(jnp.float32)
    chains = jnp.broadcast_to(chain_ref[...].astype(jnp.bfloat16), (8, tokens))
    apart = jnp.dot(chains, pick.astype(jnp.bfloat16), preferred_element_type=jnp.float32)[:1]
    k_tile = steps(k, TILE, tiles)
    i_tile = steps(i, TILE, tiles)
    tile_vals = jnp.zeros((1, positions), jnp.float32)
    for a in range(tiles):
        for b in range(tiles):
            here = (k_tile == a) & (i_tile == b)
            tile_vals = jnp.where(here, tile_ref[a, b].astype(jnp.float32), tile_vals)
    return jnp.where(apart == 0.0, 1.0, tile_vals)


def cycle_of(cols):
    cycle = math.lcm(cols, LANES)
    return cycle // cols, cycle // LANES


def start_copies(sems, *pairs):
    copies = [pltpu.make_async_copy(src, dst, sems.at[at]) for at, (src, dst) in enumerate(pairs)]
    for copy in copies:
        copy.start()
    return copies


def fetch(sems, *pairs):
    for copy in start_copies(sems, *pairs):
        copy.wait()


def project_kernel(
    rows, cols, tile_hbm, chain_hbm, pair_hbm, gain_hbm, w_hbm, message_hbm, normed_hbm,
    tile_ref, chain_ref, pair_ref, gain_ref, w_ref, message_ref, normed_ref, sems, out_sems,
):
    hidden = (w_ref.shape[1] - w_ref.shape[0]) // 4
    peers = message_ref.shape[0]
    own = hidden // peers
    groups = cycle_of(cols)[1]
    size = groups * LANES
    copies = start_copies(
        sems,
        (chain_hbm, chain_ref),
        (tile_hbm, tile_ref),
        (gain_hbm, gain_ref),
        (pair_hbm, pair_ref),
        (w_hbm, w_ref),
    )
    for copy in copies[:3]:
        copy.wait()
    keep = keep_of(tile_ref, chain_ref, rows, cols)
    gain = column(gain_ref[...])
    copies[4].wait()
    w_t = w_ref[:, : 4 * hidden].T
    copies[3].wait()
    cycles = [slice(start, start + size) for start in range(0, rows * cols, size)]
    for lanes in cycles:
        block = transpose(pair_ref[lanes, :])
        center = block - jnp.mean(block, axis=0, keepdims=True)
        spread = jnp.mean(center * center, axis=0, keepdims=True)
        normed_ref[:, lanes] = (center * lax.rsqrt(spread + EPS) * gain).astype(jnp.bfloat16)
    leaving = []
    for cycle, lanes in enumerate(cycles):
        projected = jnp.dot(w_t, normed_ref[:, lanes], preferred_element_type=jnp.float32)
        sides = []
        for side in range(2):
            value = projected[2 * side * hidden : (2 * side + 1) * hidden]
            gate = projected[(2 * side + 1) * hidden : (2 * side + 2) * hidden]
            sides.append((sigmoid(gate) * value * keep[:, lanes]).reshape(peers, own, size))
        both = jnp.concatenate(sides, axis=1).astype(jnp.bfloat16)
        for group in range(groups):
            line = (cycle * groups + group) * 2 * own
            message_ref[:, line : line + 2 * own, :] = both[:, :, group * LANES : (group + 1) * LANES]
        lines = slice(cycle * groups * 2 * own, (cycle + 1) * groups * 2 * own)
        leaving += start_copies(
            out_sems.at[cycle],
            (message_ref.at[:, lines, :], message_hbm.at[:, lines, :]),
            (normed_ref.at[:, lanes], normed_hbm.at[:, lanes]),
        )
    for copy in leaving:
        copy.wait()


def gate_kernel(normed_ref, w_hbm, gain_hbm, w_out_hbm, gate_ref, w_out_ref, gain_ref, done_ref, w, w_out, gain, sems):
    fetch(sems, (w_hbm, w), (w_out_hbm, w_out), (gain_hbm, gain))
    last = w_hbm.shape[1] - w_hbm.shape[0]
    gate_ref[...] = sigmoid(
        jnp.dot(w[:, last:].T, normed_ref[...], preferred_element_type=jnp.float32)
    )
    w_out_ref[...] = w_out[...].T
    gain_ref[...] = jnp.broadcast_to(column(gain[...]), gain_ref.shape)
    done_ref[...] = jnp.zeros_like(done_ref)


def unpack(message_ref, half, halves, spread_ref, own, cols):
    tokens, groups = cycle_of(cols)
    members, lines, _ = message_ref.shape
    peers = members // halves
    lane = lax.broadcasted_iota(jnp.int32, (2 * own, LANES), 1)
    cycles = lines // (2 * groups * own)
    for peer in range(peers):
        for cycle in range(cycles):
            base = cycle * groups
            held = [
                message_ref[
                    peer * halves + half, (base + group) * 2 * own : (base + group + 1) * 2 * own, :
                ].astype(jnp.float32)
                for group in range(groups)
            ]
            for token in range(tokens):
                k = (peer * cycles + cycle) * tokens + token
                for chunk in range(spread_ref.shape[0]):
                    group, off = divmod(token * cols + chunk * LANES, LANES)
                    value = held[group]
                    if off and group + 1 < groups:
                        value = jnp.where(lane >= off, value, held[group + 1])
                    if off:
                        value = pltpu.roll(value, LANES - off, axis=1)
                    spread_ref[chunk, k * 2 * own : (k + 1) * 2 * own, :] = value


def pack(spread_ref, at, own, cols):
    tokens, groups = cycle_of(cols)
    lane = lax.broadcasted_iota(jnp.int32, (own, LANES), 1)
    rolled, lines = {}, []
    for group in range(groups):
        value, here = None, 0
        while here < LANES:
            token, col = divmod(group * LANES + here, cols)
            chunk, there = divmod(col, LANES)
            shift = (here - there) % LANES
            if (token, chunk, shift) not in rolled:
                line = (at * tokens + token) * own
                piece = spread_ref[chunk, line : line + own, :]
                rolled[token, chunk, shift] = pltpu.roll(piece, shift, axis=1) if shift else piece
            piece = rolled[token, chunk, shift]
            value = piece if value is None else jnp.where(lane >= here, piece, value)
            here += min(LANES - here, LANES - there, cols - col)
        lines.append(value)
    return lines


def channel_of(spread_ref, line, stride):
    count = spread_ref.shape[1] // stride
    return jnp.concatenate(
        [spread_ref[chunk, pl.ds(line, count, stride=stride), :] for chunk in range(spread_ref.shape[0])],
        axis=1,
    ).astype(jnp.bfloat16)


def triangle_kernel(own, cols, shares, message_ref, _, mixed_ref, spread, left, left_t, right, mixed):
    halves, chunks = spread.shape[:2]
    width = chunks * LANES
    deep = right.shape[1]
    depth = spread.shape[2] // (2 * own)
    one = identity(cols, width)
    if depth < deep:
        right[:, depth:, :] = jnp.zeros((own, deep - depth, halves * width), jnp.bfloat16)
    for half in range(halves):
        unpack(message_ref, half, halves, spread.at[half], own, cols)
        if depth < deep:
            left[:, half * deep + depth : (half + 1) * deep, :] = jnp.zeros((own, deep - depth, width), jnp.bfloat16)
        for channel in range(own):
            left[channel, half * deep : half * deep + depth, :] = channel_of(spread.at[half], channel, 2 * own)
            right[channel, :depth, half * width : (half + 1) * width] = channel_of(
                spread.at[half], own + channel, 2 * own
            )
    for channel in range(own):
        both = lax.dot_general(
            one, left[channel], (((1,), (1,)), ((), ())), preferred_element_type=jnp.float32
        ).astype(jnp.bfloat16)
        for half in range(halves):
            left_t[channel, half * cols : (half + 1) * cols, :] = both[:, half * deep : (half + 1) * deep]
    for channel in range(own):
        total = jnp.dot(left_t[channel], right[channel], preferred_element_type=jnp.float32)
        for i_half in range(halves):
            for j_half in range(halves):
                for chunk in range(chunks):
                    start = j_half * width + chunk * LANES
                    mixed[i_half, j_half, chunk, pl.ds(channel, cols, stride=own), :] = total[
                        i_half * cols : (i_half + 1) * cols, start : start + LANES
                    ]
    groups = cycle_of(cols)[1]
    each = mixed_ref.shape[0] // shares
    cycles = each // (halves * groups * own)
    for share in range(shares):
        i_half, peer = divmod(share, shares // halves)
        lines = []
        for j_half in range(halves):
            for cycle in range(cycles):
                lines += pack(mixed.at[i_half, j_half], peer * cycles + cycle, own, cols)
        mixed_ref[share * each : (share + 1) * each, :] = jnp.concatenate(lines, axis=0).astype(jnp.bfloat16)


def output_kernel(own, parts, mixed_ref, gate_ref, gain_ref, w_t_ref, update_hbm, mixed, update, sems):
    members, lines, _ = mixed.shape
    members = members // parts
    mixed[...] = mixed_ref[...].astype(jnp.float32).reshape(mixed.shape)
    groups = lines // own
    steps = math.gcd(groups, 3)
    leaving = []
    for group in range(groups):
        sums = mixed[:members, group * own : (group + 1) * own, :]
        for part in range(1, parts):
            sums += mixed[part * members : (part + 1) * members, group * own : (group + 1) * own, :]
        block = sums.reshape(members * own, LANES)
        center = block - jnp.mean(block, axis=0, keepdims=True)
        spread = jnp.mean(center * center, axis=0, keepdims=True)
        normed = (center * lax.rsqrt(spread + EPS) * gain_ref[...]).astype(jnp.bfloat16)
        projected = jnp.dot(w_t_ref[...], normed, preferred_element_type=jnp.float32)
        lanes = slice(group * LANES, (group + 1) * LANES)
        update[lanes, :] = (gate_ref[:, lanes] * projected).T.astype(jnp.bfloat16)
        step, last = divmod((group + 1) * steps, groups)
        if last == 0:
            done = slice((step - 1) * (groups // steps) * LANES, (group + 1) * LANES)
            leaving += start_copies(sems.at[step - 1], (update.at[done, :], update_hbm.at[done, :]))
    for copy in leaving:
        copy.wait()


def on_device(shares, halves, pair, tile_mask, chain_ids, gain_in, w_proj, gain_mid, w_out):
    rows, cols, width = pair.shape
    hidden = w_out.shape[0]
    peers = shares // PARTS
    own = hidden // (peers * halves)
    positions = rows * cols
    groups = positions // LANES
    lines = groups * own
    cycles = groups // cycle_of(cols)[1]
    params = pltpu.CompilerParams(vmem_limit_bytes=VMEM_BYTES)
    whole_params = pltpu.CompilerParams(vmem_limit_bytes=WHOLE_VMEM_BYTES)
    tokens = chain_ids.shape[0]
    message = jax.ShapeDtypeStruct((peers * halves, 2 * lines, LANES), jnp.bfloat16)
    message, normed = pl.pallas_call(
        functools.partial(project_kernel, rows, cols),
        out_shape=(message, jax.ShapeDtypeStruct((width, positions), jnp.bfloat16)),
        in_specs=[HBM] * 5,
        out_specs=(HBM, HBM),
        scratch_shapes=[
            pltpu.SMEM(tile_mask.shape, jnp.int32),
            pltpu.VMEM((1, tokens), jnp.int32),
            pltpu.VMEM((positions, width), jnp.bfloat16),
            pltpu.VMEM((1, width), jnp.float32),
            pltpu.VMEM(w_proj.shape, jnp.bfloat16),
            pltpu.VMEM(message.shape, jnp.bfloat16),
            pltpu.VMEM((width, positions), jnp.bfloat16),
            pltpu.SemaphoreType.DMA((5,)),
            pltpu.SemaphoreType.DMA((cycles, 2)),
        ],
        compiler_params=whole_params,
        name="project",
    )(tile_mask, chain_ids[None, :], pair.reshape(positions, width), gain_in[None, :], w_proj)
    message = lax.all_to_all(
        message, ("row", "col"), split_axis=0, concat_axis=0, tiled=True
    )
    gate, w_out_t, gain, done = pl.pallas_call(
        gate_kernel,
        out_shape=(
            jax.ShapeDtypeStruct((width, positions), jnp.float32),
            jax.ShapeDtypeStruct(w_out.shape[::-1], jnp.bfloat16),
            jax.ShapeDtypeStruct((hidden, LANES), jnp.float32),
            jax.ShapeDtypeStruct((8, LANES), jnp.float32),
        ),
        in_specs=[VMEM, HBM, HBM, HBM],
        out_specs=(VMEM, VMEM, VMEM, VMEM),
        scratch_shapes=[
            pltpu.VMEM(w_proj.shape, jnp.bfloat16),
            pltpu.VMEM(w_out.shape, jnp.bfloat16),
            pltpu.VMEM((1, hidden), jnp.float32),
            pltpu.SemaphoreType.DMA((3,)),
        ],
        compiler_params=params,
        cost_estimate=pl.CostEstimate(
            flops=2 * width * width * positions, bytes_accessed=4 * width * positions, transcendentals=0
        ),
        name="gate",
    )(normed, w_proj, gain_mid[None, :], w_out)
    message, done = lax.optimization_barrier((message, done))
    chunks = pl.cdiv(cols, LANES)
    depth = peers * rows
    deep = pl.cdiv(depth, LANES) * LANES
    mixed = pl.pallas_call(
        functools.partial(triangle_kernel, own, cols, shares),
        out_shape=jax.ShapeDtypeStruct((halves * shares * lines, LANES), jnp.bfloat16),
        in_specs=[VMEM, ANY],
        out_specs=VMEM,
        scratch_shapes=[
            pltpu.VMEM((halves, chunks, depth * 2 * own, LANES), jnp.float32),
            pltpu.VMEM((own, halves * deep, chunks * LANES), jnp.bfloat16),
            pltpu.VMEM((own, halves * cols, deep), jnp.bfloat16),
            pltpu.VMEM((own, deep, halves * chunks * LANES), jnp.bfloat16),
            pltpu.VMEM((halves, halves, chunks, cols * own, LANES), jnp.float32),
        ],
        compiler_params=params,
        name="triangle",
    )(message, done)
    mixed = lax.all_to_all(
        mixed.reshape(halves * shares, lines, LANES),
        ("part", "row", "col"),
        split_axis=0,
        concat_axis=0,
        tiled=True,
    ).reshape(halves * shares * lines, LANES)
    update = pl.pallas_call(
        functools.partial(output_kernel, own, PARTS),
        out_shape=jax.ShapeDtypeStruct((positions, width), jnp.bfloat16),
        in_specs=[VMEM] * 4,
        out_specs=HBM,
        scratch_shapes=[
            pltpu.VMEM((shares * halves, lines, LANES), jnp.float32),
            pltpu.VMEM((positions, width), jnp.bfloat16),
            pltpu.SemaphoreType.DMA((math.gcd(groups, 3), 1)),
        ],
        compiler_params=params,
        name="output",
    )(mixed, gate, gain, w_out_t)
    return update.reshape(rows, cols, width)


def solution(mesh):
    grp, shares, halves = (mesh.shape[axis] for axis in ("grp", "row", "col"))
    mesh = Mesh(mesh.devices.reshape(grp, PARTS, shares // PARTS, halves), ("grp", "part", "row", "col"))
    pairs = P(("grp", "part", "row"), "col", None)
    in_specs = (pairs, P("grp", None), P("grp"), P(), P(), P(), P())
    return jax.shard_map(
        functools.partial(on_device, shares, halves),
        mesh=mesh,
        in_specs=in_specs,
        out_specs=pairs,
        check_vma=False,
    )
```

```python
import functools
import math

import jax
import jax.numpy as jnp
from jax import lax
from jax.experimental import pallas as pl
from jax.experimental.pallas import tpu as pltpu
from jax.sharding import PartitionSpec as P

TILE = 96
LANES = 128
EPS = 1e-05
PARTS = 2
VMEM_BYTES = 32 * 1024 * 1024
VMEM = pl.BlockSpec(memory_space=pltpu.VMEM)
HBM = pl.BlockSpec(memory_space=pltpu.HBM)
SMEM = pl.BlockSpec(memory_space=pltpu.SMEM)


def column(row):
    return jnp.broadcast_to(row, (8, row.shape[1])).T[:, :1]


def steps(at, width, count):
    total = jnp.zeros_like(at)
    for edge in range(1, count):
        total += (at >= edge * width).astype(jnp.int32)
    return total


def identity(rows, cols):
    same = lax.broadcasted_iota(jnp.int32, (rows, cols), 0) == lax.broadcasted_iota(jnp.int32, (rows, cols), 1)
    return same.astype(jnp.bfloat16)


def transpose(block):
    return lax.dot_general(
        identity(block.shape[1], block.shape[1]),
        block,
        (((1,), (1,)), ((), ())),
        preferred_element_type=jnp.float32,
    )


def sigmoid(values):
    return 0.5 * jnp.tanh(0.5 * values) + 0.5


def keep_of(tile_ref, chain_ref, rows, cols):
    tokens = chain_ref.shape[1]
    tiles = tile_ref.shape[1]
    positions = rows * cols
    at = lax.broadcasted_iota(jnp.int32, (1, positions), 1)
    row = steps(at, cols, rows)
    k = lax.axis_index("row") * rows + row
    i = lax.axis_index("col") * cols + at - row * cols
    token = lax.broadcasted_iota(jnp.int32, (tokens, positions), 0)
    pick = (token == k).astype(jnp.float32) - (token == i).astype(jnp.float32)
    chains = jnp.broadcast_to(chain_ref[...].astype(jnp.bfloat16), (8, tokens))
    apart = jnp.dot(chains, pick.astype(jnp.bfloat16), preferred_element_type=jnp.float32)[:1]
    k_tile = steps(k, TILE, tiles)
    i_tile = steps(i, TILE, tiles)
    tile_vals = jnp.zeros((1, positions), jnp.float32)
    for a in range(tiles):
        for b in range(tiles):
            here = (k_tile == a) & (i_tile == b)
            tile_vals = jnp.where(here, tile_ref[a, b].astype(jnp.float32), tile_vals)
    return jnp.where(apart == 0.0, 1.0, tile_vals)


def cycle_of(cols):
    cycle = math.lcm(cols, LANES)
    return cycle // cols, cycle // LANES


def start_copies(sems, *pairs):
    copies = [pltpu.make_async_copy(src, dst, sems.at[at]) for at, (src, dst) in enumerate(pairs)]
    for copy in copies:
        copy.start()
    return copies


def fetch(sems, *pairs):
    for copy in start_copies(sems, *pairs):
        copy.wait()


def project_kernel(
    rows, cols, tile_hbm, chain_hbm, pair_hbm, gain_hbm, w_hbm, gain_mid_hbm, w_out_hbm,
    message_ref, gate_ref, w_out_ref, gain_mid_ref,
    tile_ref, chain_ref, pair_ref, gain_ref, w_ref, gain_mid, w_out, normed_ref, sems,
):
    hidden = (w_ref.shape[1] - w_ref.shape[0]) // 4
    peers = message_ref.shape[0]
    own = hidden // peers
    groups = cycle_of(cols)[1]
    size = groups * LANES
    copies = start_copies(
        sems,
        (chain_hbm, chain_ref),
        (tile_hbm, tile_ref),
        (gain_hbm, gain_ref),
        (pair_hbm, pair_ref),
        (w_hbm, w_ref),
        (gain_mid_hbm, gain_mid),
        (w_out_hbm, w_out),
    )
    for copy in copies[:3]:
        copy.wait()
    keep = keep_of(tile_ref, chain_ref, rows, cols)
    gain = column(gain_ref[...])
    copies[4].wait()
    w_t = w_ref[...].T
    copies[3].wait()
    cycles = [slice(start, start + size) for start in range(0, rows * cols, size)]
    for lanes in cycles:
        block = transpose(pair_ref[lanes, :])
        center = block - jnp.mean(block, axis=0, keepdims=True)
        spread = jnp.mean(center * center, axis=0, keepdims=True)
        normed_ref[:, lanes] = (center * lax.rsqrt(spread + EPS) * gain).astype(jnp.bfloat16)
    for cycle, lanes in enumerate(cycles):
        projected = jnp.dot(w_t, normed_ref[:, lanes], preferred_element_type=jnp.float32)
        sides = []
        for side in range(2):
            value = projected[2 * side * hidden : (2 * side + 1) * hidden]
            gate = projected[(2 * side + 1) * hidden : (2 * side + 2) * hidden]
            sides.append((sigmoid(gate) * value * keep[:, lanes]).reshape(peers, own, size))
        both = jnp.concatenate(sides, axis=1).astype(jnp.bfloat16)
        for group in range(groups):
            line = (cycle * groups + group) * 2 * own
            message_ref[:, line : line + 2 * own, :] = both[:, :, group * LANES : (group + 1) * LANES]
        gate_ref[:, lanes] = sigmoid(projected[4 * hidden :])
    for copy in copies[5:]:
        copy.wait()
    w_out_ref[...] = w_out[...].T
    gain_mid_ref[...] = jnp.broadcast_to(column(gain_mid[...]), gain_mid_ref.shape)


def unpack(message_ref, half, halves, spread_ref, own, cols):
    tokens, groups = cycle_of(cols)
    members, lines, _ = message_ref.shape
    peers = members // halves
    lane = lax.broadcasted_iota(jnp.int32, (2 * own, LANES), 1)
    cycles = lines // (2 * groups * own)
    for peer in range(peers):
        for cycle in range(cycles):
            base = cycle * groups
            held = [
                message_ref[
                    peer * halves + half, (base + group) * 2 * own : (base + group + 1) * 2 * own, :
                ].astype(jnp.float32)
                for group in range(groups)
            ]
            for token in range(tokens):
                k = (peer * cycles + cycle) * tokens + token
                for chunk in range(spread_ref.shape[0]):
                    group, off = divmod(token * cols + chunk * LANES, LANES)
                    value = held[group]
                    if off and group + 1 < groups:
                        value = jnp.where(lane >= off, value, held[group + 1])
                    if off:
                        value = pltpu.roll(value, LANES - off, axis=1)
                    spread_ref[chunk, k * 2 * own : (k + 1) * 2 * own, :] = value


def pack(spread_ref, at, own, cols):
    tokens, groups = cycle_of(cols)
    lane = lax.broadcasted_iota(jnp.int32, (own, LANES), 1)
    rolled, lines = {}, []
    for group in range(groups):
        value, here = None, 0
        while here < LANES:
            token, col = divmod(group * LANES + here, cols)
            chunk, there = divmod(col, LANES)
            shift = (here - there) % LANES
            if (token, chunk, shift) not in rolled:
                line = (at * tokens + token) * own
                piece = spread_ref[chunk, line : line + own, :]
                rolled[token, chunk, shift] = pltpu.roll(piece, shift, axis=1) if shift else piece
            piece = rolled[token, chunk, shift]
            value = piece if value is None else jnp.where(lane >= here, piece, value)
            here += min(LANES - here, LANES - there, cols - col)
        lines.append(value)
    return lines


def channel_of(spread_ref, line, stride):
    count = spread_ref.shape[1] // stride
    return jnp.concatenate(
        [spread_ref[chunk, pl.ds(line, count, stride=stride), :] for chunk in range(spread_ref.shape[0])],
        axis=1,
    ).astype(jnp.bfloat16)


def triangle_kernel(own, cols, shares, message_ref, mixed_ref, spread, left, left_t, right, mixed):
    halves, chunks = spread.shape[:2]
    width = chunks * LANES
    deep = right.shape[1]
    depth = spread.shape[2] // (2 * own)
    one = identity(cols, width)
    if depth < deep:
        right[:, depth:, :] = jnp.zeros((own, deep - depth, halves * width), jnp.bfloat16)
    for half in range(halves):
        unpack(message_ref, half, halves, spread.at[half], own, cols)
        if depth < deep:
            left[:, half * deep + depth : (half + 1) * deep, :] = jnp.zeros((own, deep - depth, width), jnp.bfloat16)
        for channel in range(own):
            left[channel, half * deep : half * deep + depth, :] = channel_of(spread.at[half], channel, 2 * own)
            right[channel, :depth, half * width : (half + 1) * width] = channel_of(
                spread.at[half], own + channel, 2 * own
            )
    for channel in range(own):
        both = lax.dot_general(
            one, left[channel], (((1,), (1,)), ((), ())), preferred_element_type=jnp.float32
        ).astype(jnp.bfloat16)
        for half in range(halves):
            left_t[channel, half * cols : (half + 1) * cols, :] = both[:, half * deep : (half + 1) * deep]
    for channel in range(own):
        total = jnp.dot(left_t[channel], right[channel], preferred_element_type=jnp.float32)
        for i_half in range(halves):
            for j_half in range(halves):
                for chunk in range(chunks):
                    start = j_half * width + chunk * LANES
                    mixed[i_half, j_half, chunk, pl.ds(channel, cols, stride=own), :] = total[
                        i_half * cols : (i_half + 1) * cols, start : start + LANES
                    ]
    groups = cycle_of(cols)[1]
    each = mixed_ref.shape[0] // shares
    cycles = each // (halves * groups * own)
    for share in range(shares):
        i_half, peer = divmod(share, shares // halves)
        lines = []
        for j_half in range(halves):
            for cycle in range(cycles):
                lines += pack(mixed.at[i_half, j_half], peer * cycles + cycle, own, cols)
        mixed_ref[share * each : (share + 1) * each, :] = jnp.concatenate(lines, axis=0).astype(jnp.bfloat16)


def output_kernel(own, parts, mixed_ref, gate_ref, gain_ref, w_t_ref, update_hbm, mixed, update, sems):
    members, lines, _ = mixed.shape
    members = members // parts
    mixed[...] = mixed_ref[...].astype(jnp.float32).reshape(mixed.shape)
    groups = lines // own
    steps = math.gcd(groups, 3)
    leaving = []
    for group in range(groups):
        sums = mixed[:members, group * own : (group + 1) * own, :]
        for part in range(1, parts):
            sums += mixed[part * members : (part + 1) * members, group * own : (group + 1) * own, :]
        block = sums.reshape(members * own, LANES)
        center = block - jnp.mean(block, axis=0, keepdims=True)
        spread = jnp.mean(center * center, axis=0, keepdims=True)
        normed = (center * lax.rsqrt(spread + EPS) * gain_ref[...]).astype(jnp.bfloat16)
        projected = jnp.dot(w_t_ref[...], normed, preferred_element_type=jnp.float32)
        lanes = slice(group * LANES, (group + 1) * LANES)
        update[lanes, :] = (gate_ref[:, lanes] * projected).T.astype(jnp.bfloat16)
        step, last = divmod((group + 1) * steps, groups)
        if last == 0:
            done = slice((step - 1) * (groups // steps) * LANES, (group + 1) * LANES)
            leaving += start_copies(sems.at[step - 1], (update.at[done, :], update_hbm.at[done, :]))
    for copy in leaving:
        copy.wait()


def on_device(shares, halves, pair, tile_mask, chain_ids, gain_in, w_proj, gain_mid, w_out):
    rows, cols, width = pair.shape
    hidden = w_out.shape[0]
    peers = shares // PARTS
    own = hidden // (peers * halves)
    positions = rows * cols
    groups = positions // LANES
    lines = groups * own
    cycles = groups // cycle_of(cols)[1]
    params = pltpu.CompilerParams(vmem_limit_bytes=VMEM_BYTES)
    tokens = chain_ids.shape[0]
    message = jax.ShapeDtypeStruct((peers * halves, 2 * lines, LANES), jnp.bfloat16)
    message, gate, w_out_t, gain = pl.pallas_call(
        functools.partial(project_kernel, rows, cols),
        out_shape=(
            message,
            jax.ShapeDtypeStruct((width, positions), jnp.float32),
            jax.ShapeDtypeStruct(w_out.shape[::-1], jnp.bfloat16),
            jax.ShapeDtypeStruct((hidden, LANES), jnp.float32),
        ),
        in_specs=[HBM] * 7,
        out_specs=[VMEM] * 4,
        scratch_shapes=[
            pltpu.SMEM(tile_mask.shape, jnp.int32),
            pltpu.VMEM((1, tokens), jnp.int32),
            pltpu.VMEM((positions, width), jnp.bfloat16),
            pltpu.VMEM((1, width), jnp.float32),
            pltpu.VMEM(w_proj.shape, jnp.bfloat16),
            pltpu.VMEM((1, hidden), jnp.float32),
            pltpu.VMEM(w_out.shape, jnp.bfloat16),
            pltpu.VMEM((width, positions), jnp.bfloat16),
            pltpu.SemaphoreType.DMA((7,)),
        ],
        compiler_params=params,
        name="project",
    )(
        *[
            pltpu.with_memory_space_constraint(value, pltpu.HBM)
            for value in (
                tile_mask,
                chain_ids[None, :],
                pair.reshape(positions, width),
                gain_in[None, :],
                w_proj,
                gain_mid[None, :],
                w_out,
            )
        ]
    )
    message = lax.all_to_all(
        message,
        ("row", "col"),
        split_axis=0,
        concat_axis=0,
        axis_index_groups=[
            list(range(part * peers * halves, (part + 1) * peers * halves))
            for part in range(PARTS)
        ],
        tiled=True,
    )
    chunks = pl.cdiv(cols, LANES)
    depth = peers * rows
    deep = pl.cdiv(depth, LANES) * LANES
    mixed = pl.pallas_call(
        functools.partial(triangle_kernel, own, cols, shares),
        out_shape=jax.ShapeDtypeStruct((halves * shares * lines, LANES), jnp.bfloat16),
        in_specs=[VMEM],
        out_specs=VMEM,
        scratch_shapes=[
            pltpu.VMEM((halves, chunks, depth * 2 * own, LANES), jnp.float32),
            pltpu.VMEM((own, halves * deep, chunks * LANES), jnp.bfloat16),
            pltpu.VMEM((own, halves * cols, deep), jnp.bfloat16),
            pltpu.VMEM((own, deep, halves * chunks * LANES), jnp.bfloat16),
            pltpu.VMEM((halves, halves, chunks, cols * own, LANES), jnp.float32),
        ],
        compiler_params=params,
        name="triangle",
    )(message)
    mixed = lax.all_to_all(
        mixed.reshape(halves * shares, lines, LANES),
        ("row", "col"),
        split_axis=0,
        concat_axis=0,
        tiled=True,
    ).reshape(halves * shares * lines, LANES)
    update = pl.pallas_call(
        functools.partial(output_kernel, own, PARTS),
        out_shape=jax.ShapeDtypeStruct((positions, width), jnp.bfloat16),
        in_specs=[VMEM] * 4,
        out_specs=HBM,
        scratch_shapes=[
            pltpu.VMEM((shares * halves, lines, LANES), jnp.float32),
            pltpu.VMEM((positions, width), jnp.bfloat16),
            pltpu.SemaphoreType.DMA((math.gcd(groups, 3), 1)),
        ],
        compiler_params=params,
        name="output",
    )(mixed, gate, gain, w_out_t)
    return update.reshape(rows, cols, width)


def solution(mesh):
    in_specs = (P(("grp", "row"), "col", None), P("grp", None), P("grp"), P(), P(), P(), P())
    out_specs = P(("grp", "row"), "col", None)
    return jax.shard_map(
        functools.partial(on_device, mesh.shape["row"], mesh.shape["col"]),
        mesh=mesh,
        in_specs=in_specs,
        out_specs=out_specs,
        check_vma=False,
    )
```

```python
import functools
import math

import jax
import jax.numpy as jnp
from jax import lax
from jax.experimental import pallas as pl
from jax.experimental.pallas import tpu as pltpu
from jax.sharding import PartitionSpec as P

TILE = 96
LANES = 128
EPS = 1e-05
OWN = 4
VMEM_BYTES = 32 * 1024 * 1024
ROWS = 8
VMEM = pl.BlockSpec(memory_space=pltpu.VMEM)
HBM = pl.BlockSpec(memory_space=pltpu.HBM)
SMEM = pl.BlockSpec(memory_space=pltpu.SMEM)


def column(row):
    return jnp.broadcast_to(row, (8, row.shape[1])).T[:, :1]


def steps(at, width, count):
    total = jnp.zeros_like(at)
    for edge in range(1, count):
        total += (at >= edge * width).astype(jnp.int32)
    return total


def identity(rows, cols):
    same = lax.broadcasted_iota(jnp.int32, (rows, cols), 0) == lax.broadcasted_iota(jnp.int32, (rows, cols), 1)
    return same.astype(jnp.bfloat16)


def transpose(block):
    return lax.dot_general(
        identity(block.shape[1], block.shape[1]),
        block,
        (((1,), (1,)), ((), ())),
        preferred_element_type=jnp.float32,
    )


def sigmoid(values):
    return 0.5 * jnp.tanh(0.5 * values) + 0.5


def keep_of(tile_ref, chain_ref, rows, cols):
    tokens = chain_ref.shape[1]
    tiles = tile_ref.shape[1]
    positions = rows * cols
    at = lax.broadcasted_iota(jnp.int32, (1, positions), 1)
    row = steps(at, cols, rows)
    k = lax.axis_index("row") * rows + row
    i = lax.axis_index("col") * cols + at - row * cols
    token = lax.broadcasted_iota(jnp.int32, (tokens, positions), 0)
    pick = (token == k).astype(jnp.float32) - (token == i).astype(jnp.float32)
    chains = jnp.broadcast_to(chain_ref[...].astype(jnp.bfloat16), (8, tokens))
    apart = jnp.dot(chains, pick.astype(jnp.bfloat16), preferred_element_type=jnp.float32)[:1]
    k_tile = steps(k, TILE, tiles)
    i_tile = steps(i, TILE, tiles)
    tile_vals = jnp.zeros((1, positions), jnp.float32)
    for a in range(tiles):
        for b in range(tiles):
            here = (k_tile == a) & (i_tile == b)
            tile_vals = jnp.where(here, tile_ref[a, b].astype(jnp.float32), tile_vals)
    return jnp.where(apart == 0.0, 1.0, tile_vals)


def cycle_of(cols):
    cycle = math.lcm(cols, LANES)
    return cycle // cols, cycle // LANES


def start_copies(sems, *pairs):
    copies = [pltpu.make_async_copy(src, dst, sems.at[at]) for at, (src, dst) in enumerate(pairs)]
    for copy in copies:
        copy.start()
    return copies


def fetch(sems, *pairs):
    for copy in start_copies(sems, *pairs):
        copy.wait()


def turn_pairs(first, second):
    axis = first.ndim - 2
    upper = lax.broadcasted_iota(jnp.int32, first.shape, axis) < OWN
    return (
        jnp.where(upper, first, pltpu.roll(second, OWN, axis=axis)),
        jnp.where(upper, pltpu.roll(first, OWN, axis=axis), second),
    )


def sides_by_member(left, right):
    lines, width = left.shape
    pairs = turn_pairs(left.reshape(-1, ROWS, width), right.reshape(-1, ROWS, width))
    return jnp.stack(pairs, axis=1).reshape(2 * lines, width).astype(jnp.bfloat16)


def project_kernel(
    rows, cols, tile_hbm, chain_hbm, pair_hbm, gain_hbm, w_hbm, gain_mid_hbm, w_out_hbm,
    message_ref, gate_ref, w_out_ref, gain_mid_ref,
    tile_ref, chain_ref, pair_ref, gain_ref, w_ref, gain_mid, w_out, normed_ref, sems,
):
    hidden = (w_ref.shape[1] - w_ref.shape[0]) // 4
    members = message_ref.shape[0]
    size = cycle_of(cols)[1] * LANES
    copies = start_copies(
        sems,
        (chain_hbm, chain_ref),
        (tile_hbm, tile_ref),
        (gain_hbm, gain_ref),
        (pair_hbm, pair_ref),
        (w_hbm, w_ref),
        (gain_mid_hbm, gain_mid),
        (w_out_hbm, w_out),
    )
    for copy in copies[:3]:
        copy.wait()
    keep = keep_of(tile_ref, chain_ref, rows, cols)
    gain = column(gain_ref[...])
    copies[4].wait()
    w_t = w_ref[...].astype(jnp.float32).T
    w_value = sides_by_member(w_t[:hidden], w_t[2 * hidden : 3 * hidden])
    w_gate = sides_by_member(w_t[hidden : 2 * hidden], w_t[3 * hidden : 4 * hidden])
    w_out_gate = w_t[4 * hidden :].astype(jnp.bfloat16)
    copies[3].wait()
    cycles = [slice(start, start + size) for start in range(0, rows * cols, size)]
    for lanes in cycles:
        block = transpose(pair_ref[lanes, :])
        center = block - jnp.mean(block, axis=0, keepdims=True)
        spread = jnp.mean(center * center, axis=0, keepdims=True)
        normed_ref[:, lanes] = (center * lax.rsqrt(spread + EPS) * gain).astype(jnp.bfloat16)
    for lanes in cycles:
        normed = normed_ref[:, lanes]
        value = jnp.dot(w_value, normed, preferred_element_type=jnp.float32)
        gate = jnp.dot(w_gate, normed, preferred_element_type=jnp.float32)
        sent = (sigmoid(gate) * value * keep[:, lanes]).reshape(members, ROWS, size)
        message_ref[:, :, lanes] = sent.astype(jnp.bfloat16)
        gate_ref[:, lanes] = sigmoid(jnp.dot(w_out_gate, normed, preferred_element_type=jnp.float32))
    for copy in copies[5:]:
        copy.wait()
    w_out_ref[...] = w_out[...].T
    gain_mid_ref[...] = jnp.broadcast_to(column(gain_mid[...]), gain_mid_ref.shape)


def unpack(message, half, halves, spread_ref, cols):
    tokens, groups = cycle_of(cols)
    members, _, positions = message.shape
    lane = lax.broadcasted_iota(jnp.int32, (ROWS, LANES), 1)
    cycles = positions // (LANES * groups)
    for peer in range(members // halves):
        for cycle in range(cycles):
            base = cycle * groups
            held = [
                message[peer * halves + half, :, (base + group) * LANES : (base + group + 1) * LANES].astype(
                    jnp.float32
                )
                for group in range(groups)
            ]
            for token in range(tokens):
                k = (peer * cycles + cycle) * tokens + token
                for chunk in range(spread_ref.shape[0]):
                    group, off = divmod(token * cols + chunk * LANES, LANES)
                    value = held[group]
                    if off and group + 1 < groups:
                        value = jnp.where(lane >= off, value, held[group + 1])
                    if off:
                        value = pltpu.roll(value, LANES - off, axis=1)
                    spread_ref[chunk, k * ROWS : (k + 1) * ROWS, :] = value


def pack(spread_ref, at, cols):
    tokens, groups = cycle_of(cols)
    lane = lax.broadcasted_iota(jnp.int32, (ROWS, LANES), 1)
    rolled, lines = {}, []
    for group in range(groups):
        value, here = None, 0
        while here < LANES:
            token, col = divmod(group * LANES + here, cols)
            chunk, there = divmod(col, LANES)
            shift = (here - there) % LANES
            if (token, chunk, shift) not in rolled:
                line = (at * tokens + token) * ROWS
                piece = spread_ref[chunk, line : line + ROWS, :]
                rolled[token, chunk, shift] = pltpu.roll(piece, shift, axis=1) if shift else piece
            piece = rolled[token, chunk, shift]
            value = piece if value is None else jnp.where(lane >= here, piece, value)
            here += min(LANES - here, LANES - there, cols - col)
        lines.append(value)
    return lines


def channel_of(spread_ref, line, stride):
    count = spread_ref.shape[1] // stride
    return jnp.concatenate(
        [spread_ref[chunk, pl.ds(line, count, stride=stride), :] for chunk in range(spread_ref.shape[0])],
        axis=1,
    ).astype(jnp.bfloat16)


def triangle_kernel(cols, shares, message_ref, mixed_ref, spread, left, left_t, right, mixed):
    halves, chunks = spread.shape[:2]
    width = chunks * LANES
    deep = right.shape[1]
    depth = spread.shape[2] // ROWS
    one = identity(cols, width)
    if depth < deep:
        right[:, depth:, :] = jnp.zeros((OWN, deep - depth, halves * width), jnp.bfloat16)
    for half in range(halves):
        unpack(message_ref, half, halves, spread.at[half], cols)
        if depth < deep:
            left[:, half * deep + depth : (half + 1) * deep, :] = jnp.zeros((OWN, deep - depth, width), jnp.bfloat16)
        for channel in range(OWN):
            left[channel, half * deep : half * deep + depth, :] = channel_of(spread.at[half], channel, ROWS)
            right[channel, :depth, half * width : (half + 1) * width] = channel_of(
                spread.at[half], OWN + channel, ROWS
            )
    for channel in range(OWN):
        both = lax.dot_general(
            one, left[channel], (((1,), (1,)), ((), ())), preferred_element_type=jnp.float32
        ).astype(jnp.bfloat16)
        for half in range(halves):
            left_t[channel, half * cols : (half + 1) * cols, :] = both[:, half * deep : (half + 1) * deep]
    for channel in range(OWN):
        total = jnp.dot(left_t[channel], right[channel], preferred_element_type=jnp.float32)
        for i_half in range(halves):
            for j_half in range(halves):
                for chunk in range(chunks):
                    start = j_half * width + chunk * LANES
                    mixed[i_half, chunk, pl.ds(j_half * OWN + channel, cols, stride=ROWS), :] = total[
                        i_half * cols : (i_half + 1) * cols, start : start + LANES
                    ]
    groups = cycle_of(cols)[1]
    cycles = mixed_ref.shape[2] // (LANES * groups)
    for share in range(shares):
        i_half, peer = divmod(share, shares // halves)
        for cycle in range(cycles):
            for group, line in enumerate(pack(mixed.at[i_half], peer * cycles + cycle, cols)):
                start = (cycle * groups + group) * LANES
                for j_half in range(halves):
                    mixed_ref[share * halves + j_half, :, start : start + LANES] = line[
                        j_half * OWN : (j_half + 1) * OWN
                    ].astype(jnp.bfloat16)


def output_kernel(parts, mixed_ref, gate_ref, gain_ref, w_t_ref, update_hbm, mixed, update, sems):
    members = mixed_ref.shape[0] // parts
    groups = update.shape[0] // LANES
    steps = math.gcd(groups, 3)
    for member in range(members):
        sums = mixed_ref[member].astype(jnp.float32)
        for part in range(1, parts):
            sums += mixed_ref[part * members + member].astype(jnp.float32)
        mixed[member * OWN : (member + 1) * OWN, :] = sums
    leaving = []
    for group in range(groups):
        lanes = slice(group * LANES, (group + 1) * LANES)
        block = mixed[:, lanes]
        center = block - jnp.mean(block, axis=0, keepdims=True)
        spread = jnp.mean(center * center, axis=0, keepdims=True)
        normed = (center * lax.rsqrt(spread + EPS) * gain_ref[...]).astype(jnp.bfloat16)
        projected = jnp.dot(w_t_ref[...], normed, preferred_element_type=jnp.float32)
        update[lanes, :] = (gate_ref[:, lanes] * projected).T.astype(jnp.bfloat16)
        step, last = divmod((group + 1) * steps, groups)
        if last == 0:
            done = slice((step - 1) * (groups // steps) * LANES, (group + 1) * LANES)
            leaving += start_copies(sems.at[step - 1], (update.at[done, :], update_hbm.at[done, :]))
    for copy in leaving:
        copy.wait()


def on_device(shares, halves, pair, tile_mask, chain_ids, gain_in, w_proj, gain_mid, w_out):
    rows, cols, width = pair.shape
    hidden = w_out.shape[0]
    devices = shares * halves
    members = hidden // OWN
    parts = devices // members
    positions = rows * cols
    params = pltpu.CompilerParams(vmem_limit_bytes=VMEM_BYTES)
    tokens = chain_ids.shape[0]
    message, gate, w_out_t, gain = pl.pallas_call(
        functools.partial(project_kernel, rows, cols),
        out_shape=(
            jax.ShapeDtypeStruct((members, ROWS, positions), jnp.bfloat16),
            jax.ShapeDtypeStruct((width, positions), jnp.float32),
            jax.ShapeDtypeStruct(w_out.shape[::-1], jnp.bfloat16),
            jax.ShapeDtypeStruct((hidden, LANES), jnp.float32),
        ),
        in_specs=[HBM] * 7,
        out_specs=[VMEM] * 4,
        scratch_shapes=[
            pltpu.SMEM(tile_mask.shape, jnp.int32),
            pltpu.VMEM((1, tokens), jnp.int32),
            pltpu.VMEM((positions, width), jnp.bfloat16),
            pltpu.VMEM((1, width), jnp.float32),
            pltpu.VMEM(w_proj.shape, jnp.bfloat16),
            pltpu.VMEM((1, hidden), jnp.float32),
            pltpu.VMEM(w_out.shape, jnp.bfloat16),
            pltpu.VMEM((width, positions), jnp.bfloat16),
            pltpu.SemaphoreType.DMA((7,)),
        ],
        compiler_params=params,
        name="project",
    )(
        *[
            pltpu.with_memory_space_constraint(value, pltpu.HBM)
            for value in (
                tile_mask,
                chain_ids[None, :],
                pair.reshape(positions, width),
                gain_in[None, :],
                w_proj,
                gain_mid[None, :],
                w_out,
            )
        ]
    )
    message = lax.all_to_all(
        message,
        ("row", "col"),
        split_axis=0,
        concat_axis=0,
        axis_index_groups=None
        if parts == 1
        else [list(range(part * members, (part + 1) * members)) for part in range(parts)],
        tiled=True,
    )
    chunks = pl.cdiv(cols, LANES)
    depth = members // halves * rows
    deep = pl.cdiv(depth, LANES) * LANES
    mixed = pl.pallas_call(
        functools.partial(triangle_kernel, cols, shares),
        out_shape=jax.ShapeDtypeStruct((devices, OWN, positions), jnp.bfloat16),
        in_specs=[VMEM],
        out_specs=VMEM,
        scratch_shapes=[
            pltpu.VMEM((halves, chunks, depth * ROWS, LANES), jnp.float32),
            pltpu.VMEM((OWN, halves * deep, chunks * LANES), jnp.bfloat16),
            pltpu.VMEM((OWN, halves * cols, deep), jnp.bfloat16),
            pltpu.VMEM((OWN, deep, halves * chunks * LANES), jnp.bfloat16),
            pltpu.VMEM((halves, chunks, cols * ROWS, LANES), jnp.float32),
        ],
        compiler_params=params,
        name="triangle",
    )(message)
    mixed = lax.all_to_all(mixed, ("row", "col"), split_axis=0, concat_axis=0, tiled=True)
    groups = positions // LANES
    update = pl.pallas_call(
        functools.partial(output_kernel, parts),
        out_shape=jax.ShapeDtypeStruct((positions, width), jnp.bfloat16),
        in_specs=[VMEM] * 4,
        out_specs=HBM,
        scratch_shapes=[
            pltpu.VMEM((hidden, positions), jnp.float32),
            pltpu.VMEM((positions, width), jnp.bfloat16),
            pltpu.SemaphoreType.DMA((math.gcd(groups, 3), 1)),
        ],
        compiler_params=params,
        name="output",
    )(mixed, gate, gain, w_out_t)
    return update.reshape(rows, cols, width)


def solution(mesh):
    in_specs = (P(("grp", "row"), "col", None), P("grp", None), P("grp"), P(), P(), P(), P())
    out_specs = P(("grp", "row"), "col", None)
    return jax.shard_map(
        functools.partial(on_device, mesh.shape["row"], mesh.shape["col"]),
        mesh=mesh,
        in_specs=in_specs,
        out_specs=out_specs,
        check_vma=False,
    )
```

```python
import functools
import math

import jax
import jax.numpy as jnp
from jax import lax
from jax.experimental import pallas as pl
from jax.experimental.pallas import tpu as pltpu
from jax.sharding import PartitionSpec as P

TILE = 96
LANES = 128
EPS = 1e-05
PARTS = 2
VMEM_BYTES = 32 * 1024 * 1024
VMEM = pl.BlockSpec(memory_space=pltpu.VMEM)
HBM = pl.BlockSpec(memory_space=pltpu.HBM)
SMEM = pl.BlockSpec(memory_space=pltpu.SMEM)


def column(row):
    return jnp.broadcast_to(row, (8, row.shape[1])).T[:, :1]


def steps(at, width, count):
    total = jnp.zeros_like(at)
    for edge in range(1, count):
        total += (at >= edge * width).astype(jnp.int32)
    return total


def identity(rows, cols):
    same = lax.broadcasted_iota(jnp.int32, (rows, cols), 0) == lax.broadcasted_iota(jnp.int32, (rows, cols), 1)
    return same.astype(jnp.bfloat16)


def transpose(block):
    return lax.dot_general(
        identity(block.shape[1], block.shape[1]),
        block,
        (((1,), (1,)), ((), ())),
        preferred_element_type=jnp.float32,
    )


def keep_of(tile_ref, chain_ref, rows, cols):
    tokens = chain_ref.shape[1]
    tiles = tile_ref.shape[1]
    positions = rows * cols
    at = lax.broadcasted_iota(jnp.int32, (1, positions), 1)
    row = steps(at, cols, rows)
    k = lax.axis_index("row") * rows + row
    i = lax.axis_index("col") * cols + at - row * cols
    token = lax.broadcasted_iota(jnp.int32, (tokens, positions), 0)
    pick = (token == k).astype(jnp.float32) - (token == i).astype(jnp.float32)
    chains = jnp.broadcast_to(chain_ref[...].astype(jnp.bfloat16), (8, tokens))
    apart = jnp.dot(chains, pick.astype(jnp.bfloat16), preferred_element_type=jnp.float32)[:1]
    k_tile = steps(k, TILE, tiles)
    i_tile = steps(i, TILE, tiles)
    tile_vals = jnp.zeros((1, positions), jnp.float32)
    for a in range(tiles):
        for b in range(tiles):
            here = (k_tile == a) & (i_tile == b)
            tile_vals = jnp.where(here, tile_ref[a, b].astype(jnp.float32), tile_vals)
    return jnp.where(apart == 0.0, 1.0, tile_vals)


def cycle_of(cols):
    cycle = math.lcm(cols, LANES)
    return cycle // cols, cycle // LANES


def start_copies(sems, *pairs):
    copies = [pltpu.make_async_copy(src, dst, sems.at[at]) for at, (src, dst) in enumerate(pairs)]
    for copy in copies:
        copy.start()
    return copies


def fetch(sems, *pairs):
    for copy in start_copies(sems, *pairs):
        copy.wait()


def project_kernel(
    rows, cols, tile_hbm, chain_hbm, pair_hbm, gain_hbm, w_hbm, gain_mid_hbm, w_out_hbm,
    message_ref, gate_ref, w_out_ref, gain_mid_ref,
    tile_ref, chain_ref, pair_ref, gain_ref, w_ref, gain_mid, w_out, normed_ref, sems,
):
    hidden = (w_ref.shape[1] - w_ref.shape[0]) // 4
    peers = message_ref.shape[0]
    own = hidden // peers
    groups = cycle_of(cols)[1]
    size = groups * LANES
    cycles = [slice(start, start + size) for start in range(0, rows * cols, size)]
    copies = start_copies(
        sems,
        (chain_hbm, chain_ref),
        (tile_hbm, tile_ref),
        (gain_hbm, gain_ref),
        (w_hbm, w_ref),
        (gain_mid_hbm, gain_mid),
        (w_out_hbm, w_out),
        *[(pair_hbm.at[lanes, :], pair_ref.at[lanes, :]) for lanes in cycles],
    )
    for copy in copies[:3]:
        copy.wait()
    keep = keep_of(tile_ref, chain_ref, rows, cols)
    gain = column(gain_ref[...])
    copies[3].wait()
    w_t = jnp.concatenate(
        [
            0.5 * transpose(w_ref[:, start : start + LANES])
            for start in range(0, w_ref.shape[1], LANES)
        ],
        axis=0,
    ).astype(jnp.bfloat16)
    for copy, lanes in zip(copies[6:], cycles):
        copy.wait()
        block = transpose(pair_ref[lanes, :])
        center = block - jnp.mean(block, axis=0, keepdims=True)
        spread = jnp.mean(center * center, axis=0, keepdims=True)
        normed_ref[:, lanes] = (center * lax.rsqrt(spread + EPS) * gain).astype(jnp.bfloat16)
    for cycle, lanes in enumerate(cycles):
        projected = jnp.dot(w_t, normed_ref[:, lanes], preferred_element_type=jnp.float32)
        sides = []
        for side in range(2):
            value = projected[2 * side * hidden : (2 * side + 1) * hidden]
            gate = projected[(2 * side + 1) * hidden : (2 * side + 2) * hidden]
            sides.append(((jnp.tanh(gate) + 1.0) * value * keep[:, lanes]).reshape(peers, own, size))
        both = jnp.concatenate(sides, axis=1).astype(jnp.bfloat16)
        for group in range(groups):
            line = (cycle * groups + group) * 2 * own
            message_ref[:, line : line + 2 * own, :] = both[:, :, group * LANES : (group + 1) * LANES]
        gate_ref[:, lanes] = 0.5 * jnp.tanh(projected[4 * hidden :]) + 0.5
    for copy in copies[4:6]:
        copy.wait()
    w_out_ref[...] = transpose(w_out[...]).astype(jnp.bfloat16)
    gain_mid_ref[...] = jnp.broadcast_to(column(gain_mid[...]), gain_mid_ref.shape)


def unpack(message_ref, half, halves, spread_ref, own, cols):
    tokens, groups = cycle_of(cols)
    members, lines, _ = message_ref.shape
    peers = members // halves
    lane = lax.broadcasted_iota(jnp.int32, (2 * own, LANES), 1)
    cycles = lines // (2 * groups * own)
    for peer in range(peers):
        for cycle in range(cycles):
            base = cycle * groups
            held = [
                message_ref[peer * halves + half, (base + group) * 2 * own : (base + group + 1) * 2 * own, :]
                for group in range(groups)
            ]
            for token in range(tokens):
                k = (peer * cycles + cycle) * tokens + token
                for chunk in range(spread_ref.shape[0]):
                    group, off = divmod(token * cols + chunk * LANES, LANES)
                    value = held[group]
                    if off and group + 1 < groups:
                        value = jnp.where(lane >= off, value, held[group + 1])
                    if off:
                        value = pltpu.roll(value, LANES - off, axis=1)
                    spread_ref[chunk, k * 2 * own : (k + 1) * 2 * own, :] = value.astype(jnp.float32)


def pack(spread_ref, at, own, cols):
    tokens, groups = cycle_of(cols)
    lane = lax.broadcasted_iota(jnp.int32, (own, LANES), 1)
    rolled, lines = {}, []
    for group in range(groups):
        value, here = None, 0
        while here < LANES:
            token, col = divmod(group * LANES + here, cols)
            chunk, there = divmod(col, LANES)
            shift = (here - there) % LANES
            if (token, chunk, shift) not in rolled:
                line = (at * tokens + token) * own
                piece = spread_ref[chunk, line : line + own, :]
                rolled[token, chunk, shift] = pltpu.roll(piece, shift, axis=1) if shift else piece
            piece = rolled[token, chunk, shift]
            value = piece if value is None else jnp.where(lane >= here, piece, value)
            here += min(LANES - here, LANES - there, cols - col)
        lines.append(value)
    return lines


def channel_of(spread_ref, line, stride):
    count = spread_ref.shape[1] // stride
    return jnp.concatenate(
        [spread_ref[chunk, pl.ds(line, count, stride=stride), :] for chunk in range(spread_ref.shape[0])],
        axis=1,
    ).astype(jnp.bfloat16)


def triangle_kernel(own, cols, shares, message_ref, mixed_ref, spread, left, left_t, right, mixed):
    halves, chunks = spread.shape[:2]
    width = chunks * LANES
    deep = right.shape[1]
    depth = spread.shape[2] // (2 * own)
    one = identity(cols, width)
    if depth < deep:
        right[:, depth:, :] = jnp.zeros((own, deep - depth, halves * width), jnp.bfloat16)
    for half in range(halves):
        unpack(message_ref, half, halves, spread.at[half], own, cols)
        if depth < deep:
            left[:, half * deep + depth : (half + 1) * deep, :] = jnp.zeros((own, deep - depth, width), jnp.bfloat16)
        for channel in range(own):
            left[channel, half * deep : half * deep + depth, :] = channel_of(spread.at[half], channel, 2 * own)
            right[channel, :depth, half * width : (half + 1) * width] = channel_of(
                spread.at[half], own + channel, 2 * own
            )
    for channel in range(own):
        both = lax.dot_general(
            one, left[channel], (((1,), (1,)), ((), ())), preferred_element_type=jnp.float32
        ).astype(jnp.bfloat16)
        for half in range(halves):
            left_t[channel, half * cols : (half + 1) * cols, :] = both[:, half * deep : (half + 1) * deep]
    for channel in range(own):
        total = jnp.dot(left_t[channel], right[channel], preferred_element_type=jnp.float32)
        for i_half in range(halves):
            for j_half in range(halves):
                for chunk in range(chunks):
                    start = j_half * width + chunk * LANES
                    mixed[i_half, j_half, chunk, pl.ds(channel, cols, stride=own), :] = total[
                        i_half * cols : (i_half + 1) * cols, start : start + LANES
                    ]
    groups = cycle_of(cols)[1]
    each = mixed_ref.shape[0] // shares
    cycles = each // (halves * groups * own)
    for share in range(shares):
        i_half, peer = divmod(share, shares // halves)
        lines = []
        for j_half in range(halves):
            for cycle in range(cycles):
                lines += pack(mixed.at[i_half, j_half], peer * cycles + cycle, own, cols)
        mixed_ref[share * each : (share + 1) * each, :] = jnp.concatenate(lines, axis=0).astype(jnp.bfloat16)


def output_kernel(own, parts, mixed_ref, gate_ref, gain_ref, w_t_ref, update_hbm, mixed, update, sems):
    members, lines, _ = mixed.shape
    members = members // parts
    mixed[...] = mixed_ref[...].astype(jnp.float32).reshape(mixed.shape)
    groups = lines // own
    steps = math.gcd(groups, 3)
    leaving = []
    for group in range(groups):
        sums = mixed[:members, group * own : (group + 1) * own, :]
        for part in range(1, parts):
            sums += mixed[part * members : (part + 1) * members, group * own : (group + 1) * own, :]
        block = sums.reshape(members * own, LANES)
        center = block - jnp.mean(block, axis=0, keepdims=True)
        spread = jnp.mean(center * center, axis=0, keepdims=True)
        normed = (center * lax.rsqrt(spread + EPS) * gain_ref[...]).astype(jnp.bfloat16)
        projected = jnp.dot(w_t_ref[...], normed, preferred_element_type=jnp.float32)
        lanes = slice(group * LANES, (group + 1) * LANES)
        update[lanes, :] = (gate_ref[:, lanes] * projected).T.astype(jnp.bfloat16)
        step, last = divmod((group + 1) * steps, groups)
        if last == 0:
            done = slice((step - 1) * (groups // steps) * LANES, (group + 1) * LANES)
            leaving += start_copies(sems.at[step - 1], (update.at[done, :], update_hbm.at[done, :]))
    for copy in leaving:
        copy.wait()


def on_device(shares, halves, pair, tile_mask, chain_ids, gain_in, w_proj, gain_mid, w_out):
    rows, cols, width = pair.shape
    hidden = w_out.shape[0]
    peers = shares // PARTS
    own = hidden // (peers * halves)
    positions = rows * cols
    groups = positions // LANES
    lines = groups * own
    cycles = groups // cycle_of(cols)[1]
    params = pltpu.CompilerParams(vmem_limit_bytes=VMEM_BYTES)
    tokens = chain_ids.shape[0]
    message = jax.ShapeDtypeStruct((peers * halves, 2 * lines, LANES), jnp.bfloat16)
    message, gate, w_out_t, gain = pl.pallas_call(
        functools.partial(project_kernel, rows, cols),
        out_shape=(
            message,
            jax.ShapeDtypeStruct((width, positions), jnp.float32),
            jax.ShapeDtypeStruct(w_out.shape[::-1], jnp.bfloat16),
            jax.ShapeDtypeStruct((hidden, LANES), jnp.float32),
        ),
        in_specs=[HBM] * 7,
        out_specs=[VMEM] * 4,
        scratch_shapes=[
            pltpu.SMEM(tile_mask.shape, jnp.int32),
            pltpu.VMEM((1, tokens), jnp.int32),
            pltpu.VMEM((positions, width), jnp.bfloat16),
            pltpu.VMEM((1, width), jnp.float32),
            pltpu.VMEM(w_proj.shape, jnp.bfloat16),
            pltpu.VMEM((1, hidden), jnp.float32),
            pltpu.VMEM(w_out.shape, jnp.bfloat16),
            pltpu.VMEM((width, positions), jnp.bfloat16),
            pltpu.SemaphoreType.DMA((6 + groups // cycle_of(cols)[1],)),
        ],
        compiler_params=params,
        name="project",
    )(
        *[
            pltpu.with_memory_space_constraint(value, pltpu.HBM)
            for value in (
                tile_mask,
                chain_ids[None, :],
                pair.reshape(positions, width),
                gain_in[None, :],
                w_proj,
                gain_mid[None, :],
                w_out,
            )
        ]
    )
    message = lax.all_to_all(
        message,
        ("row", "col"),
        split_axis=0,
        concat_axis=0,
        axis_index_groups=[
            list(range(part * peers * halves, (part + 1) * peers * halves))
            for part in range(PARTS)
        ],
        tiled=True,
    )
    chunks = pl.cdiv(cols, LANES)
    depth = peers * rows
    deep = pl.cdiv(depth, LANES) * LANES
    mixed = pl.pallas_call(
        functools.partial(triangle_kernel, own, cols, shares),
        out_shape=jax.ShapeDtypeStruct((halves * shares * lines, LANES), jnp.bfloat16),
        in_specs=[VMEM],
        out_specs=VMEM,
        scratch_shapes=[
            pltpu.VMEM((halves, chunks, depth * 2 * own, LANES), jnp.float32),
            pltpu.VMEM((own, halves * deep, chunks * LANES), jnp.bfloat16),
            pltpu.VMEM((own, halves * cols, deep), jnp.bfloat16),
            pltpu.VMEM((own, deep, halves * chunks * LANES), jnp.bfloat16),
            pltpu.VMEM((halves, halves, chunks, cols * own, LANES), jnp.float32),
        ],
        compiler_params=params,
        name="triangle",
    )(message)
    mixed = lax.all_to_all(
        mixed.reshape(halves * shares, lines, LANES),
        ("row", "col"),
        split_axis=0,
        concat_axis=0,
        tiled=True,
    ).reshape(halves * shares * lines, LANES)
    update = pl.pallas_call(
        functools.partial(output_kernel, own, PARTS),
        out_shape=jax.ShapeDtypeStruct((positions, width), jnp.bfloat16),
        in_specs=[VMEM] * 4,
        out_specs=HBM,
        scratch_shapes=[
            pltpu.VMEM((shares * halves, lines, LANES), jnp.float32),
            pltpu.VMEM((positions, width), jnp.bfloat16),
            pltpu.SemaphoreType.DMA((math.gcd(groups, 3), 1)),
        ],
        compiler_params=params,
        name="output",
    )(mixed, gate, gain, w_out_t)
    return update.reshape(rows, cols, width)


def solution(mesh):
    in_specs = (P(("grp", "row"), "col", None), P("grp", None), P("grp"), P(), P(), P(), P())
    out_specs = P(("grp", "row"), "col", None)
    return jax.shard_map(
        functools.partial(on_device, mesh.shape["row"], mesh.shape["col"]),
        mesh=mesh,
        in_specs=in_specs,
        out_specs=out_specs,
        check_vma=False,
    )
```

```python
import functools
import math

import jax
import jax.numpy as jnp
from jax import lax
from jax.experimental import pallas as pl
from jax.experimental.pallas import tpu as pltpu
from jax.sharding import PartitionSpec as P

TILE = 96
LANES = 128
EPS = 1e-05
PARTS = 2
VMEM_BYTES = 32 * 1024 * 1024
VMEM = pl.BlockSpec(memory_space=pltpu.VMEM)
HBM = pl.BlockSpec(memory_space=pltpu.HBM)
SMEM = pl.BlockSpec(memory_space=pltpu.SMEM)


def column(row):
    return jnp.broadcast_to(row, (8, row.shape[1])).T[:, :1]


def steps(at, width, count):
    total = jnp.zeros_like(at)
    for edge in range(1, count):
        total += (at >= edge * width).astype(jnp.int32)
    return total


def identity(rows, cols):
    same = lax.broadcasted_iota(jnp.int32, (rows, cols), 0) == lax.broadcasted_iota(jnp.int32, (rows, cols), 1)
    return same.astype(jnp.bfloat16)


def transpose(block):
    return lax.dot_general(
        identity(block.shape[1], block.shape[1]),
        block,
        (((1,), (1,)), ((), ())),
        preferred_element_type=jnp.float32,
    )


def keep_of(tile_ref, chain_ref, rows, cols):
    tokens = chain_ref.shape[1]
    tiles = tile_ref.shape[1]
    positions = rows * cols
    at = lax.broadcasted_iota(jnp.int32, (1, positions), 1)
    row = steps(at, cols, rows)
    k = lax.axis_index("row") * rows + row
    i = lax.axis_index("col") * cols + at - row * cols
    token = lax.broadcasted_iota(jnp.int32, (tokens, positions), 0)
    pick = (token == k).astype(jnp.float32) - (token == i).astype(jnp.float32)
    chains = jnp.broadcast_to(chain_ref[...].astype(jnp.bfloat16), (8, tokens))
    apart = jnp.dot(chains, pick.astype(jnp.bfloat16), preferred_element_type=jnp.float32)[:1]
    k_tile = steps(k, TILE, tiles)
    i_tile = steps(i, TILE, tiles)
    tile_vals = jnp.zeros((1, positions), jnp.float32)
    for a in range(tiles):
        for b in range(tiles):
            here = (k_tile == a) & (i_tile == b)
            tile_vals = jnp.where(here, tile_ref[a, b].astype(jnp.float32), tile_vals)
    return jnp.where(apart == 0.0, 1.0, tile_vals)


def cycle_of(cols):
    cycle = math.lcm(cols, LANES)
    return cycle // cols, cycle // LANES


def start_copies(sems, *pairs):
    copies = [pltpu.make_async_copy(src, dst, sems.at[at]) for at, (src, dst) in enumerate(pairs)]
    for copy in copies:
        copy.start()
    return copies


def fetch(sems, *pairs):
    for copy in start_copies(sems, *pairs):
        copy.wait()


def project_kernel(
    rows, cols, tile_hbm, chain_hbm, pair_hbm, gain_hbm, w_hbm, message_ref, gate_ref,
    tile_ref, chain_ref, pair_ref, gain_ref, w_ref, normed_ref, sems,
):
    hidden = (w_ref.shape[1] - w_ref.shape[0]) // 4
    peers = message_ref.shape[0]
    own = hidden // peers
    groups = cycle_of(cols)[1]
    size = groups * LANES
    cycles = [slice(start, start + size) for start in range(0, rows * cols, size)]
    copies = start_copies(
        sems,
        (chain_hbm, chain_ref),
        (tile_hbm, tile_ref),
        (gain_hbm, gain_ref),
        (pair_hbm, pair_ref),
        (w_hbm, w_ref),
    )
    for copy in copies[:3]:
        copy.wait()
    keep = keep_of(tile_ref, chain_ref, rows, cols)
    gain = column(gain_ref[...])
    copies[4].wait()
    w_t = jnp.concatenate(
        [
            0.5 * transpose(w_ref[:, start : start + LANES])
            for start in range(0, w_ref.shape[1], LANES)
        ],
        axis=0,
    ).astype(jnp.bfloat16)
    copies[3].wait()
    for lanes in cycles:
        block = transpose(pair_ref[lanes, :])
        center = block - jnp.mean(block, axis=0, keepdims=True)
        spread = jnp.mean(center * center, axis=0, keepdims=True)
        normed_ref[:, lanes] = (center * lax.rsqrt(spread + EPS) * gain).astype(jnp.bfloat16)
    for cycle, lanes in enumerate(cycles):
        projected = jnp.dot(w_t, normed_ref[:, lanes], preferred_element_type=jnp.float32)
        sides = []
        for side in range(2):
            value = projected[2 * side * hidden : (2 * side + 1) * hidden]
            gate = projected[(2 * side + 1) * hidden : (2 * side + 2) * hidden]
            sides.append(((jnp.tanh(gate) + 1.0) * value * keep[:, lanes]).reshape(peers, own, size))
        both = jnp.concatenate(sides, axis=1).astype(jnp.bfloat16)
        for group in range(groups):
            line = (cycle * groups + group) * 2 * own
            message_ref[:, line : line + 2 * own, :] = both[:, :, group * LANES : (group + 1) * LANES]
        gate_ref[:, lanes] = 0.5 * jnp.tanh(projected[4 * hidden :]) + 0.5


def unpack(message_ref, half, halves, spread_ref, own, cols):
    tokens, groups = cycle_of(cols)
    members, lines, _ = message_ref.shape
    peers = members // halves
    lane = lax.broadcasted_iota(jnp.int32, (2 * own, LANES), 1)
    cycles = lines // (2 * groups * own)
    for peer in range(peers):
        for cycle in range(cycles):
            base = cycle * groups
            held = [
                message_ref[
                    peer * halves + half, (base + group) * 2 * own : (base + group + 1) * 2 * own, :
                ].astype(jnp.float32)
                for group in range(groups)
            ]
            for token in range(tokens):
                k = (peer * cycles + cycle) * tokens + token
                for chunk in range(spread_ref.shape[0]):
                    group, off = divmod(token * cols + chunk * LANES, LANES)
                    value = held[group]
                    if off and group + 1 < groups:
                        value = jnp.where(lane >= off, value, held[group + 1])
                    if off:
                        value = pltpu.roll(value, LANES - off, axis=1)
                    spread_ref[chunk, k * 2 * own : (k + 1) * 2 * own, :] = value


def pack(spread_ref, at, own, cols):
    tokens, groups = cycle_of(cols)
    lane = lax.broadcasted_iota(jnp.int32, (own, LANES), 1)
    rolled, lines = {}, []
    for group in range(groups):
        value, here = None, 0
        while here < LANES:
            token, col = divmod(group * LANES + here, cols)
            chunk, there = divmod(col, LANES)
            shift = (here - there) % LANES
            if (token, chunk, shift) not in rolled:
                line = (at * tokens + token) * own
                piece = spread_ref[chunk, line : line + own, :]
                rolled[token, chunk, shift] = pltpu.roll(piece, shift, axis=1) if shift else piece
            piece = rolled[token, chunk, shift]
            value = piece if value is None else jnp.where(lane >= here, piece, value)
            here += min(LANES - here, LANES - there, cols - col)
        lines.append(value)
    return lines


def channel_of(spread_ref, line, stride):
    count = spread_ref.shape[1] // stride
    return jnp.concatenate(
        [spread_ref[chunk, pl.ds(line, count, stride=stride), :] for chunk in range(spread_ref.shape[0])],
        axis=1,
    ).astype(jnp.bfloat16)


def triangle_kernel(
    own, cols, shares, message_ref, gain_hbm, w_out_hbm, mixed_ref, gain_ref, w_out_ref,
    spread, left, left_t, right, mixed, gain, w_out, sems,
):
    copies = start_copies(sems, (gain_hbm, gain), (w_out_hbm, w_out))
    halves, chunks = spread.shape[:2]
    width = chunks * LANES
    deep = right.shape[1]
    depth = spread.shape[2] // (2 * own)
    one = identity(cols, width)
    if depth < deep:
        right[:, depth:, :] = jnp.zeros((own, deep - depth, halves * width), jnp.bfloat16)
    for half in range(halves):
        unpack(message_ref, half, halves, spread.at[half], own, cols)
        if depth < deep:
            left[:, half * deep + depth : (half + 1) * deep, :] = jnp.zeros((own, deep - depth, width), jnp.bfloat16)
        for channel in range(own):
            left[channel, half * deep : half * deep + depth, :] = channel_of(spread.at[half], channel, 2 * own)
            right[channel, :depth, half * width : (half + 1) * width] = channel_of(
                spread.at[half], own + channel, 2 * own
            )
    for channel in range(own):
        both = lax.dot_general(
            one, left[channel], (((1,), (1,)), ((), ())), preferred_element_type=jnp.float32
        ).astype(jnp.bfloat16)
        for half in range(halves):
            left_t[channel, half * cols : (half + 1) * cols, :] = both[:, half * deep : (half + 1) * deep]
    for channel in range(own):
        total = jnp.dot(left_t[channel], right[channel], preferred_element_type=jnp.float32)
        for i_half in range(halves):
            for j_half in range(halves):
                for chunk in range(chunks):
                    start = j_half * width + chunk * LANES
                    mixed[i_half, j_half, chunk, pl.ds(channel, cols, stride=own), :] = total[
                        i_half * cols : (i_half + 1) * cols, start : start + LANES
                    ]
    groups = cycle_of(cols)[1]
    each = mixed_ref.shape[0] // shares
    cycles = each // (halves * groups * own)
    for share in range(shares):
        i_half, peer = divmod(share, shares // halves)
        lines = []
        for j_half in range(halves):
            for cycle in range(cycles):
                lines += pack(mixed.at[i_half, j_half], peer * cycles + cycle, own, cols)
        mixed_ref[share * each : (share + 1) * each, :] = jnp.concatenate(lines, axis=0).astype(jnp.bfloat16)
    for copy in copies:
        copy.wait()
    gain_ref[...] = jnp.broadcast_to(column(gain[...]), gain_ref.shape)
    w_out_ref[...] = transpose(w_out[...]).astype(jnp.bfloat16)


def output_kernel(own, parts, mixed_ref, gate_ref, gain_ref, w_t_ref, update_hbm, mixed, update, sems):
    members, lines, _ = mixed.shape
    members = members // parts
    mixed[...] = mixed_ref[...].astype(jnp.float32).reshape(mixed.shape)
    groups = lines // own
    steps = math.gcd(groups, 3)
    leaving = []
    for group in range(groups):
        sums = mixed[:members, group * own : (group + 1) * own, :]
        for part in range(1, parts):
            sums += mixed[part * members : (part + 1) * members, group * own : (group + 1) * own, :]
        block = sums.reshape(members * own, LANES)
        center = block - jnp.mean(block, axis=0, keepdims=True)
        spread = jnp.mean(center * center, axis=0, keepdims=True)
        normed = (center * lax.rsqrt(spread + EPS) * gain_ref[...]).astype(jnp.bfloat16)
        projected = jnp.dot(w_t_ref[...], normed, preferred_element_type=jnp.float32)
        lanes = slice(group * LANES, (group + 1) * LANES)
        update[lanes, :] = (gate_ref[:, lanes] * projected).T.astype(jnp.bfloat16)
        step, last = divmod((group + 1) * steps, groups)
        if last == 0:
            done = slice((step - 1) * (groups // steps) * LANES, (group + 1) * LANES)
            leaving += start_copies(sems.at[step - 1], (update.at[done, :], update_hbm.at[done, :]))
    for copy in leaving:
        copy.wait()


def in_hbm(value):
    return pltpu.with_memory_space_constraint(value, pltpu.HBM)


def on_device(shares, halves, pair, tile_mask, chain_ids, gain_in, w_proj, gain_mid, w_out):
    rows, cols, width = pair.shape
    hidden = w_out.shape[0]
    peers = shares // PARTS
    own = hidden // (peers * halves)
    positions = rows * cols
    groups = positions // LANES
    lines = groups * own
    cycles = groups // cycle_of(cols)[1]
    params = pltpu.CompilerParams(vmem_limit_bytes=VMEM_BYTES)
    tokens = chain_ids.shape[0]
    message = jax.ShapeDtypeStruct((peers * halves, 2 * lines, LANES), jnp.bfloat16)
    message, gate = pl.pallas_call(
        functools.partial(project_kernel, rows, cols),
        out_shape=(
            message,
            jax.ShapeDtypeStruct((width, positions), jnp.float32),
        ),
        in_specs=[HBM] * 5,
        out_specs=[VMEM] * 2,
        scratch_shapes=[
            pltpu.SMEM(tile_mask.shape, jnp.int32),
            pltpu.VMEM((1, tokens), jnp.int32),
            pltpu.VMEM((positions, width), jnp.bfloat16),
            pltpu.VMEM((1, width), jnp.float32),
            pltpu.VMEM(w_proj.shape, jnp.bfloat16),
            pltpu.VMEM((width, positions), jnp.bfloat16),
            pltpu.SemaphoreType.DMA((5,)),
        ],
        compiler_params=params,
        name="project",
    )(
        in_hbm(tile_mask),
        in_hbm(chain_ids[None, :]),
        in_hbm(pair.reshape(positions, width)),
        in_hbm(gain_in[None, :]),
        in_hbm(w_proj),
    )
    message = lax.all_to_all(
        message,
        ("row", "col"),
        split_axis=0,
        concat_axis=0,
        axis_index_groups=[
            list(range(part * peers * halves, (part + 1) * peers * halves))
            for part in range(PARTS)
        ],
        tiled=True,
    )
    chunks = pl.cdiv(cols, LANES)
    depth = peers * rows
    deep = pl.cdiv(depth, LANES) * LANES
    mixed, gain, w_out_t = pl.pallas_call(
        functools.partial(triangle_kernel, own, cols, shares),
        out_shape=(
            jax.ShapeDtypeStruct((halves * shares * lines, LANES), jnp.bfloat16),
            jax.ShapeDtypeStruct((hidden, LANES), jnp.float32),
            jax.ShapeDtypeStruct(w_out.shape[::-1], jnp.bfloat16),
        ),
        in_specs=[VMEM, HBM, HBM],
        out_specs=[VMEM] * 3,
        scratch_shapes=[
            pltpu.VMEM((halves, chunks, depth * 2 * own, LANES), jnp.float32),
            pltpu.VMEM((own, halves * deep, chunks * LANES), jnp.bfloat16),
            pltpu.VMEM((own, halves * cols, deep), jnp.bfloat16),
            pltpu.VMEM((own, deep, halves * chunks * LANES), jnp.bfloat16),
            pltpu.VMEM((halves, halves, chunks, cols * own, LANES), jnp.float32),
            pltpu.VMEM((1, hidden), jnp.float32),
            pltpu.VMEM(w_out.shape, jnp.bfloat16),
            pltpu.SemaphoreType.DMA((2,)),
        ],
        compiler_params=params,
        name="triangle",
    )(message, in_hbm(gain_mid[None, :]), in_hbm(w_out))
    mixed = lax.all_to_all(
        mixed.reshape(halves * shares, lines, LANES),
        ("row", "col"),
        split_axis=0,
        concat_axis=0,
        tiled=True,
    ).reshape(halves * shares * lines, LANES)
    update = pl.pallas_call(
        functools.partial(output_kernel, own, PARTS),
        out_shape=jax.ShapeDtypeStruct((positions, width), jnp.bfloat16),
        in_specs=[VMEM] * 4,
        out_specs=HBM,
        scratch_shapes=[
            pltpu.VMEM((shares * halves, lines, LANES), jnp.float32),
            pltpu.VMEM((positions, width), jnp.bfloat16),
            pltpu.SemaphoreType.DMA((math.gcd(groups, 3), 1)),
        ],
        compiler_params=params,
        name="output",
    )(mixed, gate, gain, w_out_t)
    return update.reshape(rows, cols, width)


def solution(mesh):
    in_specs = (P(("grp", "row"), "col", None), P("grp", None), P("grp"), P(), P(), P(), P())
    out_specs = P(("grp", "row"), "col", None)
    return jax.shard_map(
        functools.partial(on_device, mesh.shape["row"], mesh.shape["col"]),
        mesh=mesh,
        in_specs=in_specs,
        out_specs=out_specs,
        check_vma=False,
    )
```

```python
import functools
import math

import jax
import jax.numpy as jnp
from jax import lax
from jax.experimental import pallas as pl
from jax.experimental.pallas import tpu as pltpu
from jax.sharding import PartitionSpec as P

TILE = 96
LANES = 128
EPS = 1e-05
PARTS = 2
VMEM_BYTES = 32 * 1024 * 1024
VMEM = pl.BlockSpec(memory_space=pltpu.VMEM)
HBM = pl.BlockSpec(memory_space=pltpu.HBM)
SMEM = pl.BlockSpec(memory_space=pltpu.SMEM)


def column(row):
    return jnp.broadcast_to(row, (8, row.shape[1])).T[:, :1]


def steps(at, width, count):
    total = jnp.zeros_like(at)
    for edge in range(1, count):
        total += (at >= edge * width).astype(jnp.int32)
    return total


def identity(rows, cols):
    same = lax.broadcasted_iota(jnp.int32, (rows, cols), 0) == lax.broadcasted_iota(jnp.int32, (rows, cols), 1)
    return same.astype(jnp.bfloat16)


def transpose(block, by=None):
    return lax.dot_general(
        identity(block.shape[1], block.shape[1]) if by is None else by,
        block,
        (((1,), (1,)), ((), ())),
        preferred_element_type=jnp.float32,
    )


def keep_of(tile_ref, chain_ref, rows, cols):
    tokens = chain_ref.shape[1]
    tiles = tile_ref.shape[1]
    positions = rows * cols
    at = lax.broadcasted_iota(jnp.int32, (1, positions), 1)
    row = steps(at, cols, rows)
    k = lax.axis_index("row") * rows + row
    i = lax.axis_index("col") * cols + at - row * cols
    token = lax.broadcasted_iota(jnp.int32, (tokens, positions), 0)
    pick = (token == k).astype(jnp.float32) - (token == i).astype(jnp.float32)
    chains = jnp.broadcast_to(chain_ref[...].astype(jnp.bfloat16), (8, tokens))
    apart = jnp.dot(chains, pick.astype(jnp.bfloat16), preferred_element_type=jnp.float32)[:1]
    k_tile = steps(k, TILE, tiles)
    i_tile = steps(i, TILE, tiles)
    tile_vals = jnp.zeros((1, positions), jnp.float32)
    for a in range(tiles):
        for b in range(tiles):
            here = (k_tile == a) & (i_tile == b)
            tile_vals = jnp.where(here, tile_ref[a, b].astype(jnp.float32), tile_vals)
    return jnp.where(apart == 0.0, 1.0, tile_vals)


def cycle_of(cols):
    cycle = math.lcm(cols, LANES)
    return cycle // cols, cycle // LANES


def start_copies(sems, *pairs):
    copies = [pltpu.make_async_copy(src, dst, sems.at[at]) for at, (src, dst) in enumerate(pairs)]
    for copy in copies:
        copy.start()
    return copies


def fetch(sems, *pairs):
    for copy in start_copies(sems, *pairs):
        copy.wait()


def project_kernel(
    rows, cols, tile_hbm, chain_hbm, pair_hbm, gain_hbm, w_hbm, gain_mid_hbm, w_out_hbm,
    message_ref, gate_ref, w_out_ref, gain_mid_ref,
    tile_ref, chain_ref, pair_ref, gain_ref, w_ref, gain_mid, w_out, normed_ref, sems,
):
    hidden = (w_ref.shape[1] - w_ref.shape[0]) // 4
    peers = message_ref.shape[0]
    own = hidden // peers
    groups = cycle_of(cols)[1]
    size = groups * LANES
    cycles = [slice(start, start + size) for start in range(0, rows * cols, size)]
    copies = start_copies(
        sems,
        (chain_hbm, chain_ref),
        (tile_hbm, tile_ref),
        (gain_hbm, gain_ref),
        (pair_hbm, pair_ref),
        (w_hbm, w_ref),
        (gain_mid_hbm, gain_mid),
        (w_out_hbm, w_out),
    )
    for copy in copies[:3]:
        copy.wait()
    keep = keep_of(tile_ref, chain_ref, rows, cols)
    gain = column(gain_ref[...])
    copies[4].wait()
    w_t = jnp.concatenate(
        [
            0.5 * transpose(w_ref[:, start : start + LANES])
            for start in range(0, w_ref.shape[1], LANES)
        ],
        axis=0,
    ).astype(jnp.bfloat16)
    copies[3].wait()
    width = pair_ref.shape[1]
    centering = (identity(width, width).astype(jnp.float32) - 1.0 / width).astype(jnp.bfloat16)
    for lanes in cycles:
        center = transpose(pair_ref[lanes, :], centering)
        spread = jnp.mean(center * center, axis=0, keepdims=True)
        normed_ref[:, lanes] = (center * lax.rsqrt(spread + EPS) * gain).astype(jnp.bfloat16)
    for lanes in cycles:
        projected = jnp.dot(w_t, normed_ref[:, lanes], preferred_element_type=jnp.float32)
        sides = []
        for side in range(2):
            value = projected[2 * side * hidden : (2 * side + 1) * hidden]
            gate = projected[(2 * side + 1) * hidden : (2 * side + 2) * hidden]
            sides.append(((jnp.tanh(gate) + 1.0) * value * keep[:, lanes]).reshape(peers, own, size))
        message_ref[:, :, lanes] = jnp.concatenate(sides, axis=1).astype(jnp.bfloat16)
        gate_ref[:, lanes] = 0.5 * jnp.tanh(projected[4 * hidden :]) + 0.5
    for copy in copies[5:]:
        copy.wait()
    w_out_ref[...] = transpose(w_out[...]).astype(jnp.bfloat16)
    gain_mid_ref[...] = jnp.broadcast_to(column(gain_mid[...]), gain_mid_ref.shape)


def unpack(message_ref, half, halves, spread_ref, own, cols):
    tokens, groups = cycle_of(cols)
    members, _, positions = message_ref.shape
    lane = lax.broadcasted_iota(jnp.int32, (2 * own, LANES), 1)
    cycles = positions // (LANES * groups)
    for peer in range(members // halves):
        for cycle in range(cycles):
            starts = [(cycle * groups + group) * LANES for group in range(groups)]
            held = [
                message_ref[peer * halves + half, :, start : start + LANES].astype(jnp.float32) for start in starts
            ]
            for token in range(tokens):
                k = (peer * cycles + cycle) * tokens + token
                for chunk in range(spread_ref.shape[0]):
                    group, off = divmod(token * cols + chunk * LANES, LANES)
                    value = held[group]
                    if off and group + 1 < groups:
                        value = jnp.where(lane >= off, value, held[group + 1])
                    if off:
                        value = pltpu.roll(value, LANES - off, axis=1)
                    spread_ref[chunk, k * 2 * own : (k + 1) * 2 * own, :] = value


def pack(spread_ref, at, own, cols):
    tokens, groups = cycle_of(cols)
    lane = lax.broadcasted_iota(jnp.int32, (own, LANES), 1)
    rolled, lines = {}, []
    for group in range(groups):
        value, here = None, 0
        while here < LANES:
            token, col = divmod(group * LANES + here, cols)
            chunk, there = divmod(col, LANES)
            shift = (here - there) % LANES
            if (token, chunk, shift) not in rolled:
                line = (at * tokens + token) * own
                piece = spread_ref[chunk, line : line + own, :]
                rolled[token, chunk, shift] = pltpu.roll(piece, shift, axis=1) if shift else piece
            piece = rolled[token, chunk, shift]
            value = piece if value is None else jnp.where(lane >= here, piece, value)
            here += min(LANES - here, LANES - there, cols - col)
        lines.append(value)
    return lines


def channel_of(spread_ref, line, stride):
    count = spread_ref.shape[1] // stride
    return jnp.concatenate(
        [spread_ref[chunk, pl.ds(line, count, stride=stride), :] for chunk in range(spread_ref.shape[0])],
        axis=1,
    ).astype(jnp.bfloat16)


def triangle_kernel(own, cols, shares, message_ref, mixed_ref, spread, left, left_t, right, mixed):
    halves, chunks = spread.shape[:2]
    width = chunks * LANES
    deep = right.shape[1]
    depth = spread.shape[2] // (2 * own)
    one = identity(cols, width)
    if depth < deep:
        right[:, depth:, :] = jnp.zeros((own, deep - depth, halves * width), jnp.bfloat16)
    for half in range(halves):
        unpack(message_ref, half, halves, spread.at[half], own, cols)
        if depth < deep:
            left[:, half * deep + depth : (half + 1) * deep, :] = jnp.zeros((own, deep - depth, width), jnp.bfloat16)
        for channel in range(own):
            left[channel, half * deep : half * deep + depth, :] = channel_of(spread.at[half], channel, 2 * own)
            right[channel, :depth, half * width : (half + 1) * width] = channel_of(
                spread.at[half], own + channel, 2 * own
            )
    for channel in range(own):
        both = lax.dot_general(
            one, left[channel], (((1,), (1,)), ((), ())), preferred_element_type=jnp.float32
        ).astype(jnp.bfloat16)
        for half in range(halves):
            left_t[channel, half * cols : (half + 1) * cols, :] = both[:, half * deep : (half + 1) * deep]
    for channel in range(own):
        total = jnp.dot(left_t[channel], right[channel], preferred_element_type=jnp.float32)
        for i_half in range(halves):
            for j_half in range(halves):
                for chunk in range(chunks):
                    start = j_half * width + chunk * LANES
                    mixed[i_half, j_half, chunk, pl.ds(channel, cols, stride=own), :] = total[
                        i_half * cols : (i_half + 1) * cols, start : start + LANES
                    ]
    groups = cycle_of(cols)[1]
    cycles = mixed_ref.shape[2] // (groups * LANES)
    for share in range(shares):
        i_half, peer = divmod(share, shares // halves)
        for j_half in range(halves):
            for cycle in range(cycles):
                for group, line in enumerate(pack(mixed.at[i_half, j_half], peer * cycles + cycle, own, cols)):
                    start = (cycle * groups + group) * LANES
                    mixed_ref[share * halves + j_half, :, start : start + LANES] = line.astype(jnp.bfloat16)


def output_kernel(parts, mixed_ref, gate_ref, gain_ref, w_t_ref, update_hbm, update, sems):
    members = mixed_ref.shape[0] // parts
    groups = update.shape[0] // LANES
    steps = sems.shape[0]
    leaving = []
    for group in range(groups):
        lanes = slice(group * LANES, (group + 1) * LANES)
        sums = mixed_ref[:members, :, lanes].astype(jnp.float32)
        for part in range(1, parts):
            sums += mixed_ref[part * members : (part + 1) * members, :, lanes].astype(jnp.float32)
        block = sums.reshape(-1, LANES)
        center = block - jnp.mean(block, axis=0, keepdims=True)
        spread = jnp.mean(center * center, axis=0, keepdims=True)
        normed = (center * lax.rsqrt(spread + EPS) * gain_ref[...]).astype(jnp.bfloat16)
        projected = jnp.dot(w_t_ref[...], normed, preferred_element_type=jnp.float32)
        update[lanes, :] = (gate_ref[:, lanes] * projected).T.astype(jnp.bfloat16)
        step, last = divmod((group + 1) * steps, groups)
        if last == 0:
            done = slice((step - 1) * (groups // steps) * LANES, (group + 1) * LANES)
            leaving += start_copies(sems.at[step - 1], (update.at[done, :], update_hbm.at[done, :]))
    for copy in leaving:
        copy.wait()


def in_hbm(value):
    return pltpu.with_memory_space_constraint(value, pltpu.HBM)


def on_device(shares, halves, pair, tile_mask, chain_ids, gain_in, w_proj, gain_mid, w_out):
    rows, cols, width = pair.shape
    hidden = w_out.shape[0]
    peers = shares // PARTS
    own = hidden // (peers * halves)
    positions = rows * cols
    groups = positions // LANES
    params = pltpu.CompilerParams(vmem_limit_bytes=VMEM_BYTES)
    tokens = chain_ids.shape[0]
    message, gate, w_out_t, gain = pl.pallas_call(
        functools.partial(project_kernel, rows, cols),
        out_shape=(
            jax.ShapeDtypeStruct((peers * halves, 2 * own, positions), jnp.bfloat16),
            jax.ShapeDtypeStruct((width, positions), jnp.float32),
            jax.ShapeDtypeStruct(w_out.shape[::-1], jnp.bfloat16),
            jax.ShapeDtypeStruct((hidden, LANES), jnp.float32),
        ),
        in_specs=[HBM] * 7,
        out_specs=[VMEM] * 4,
        scratch_shapes=[
            pltpu.SMEM(tile_mask.shape, jnp.int32),
            pltpu.VMEM((1, tokens), jnp.int32),
            pltpu.VMEM((positions, width), jnp.bfloat16),
            pltpu.VMEM((1, width), jnp.float32),
            pltpu.VMEM(w_proj.shape, jnp.bfloat16),
            pltpu.VMEM((1, hidden), jnp.float32),
            pltpu.VMEM(w_out.shape, jnp.bfloat16),
            pltpu.VMEM((width, positions), jnp.bfloat16),
            pltpu.SemaphoreType.DMA((7,)),
        ],
        compiler_params=params,
        name="project",
    )(
        in_hbm(tile_mask),
        in_hbm(chain_ids[None, :]),
        in_hbm(pair.reshape(positions, width)),
        in_hbm(gain_in[None, :]),
        in_hbm(w_proj),
        in_hbm(gain_mid[None, :]),
        in_hbm(w_out),
    )
    members = peers * halves
    message = lax.all_to_all(
        message,
        ("row", "col"),
        split_axis=0,
        concat_axis=0,
        axis_index_groups=[list(range(part * members, (part + 1) * members)) for part in range(PARTS)],
        tiled=True,
    )
    chunks = pl.cdiv(cols, LANES)
    depth = peers * rows
    deep = pl.cdiv(depth, LANES) * LANES
    mixed = pl.pallas_call(
        functools.partial(triangle_kernel, own, cols, shares),
        out_shape=jax.ShapeDtypeStruct((shares * halves, own, positions), jnp.bfloat16),
        in_specs=[VMEM],
        out_specs=VMEM,
        scratch_shapes=[
            pltpu.VMEM((halves, chunks, depth * 2 * own, LANES), jnp.float32),
            pltpu.VMEM((own, halves * deep, chunks * LANES), jnp.bfloat16),
            pltpu.VMEM((own, halves * cols, deep), jnp.bfloat16),
            pltpu.VMEM((own, deep, halves * chunks * LANES), jnp.bfloat16),
            pltpu.VMEM((halves, halves, chunks, cols * own, LANES), jnp.float32),
        ],
        compiler_params=params,
        name="triangle",
    )(message)
    mixed = lax.all_to_all(mixed, ("row", "col"), split_axis=0, concat_axis=0, tiled=True)
    update = pl.pallas_call(
        functools.partial(output_kernel, PARTS),
        out_shape=jax.ShapeDtypeStruct((positions, width), jnp.bfloat16),
        in_specs=[VMEM] * 4,
        out_specs=HBM,
        scratch_shapes=[
            pltpu.VMEM((positions, width), jnp.bfloat16),
            pltpu.SemaphoreType.DMA((math.gcd(groups, 3), 1)),
        ],
        compiler_params=params,
        name="output",
    )(mixed, gate, gain, w_out_t)
    return update.reshape(rows, cols, width)


def solution(mesh):
    in_specs = (P(("grp", "row"), "col", None), P("grp", None), P("grp"), P(), P(), P(), P())
    out_specs = P(("grp", "row"), "col", None)
    return jax.shard_map(
        functools.partial(on_device, mesh.shape["row"], mesh.shape["col"]),
        mesh=mesh,
        in_specs=in_specs,
        out_specs=out_specs,
        check_vma=False,
    )
```

```python
import functools
import math

import jax
import jax.numpy as jnp
from jax import lax
from jax.experimental import pallas as pl
from jax.experimental.pallas import tpu as pltpu
from jax.sharding import PartitionSpec as P

TILE = 96
LANES = 128
EPS = 1e-05
PARTS = 2
VMEM_BYTES = 32 * 1024 * 1024
VMEM = pl.BlockSpec(memory_space=pltpu.VMEM)
HBM = pl.BlockSpec(memory_space=pltpu.HBM)
SMEM = pl.BlockSpec(memory_space=pltpu.SMEM)


def column(row):
    return jnp.broadcast_to(row, (8, row.shape[1])).T[:, :1]


def steps(at, width, count):
    total = jnp.zeros_like(at)
    for edge in range(1, count):
        total += (at >= edge * width).astype(jnp.int32)
    return total


def identity(rows, cols):
    same = lax.broadcasted_iota(jnp.int32, (rows, cols), 0) == lax.broadcasted_iota(jnp.int32, (rows, cols), 1)
    return same.astype(jnp.bfloat16)


def transpose(block, by=None):
    return lax.dot_general(
        identity(block.shape[1], block.shape[1]) if by is None else by,
        block,
        (((1,), (1,)), ((), ())),
        preferred_element_type=jnp.float32,
    )


def keep_of(tile_ref, chain_ref, rows, cols):
    tokens = chain_ref.shape[1]
    tiles = tile_ref.shape[1]
    positions = rows * cols
    at = lax.broadcasted_iota(jnp.int32, (1, positions), 1)
    row = steps(at, cols, rows)
    k = lax.axis_index("row") * rows + row
    i = lax.axis_index("col") * cols + at - row * cols
    token = lax.broadcasted_iota(jnp.int32, (tokens, positions), 0)
    pick = (token == k).astype(jnp.float32) - (token == i).astype(jnp.float32)
    chains = jnp.broadcast_to(chain_ref[...].astype(jnp.bfloat16), (8, tokens))
    apart = jnp.dot(chains, pick.astype(jnp.bfloat16), preferred_element_type=jnp.float32)[:1]
    k_tile = steps(k, TILE, tiles)
    i_tile = steps(i, TILE, tiles)
    tile_vals = jnp.zeros((1, positions), jnp.float32)
    for a in range(tiles):
        for b in range(tiles):
            here = (k_tile == a) & (i_tile == b)
            tile_vals = jnp.where(here, tile_ref[a, b].astype(jnp.float32), tile_vals)
    return jnp.where(apart == 0.0, 1.0, tile_vals)


def cycle_of(cols):
    cycle = math.lcm(cols, LANES)
    return cycle // cols, cycle // LANES


def start_copies(sems, *pairs):
    copies = [pltpu.make_async_copy(src, dst, sems.at[at]) for at, (src, dst) in enumerate(pairs)]
    for copy in copies:
        copy.start()
    return copies


def fetch(sems, *pairs):
    for copy in start_copies(sems, *pairs):
        copy.wait()


def project_kernel(
    rows, cols, tile_hbm, chain_hbm, pair_hbm, gain_hbm, w_hbm, gain_mid_hbm, w_out_hbm,
    message_ref, gate_ref, w_out_ref, gain_mid_ref,
    tile_ref, chain_ref, pair_ref, gain_ref, w_ref, gain_mid, w_out, w_t_ref, keep_ref, sems,
):
    hidden = (w_ref.shape[1] - w_ref.shape[0]) // 4
    peers = message_ref.shape[0]
    own = hidden // peers
    groups = cycle_of(cols)[1]
    size = groups * LANES
    copies = start_copies(
        sems,
        (chain_hbm, chain_ref),
        (tile_hbm, tile_ref),
        (gain_hbm, gain_ref),
        (pair_hbm, pair_ref),
        (w_hbm, w_ref),
        (gain_mid_hbm, gain_mid),
        (w_out_hbm, w_out),
    )
    for copy in copies[:3]:
        copy.wait()
    keep = keep_of(tile_ref, chain_ref, rows, cols)
    gain = column(gain_ref[...])
    copies[4].wait()
    for start in range(0, w_ref.shape[1], LANES):
        lines = slice(start, start + LANES)
        w_t_ref[lines, :] = (0.5 * transpose(w_ref[:, lines])).astype(jnp.bfloat16)
    copies[3].wait()
    width = pair_ref.shape[1]
    centering = (identity(width, width).astype(jnp.float32) - 1.0 / width).astype(jnp.bfloat16)
    keep_ref[...] = keep

    @pl.loop(0, rows * cols // size)
    def _(cycle):
        start = pl.multiple_of(cycle * size, LANES)
        lanes = pl.ds(start, size)
        center = transpose(pair_ref[lanes, :], centering)
        spread = jnp.mean(center * center, axis=0, keepdims=True)
        normed = (center * lax.rsqrt(spread + EPS) * gain).astype(jnp.bfloat16)
        projected = jnp.dot(w_t_ref[...], normed, preferred_element_type=jnp.float32)
        sides = []
        for side in range(2):
            value = projected[2 * side * hidden : (2 * side + 1) * hidden]
            gate = projected[(2 * side + 1) * hidden : (2 * side + 2) * hidden]
            sides.append(((jnp.tanh(gate) + 1.0) * value * keep_ref[:, lanes]).reshape(peers, own, size))
        message_ref[:, :, lanes] = jnp.concatenate(sides, axis=1).astype(jnp.bfloat16)
        gate_ref[:, lanes] = 0.5 * jnp.tanh(projected[4 * hidden :]) + 0.5

    for copy in copies[5:]:
        copy.wait()
    w_out_ref[...] = transpose(w_out[...]).astype(jnp.bfloat16)
    gain_mid_ref[...] = jnp.broadcast_to(column(gain_mid[...]), gain_mid_ref.shape)


def unpack(message_ref, half, halves, spread_ref, own, cols):
    tokens, groups = cycle_of(cols)
    members, _, positions = message_ref.shape
    lane = lax.broadcasted_iota(jnp.int32, (2 * own, LANES), 1)
    cycles = positions // (LANES * groups)
    lines = cycles * tokens * 2 * own

    @pl.loop(0, members // halves)
    def _(peer):
        for cycle in range(cycles):
            starts = [(cycle * groups + group) * LANES for group in range(groups)]
            held = [
                message_ref[peer * halves + half, :, start : start + LANES].astype(jnp.float32) for start in starts
            ]
            for token in range(tokens):
                at = pl.multiple_of(peer * lines, 8) + (cycle * tokens + token) * 2 * own
                for chunk in range(spread_ref.shape[0]):
                    group, off = divmod(token * cols + chunk * LANES, LANES)
                    value = held[group]
                    if off and group + 1 < groups:
                        value = jnp.where(lane >= off, value, held[group + 1])
                    if off:
                        value = pltpu.roll(value, LANES - off, axis=1)
                    spread_ref[chunk, pl.ds(at, 2 * own), :] = value


def pack(spread_ref, at, own, cols):
    tokens, groups = cycle_of(cols)
    lane = lax.broadcasted_iota(jnp.int32, (own, LANES), 1)
    rolled, lines = {}, []
    for group in range(groups):
        value, here = None, 0
        while here < LANES:
            token, col = divmod(group * LANES + here, cols)
            chunk, there = divmod(col, LANES)
            shift = (here - there) % LANES
            if (token, chunk, shift) not in rolled:
                line = pl.multiple_of(at * tokens * own, 8) + token * own
                piece = spread_ref[chunk, pl.ds(line, own), :]
                rolled[token, chunk, shift] = pltpu.roll(piece, shift, axis=1) if shift else piece
            piece = rolled[token, chunk, shift]
            value = piece if value is None else jnp.where(lane >= here, piece, value)
            here += min(LANES - here, LANES - there, cols - col)
        lines.append(value)
    return lines


def channel_of(spread_ref, line, stride):
    count = spread_ref.shape[1] // stride
    return jnp.concatenate(
        [spread_ref[chunk, pl.ds(line, count, stride=stride), :] for chunk in range(spread_ref.shape[0])],
        axis=1,
    ).astype(jnp.bfloat16)


def triangle_kernel(own, cols, shares, message_ref, mixed_ref, spread, left, left_t, right, mixed):
    halves, chunks = spread.shape[:2]
    width = chunks * LANES
    deep = right.shape[1]
    depth = spread.shape[2] // (2 * own)
    one = identity(cols, width)
    if depth < deep:
        right[:, depth:, :] = jnp.zeros((own, deep - depth, halves * width), jnp.bfloat16)
    for half in range(halves):
        unpack(message_ref, half, halves, spread.at[half], own, cols)
        if depth < deep:
            left[:, half * deep + depth : (half + 1) * deep, :] = jnp.zeros((own, deep - depth, width), jnp.bfloat16)
        for channel in range(own):
            left[channel, half * deep : half * deep + depth, :] = channel_of(spread.at[half], channel, 2 * own)
            right[channel, :depth, half * width : (half + 1) * width] = channel_of(
                spread.at[half], own + channel, 2 * own
            )
    for channel in range(own):
        both = lax.dot_general(
            one, left[channel], (((1,), (1,)), ((), ())), preferred_element_type=jnp.float32
        ).astype(jnp.bfloat16)
        for half in range(halves):
            left_t[channel, half * cols : (half + 1) * cols, :] = both[:, half * deep : (half + 1) * deep]
    for channel in range(own):
        total = jnp.dot(left_t[channel], right[channel], preferred_element_type=jnp.float32)
        for i_half in range(halves):
            for j_half in range(halves):
                for chunk in range(chunks):
                    start = j_half * width + chunk * LANES
                    mixed[i_half, j_half, chunk, pl.ds(channel, cols, stride=own), :] = total[
                        i_half * cols : (i_half + 1) * cols, start : start + LANES
                    ]
    groups = cycle_of(cols)[1]
    cycles = mixed_ref.shape[2] // (groups * LANES)

    @pl.loop(0, shares // halves)
    def _(peer):
        for i_half in range(halves):
            for j_half in range(halves):
                member = (i_half * (shares // halves) + peer) * halves + j_half
                for cycle in range(cycles):
                    at = peer * cycles + cycle
                    for group, line in enumerate(pack(mixed.at[i_half, j_half], at, own, cols)):
                        start = (cycle * groups + group) * LANES
                        mixed_ref[member, :, start : start + LANES] = line.astype(jnp.bfloat16)


def output_kernel(parts, mixed_ref, gate_ref, gain_ref, w_t_ref, update_hbm, update, sems):
    members = mixed_ref.shape[0] // parts
    groups = update.shape[0] // LANES
    steps = sems.shape[0]
    size = groups // steps * LANES

    def leave(step):
        lines = pl.ds(pl.multiple_of(step * size, LANES), size)
        return pltpu.make_async_copy(update.at[lines, :], update_hbm.at[lines, :], sems.at[step])

    @pl.loop(0, steps)
    def _(step):
        for group in range(groups // steps):
            lanes = pl.ds(pl.multiple_of(step * size, LANES) + group * LANES, LANES)
            sums = mixed_ref[:members, :, lanes].astype(jnp.float32)
            for part in range(1, parts):
                sums += mixed_ref[part * members : (part + 1) * members, :, lanes].astype(jnp.float32)
            block = sums.reshape(-1, LANES)
            center = block - jnp.mean(block, axis=0, keepdims=True)
            spread = jnp.mean(center * center, axis=0, keepdims=True)
            normed = (center * lax.rsqrt(spread + EPS) * gain_ref[...]).astype(jnp.bfloat16)
            projected = jnp.dot(w_t_ref[...], normed, preferred_element_type=jnp.float32)
            update[lanes, :] = (gate_ref[:, lanes] * projected).T.astype(jnp.bfloat16)
        leave(step).start()

    for step in range(steps):
        leave(step).wait()


def in_hbm(value):
    return pltpu.with_memory_space_constraint(value, pltpu.HBM)


def on_device(shares, halves, pair, tile_mask, chain_ids, gain_in, w_proj, gain_mid, w_out):
    rows, cols, width = pair.shape
    hidden = w_out.shape[0]
    peers = shares // PARTS
    own = hidden // (peers * halves)
    positions = rows * cols
    groups = positions // LANES
    params = pltpu.CompilerParams(vmem_limit_bytes=VMEM_BYTES)
    tokens = chain_ids.shape[0]
    message, gate, w_out_t, gain = pl.pallas_call(
        functools.partial(project_kernel, rows, cols),
        out_shape=(
            jax.ShapeDtypeStruct((peers * halves, 2 * own, positions), jnp.bfloat16),
            jax.ShapeDtypeStruct((width, positions), jnp.float32),
            jax.ShapeDtypeStruct(w_out.shape[::-1], jnp.bfloat16),
            jax.ShapeDtypeStruct((hidden, LANES), jnp.float32),
        ),
        in_specs=[HBM] * 7,
        out_specs=[VMEM] * 4,
        scratch_shapes=[
            pltpu.SMEM(tile_mask.shape, jnp.int32),
            pltpu.VMEM((1, tokens), jnp.int32),
            pltpu.VMEM((positions, width), jnp.bfloat16),
            pltpu.VMEM((1, width), jnp.float32),
            pltpu.VMEM(w_proj.shape, jnp.bfloat16),
            pltpu.VMEM((1, hidden), jnp.float32),
            pltpu.VMEM(w_out.shape, jnp.bfloat16),
            pltpu.VMEM(w_proj.shape[::-1], jnp.bfloat16),
            pltpu.VMEM((1, positions), jnp.float32),
            pltpu.SemaphoreType.DMA((7,)),
        ],
        compiler_params=params,
        name="project",
    )(
        in_hbm(tile_mask),
        in_hbm(chain_ids[None, :]),
        in_hbm(pair.reshape(positions, width)),
        in_hbm(gain_in[None, :]),
        in_hbm(w_proj),
        in_hbm(gain_mid[None, :]),
        in_hbm(w_out),
    )
    members = peers * halves
    message = lax.all_to_all(
        message,
        ("row", "col"),
        split_axis=0,
        concat_axis=0,
        axis_index_groups=[list(range(part * members, (part + 1) * members)) for part in range(PARTS)],
        tiled=True,
    )
    chunks = pl.cdiv(cols, LANES)
    depth = peers * rows
    deep = pl.cdiv(depth, LANES) * LANES
    mixed = pl.pallas_call(
        functools.partial(triangle_kernel, own, cols, shares),
        out_shape=jax.ShapeDtypeStruct((shares * halves, own, positions), jnp.bfloat16),
        in_specs=[VMEM],
        out_specs=VMEM,
        scratch_shapes=[
            pltpu.VMEM((halves, chunks, depth * 2 * own, LANES), jnp.float32),
            pltpu.VMEM((own, halves * deep, chunks * LANES), jnp.bfloat16),
            pltpu.VMEM((own, halves * cols, deep), jnp.bfloat16),
            pltpu.VMEM((own, deep, halves * chunks * LANES), jnp.bfloat16),
            pltpu.VMEM((halves, halves, chunks, cols * own, LANES), jnp.float32),
        ],
        compiler_params=params,
        name="triangle",
    )(message)
    mixed = lax.all_to_all(mixed, ("row", "col"), split_axis=0, concat_axis=0, tiled=True)
    update = pl.pallas_call(
        functools.partial(output_kernel, PARTS),
        out_shape=jax.ShapeDtypeStruct((positions, width), jnp.bfloat16),
        in_specs=[VMEM] * 4,
        out_specs=HBM,
        scratch_shapes=[
            pltpu.VMEM((positions, width), jnp.bfloat16),
            pltpu.SemaphoreType.DMA((math.gcd(groups, 3),)),
        ],
        compiler_params=params,
        name="output",
    )(mixed, gate, gain, w_out_t)
    return update.reshape(rows, cols, width)


def solution(mesh):
    in_specs = (P(("grp", "row"), "col", None), P("grp", None), P("grp"), P(), P(), P(), P())
    out_specs = P(("grp", "row"), "col", None)
    return jax.shard_map(
        functools.partial(on_device, mesh.shape["row"], mesh.shape["col"]),
        mesh=mesh,
        in_specs=in_specs,
        out_specs=out_specs,
        check_vma=False,
    )
```

```python
import functools
import math

import jax
import jax.numpy as jnp
from jax import lax
from jax.experimental import pallas as pl
from jax.experimental.pallas import tpu as pltpu
from jax.sharding import PartitionSpec as P

TILE = 96
LANES = 128
EPS = 1e-05
PARTS = 2
VMEM_BYTES = 32 * 1024 * 1024
VMEM = pl.BlockSpec(memory_space=pltpu.VMEM)
HBM = pl.BlockSpec(memory_space=pltpu.HBM)
SMEM = pl.BlockSpec(memory_space=pltpu.SMEM)


def column(row):
    return jnp.broadcast_to(row, (8, row.shape[1])).T[:, :1]


def steps(at, width, count):
    total = jnp.zeros_like(at)
    for edge in range(1, count):
        total += (at >= edge * width).astype(jnp.int32)
    return total


def identity(rows, cols):
    same = lax.broadcasted_iota(jnp.int32, (rows, cols), 0) == lax.broadcasted_iota(jnp.int32, (rows, cols), 1)
    return same.astype(jnp.bfloat16)


def transpose(block):
    return lax.dot_general(
        identity(block.shape[1], block.shape[1]),
        block,
        (((1,), (1,)), ((), ())),
        preferred_element_type=jnp.float32,
    )


def keep_of(tile_ref, chain_ref, rows, cols):
    tokens = chain_ref.shape[1]
    tiles = tile_ref.shape[1]
    positions = rows * cols
    at = lax.broadcasted_iota(jnp.int32, (1, positions), 1)
    row = steps(at, cols, rows)
    k = lax.axis_index("row") * rows + row
    i = lax.axis_index("col") * cols + at - row * cols
    token = lax.broadcasted_iota(jnp.int32, (tokens, positions), 0)
    pick = (token == k).astype(jnp.float32) - (token == i).astype(jnp.float32)
    chains = jnp.broadcast_to(chain_ref[...].astype(jnp.bfloat16), (8, tokens))
    apart = jnp.dot(chains, pick.astype(jnp.bfloat16), preferred_element_type=jnp.float32)[:1]
    k_tile = steps(k, TILE, tiles)
    i_tile = steps(i, TILE, tiles)
    tile_vals = jnp.zeros((1, positions), jnp.float32)
    for a in range(tiles):
        for b in range(tiles):
            here = (k_tile == a) & (i_tile == b)
            tile_vals = jnp.where(here, tile_ref[a, b].astype(jnp.float32), tile_vals)
    return jnp.where(apart == 0.0, 1.0, tile_vals)


def cycle_of(cols):
    cycle = math.lcm(cols, LANES)
    return cycle // cols, cycle // LANES


def start_copies(sems, *pairs):
    copies = [pltpu.make_async_copy(src, dst, sems.at[at]) for at, (src, dst) in enumerate(pairs)]
    for copy in copies:
        copy.start()
    return copies


def fetch(sems, *pairs):
    for copy in start_copies(sems, *pairs):
        copy.wait()


def project_kernel(
    rows, cols, tile_hbm, chain_hbm, pair_hbm, gain_hbm, w_hbm, gain_mid_hbm, w_out_hbm,
    message_ref, gate_ref, w_out_ref, gain_mid_ref,
    tile_ref, chain_ref, pair_ref, gain_ref, w_ref, gain_mid, w_out, normed_ref, sems,
):
    hidden = (w_ref.shape[1] - w_ref.shape[0]) // 4
    peers = message_ref.shape[0]
    own = hidden // peers
    groups = cycle_of(cols)[1]
    size = groups * LANES
    cycles = [slice(start, start + size) for start in range(0, rows * cols, size)]
    copies = start_copies(
        sems,
        (pair_hbm, pair_ref),
        (w_hbm, w_ref),
        (gain_hbm, gain_ref),
        (chain_hbm, chain_ref),
        (tile_hbm, tile_ref),
        (gain_mid_hbm, gain_mid),
        (w_out_hbm, w_out),
    )
    copies[0].wait()
    blocks = [transpose(pair_ref[lanes, :]) for lanes in cycles]
    copies[1].wait()
    w_t = jnp.concatenate(
        [
            0.5 * transpose(w_ref[:, start : start + LANES])
            for start in range(0, w_ref.shape[1], LANES)
        ],
        axis=0,
    ).astype(jnp.bfloat16)
    copies[2].wait()
    gain = column(gain_ref[...])
    for lanes, block in zip(cycles, blocks):
        center = block - jnp.mean(block, axis=0, keepdims=True)
        spread = jnp.mean(center * center, axis=0, keepdims=True)
        normed_ref[:, lanes] = (center * lax.rsqrt(spread + EPS) * gain).astype(jnp.bfloat16)
    copies[3].wait()
    copies[4].wait()
    keep = keep_of(tile_ref, chain_ref, rows, cols)
    for cycle, lanes in enumerate(cycles):
        projected = jnp.dot(w_t, normed_ref[:, lanes], preferred_element_type=jnp.float32)
        sides = []
        for side in range(2):
            value = projected[2 * side * hidden : (2 * side + 1) * hidden]
            gate = projected[(2 * side + 1) * hidden : (2 * side + 2) * hidden]
            sides.append(((jnp.tanh(gate) + 1.0) * value * keep[:, lanes]).reshape(peers, own, size))
        both = jnp.concatenate(sides, axis=1).astype(jnp.bfloat16)
        for group in range(groups):
            line = (cycle * groups + group) * 2 * own
            message_ref[:, line : line + 2 * own, :] = both[:, :, group * LANES : (group + 1) * LANES]
        gate_ref[:, lanes] = 0.5 * jnp.tanh(projected[4 * hidden :]) + 0.5
    for copy in copies[5:]:
        copy.wait()
    w_out_ref[...] = transpose(w_out[...]).astype(jnp.bfloat16)
    gain_mid_ref[...] = jnp.broadcast_to(column(gain_mid[...]), gain_mid_ref.shape)


def unpack(message_ref, half, halves, spread_ref, own, cols):
    tokens, groups = cycle_of(cols)
    members, lines, _ = message_ref.shape
    peers = members // halves
    lane = lax.broadcasted_iota(jnp.int32, (2 * own, LANES), 1)
    cycles = lines // (2 * groups * own)
    for peer in range(peers):
        for cycle in range(cycles):
            base = cycle * groups
            held = [
                message_ref[
                    peer * halves + half, (base + group) * 2 * own : (base + group + 1) * 2 * own, :
                ].astype(jnp.float32)
                for group in range(groups)
            ]
            for token in range(tokens):
                k = (peer * cycles + cycle) * tokens + token
                for chunk in range(spread_ref.shape[0]):
                    group, off = divmod(token * cols + chunk * LANES, LANES)
                    value = held[group]
                    if off and group + 1 < groups:
                        value = jnp.where(lane >= off, value, held[group + 1])
                    if off:
                        value = pltpu.roll(value, LANES - off, axis=1)
                    spread_ref[chunk, k * 2 * own : (k + 1) * 2 * own, :] = value


def pack(spread_ref, at, own, cols):
    tokens, groups = cycle_of(cols)
    lane = lax.broadcasted_iota(jnp.int32, (own, LANES), 1)
    rolled, lines = {}, []
    for group in range(groups):
        value, here = None, 0
        while here < LANES:
            token, col = divmod(group * LANES + here, cols)
            chunk, there = divmod(col, LANES)
            shift = (here - there) % LANES
            if (token, chunk, shift) not in rolled:
                line = (at * tokens + token) * own
                piece = spread_ref[chunk, line : line + own, :]
                rolled[token, chunk, shift] = pltpu.roll(piece, shift, axis=1) if shift else piece
            piece = rolled[token, chunk, shift]
            value = piece if value is None else jnp.where(lane >= here, piece, value)
            here += min(LANES - here, LANES - there, cols - col)
        lines.append(value)
    return lines


def channel_of(spread_ref, line, stride):
    count = spread_ref.shape[1] // stride
    return jnp.concatenate(
        [spread_ref[chunk, pl.ds(line, count, stride=stride), :] for chunk in range(spread_ref.shape[0])],
        axis=1,
    ).astype(jnp.bfloat16)


def triangle_kernel(own, cols, shares, message_ref, mixed_ref, spread, left, left_t, right, mixed):
    halves, chunks = spread.shape[:2]
    width = chunks * LANES
    deep = right.shape[1]
    depth = spread.shape[2] // (2 * own)
    one = identity(cols, width)
    if depth < deep:
        right[:, depth:, :] = jnp.zeros((own, deep - depth, halves * width), jnp.bfloat16)
    for half in range(halves):
        unpack(message_ref, half, halves, spread.at[half], own, cols)
        if depth < deep:
            left[:, half * deep + depth : (half + 1) * deep, :] = jnp.zeros((own, deep - depth, width), jnp.bfloat16)
        for channel in range(own):
            left[channel, half * deep : half * deep + depth, :] = channel_of(spread.at[half], channel, 2 * own)
            right[channel, :depth, half * width : (half + 1) * width] = channel_of(
                spread.at[half], own + channel, 2 * own
            )
    for channel in range(own):
        both = lax.dot_general(
            one, left[channel], (((1,), (1,)), ((), ())), preferred_element_type=jnp.float32
        ).astype(jnp.bfloat16)
        for half in range(halves):
            left_t[channel, half * cols : (half + 1) * cols, :] = both[:, half * deep : (half + 1) * deep]
    for channel in range(own):
        total = jnp.dot(left_t[channel], right[channel], preferred_element_type=jnp.float32)
        for i_half in range(halves):
            for j_half in range(halves):
                for chunk in range(chunks):
                    start = j_half * width + chunk * LANES
                    mixed[i_half, j_half, chunk, pl.ds(channel, cols, stride=own), :] = total[
                        i_half * cols : (i_half + 1) * cols, start : start + LANES
                    ]
    groups = cycle_of(cols)[1]
    each = mixed_ref.shape[0] // shares
    cycles = each // (halves * groups * own)
    for share in range(shares):
        i_half, peer = divmod(share, shares // halves)
        lines = []
        for j_half in range(halves):
            for cycle in range(cycles):
                lines += pack(mixed.at[i_half, j_half], peer * cycles + cycle, own, cols)
        mixed_ref[share * each : (share + 1) * each, :] = jnp.concatenate(lines, axis=0).astype(jnp.bfloat16)


def output_kernel(own, parts, mixed_ref, gate_ref, gain_ref, w_t_ref, update_hbm, mixed, update, sems):
    members, lines, _ = mixed.shape
    members = members // parts
    mixed[...] = mixed_ref[...].astype(jnp.float32).reshape(mixed.shape)
    groups = lines // own
    steps = math.gcd(groups, 3)
    leaving = []
    for group in range(groups):
        sums = mixed[:members, group * own : (group + 1) * own, :]
        for part in range(1, parts):
            sums += mixed[part * members : (part + 1) * members, group * own : (group + 1) * own, :]
        block = sums.reshape(members * own, LANES)
        center = block - jnp.mean(block, axis=0, keepdims=True)
        spread = jnp.mean(center * center, axis=0, keepdims=True)
        normed = (center * lax.rsqrt(spread + EPS) * gain_ref[...]).astype(jnp.bfloat16)
        projected = jnp.dot(w_t_ref[...], normed, preferred_element_type=jnp.float32)
        lanes = slice(group * LANES, (group + 1) * LANES)
        update[lanes, :] = (gate_ref[:, lanes] * projected).T.astype(jnp.bfloat16)
        step, last = divmod((group + 1) * steps, groups)
        if last == 0:
            done = slice((step - 1) * (groups // steps) * LANES, (group + 1) * LANES)
            leaving += start_copies(sems.at[step - 1], (update.at[done, :], update_hbm.at[done, :]))
    for copy in leaving:
        copy.wait()


def in_hbm(value):
    return pltpu.with_memory_space_constraint(value, pltpu.HBM)


def on_device(shares, halves, pair, tile_mask, chain_ids, gain_in, w_proj, gain_mid, w_out):
    rows, cols, width = pair.shape
    hidden = w_out.shape[0]
    peers = shares // PARTS
    own = hidden // (peers * halves)
    positions = rows * cols
    groups = positions // LANES
    lines = groups * own
    cycles = groups // cycle_of(cols)[1]
    params = pltpu.CompilerParams(vmem_limit_bytes=VMEM_BYTES)
    tokens = chain_ids.shape[0]
    message = jax.ShapeDtypeStruct((peers * halves, 2 * lines, LANES), jnp.bfloat16)
    message, gate, w_out_t, gain = pl.pallas_call(
        functools.partial(project_kernel, rows, cols),
        out_shape=(
            message,
            jax.ShapeDtypeStruct((width, positions), jnp.float32),
            jax.ShapeDtypeStruct(w_out.shape[::-1], jnp.bfloat16),
            jax.ShapeDtypeStruct((hidden, LANES), jnp.float32),
        ),
        in_specs=[HBM] * 7,
        out_specs=[VMEM] * 4,
        scratch_shapes=[
            pltpu.SMEM(tile_mask.shape, jnp.int32),
            pltpu.VMEM((1, tokens), jnp.int32),
            pltpu.VMEM((positions, width), jnp.bfloat16),
            pltpu.VMEM((1, width), jnp.float32),
            pltpu.VMEM(w_proj.shape, jnp.bfloat16),
            pltpu.VMEM((1, hidden), jnp.float32),
            pltpu.VMEM(w_out.shape, jnp.bfloat16),
            pltpu.VMEM((width, positions), jnp.bfloat16),
            pltpu.SemaphoreType.DMA((7,)),
        ],
        compiler_params=params,
        name="project",
    )(
        in_hbm(tile_mask),
        in_hbm(chain_ids[None, :]),
        in_hbm(pair.reshape(positions, width)),
        in_hbm(gain_in[None, :]),
        in_hbm(w_proj),
        in_hbm(gain_mid[None, :]),
        in_hbm(w_out),
    )
    message = lax.all_to_all(
        message,
        ("row", "col"),
        split_axis=0,
        concat_axis=0,
        axis_index_groups=[
            list(range(part * peers * halves, (part + 1) * peers * halves))
            for part in range(PARTS)
        ],
        tiled=True,
    )
    chunks = pl.cdiv(cols, LANES)
    depth = peers * rows
    deep = pl.cdiv(depth, LANES) * LANES
    mixed = pl.pallas_call(
        functools.partial(triangle_kernel, own, cols, shares),
        out_shape=jax.ShapeDtypeStruct((halves * shares * lines, LANES), jnp.bfloat16),
        in_specs=[VMEM],
        out_specs=VMEM,
        scratch_shapes=[
            pltpu.VMEM((halves, chunks, depth * 2 * own, LANES), jnp.float32),
            pltpu.VMEM((own, halves * deep, chunks * LANES), jnp.bfloat16),
            pltpu.VMEM((own, halves * cols, deep), jnp.bfloat16),
            pltpu.VMEM((own, deep, halves * chunks * LANES), jnp.bfloat16),
            pltpu.VMEM((halves, halves, chunks, cols * own, LANES), jnp.float32),
        ],
        compiler_params=params,
        name="triangle",
    )(message)
    mixed = lax.all_to_all(
        mixed.reshape(halves * shares, lines, LANES),
        ("row", "col"),
        split_axis=0,
        concat_axis=0,
        tiled=True,
    ).reshape(halves * shares * lines, LANES)
    update = pl.pallas_call(
        functools.partial(output_kernel, own, PARTS),
        out_shape=jax.ShapeDtypeStruct((positions, width), jnp.bfloat16),
        in_specs=[VMEM] * 4,
        out_specs=HBM,
        scratch_shapes=[
            pltpu.VMEM((shares * halves, lines, LANES), jnp.float32),
            pltpu.VMEM((positions, width), jnp.bfloat16),
            pltpu.SemaphoreType.DMA((math.gcd(groups, 3), 1)),
        ],
        compiler_params=params,
        name="output",
    )(mixed, gate, gain, w_out_t)
    return update.reshape(rows, cols, width)


def solution(mesh):
    in_specs = (P(("grp", "row"), "col", None), P("grp", None), P("grp"), P(), P(), P(), P())
    out_specs = P(("grp", "row"), "col", None)
    return jax.shard_map(
        functools.partial(on_device, mesh.shape["row"], mesh.shape["col"]),
        mesh=mesh,
        in_specs=in_specs,
        out_specs=out_specs,
        check_vma=False,
    )
```

```python
import functools
import math

import jax
import jax.numpy as jnp
from jax import lax
from jax.experimental import pallas as pl
from jax.experimental.pallas import tpu as pltpu
from jax.sharding import PartitionSpec as P

TILE = 96
LANES = 128
EPS = 1e-05
PARTS = 2
VMEM_BYTES = 32 * 1024 * 1024
VMEM = pl.BlockSpec(memory_space=pltpu.VMEM)
HBM = pl.BlockSpec(memory_space=pltpu.HBM)
SMEM = pl.BlockSpec(memory_space=pltpu.SMEM)


def column(row):
    return jnp.broadcast_to(row, (8, row.shape[1])).T[:, :1]


def steps(at, width, count):
    total = jnp.zeros_like(at)
    for edge in range(1, count):
        total += (at >= edge * width).astype(jnp.int32)
    return total


def identity(rows, cols):
    same = lax.broadcasted_iota(jnp.int32, (rows, cols), 0) == lax.broadcasted_iota(jnp.int32, (rows, cols), 1)
    return same.astype(jnp.bfloat16)


def transpose(block):
    return lax.dot_general(
        identity(block.shape[1], block.shape[1]),
        block,
        (((1,), (1,)), ((), ())),
        preferred_element_type=jnp.float32,
    )


def keep_of(tile_ref, chain_ref, rows, cols):
    tokens = chain_ref.shape[1]
    tiles = tile_ref.shape[1]
    positions = rows * cols
    at = lax.broadcasted_iota(jnp.int32, (1, positions), 1)
    row = steps(at, cols, rows)
    k = lax.axis_index("row") * rows + row
    i = lax.axis_index("col") * cols + at - row * cols
    token = lax.broadcasted_iota(jnp.int32, (tokens, positions), 0)
    pick = (token == k).astype(jnp.float32) - (token == i).astype(jnp.float32)
    chains = jnp.broadcast_to(chain_ref[...].astype(jnp.bfloat16), (8, tokens))
    apart = jnp.dot(chains, pick.astype(jnp.bfloat16), preferred_element_type=jnp.float32)[:1]
    k_tile = steps(k, TILE, tiles)
    i_tile = steps(i, TILE, tiles)
    tile_vals = jnp.zeros((1, positions), jnp.float32)
    for a in range(tiles):
        for b in range(tiles):
            here = (k_tile == a) & (i_tile == b)
            tile_vals = jnp.where(here, tile_ref[a, b].astype(jnp.float32), tile_vals)
    return jnp.where(apart == 0.0, 1.0, tile_vals)


def cycle_of(cols):
    cycle = math.lcm(cols, LANES)
    return cycle // cols, cycle // LANES


def start_copies(sems, *pairs):
    copies = [pltpu.make_async_copy(src, dst, sems.at[at]) for at, (src, dst) in enumerate(pairs)]
    for copy in copies:
        copy.start()
    return copies


def fetch(sems, *pairs):
    for copy in start_copies(sems, *pairs):
        copy.wait()


def project_kernel(
    rows, cols, tile_hbm, chain_hbm, pair_hbm, gain_hbm, w_hbm, w_out_hbm, message_ref, gate_ref, w_out_ref,
    tile_ref, chain_ref, pair_ref, gain_ref, w_ref, w_out, normed_ref, sems,
):
    hidden = (w_ref.shape[1] - w_ref.shape[0]) // 4
    peers = message_ref.shape[0]
    own = hidden // peers
    groups = cycle_of(cols)[1]
    size = groups * LANES
    cycles = [slice(start, start + size) for start in range(0, rows * cols, size)]
    copies = start_copies(
        sems,
        (chain_hbm, chain_ref),
        (tile_hbm, tile_ref),
        (gain_hbm, gain_ref),
        (pair_hbm, pair_ref),
        (w_hbm, w_ref),
        (w_out_hbm, w_out),
    )
    for copy in copies[:3]:
        copy.wait()
    keep = keep_of(tile_ref, chain_ref, rows, cols)
    gain = column(gain_ref[...])
    copies[4].wait()
    w_t = jnp.concatenate(
        [
            0.5 * transpose(w_ref[:, start : start + LANES])
            for start in range(0, w_ref.shape[1], LANES)
        ],
        axis=0,
    ).astype(jnp.bfloat16)
    copies[3].wait()
    for lanes in cycles:
        block = transpose(pair_ref[lanes, :])
        center = block - jnp.mean(block, axis=0, keepdims=True)
        spread = jnp.mean(center * center, axis=0, keepdims=True)
        normed_ref[:, lanes] = (center * lax.rsqrt(spread + EPS) * gain).astype(jnp.bfloat16)
    for cycle, lanes in enumerate(cycles):
        projected = jnp.dot(w_t, normed_ref[:, lanes], preferred_element_type=jnp.float32)
        sides = []
        for side in range(2):
            value = projected[2 * side * hidden : (2 * side + 1) * hidden]
            gate = projected[(2 * side + 1) * hidden : (2 * side + 2) * hidden]
            sides.append(((jnp.tanh(gate) + 1.0) * value * keep[:, lanes]).reshape(peers, own, size))
        both = jnp.concatenate(sides, axis=1).astype(jnp.bfloat16)
        for group in range(groups):
            line = (cycle * groups + group) * 2 * own
            message_ref[:, line : line + 2 * own, :] = both[:, :, group * LANES : (group + 1) * LANES]
        gate_ref[:, lanes] = 0.5 * jnp.tanh(projected[4 * hidden :]) + 0.5
    copies[5].wait()
    w_out_ref[...] = transpose(w_out[...]).astype(jnp.bfloat16)


def unpack(message_ref, half, halves, spread_ref, own, cols):
    tokens, groups = cycle_of(cols)
    members, lines, _ = message_ref.shape
    peers = members // halves
    lane = lax.broadcasted_iota(jnp.int32, (2 * own, LANES), 1)
    cycles = lines // (2 * groups * own)
    for peer in range(peers):
        for cycle in range(cycles):
            base = cycle * groups
            held = [
                message_ref[
                    peer * halves + half, (base + group) * 2 * own : (base + group + 1) * 2 * own, :
                ].astype(jnp.float32)
                for group in range(groups)
            ]
            for token in range(tokens):
                k = (peer * cycles + cycle) * tokens + token
                for chunk in range(spread_ref.shape[0]):
                    group, off = divmod(token * cols + chunk * LANES, LANES)
                    value = held[group]
                    if off and group + 1 < groups:
                        value = jnp.where(lane >= off, value, held[group + 1])
                    if off:
                        value = pltpu.roll(value, LANES - off, axis=1)
                    spread_ref[chunk, k * 2 * own : (k + 1) * 2 * own, :] = value


def pack(spread_ref, at, own, cols):
    tokens, groups = cycle_of(cols)
    lane = lax.broadcasted_iota(jnp.int32, (own, LANES), 1)
    rolled, lines = {}, []
    for group in range(groups):
        value, here = None, 0
        while here < LANES:
            token, col = divmod(group * LANES + here, cols)
            chunk, there = divmod(col, LANES)
            shift = (here - there) % LANES
            if (token, chunk, shift) not in rolled:
                line = (at * tokens + token) * own
                piece = spread_ref[chunk, line : line + own, :]
                rolled[token, chunk, shift] = pltpu.roll(piece, shift, axis=1) if shift else piece
            piece = rolled[token, chunk, shift]
            value = piece if value is None else jnp.where(lane >= here, piece, value)
            here += min(LANES - here, LANES - there, cols - col)
        lines.append(value)
    return lines


def channel_of(spread_ref, line, stride):
    count = spread_ref.shape[1] // stride
    return jnp.concatenate(
        [spread_ref[chunk, pl.ds(line, count, stride=stride), :] for chunk in range(spread_ref.shape[0])],
        axis=1,
    ).astype(jnp.bfloat16)


def triangle_kernel(
    own, cols, shares, message_ref, gain_ref, mixed_ref, column_ref, spread, left, left_t, right, mixed
):
    column_ref[...] = jnp.broadcast_to(column(gain_ref[...]), column_ref.shape)
    halves, chunks = spread.shape[:2]
    width = chunks * LANES
    deep = right.shape[1]
    depth = spread.shape[2] // (2 * own)
    one = identity(cols, width)
    if depth < deep:
        right[:, depth:, :] = jnp.zeros((own, deep - depth, halves * width), jnp.bfloat16)
    for half in range(halves):
        unpack(message_ref, half, halves, spread.at[half], own, cols)
        if depth < deep:
            left[:, half * deep + depth : (half + 1) * deep, :] = jnp.zeros((own, deep - depth, width), jnp.bfloat16)
        for channel in range(own):
            left[channel, half * deep : half * deep + depth, :] = channel_of(spread.at[half], channel, 2 * own)
            right[channel, :depth, half * width : (half + 1) * width] = channel_of(
                spread.at[half], own + channel, 2 * own
            )
    for channel in range(own):
        both = lax.dot_general(
            one, left[channel], (((1,), (1,)), ((), ())), preferred_element_type=jnp.float32
        ).astype(jnp.bfloat16)
        for half in range(halves):
            left_t[channel, half * cols : (half + 1) * cols, :] = both[:, half * deep : (half + 1) * deep]
    for channel in range(own):
        total = jnp.dot(left_t[channel], right[channel], preferred_element_type=jnp.float32)
        for i_half in range(halves):
            for j_half in range(halves):
                for chunk in range(chunks):
                    start = j_half * width + chunk * LANES
                    mixed[i_half, j_half, chunk, pl.ds(channel, cols, stride=own), :] = total[
                        i_half * cols : (i_half + 1) * cols, start : start + LANES
                    ]
    groups = cycle_of(cols)[1]
    each = mixed_ref.shape[0] // shares
    cycles = each // (halves * groups * own)
    for share in range(shares):
        i_half, peer = divmod(share, shares // halves)
        lines = []
        for j_half in range(halves):
            for cycle in range(cycles):
                lines += pack(mixed.at[i_half, j_half], peer * cycles + cycle, own, cols)
        mixed_ref[share * each : (share + 1) * each, :] = jnp.concatenate(lines, axis=0).astype(jnp.bfloat16)


def output_kernel(own, parts, mixed_ref, gate_ref, gain_ref, w_t_ref, update_hbm, mixed, update, sems):
    members, lines, _ = mixed.shape
    members = members // parts
    mixed[...] = mixed_ref[...].astype(jnp.float32).reshape(mixed.shape)
    groups = lines // own
    steps = math.gcd(groups, 3)
    leaving = []
    for group in range(groups):
        sums = mixed[:members, group * own : (group + 1) * own, :]
        for part in range(1, parts):
            sums += mixed[part * members : (part + 1) * members, group * own : (group + 1) * own, :]
        block = sums.reshape(members * own, LANES)
        center = block - jnp.mean(block, axis=0, keepdims=True)
        spread = jnp.mean(center * center, axis=0, keepdims=True)
        normed = (center * lax.rsqrt(spread + EPS) * gain_ref[...]).astype(jnp.bfloat16)
        projected = jnp.dot(w_t_ref[...], normed, preferred_element_type=jnp.float32)
        lanes = slice(group * LANES, (group + 1) * LANES)
        update[lanes, :] = (gate_ref[:, lanes] * projected).T.astype(jnp.bfloat16)
        step, last = divmod((group + 1) * steps, groups)
        if last == 0:
            done = slice((step - 1) * (groups // steps) * LANES, (group + 1) * LANES)
            leaving += start_copies(sems.at[step - 1], (update.at[done, :], update_hbm.at[done, :]))
    for copy in leaving:
        copy.wait()


def in_hbm(value):
    return pltpu.with_memory_space_constraint(value, pltpu.HBM)


def on_device(shares, halves, pair, tile_mask, chain_ids, gain_in, w_proj, gain_mid, w_out):
    rows, cols, width = pair.shape
    hidden = w_out.shape[0]
    peers = shares // PARTS
    own = hidden // (peers * halves)
    positions = rows * cols
    groups = positions // LANES
    lines = groups * own
    cycles = groups // cycle_of(cols)[1]
    params = pltpu.CompilerParams(vmem_limit_bytes=VMEM_BYTES)
    tokens = chain_ids.shape[0]
    message = jax.ShapeDtypeStruct((peers * halves, 2 * lines, LANES), jnp.bfloat16)
    gain_mid = lax.ppermute(gain_mid, "col", [(half, (half + 1) % halves) for half in range(halves)])
    message, gate, w_out_t = pl.pallas_call(
        functools.partial(project_kernel, rows, cols),
        out_shape=(
            message,
            jax.ShapeDtypeStruct((width, positions), jnp.float32),
            jax.ShapeDtypeStruct(w_out.shape[::-1], jnp.bfloat16),
        ),
        in_specs=[HBM] * 6,
        out_specs=[VMEM] * 3,
        scratch_shapes=[
            pltpu.SMEM(tile_mask.shape, jnp.int32),
            pltpu.VMEM((1, tokens), jnp.int32),
            pltpu.VMEM((positions, width), jnp.bfloat16),
            pltpu.VMEM((1, width), jnp.float32),
            pltpu.VMEM(w_proj.shape, jnp.bfloat16),
            pltpu.VMEM(w_out.shape, jnp.bfloat16),
            pltpu.VMEM((width, positions), jnp.bfloat16),
            pltpu.SemaphoreType.DMA((6,)),
        ],
        compiler_params=params,
        name="project",
    )(
        in_hbm(tile_mask),
        in_hbm(chain_ids[None, :]),
        in_hbm(pair.reshape(positions, width)),
        in_hbm(gain_in[None, :]),
        in_hbm(w_proj),
        in_hbm(w_out),
    )
    message, gain_mid = lax.optimization_barrier((message, gain_mid))
    message = lax.all_to_all(
        message,
        ("row", "col"),
        split_axis=0,
        concat_axis=0,
        axis_index_groups=[
            list(range(part * peers * halves, (part + 1) * peers * halves))
            for part in range(PARTS)
        ],
        tiled=True,
    )
    chunks = pl.cdiv(cols, LANES)
    depth = peers * rows
    deep = pl.cdiv(depth, LANES) * LANES
    mixed, gain = pl.pallas_call(
        functools.partial(triangle_kernel, own, cols, shares),
        out_shape=(
            jax.ShapeDtypeStruct((halves * shares * lines, LANES), jnp.bfloat16),
            jax.ShapeDtypeStruct((hidden, LANES), jnp.float32),
        ),
        in_specs=[VMEM, VMEM],
        out_specs=[VMEM, VMEM],
        scratch_shapes=[
            pltpu.VMEM((halves, chunks, depth * 2 * own, LANES), jnp.float32),
            pltpu.VMEM((own, halves * deep, chunks * LANES), jnp.bfloat16),
            pltpu.VMEM((own, halves * cols, deep), jnp.bfloat16),
            pltpu.VMEM((own, deep, halves * chunks * LANES), jnp.bfloat16),
            pltpu.VMEM((halves, halves, chunks, cols * own, LANES), jnp.float32),
        ],
        compiler_params=params,
        name="triangle",
    )(message, gain_mid[None, :])
    mixed = lax.all_to_all(
        mixed.reshape(halves * shares, lines, LANES),
        ("row", "col"),
        split_axis=0,
        concat_axis=0,
        tiled=True,
    ).reshape(halves * shares * lines, LANES)
    update = pl.pallas_call(
        functools.partial(output_kernel, own, PARTS),
        out_shape=jax.ShapeDtypeStruct((positions, width), jnp.bfloat16),
        in_specs=[VMEM] * 4,
        out_specs=HBM,
        scratch_shapes=[
            pltpu.VMEM((shares * halves, lines, LANES), jnp.float32),
            pltpu.VMEM((positions, width), jnp.bfloat16),
            pltpu.SemaphoreType.DMA((math.gcd(groups, 3), 1)),
        ],
        compiler_params=params,
        name="output",
    )(mixed, gate, gain, w_out_t)
    return update.reshape(rows, cols, width)


def solution(mesh):
    in_specs = (P(("grp", "row"), "col", None), P("grp", None), P("grp"), P(), P(), P(), P())
    out_specs = P(("grp", "row"), "col", None)
    return jax.shard_map(
        functools.partial(on_device, mesh.shape["row"], mesh.shape["col"]),
        mesh=mesh,
        in_specs=in_specs,
        out_specs=out_specs,
        check_vma=False,
    )
```

```python
import functools
import math

import jax
import jax.numpy as jnp
from jax import lax
from jax.experimental import pallas as pl
from jax.experimental.pallas import tpu as pltpu
from jax.sharding import PartitionSpec as P

TILE = 96
LANES = 128
EPS = 1e-05
PARTS = 2
VMEM_BYTES = 32 * 1024 * 1024
VMEM = pl.BlockSpec(memory_space=pltpu.VMEM)
HBM = pl.BlockSpec(memory_space=pltpu.HBM)
SMEM = pl.BlockSpec(memory_space=pltpu.SMEM)


def column(row):
    return jnp.broadcast_to(row, (8, row.shape[1])).T[:, :1]


def steps(at, width, count):
    total = jnp.zeros_like(at)
    for edge in range(1, count):
        total += (at >= edge * width).astype(jnp.int32)
    return total


def identity(rows, cols):
    same = lax.broadcasted_iota(jnp.int32, (rows, cols), 0) == lax.broadcasted_iota(jnp.int32, (rows, cols), 1)
    return same.astype(jnp.bfloat16)


def transpose(block):
    return lax.dot_general(
        identity(block.shape[1], block.shape[1]),
        block,
        (((1,), (1,)), ((), ())),
        preferred_element_type=jnp.float32,
    )


def keep_of(tile_ref, chain_ref, rows, cols):
    tokens = chain_ref.shape[1]
    tiles = tile_ref.shape[1]
    positions = rows * cols
    at = lax.broadcasted_iota(jnp.int32, (1, positions), 1)
    row = steps(at, cols, rows)
    k = lax.axis_index("row") * rows + row
    i = lax.axis_index("col") * cols + at - row * cols
    token = lax.broadcasted_iota(jnp.int32, (tokens, positions), 0)
    pick = (token == k).astype(jnp.float32) - (token == i).astype(jnp.float32)
    chains = jnp.broadcast_to(chain_ref[...].astype(jnp.bfloat16), (8, tokens))
    apart = jnp.dot(chains, pick.astype(jnp.bfloat16), preferred_element_type=jnp.float32)[:1]
    k_tile = steps(k, TILE, tiles)
    i_tile = steps(i, TILE, tiles)
    tile_vals = jnp.zeros((1, positions), jnp.float32)
    for a in range(tiles):
        for b in range(tiles):
            here = (k_tile == a) & (i_tile == b)
            tile_vals = jnp.where(here, tile_ref[a, b].astype(jnp.float32), tile_vals)
    return jnp.where(apart == 0.0, 1.0, tile_vals)


def cycle_of(cols):
    cycle = math.lcm(cols, LANES)
    return cycle // cols, cycle // LANES


def start_copies(sems, *pairs):
    copies = [pltpu.make_async_copy(src, dst, sems.at[at]) for at, (src, dst) in enumerate(pairs)]
    for copy in copies:
        copy.start()
    return copies


def fetch(sems, *pairs):
    for copy in start_copies(sems, *pairs):
        copy.wait()


def project_kernel(
    rows, cols, tile_hbm, chain_hbm, pair_hbm, gain_hbm, w_hbm, gain_mid_hbm, w_out_hbm,
    message_ref, gate_ref, w_out_ref, gain_mid_ref,
    tile_ref, chain_ref, pair_ref, gain_ref, w_ref, gain_mid, w_out, normed_ref, sems,
):
    hidden = (w_ref.shape[1] - w_ref.shape[0]) // 4
    peers = message_ref.shape[0]
    own = hidden // peers
    groups = cycle_of(cols)[1]
    size = groups * LANES
    cycles = [slice(start, start + size) for start in range(0, rows * cols, size)]
    copies = start_copies(
        sems,
        (chain_hbm, chain_ref),
        (tile_hbm, tile_ref),
        (gain_hbm, gain_ref),
        (pair_hbm, pair_ref),
        (w_hbm, w_ref),
        (gain_mid_hbm, gain_mid),
        (w_out_hbm, w_out),
    )
    for copy in copies[:3]:
        copy.wait()
    keep = keep_of(tile_ref, chain_ref, rows, cols)
    gain = column(gain_ref[...])
    copies[4].wait()
    w_t = jnp.concatenate(
        [
            0.5 * transpose(w_ref[:, start : start + LANES])
            for start in range(0, w_ref.shape[1], LANES)
        ],
        axis=0,
    ).astype(jnp.bfloat16)
    copies[3].wait()
    for lanes in cycles:
        block = transpose(pair_ref[lanes, :])
        center = block - jnp.mean(block, axis=0, keepdims=True)
        spread = jnp.mean(center * center, axis=0, keepdims=True)
        normed_ref[:, lanes] = (center * lax.rsqrt(spread + EPS) * gain).astype(jnp.bfloat16)
    for cycle, lanes in enumerate(cycles):
        projected = jnp.dot(w_t, normed_ref[:, lanes], preferred_element_type=jnp.float32)
        sides = []
        for side in range(2):
            value = projected[2 * side * hidden : (2 * side + 1) * hidden]
            gate = projected[(2 * side + 1) * hidden : (2 * side + 2) * hidden]
            sides.append(((jnp.tanh(gate) + 1.0) * value * keep[:, lanes]).reshape(peers, own, size))
        both = jnp.concatenate(sides, axis=1).astype(jnp.bfloat16)
        for group in range(groups):
            line = (cycle * groups + group) * 2 * own
            message_ref[:, line : line + 2 * own, :] = both[:, :, group * LANES : (group + 1) * LANES]
        gate_ref[:, lanes] = 0.5 * jnp.tanh(projected[4 * hidden :]) + 0.5
    for copy in copies[5:]:
        copy.wait()
    gain_mid_ref[...] = jnp.broadcast_to(column(gain_mid[...]), gain_mid_ref.shape)
    w_out_ref[...] = transpose(w_out[...]).astype(jnp.bfloat16)


def unpack(message_ref, half, halves, spread_ref, own, cols):
    tokens, groups = cycle_of(cols)
    members, lines, _ = message_ref.shape
    peers = members // halves
    lane = lax.broadcasted_iota(jnp.int32, (2 * own, LANES), 1)
    cycles = lines // (2 * groups * own)
    for peer in range(peers):
        for cycle in range(cycles):
            base = cycle * groups
            held = [
                message_ref[
                    peer * halves + half, (base + group) * 2 * own : (base + group + 1) * 2 * own, :
                ].astype(jnp.float32)
                for group in range(groups)
            ]
            for token in range(tokens):
                k = (peer * cycles + cycle) * tokens + token
                for chunk in range(spread_ref.shape[0]):
                    group, off = divmod(token * cols + chunk * LANES, LANES)
                    value = held[group]
                    if off and group + 1 < groups:
                        value = jnp.where(lane >= off, value, held[group + 1])
                    if off:
                        value = pltpu.roll(value, LANES - off, axis=1)
                    spread_ref[chunk, k * 2 * own : (k + 1) * 2 * own, :] = value


def pack(spread_ref, at, own, cols):
    tokens, groups = cycle_of(cols)
    lane = lax.broadcasted_iota(jnp.int32, (own, LANES), 1)
    rolled, lines = {}, []
    for group in range(groups):
        value, here = None, 0
        while here < LANES:
            token, col = divmod(group * LANES + here, cols)
            chunk, there = divmod(col, LANES)
            shift = (here - there) % LANES
            if (token, chunk, shift) not in rolled:
                line = (at * tokens + token) * own
                piece = spread_ref[chunk, line : line + own, :]
                rolled[token, chunk, shift] = pltpu.roll(piece, shift, axis=1) if shift else piece
            piece = rolled[token, chunk, shift]
            value = piece if value is None else jnp.where(lane >= here, piece, value)
            here += min(LANES - here, LANES - there, cols - col)
        lines.append(value)
    return lines


def channel_of(spread_ref, line, stride):
    count = spread_ref.shape[1] // stride
    return jnp.concatenate(
        [spread_ref[chunk, pl.ds(line, count, stride=stride), :] for chunk in range(spread_ref.shape[0])],
        axis=1,
    ).astype(jnp.bfloat16)


def triangle_kernel(own, cols, shares, message_ref, mixed_ref, spread, left_t, mixed):
    halves, chunks = spread.shape[:2]
    width = chunks * LANES
    depth = spread.shape[2] // (2 * own)
    deep = left_t.shape[2]
    one = identity(cols, width)
    padding = [jnp.zeros((deep - depth, width), jnp.bfloat16)] if depth < deep else []
    for half in range(halves):
        unpack(message_ref, half, halves, spread.at[half], own, cols)

    def operand(channel, half):
        return jnp.concatenate([channel_of(spread.at[half], channel, 2 * own)] + padding, axis=0)

    for channel in range(own):
        left = jnp.concatenate([operand(channel, half) for half in range(halves)], axis=0)
        both = lax.dot_general(
            one, left, (((1,), (1,)), ((), ())), preferred_element_type=jnp.float32
        ).astype(jnp.bfloat16)
        for half in range(halves):
            left_t[channel, half * cols : (half + 1) * cols, :] = both[:, half * deep : (half + 1) * deep]
    for channel in range(own):
        right = jnp.concatenate([operand(own + channel, half) for half in range(halves)], axis=1)
        total = jnp.dot(left_t[channel], right, preferred_element_type=jnp.float32)
        for i_half in range(halves):
            for j_half in range(halves):
                for chunk in range(chunks):
                    start = j_half * width + chunk * LANES
                    mixed[i_half, j_half, chunk, pl.ds(channel, cols, stride=own), :] = total[
                        i_half * cols : (i_half + 1) * cols, start : start + LANES
                    ]
    groups = cycle_of(cols)[1]
    each = mixed_ref.shape[0] // shares
    cycles = each // (halves * groups * own)
    for share in range(shares):
        i_half, peer = divmod(share, shares // halves)
        lines = []
        for j_half in range(halves):
            for cycle in range(cycles):
                lines += pack(mixed.at[i_half, j_half], peer * cycles + cycle, own, cols)
        mixed_ref[share * each : (share + 1) * each, :] = jnp.concatenate(lines, axis=0).astype(jnp.bfloat16)


def output_kernel(own, parts, mixed_ref, gate_ref, gain_ref, w_t_ref, update_hbm, mixed, update, sems):
    members, lines, _ = mixed.shape
    members = members // parts
    mixed[...] = mixed_ref[...].astype(jnp.float32).reshape(mixed.shape)
    groups = lines // own
    steps = math.gcd(groups, 3)
    leaving = []
    for group in range(groups):
        sums = mixed[:members, group * own : (group + 1) * own, :]
        for part in range(1, parts):
            sums += mixed[part * members : (part + 1) * members, group * own : (group + 1) * own, :]
        block = sums.reshape(members * own, LANES)
        center = block - jnp.mean(block, axis=0, keepdims=True)
        spread = jnp.mean(center * center, axis=0, keepdims=True)
        normed = (center * lax.rsqrt(spread + EPS) * gain_ref[...]).astype(jnp.bfloat16)
        projected = jnp.dot(w_t_ref[...], normed, preferred_element_type=jnp.float32)
        lanes = slice(group * LANES, (group + 1) * LANES)
        update[lanes, :] = (gate_ref[:, lanes] * projected).T.astype(jnp.bfloat16)
        step, last = divmod((group + 1) * steps, groups)
        if last == 0:
            done = slice((step - 1) * (groups // steps) * LANES, (group + 1) * LANES)
            leaving += start_copies(sems.at[step - 1], (update.at[done, :], update_hbm.at[done, :]))
    for copy in leaving:
        copy.wait()


def in_hbm(value):
    return pltpu.with_memory_space_constraint(value, pltpu.HBM)


def on_device(shares, halves, pair, tile_mask, chain_ids, gain_in, w_proj, gain_mid, w_out):
    rows, cols, width = pair.shape
    hidden = w_out.shape[0]
    peers = shares // PARTS
    own = hidden // (peers * halves)
    positions = rows * cols
    groups = positions // LANES
    lines = groups * own
    cycles = groups // cycle_of(cols)[1]
    params = pltpu.CompilerParams(vmem_limit_bytes=VMEM_BYTES)
    tokens = chain_ids.shape[0]
    message = jax.ShapeDtypeStruct((peers * halves, 2 * lines, LANES), jnp.bfloat16)
    message, gate, w_out_t, gain = pl.pallas_call(
        functools.partial(project_kernel, rows, cols),
        out_shape=(
            message,
            jax.ShapeDtypeStruct((width, positions), jnp.float32),
            jax.ShapeDtypeStruct(w_out.shape[::-1], jnp.bfloat16),
            jax.ShapeDtypeStruct((hidden, LANES), jnp.float32),
        ),
        in_specs=[HBM] * 7,
        out_specs=[VMEM] * 4,
        scratch_shapes=[
            pltpu.SMEM(tile_mask.shape, jnp.int32),
            pltpu.VMEM((1, tokens), jnp.int32),
            pltpu.VMEM((positions, width), jnp.bfloat16),
            pltpu.VMEM((1, width), jnp.float32),
            pltpu.VMEM(w_proj.shape, jnp.bfloat16),
            pltpu.VMEM((1, hidden), jnp.float32),
            pltpu.VMEM(w_out.shape, jnp.bfloat16),
            pltpu.VMEM((width, positions), jnp.bfloat16),
            pltpu.SemaphoreType.DMA((7,)),
        ],
        compiler_params=params,
        name="project",
    )(
        in_hbm(tile_mask),
        in_hbm(chain_ids[None, :]),
        in_hbm(pair.reshape(positions, width)),
        in_hbm(gain_in[None, :]),
        in_hbm(w_proj),
        in_hbm(gain_mid[None, :]),
        in_hbm(w_out),
    )
    message = lax.all_to_all(
        message,
        ("row", "col"),
        split_axis=0,
        concat_axis=0,
        axis_index_groups=[
            list(range(part * peers * halves, (part + 1) * peers * halves))
            for part in range(PARTS)
        ],
        tiled=True,
    )
    chunks = pl.cdiv(cols, LANES)
    depth = peers * rows
    deep = pl.cdiv(depth, LANES) * LANES
    mixed = pl.pallas_call(
        functools.partial(triangle_kernel, own, cols, shares),
        out_shape=jax.ShapeDtypeStruct((halves * shares * lines, LANES), jnp.bfloat16),
        in_specs=[VMEM],
        out_specs=VMEM,
        scratch_shapes=[
            pltpu.VMEM((halves, chunks, depth * 2 * own, LANES), jnp.float32),
            pltpu.VMEM((own, halves * cols, deep), jnp.bfloat16),
            pltpu.VMEM((halves, halves, chunks, cols * own, LANES), jnp.float32),
        ],
        compiler_params=params,
        name="triangle",
    )(message)
    mixed = lax.all_to_all(
        mixed.reshape(halves * shares, lines, LANES),
        ("row", "col"),
        split_axis=0,
        concat_axis=0,
        tiled=True,
    ).reshape(halves * shares * lines, LANES)
    update = pl.pallas_call(
        functools.partial(output_kernel, own, PARTS),
        out_shape=jax.ShapeDtypeStruct((positions, width), jnp.bfloat16),
        in_specs=[VMEM] * 4,
        out_specs=HBM,
        scratch_shapes=[
            pltpu.VMEM((shares * halves, lines, LANES), jnp.float32),
            pltpu.VMEM((positions, width), jnp.bfloat16),
            pltpu.SemaphoreType.DMA((math.gcd(groups, 3), 1)),
        ],
        compiler_params=params,
        name="output",
    )(mixed, gate, gain, w_out_t)
    return update.reshape(rows, cols, width)


def solution(mesh):
    in_specs = (P(("grp", "row"), "col", None), P("grp", None), P("grp"), P(), P(), P(), P())
    out_specs = P(("grp", "row"), "col", None)
    return jax.shard_map(
        functools.partial(on_device, mesh.shape["row"], mesh.shape["col"]),
        mesh=mesh,
        in_specs=in_specs,
        out_specs=out_specs,
        check_vma=False,
    )
```

```python
import functools
import math

import jax
import jax.numpy as jnp
from jax import lax
from jax.experimental import pallas as pl
from jax.experimental.pallas import tpu as pltpu
from jax.sharding import PartitionSpec as P

TILE = 96
LANES = 128
EPS = 1e-05
PARTS = 2
VMEM_BYTES = 32 * 1024 * 1024
VMEM = pl.BlockSpec(memory_space=pltpu.VMEM)
HBM = pl.BlockSpec(memory_space=pltpu.HBM)
SMEM = pl.BlockSpec(memory_space=pltpu.SMEM)


def column(row):
    return jnp.broadcast_to(row, (8, row.shape[1])).T[:, :1]


def steps(at, width, count):
    total = jnp.zeros_like(at)
    for edge in range(1, count):
        total += (at >= edge * width).astype(jnp.int32)
    return total


def identity(rows, cols):
    same = lax.broadcasted_iota(jnp.int32, (rows, cols), 0) == lax.broadcasted_iota(jnp.int32, (rows, cols), 1)
    return same.astype(jnp.bfloat16)


def transpose(block):
    return lax.dot_general(
        identity(block.shape[1], block.shape[1]),
        block,
        (((1,), (1,)), ((), ())),
        preferred_element_type=jnp.float32,
    )


def keep_of(tile_ref, chain_ref, rows, cols):
    tokens = chain_ref.shape[1]
    tiles = tile_ref.shape[1]
    positions = rows * cols
    at = lax.broadcasted_iota(jnp.int32, (1, positions), 1)
    row = steps(at, cols, rows)
    k = lax.axis_index("row") * rows + row
    i = lax.axis_index("col") * cols + at - row * cols
    token = lax.broadcasted_iota(jnp.int32, (tokens, positions), 0)
    pick = (token == k).astype(jnp.float32) - (token == i).astype(jnp.float32)
    chains = jnp.broadcast_to(chain_ref[...].astype(jnp.bfloat16), (8, tokens))
    apart = jnp.dot(chains, pick.astype(jnp.bfloat16), preferred_element_type=jnp.float32)[:1]
    k_tile = steps(k, TILE, tiles)
    i_tile = steps(i, TILE, tiles)
    tile_vals = jnp.zeros((1, positions), jnp.float32)
    for a in range(tiles):
        for b in range(tiles):
            here = (k_tile == a) & (i_tile == b)
            tile_vals = jnp.where(here, tile_ref[a, b].astype(jnp.float32), tile_vals)
    return jnp.where(apart == 0.0, 1.0, tile_vals)


def cycle_of(cols):
    cycle = math.lcm(cols, LANES)
    return cycle // cols, cycle // LANES


def start_copies(sems, *pairs):
    copies = [pltpu.make_async_copy(src, dst, sems.at[at]) for at, (src, dst) in enumerate(pairs)]
    for copy in copies:
        copy.start()
    return copies


def fetch(sems, *pairs):
    for copy in start_copies(sems, *pairs):
        copy.wait()


def project_kernel(
    rows, cols, tile_hbm, chain_hbm, pair_hbm, gain_hbm, w_hbm, gain_mid_hbm, w_out_hbm,
    message_ref, gate_ref, w_out_ref, gain_mid_ref,
    tile_ref, chain_ref, pair_ref, gain_ref, w_ref, gain_mid, w_out, normed_ref, sems,
):
    hidden = (w_ref.shape[1] - w_ref.shape[0]) // 4
    peers = message_ref.shape[0]
    own = hidden // peers
    groups = cycle_of(cols)[1]
    size = groups * LANES
    cycles = [slice(start, start + size) for start in range(0, rows * cols, size)]
    copies = start_copies(
        sems,
        (chain_hbm, chain_ref),
        (tile_hbm, tile_ref),
        (gain_hbm, gain_ref),
        (pair_hbm, pair_ref),
        (w_hbm, w_ref),
        (gain_mid_hbm, gain_mid),
        (w_out_hbm, w_out),
    )
    for copy in copies[:3]:
        copy.wait()
    keep = keep_of(tile_ref, chain_ref, rows, cols)
    gain = column(gain_ref[...])
    copies[4].wait()
    w_t = (w_ref[...] * 0.5).T
    copies[3].wait()
    for lanes in cycles:
        block = transpose(pair_ref[lanes, :])
        center = block - jnp.mean(block, axis=0, keepdims=True)
        spread = jnp.mean(center * center, axis=0, keepdims=True)
        normed_ref[:, lanes] = (center * lax.rsqrt(spread + EPS) * gain).astype(jnp.bfloat16)
    for copy in copies[5:]:
        copy.wait()
    gain_mid_ref[...] = jnp.broadcast_to(column(gain_mid[...]), gain_mid_ref.shape)
    w_out_ref[...] = w_out[...].T
    for cycle, lanes in enumerate(cycles):
        projected = jnp.dot(w_t, normed_ref[:, lanes], preferred_element_type=jnp.float32)
        sides = []
        for side in range(2):
            value = projected[2 * side * hidden : (2 * side + 1) * hidden]
            gate = projected[(2 * side + 1) * hidden : (2 * side + 2) * hidden]
            sides.append(((jnp.tanh(gate) + 1.0) * value * keep[:, lanes]).reshape(peers, own, size))
        both = jnp.concatenate(sides, axis=1).astype(jnp.bfloat16)
        for group in range(groups):
            line = (cycle * groups + group) * 2 * own
            message_ref[:, line : line + 2 * own, :] = both[:, :, group * LANES : (group + 1) * LANES]
        gate_ref[:, lanes] = 0.5 * jnp.tanh(projected[4 * hidden :]) + 0.5


def unpack(message_ref, half, halves, spread_ref, own, cols):
    tokens, groups = cycle_of(cols)
    members, lines, _ = message_ref.shape
    peers = members // halves
    lane = lax.broadcasted_iota(jnp.int32, (2 * own, LANES), 1)
    cycles = lines // (2 * groups * own)
    for peer in range(peers):
        for cycle in range(cycles):
            base = cycle * groups
            held = [
                message_ref[
                    peer * halves + half, (base + group) * 2 * own : (base + group + 1) * 2 * own, :
                ].astype(jnp.float32)
                for group in range(groups)
            ]
            for token in range(tokens):
                k = (peer * cycles + cycle) * tokens + token
                for chunk in range(spread_ref.shape[0]):
                    group, off = divmod(token * cols + chunk * LANES, LANES)
                    value = held[group]
                    if off and group + 1 < groups:
                        value = jnp.where(lane >= off, value, held[group + 1])
                    if off:
                        value = pltpu.roll(value, LANES - off, axis=1)
                    spread_ref[chunk, k * 2 * own : (k + 1) * 2 * own, :] = value


def pack(spread_ref, at, own, cols):
    tokens, groups = cycle_of(cols)
    lane = lax.broadcasted_iota(jnp.int32, (own, LANES), 1)
    rolled, lines = {}, []
    for group in range(groups):
        value, here = None, 0
        while here < LANES:
            token, col = divmod(group * LANES + here, cols)
            chunk, there = divmod(col, LANES)
            shift = (here - there) % LANES
            if (token, chunk, shift) not in rolled:
                line = (at * tokens + token) * own
                piece = spread_ref[chunk, line : line + own, :]
                rolled[token, chunk, shift] = pltpu.roll(piece, shift, axis=1) if shift else piece
            piece = rolled[token, chunk, shift]
            value = piece if value is None else jnp.where(lane >= here, piece, value)
            here += min(LANES - here, LANES - there, cols - col)
        lines.append(value)
    return lines


def channel_of(spread_ref, line, stride):
    count = spread_ref.shape[1] // stride
    return jnp.concatenate(
        [spread_ref[chunk, pl.ds(line, count, stride=stride), :] for chunk in range(spread_ref.shape[0])],
        axis=1,
    ).astype(jnp.bfloat16)


def triangle_kernel(own, cols, shares, message_ref, mixed_ref, spread, left_t, mixed):
    halves, chunks = spread.shape[:2]
    width = chunks * LANES
    depth = spread.shape[2] // (2 * own)
    deep = left_t.shape[2]
    one = identity(cols, width)
    padding = [jnp.zeros((deep - depth, width), jnp.bfloat16)] if depth < deep else []
    for half in range(halves):
        unpack(message_ref, half, halves, spread.at[half], own, cols)

    def operand(channel, half):
        return jnp.concatenate([channel_of(spread.at[half], channel, 2 * own)] + padding, axis=0)

    for channel in range(own):
        left = jnp.concatenate([operand(channel, half) for half in range(halves)], axis=0)
        both = lax.dot_general(
            one, left, (((1,), (1,)), ((), ())), preferred_element_type=jnp.float32
        ).astype(jnp.bfloat16)
        for half in range(halves):
            left_t[channel, half * cols : (half + 1) * cols, :] = both[:, half * deep : (half + 1) * deep]
    for channel in range(own):
        right = jnp.concatenate([operand(own + channel, half) for half in range(halves)], axis=1)
        total = jnp.dot(left_t[channel], right, preferred_element_type=jnp.float32)
        for i_half in range(halves):
            for j_half in range(halves):
                for chunk in range(chunks):
                    start = j_half * width + chunk * LANES
                    mixed[i_half, j_half, chunk, pl.ds(channel, cols, stride=own), :] = total[
                        i_half * cols : (i_half + 1) * cols, start : start + LANES
                    ]
    groups = cycle_of(cols)[1]
    each = mixed_ref.shape[0] // shares
    cycles = each // (halves * groups * own)
    for share in range(shares):
        i_half, peer = divmod(share, shares // halves)
        lines = []
        for j_half in range(halves):
            for cycle in range(cycles):
                lines += pack(mixed.at[i_half, j_half], peer * cycles + cycle, own, cols)
        mixed_ref[share * each : (share + 1) * each, :] = jnp.concatenate(lines, axis=0).astype(jnp.bfloat16)


def output_kernel(own, parts, mixed_ref, gate_ref, gain_ref, w_t_ref, update_hbm, mixed, update, sems):
    members, lines, _ = mixed.shape
    members = members // parts
    mixed[...] = mixed_ref[...].astype(jnp.float32).reshape(mixed.shape)
    groups = lines // own
    steps = math.gcd(groups, 3)
    leaving = []
    for group in range(groups):
        sums = mixed[:members, group * own : (group + 1) * own, :]
        for part in range(1, parts):
            sums += mixed[part * members : (part + 1) * members, group * own : (group + 1) * own, :]
        block = sums.reshape(members * own, LANES)
        center = block - jnp.mean(block, axis=0, keepdims=True)
        spread = jnp.mean(center * center, axis=0, keepdims=True)
        normed = (center * lax.rsqrt(spread + EPS) * gain_ref[...]).astype(jnp.bfloat16)
        projected = jnp.dot(w_t_ref[...], normed, preferred_element_type=jnp.float32)
        lanes = slice(group * LANES, (group + 1) * LANES)
        update[lanes, :] = (gate_ref[:, lanes] * projected).T.astype(jnp.bfloat16)
        step, last = divmod((group + 1) * steps, groups)
        if last == 0:
            done = slice((step - 1) * (groups // steps) * LANES, (group + 1) * LANES)
            leaving += start_copies(sems.at[step - 1], (update.at[done, :], update_hbm.at[done, :]))
    for copy in leaving:
        copy.wait()


def in_hbm(value):
    return pltpu.with_memory_space_constraint(value, pltpu.HBM)


def on_device(shares, halves, pair, tile_mask, chain_ids, gain_in, w_proj, gain_mid, w_out):
    rows, cols, width = pair.shape
    hidden = w_out.shape[0]
    peers = shares // PARTS
    own = hidden // (peers * halves)
    positions = rows * cols
    groups = positions // LANES
    lines = groups * own
    cycles = groups // cycle_of(cols)[1]
    params = pltpu.CompilerParams(vmem_limit_bytes=VMEM_BYTES)
    tokens = chain_ids.shape[0]
    message = jax.ShapeDtypeStruct((peers * halves, 2 * lines, LANES), jnp.bfloat16)
    message, gate, w_out_t, gain = pl.pallas_call(
        functools.partial(project_kernel, rows, cols),
        out_shape=(
            message,
            jax.ShapeDtypeStruct((width, positions), jnp.float32),
            jax.ShapeDtypeStruct(w_out.shape[::-1], jnp.bfloat16),
            jax.ShapeDtypeStruct((hidden, LANES), jnp.float32),
        ),
        in_specs=[HBM] * 7,
        out_specs=[VMEM] * 4,
        scratch_shapes=[
            pltpu.SMEM(tile_mask.shape, jnp.int32),
            pltpu.VMEM((1, tokens), jnp.int32),
            pltpu.VMEM((positions, width), jnp.bfloat16),
            pltpu.VMEM((1, width), jnp.float32),
            pltpu.VMEM(w_proj.shape, jnp.bfloat16),
            pltpu.VMEM((1, hidden), jnp.float32),
            pltpu.VMEM(w_out.shape, jnp.bfloat16),
            pltpu.VMEM((width, positions), jnp.bfloat16),
            pltpu.SemaphoreType.DMA((7,)),
        ],
        compiler_params=params,
        name="project",
    )(
        in_hbm(tile_mask),
        in_hbm(chain_ids[None, :]),
        in_hbm(pair.reshape(positions, width)),
        in_hbm(gain_in[None, :]),
        in_hbm(w_proj),
        in_hbm(gain_mid[None, :]),
        in_hbm(w_out),
    )
    message = lax.all_to_all(
        message,
        ("row", "col"),
        split_axis=0,
        concat_axis=0,
        axis_index_groups=[
            list(range(part * peers * halves, (part + 1) * peers * halves))
            for part in range(PARTS)
        ],
        tiled=True,
    )
    chunks = pl.cdiv(cols, LANES)
    depth = peers * rows
    deep = pl.cdiv(depth, LANES) * LANES
    mixed = pl.pallas_call(
        functools.partial(triangle_kernel, own, cols, shares),
        out_shape=jax.ShapeDtypeStruct((halves * shares * lines, LANES), jnp.bfloat16),
        in_specs=[VMEM],
        out_specs=VMEM,
        scratch_shapes=[
            pltpu.VMEM((halves, chunks, depth * 2 * own, LANES), jnp.float32),
            pltpu.VMEM((own, halves * cols, deep), jnp.bfloat16),
            pltpu.VMEM((halves, halves, chunks, cols * own, LANES), jnp.float32),
        ],
        compiler_params=params,
        name="triangle",
    )(message)
    mixed = lax.all_to_all(
        mixed.reshape(halves * shares, lines, LANES),
        ("row", "col"),
        split_axis=0,
        concat_axis=0,
        tiled=True,
    ).reshape(halves * shares * lines, LANES)
    update = pl.pallas_call(
        functools.partial(output_kernel, own, PARTS),
        out_shape=jax.ShapeDtypeStruct((positions, width), jnp.bfloat16),
        in_specs=[VMEM] * 4,
        out_specs=HBM,
        scratch_shapes=[
            pltpu.VMEM((shares * halves, lines, LANES), jnp.float32),
            pltpu.VMEM((positions, width), jnp.bfloat16),
            pltpu.SemaphoreType.DMA((math.gcd(groups, 3), 1)),
        ],
        compiler_params=params,
        name="output",
    )(mixed, gate, gain, w_out_t)
    return update.reshape(rows, cols, width)


def solution(mesh):
    in_specs = (P(("grp", "row"), "col", None), P("grp", None), P("grp"), P(), P(), P(), P())
    out_specs = P(("grp", "row"), "col", None)
    return jax.shard_map(
        functools.partial(on_device, mesh.shape["row"], mesh.shape["col"]),
        mesh=mesh,
        in_specs=in_specs,
        out_specs=out_specs,
        check_vma=False,
    )
```

```python
import functools
import math

import jax
import jax.numpy as jnp
from jax import lax
from jax.experimental import pallas as pl
from jax.experimental.pallas import tpu as pltpu
from jax.sharding import PartitionSpec as P

TILE = 96
LANES = 128
EPS = 1e-05
PARTS = 2
VMEM_BYTES = 32 * 1024 * 1024
VMEM = pl.BlockSpec(memory_space=pltpu.VMEM)
HBM = pl.BlockSpec(memory_space=pltpu.HBM)
SMEM = pl.BlockSpec(memory_space=pltpu.SMEM)


def column(row):
    return jnp.broadcast_to(row, (8, row.shape[1])).T[:, :1]


def steps(at, width, count):
    total = jnp.zeros_like(at)
    for edge in range(1, count):
        total += (at >= edge * width).astype(jnp.int32)
    return total


def identity(rows, cols):
    same = lax.broadcasted_iota(jnp.int32, (rows, cols), 0) == lax.broadcasted_iota(jnp.int32, (rows, cols), 1)
    return same.astype(jnp.bfloat16)


def transpose(block):
    return lax.dot_general(
        identity(block.shape[1], block.shape[1]),
        block,
        (((1,), (1,)), ((), ())),
        preferred_element_type=jnp.float32,
    )


def keep_of(tile_ref, chain_ref, rows, cols):
    tokens = chain_ref.shape[1]
    tiles = tile_ref.shape[1]
    positions = rows * cols
    at = lax.broadcasted_iota(jnp.int32, (1, positions), 1)
    row = steps(at, cols, rows)
    k = lax.axis_index("row") * rows + row
    i = lax.axis_index("col") * cols + at - row * cols
    token = lax.broadcasted_iota(jnp.int32, (tokens, positions), 0)
    pick = (token == k).astype(jnp.float32) - (token == i).astype(jnp.float32)
    chains = jnp.broadcast_to(chain_ref[...].astype(jnp.bfloat16), (8, tokens))
    apart = jnp.dot(chains, pick.astype(jnp.bfloat16), preferred_element_type=jnp.float32)[:1]
    k_tile = steps(k, TILE, tiles)
    i_tile = steps(i, TILE, tiles)
    tile_vals = jnp.zeros((1, positions), jnp.float32)
    for a in range(tiles):
        for b in range(tiles):
            here = (k_tile == a) & (i_tile == b)
            tile_vals = jnp.where(here, tile_ref[a, b].astype(jnp.float32), tile_vals)
    return jnp.where(apart == 0.0, 1.0, tile_vals)


def cycle_of(cols):
    cycle = math.lcm(cols, LANES)
    return cycle // cols, cycle // LANES


def start_copies(sems, *pairs):
    copies = [pltpu.make_async_copy(src, dst, sems.at[at]) for at, (src, dst) in enumerate(pairs)]
    for copy in copies:
        copy.start()
    return copies


def fetch(sems, *pairs):
    for copy in start_copies(sems, *pairs):
        copy.wait()


def project_kernel(
    rows, cols, tile_hbm, chain_hbm, pair_hbm, gain_hbm, w_hbm, gain_mid_hbm, w_out_hbm,
    message_ref, gate_ref, w_out_ref, gain_mid_ref,
    tile_ref, chain_ref, pair_ref, gain_ref, w_ref, gain_mid, w_out, normed_ref, sems,
):
    hidden = (w_ref.shape[1] - w_ref.shape[0]) // 4
    peers = message_ref.shape[0]
    own = hidden // peers
    groups = cycle_of(cols)[1]
    size = groups * LANES
    cycles = [slice(start, start + size) for start in range(0, rows * cols, size)]
    copies = start_copies(
        sems,
        (chain_hbm, chain_ref),
        (tile_hbm, tile_ref),
        (gain_hbm, gain_ref),
        (pair_hbm, pair_ref),
        (w_hbm, w_ref),
        (gain_mid_hbm, gain_mid),
        (w_out_hbm, w_out),
    )
    for copy in copies[:3]:
        copy.wait()
    keep = keep_of(tile_ref, chain_ref, rows, cols)
    gain = column(gain_ref[...])
    copies[4].wait()
    w_t = (w_ref[...] * 0.5).T
    copies[3].wait()
    for lanes in cycles:
        block = transpose(pair_ref[lanes, :])
        center = block - jnp.mean(block, axis=0, keepdims=True)
        spread = jnp.mean(center * center, axis=0, keepdims=True)
        normed_ref[:, lanes] = (center * lax.rsqrt(spread + EPS) * gain).astype(jnp.bfloat16)
    for copy in copies[5:]:
        copy.wait()
    gain_mid_ref[...] = jnp.broadcast_to(column(gain_mid[...]), gain_mid_ref.shape)
    w_out_ref[...] = w_out[...].T
    for cycle, lanes in enumerate(cycles):
        projected = jnp.dot(w_t, normed_ref[:, lanes], preferred_element_type=jnp.float32)
        sides = []
        for side in range(2):
            value = projected[2 * side * hidden : (2 * side + 1) * hidden]
            gate = projected[(2 * side + 1) * hidden : (2 * side + 2) * hidden]
            sides.append(((jnp.tanh(gate) + 1.0) * value * keep[:, lanes]).reshape(peers, own, size))
        both = jnp.concatenate(sides, axis=1).astype(jnp.bfloat16)
        for group in range(groups):
            line = (cycle * groups + group) * 2 * own
            message_ref[:, line : line + 2 * own, :] = both[:, :, group * LANES : (group + 1) * LANES]
        gate_ref[:, lanes] = 0.5 * jnp.tanh(projected[4 * hidden :]) + 0.5


def unpack(message_ref, half, halves, spread_ref, own, cols):
    tokens, groups = cycle_of(cols)
    members, lines, _ = message_ref.shape
    peers = members // halves
    lane = lax.broadcasted_iota(jnp.int32, (2 * own, LANES), 1)
    cycles = lines // (2 * groups * own)
    for peer in range(peers):
        for cycle in range(cycles):
            base = cycle * groups
            held = [
                message_ref[
                    peer * halves + half, (base + group) * 2 * own : (base + group + 1) * 2 * own, :
                ].astype(jnp.float32)
                for group in range(groups)
            ]
            for token in range(tokens):
                k = (peer * cycles + cycle) * tokens + token
                for chunk in range(spread_ref.shape[0]):
                    group, off = divmod(token * cols + chunk * LANES, LANES)
                    value = held[group]
                    if off and group + 1 < groups:
                        value = jnp.where(lane >= off, value, held[group + 1])
                    if off:
                        value = pltpu.roll(value, LANES - off, axis=1)
                    spread_ref[chunk, k * 2 * own : (k + 1) * 2 * own, :] = value


def pack(spread_ref, at, own, cols):
    tokens, groups = cycle_of(cols)
    lane = lax.broadcasted_iota(jnp.int32, (own, LANES), 1)
    rolled, lines = {}, []
    for group in range(groups):
        value, here = None, 0
        while here < LANES:
            token, col = divmod(group * LANES + here, cols)
            chunk, there = divmod(col, LANES)
            shift = (here - there) % LANES
            if (token, chunk, shift) not in rolled:
                line = (at * tokens + token) * own
                piece = spread_ref[chunk, line : line + own, :]
                rolled[token, chunk, shift] = pltpu.roll(piece, shift, axis=1) if shift else piece
            piece = rolled[token, chunk, shift]
            value = piece if value is None else jnp.where(lane >= here, piece, value)
            here += min(LANES - here, LANES - there, cols - col)
        lines.append(value)
    return lines


def channel_of(spread_ref, line, stride):
    count = spread_ref.shape[1] // stride
    return jnp.concatenate(
        [spread_ref[chunk, pl.ds(line, count, stride=stride), :] for chunk in range(spread_ref.shape[0])],
        axis=1,
    ).astype(jnp.bfloat16)


def triangle_kernel(own, cols, shares, message_ref, mixed_ref, spread, left_t, mixed):
    halves, chunks = spread.shape[:2]
    width = chunks * LANES
    depth = spread.shape[2] // (2 * own)
    deep = left_t.shape[2]
    one = identity(cols, width)
    padding = [jnp.zeros((deep - depth, width), jnp.bfloat16)] if depth < deep else []
    for half in range(halves):
        unpack(message_ref, half, halves, spread.at[half], own, cols)

    def operand(channel, half):
        return jnp.concatenate([channel_of(spread.at[half], channel, 2 * own)] + padding, axis=0)

    for channel in range(own):
        left = jnp.concatenate([operand(channel, half) for half in range(halves)], axis=0)
        both = lax.dot_general(
            one, left, (((1,), (1,)), ((), ())), preferred_element_type=jnp.float32
        ).astype(jnp.bfloat16)
        for half in range(halves):
            left_t[channel, half * cols : (half + 1) * cols, :] = both[:, half * deep : (half + 1) * deep]
    for channel in range(own):
        right = jnp.concatenate([operand(own + channel, half) for half in range(halves)], axis=1)
        total = jnp.dot(left_t[channel], right, preferred_element_type=jnp.float32)
        for i_half in range(halves):
            for j_half in range(halves):
                for chunk in range(chunks):
                    start = j_half * width + chunk * LANES
                    mixed[i_half, j_half, chunk, pl.ds(channel, cols, stride=own), :] = total[
                        i_half * cols : (i_half + 1) * cols, start : start + LANES
                    ]
    groups = cycle_of(cols)[1]
    each = mixed_ref.shape[0] // shares
    cycles = each // (halves * groups * own)
    for share in range(shares):
        i_half, peer = divmod(share, shares // halves)
        lines = []
        for j_half in range(halves):
            for cycle in range(cycles):
                lines += pack(mixed.at[i_half, j_half], peer * cycles + cycle, own, cols)
        mixed_ref[share * each : (share + 1) * each, :] = jnp.concatenate(lines, axis=0).astype(jnp.bfloat16)


def output_kernel(own, parts, mixed_ref, gate_ref, gain_ref, w_t_ref, update_hbm, mixed, update, sems):
    members, lines, _ = mixed.shape
    members = members // parts
    mixed[...] = mixed_ref[...].astype(jnp.float32).reshape(mixed.shape)
    groups = lines // own
    steps = math.gcd(groups, 3)
    each = groups // steps
    leaving = []
    for step in range(steps):
        blocks = []
        for group in range(step * each, (step + 1) * each):
            sums = mixed[:members, group * own : (group + 1) * own, :]
            for part in range(1, parts):
                sums += mixed[part * members : (part + 1) * members, group * own : (group + 1) * own, :]
            blocks.append(sums.reshape(members * own, LANES))
        block = jnp.concatenate(blocks, axis=1)
        center = block - jnp.mean(block, axis=0, keepdims=True)
        spread = jnp.mean(center * center, axis=0, keepdims=True)
        gain = jnp.concatenate([gain_ref[...]] * each, axis=1)
        normed = (center * lax.rsqrt(spread + EPS) * gain).astype(jnp.bfloat16)
        projected = jnp.dot(w_t_ref[...], normed, preferred_element_type=jnp.float32)
        lanes = slice(step * each * LANES, (step + 1) * each * LANES)
        update[lanes, :] = (gate_ref[:, lanes] * projected).T.astype(jnp.bfloat16)
        leaving += start_copies(sems.at[step], (update.at[lanes, :], update_hbm.at[lanes, :]))
    for copy in leaving:
        copy.wait()


def in_hbm(value):
    return pltpu.with_memory_space_constraint(value, pltpu.HBM)


def on_device(shares, halves, pair, tile_mask, chain_ids, gain_in, w_proj, gain_mid, w_out):
    rows, cols, width = pair.shape
    hidden = w_out.shape[0]
    peers = shares // PARTS
    own = hidden // (peers * halves)
    positions = rows * cols
    groups = positions // LANES
    lines = groups * own
    cycles = groups // cycle_of(cols)[1]
    params = pltpu.CompilerParams(vmem_limit_bytes=VMEM_BYTES)
    tokens = chain_ids.shape[0]
    message = jax.ShapeDtypeStruct((peers * halves, 2 * lines, LANES), jnp.bfloat16)
    message, gate, w_out_t, gain = pl.pallas_call(
        functools.partial(project_kernel, rows, cols),
        out_shape=(
            message,
            jax.ShapeDtypeStruct((width, positions), jnp.float32),
            jax.ShapeDtypeStruct(w_out.shape[::-1], jnp.bfloat16),
            jax.ShapeDtypeStruct((hidden, LANES), jnp.float32),
        ),
        in_specs=[HBM] * 7,
        out_specs=[VMEM] * 4,
        scratch_shapes=[
            pltpu.SMEM(tile_mask.shape, jnp.int32),
            pltpu.VMEM((1, tokens), jnp.int32),
            pltpu.VMEM((positions, width), jnp.bfloat16),
            pltpu.VMEM((1, width), jnp.float32),
            pltpu.VMEM(w_proj.shape, jnp.bfloat16),
            pltpu.VMEM((1, hidden), jnp.float32),
            pltpu.VMEM(w_out.shape, jnp.bfloat16),
            pltpu.VMEM((width, positions), jnp.bfloat16),
            pltpu.SemaphoreType.DMA((7,)),
        ],
        compiler_params=params,
        name="project",
    )(
        in_hbm(tile_mask),
        in_hbm(chain_ids[None, :]),
        in_hbm(pair.reshape(positions, width)),
        in_hbm(gain_in[None, :]),
        in_hbm(w_proj),
        in_hbm(gain_mid[None, :]),
        in_hbm(w_out),
    )
    message = lax.all_to_all(
        message,
        ("row", "col"),
        split_axis=0,
        concat_axis=0,
        axis_index_groups=[
            list(range(part * peers * halves, (part + 1) * peers * halves))
            for part in range(PARTS)
        ],
        tiled=True,
    )
    chunks = pl.cdiv(cols, LANES)
    depth = peers * rows
    deep = pl.cdiv(depth, LANES) * LANES
    mixed = pl.pallas_call(
        functools.partial(triangle_kernel, own, cols, shares),
        out_shape=jax.ShapeDtypeStruct((halves * shares * lines, LANES), jnp.bfloat16),
        in_specs=[VMEM],
        out_specs=VMEM,
        scratch_shapes=[
            pltpu.VMEM((halves, chunks, depth * 2 * own, LANES), jnp.float32),
            pltpu.VMEM((own, halves * cols, deep), jnp.bfloat16),
            pltpu.VMEM((halves, halves, chunks, cols * own, LANES), jnp.float32),
        ],
        compiler_params=params,
        name="triangle",
    )(message)
    mixed = lax.all_to_all(
        mixed.reshape(halves * shares, lines, LANES),
        ("row", "col"),
        split_axis=0,
        concat_axis=0,
        tiled=True,
    ).reshape(halves * shares * lines, LANES)
    update = pl.pallas_call(
        functools.partial(output_kernel, own, PARTS),
        out_shape=jax.ShapeDtypeStruct((positions, width), jnp.bfloat16),
        in_specs=[VMEM] * 4,
        out_specs=HBM,
        scratch_shapes=[
            pltpu.VMEM((shares * halves, lines, LANES), jnp.float32),
            pltpu.VMEM((positions, width), jnp.bfloat16),
            pltpu.SemaphoreType.DMA((math.gcd(groups, 3), 1)),
        ],
        compiler_params=params,
        name="output",
    )(mixed, gate, gain, w_out_t)
    return update.reshape(rows, cols, width)


def solution(mesh):
    in_specs = (P(("grp", "row"), "col", None), P("grp", None), P("grp"), P(), P(), P(), P())
    out_specs = P(("grp", "row"), "col", None)
    return jax.shard_map(
        functools.partial(on_device, mesh.shape["row"], mesh.shape["col"]),
        mesh=mesh,
        in_specs=in_specs,
        out_specs=out_specs,
        check_vma=False,
    )
```

```python
import functools
import math

import jax
import jax.numpy as jnp
from jax import lax
from jax.experimental import pallas as pl
from jax.experimental.pallas import tpu as pltpu
from jax.sharding import PartitionSpec as P

TILE = 96
LANES = 128
EPS = 1e-05
PARTS = 2
VMEM_BYTES = 32 * 1024 * 1024
VMEM = pl.BlockSpec(memory_space=pltpu.VMEM)
HBM = pl.BlockSpec(memory_space=pltpu.HBM)
SMEM = pl.BlockSpec(memory_space=pltpu.SMEM)


def column(row):
    return jnp.broadcast_to(row, (8, row.shape[1])).T[:, :1]


def steps(at, width, count):
    total = jnp.zeros_like(at)
    for edge in range(1, count):
        total += (at >= edge * width).astype(jnp.int32)
    return total


def identity(rows, cols):
    same = lax.broadcasted_iota(jnp.int32, (rows, cols), 0) == lax.broadcasted_iota(jnp.int32, (rows, cols), 1)
    return same.astype(jnp.bfloat16)


def transpose(block):
    return lax.dot_general(
        identity(block.shape[1], block.shape[1]),
        block,
        (((1,), (1,)), ((), ())),
        preferred_element_type=jnp.float32,
    )


def keep_of(tile_ref, chain_ref, rows, cols):
    tokens = chain_ref.shape[1]
    tiles = tile_ref.shape[1]
    positions = rows * cols
    at = lax.broadcasted_iota(jnp.int32, (1, positions), 1)
    row = steps(at, cols, rows)
    k = lax.axis_index("row") * rows + row
    i = lax.axis_index("col") * cols + at - row * cols
    token = lax.broadcasted_iota(jnp.int32, (tokens, positions), 0)
    pick = (token == k).astype(jnp.float32) - (token == i).astype(jnp.float32)
    chains = jnp.broadcast_to(chain_ref[...].astype(jnp.bfloat16), (8, tokens))
    apart = jnp.dot(chains, pick.astype(jnp.bfloat16), preferred_element_type=jnp.float32)[:1]
    k_tile = steps(k, TILE, tiles)
    i_tile = steps(i, TILE, tiles)
    tile_vals = jnp.zeros((1, positions), jnp.float32)
    for a in range(tiles):
        for b in range(tiles):
            here = (k_tile == a) & (i_tile == b)
            tile_vals = jnp.where(here, tile_ref[a, b].astype(jnp.float32), tile_vals)
    return jnp.where(apart == 0.0, 1.0, tile_vals)


def cycle_of(cols):
    cycle = math.lcm(cols, LANES)
    return cycle // cols, cycle // LANES


def start_copies(sems, *pairs):
    copies = [pltpu.make_async_copy(src, dst, sems.at[at]) for at, (src, dst) in enumerate(pairs)]
    for copy in copies:
        copy.start()
    return copies


def fetch(sems, *pairs):
    for copy in start_copies(sems, *pairs):
        copy.wait()


def in_first_part():
    return lax.axis_index("row") < lax.axis_size("row") // PARTS


def tail(normed_ref, w_gate_ref, gain_hbm, w_out_hbm, gate_ref, w_out_ref, gain_ref, gain, w_out, sems):
    copies = start_copies(sems, (gain_hbm, gain), (w_out_hbm, w_out))
    gate = jnp.dot(w_gate_ref[...], normed_ref[...], preferred_element_type=jnp.float32)
    gate_ref[...] = 0.5 * jnp.tanh(gate) + 0.5
    for copy in copies:
        copy.wait()
    w_out_ref[...] = w_out[...].T
    gain_ref[...] = jnp.broadcast_to(column(gain[...]), gain_ref.shape)


def project_kernel(
    rows, cols, tile_hbm, chain_hbm, pair_hbm, gain_hbm, w_hbm, gain_mid_hbm, w_out_hbm,
    message_ref, normed_ref, w_gate_ref, gate_ref, w_out_ref, gain_mid_ref,
    tile_ref, chain_ref, pair_ref, gain_ref, w_ref, gain_mid, w_out, sems,
):
    hidden = (w_ref.shape[1] - w_ref.shape[0]) // 4
    peers = message_ref.shape[0]
    own = hidden // peers
    groups = cycle_of(cols)[1]
    size = groups * LANES
    cycles = [slice(start, start + size) for start in range(0, rows * cols, size)]
    copies = start_copies(
        sems,
        (chain_hbm, chain_ref),
        (tile_hbm, tile_ref),
        (gain_hbm, gain_ref),
        (pair_hbm, pair_ref),
        (w_hbm, w_ref),
    )
    for copy in copies[:3]:
        copy.wait()
    keep = keep_of(tile_ref, chain_ref, rows, cols)
    gain = column(gain_ref[...])
    copies[4].wait()
    w_t = (w_ref[...] * 0.5).T
    w_gate_ref[...] = w_t[4 * hidden :]
    w_t = w_t[: 4 * hidden]
    copies[3].wait()
    for lanes in cycles:
        block = transpose(pair_ref[lanes, :])
        center = block - jnp.mean(block, axis=0, keepdims=True)
        spread = jnp.mean(center * center, axis=0, keepdims=True)
        normed_ref[:, lanes] = (center * lax.rsqrt(spread + EPS) * gain).astype(jnp.bfloat16)
    for cycle, lanes in enumerate(cycles):
        projected = jnp.dot(w_t, normed_ref[:, lanes], preferred_element_type=jnp.float32)
        sides = []
        for side in range(2):
            value = projected[2 * side * hidden : (2 * side + 1) * hidden]
            gate = projected[(2 * side + 1) * hidden : (2 * side + 2) * hidden]
            sides.append(((jnp.tanh(gate) + 1.0) * value * keep[:, lanes]).reshape(peers, own, size))
        both = jnp.concatenate(sides, axis=1).astype(jnp.bfloat16)
        for group in range(groups):
            line = (cycle * groups + group) * 2 * own
            message_ref[:, line : line + 2 * own, :] = both[:, :, group * LANES : (group + 1) * LANES]

    @pl.when(in_first_part())
    def _():
        tail(normed_ref, w_gate_ref, gain_mid_hbm, w_out_hbm, gate_ref, w_out_ref, gain_mid_ref, gain_mid, w_out, sems)


def unpack(message_ref, half, halves, spread_ref, own, cols):
    tokens, groups = cycle_of(cols)
    members, lines, _ = message_ref.shape
    peers = members // halves
    lane = lax.broadcasted_iota(jnp.int32, (2 * own, LANES), 1)
    cycles = lines // (2 * groups * own)
    for peer in range(peers):
        for cycle in range(cycles):
            base = cycle * groups
            held = [
                message_ref[
                    peer * halves + half, (base + group) * 2 * own : (base + group + 1) * 2 * own, :
                ].astype(jnp.float32)
                for group in range(groups)
            ]
            for token in range(tokens):
                k = (peer * cycles + cycle) * tokens + token
                for chunk in range(spread_ref.shape[0]):
                    group, off = divmod(token * cols + chunk * LANES, LANES)
                    value = held[group]
                    if off and group + 1 < groups:
                        value = jnp.where(lane >= off, value, held[group + 1])
                    if off:
                        value = pltpu.roll(value, LANES - off, axis=1)
                    spread_ref[chunk, k * 2 * own : (k + 1) * 2 * own, :] = value


def pack(spread_ref, at, own, cols):
    tokens, groups = cycle_of(cols)
    lane = lax.broadcasted_iota(jnp.int32, (own, LANES), 1)
    rolled, lines = {}, []
    for group in range(groups):
        value, here = None, 0
        while here < LANES:
            token, col = divmod(group * LANES + here, cols)
            chunk, there = divmod(col, LANES)
            shift = (here - there) % LANES
            if (token, chunk, shift) not in rolled:
                line = (at * tokens + token) * own
                piece = spread_ref[chunk, line : line + own, :]
                rolled[token, chunk, shift] = pltpu.roll(piece, shift, axis=1) if shift else piece
            piece = rolled[token, chunk, shift]
            value = piece if value is None else jnp.where(lane >= here, piece, value)
            here += min(LANES - here, LANES - there, cols - col)
        lines.append(value)
    return lines


def channel_of(spread_ref, line, stride):
    count = spread_ref.shape[1] // stride
    return jnp.concatenate(
        [spread_ref[chunk, pl.ds(line, count, stride=stride), :] for chunk in range(spread_ref.shape[0])],
        axis=1,
    ).astype(jnp.bfloat16)


def triangle_kernel(own, cols, shares, message_ref, mixed_ref, spread, left_t, mixed):
    halves, chunks = spread.shape[:2]
    width = chunks * LANES
    depth = spread.shape[2] // (2 * own)
    deep = left_t.shape[2]
    one = identity(cols, width)
    padding = [jnp.zeros((deep - depth, width), jnp.bfloat16)] if depth < deep else []
    for half in range(halves):
        unpack(message_ref, half, halves, spread.at[half], own, cols)

    def operand(channel, half):
        return jnp.concatenate([channel_of(spread.at[half], channel, 2 * own)] + padding, axis=0)

    for channel in range(own):
        left = jnp.concatenate([operand(channel, half) for half in range(halves)], axis=0)
        both = lax.dot_general(
            one, left, (((1,), (1,)), ((), ())), preferred_element_type=jnp.float32
        ).astype(jnp.bfloat16)
        for half in range(halves):
            left_t[channel, half * cols : (half + 1) * cols, :] = both[:, half * deep : (half + 1) * deep]
    for channel in range(own):
        right = jnp.concatenate([operand(own + channel, half) for half in range(halves)], axis=1)
        total = jnp.dot(left_t[channel], right, preferred_element_type=jnp.float32)
        for i_half in range(halves):
            for j_half in range(halves):
                for chunk in range(chunks):
                    start = j_half * width + chunk * LANES
                    mixed[i_half, j_half, chunk, pl.ds(channel, cols, stride=own), :] = total[
                        i_half * cols : (i_half + 1) * cols, start : start + LANES
                    ]
    groups = cycle_of(cols)[1]
    each = mixed_ref.shape[0] // shares
    cycles = each // (halves * groups * own)
    for share in range(shares):
        i_half, peer = divmod(share, shares // halves)
        lines = []
        for j_half in range(halves):
            for cycle in range(cycles):
                lines += pack(mixed.at[i_half, j_half], peer * cycles + cycle, own, cols)
        mixed_ref[share * each : (share + 1) * each, :] = jnp.concatenate(lines, axis=0).astype(jnp.bfloat16)


def output_kernel(
    own, parts, mixed_ref, gate_ref, gain_ref, w_t_ref, normed_ref, w_gate_ref, gain_hbm, w_out_hbm, update_hbm,
    mixed, update, sems, gate, w_t, gain_t, gain, w_out, tail_sems,
):
    first = in_first_part()

    @pl.when(first)
    def _():
        finish(own, parts, mixed_ref, gate_ref, gain_ref, w_t_ref, update_hbm, mixed, update, sems)

    @pl.when(jnp.logical_not(first))
    def _():
        tail(normed_ref, w_gate_ref, gain_hbm, w_out_hbm, gate, w_t, gain_t, gain, w_out, tail_sems)
        finish(own, parts, mixed_ref, gate, gain_t, w_t, update_hbm, mixed, update, sems)


def finish(own, parts, mixed_ref, gate_ref, gain_ref, w_t_ref, update_hbm, mixed, update, sems):
    members, lines, _ = mixed.shape
    members = members // parts
    mixed[...] = mixed_ref[...].astype(jnp.float32).reshape(mixed.shape)
    groups = lines // own
    steps = math.gcd(groups, 3)
    leaving = []
    for group in range(groups):
        sums = mixed[:members, group * own : (group + 1) * own, :]
        for part in range(1, parts):
            sums += mixed[part * members : (part + 1) * members, group * own : (group + 1) * own, :]
        block = sums.reshape(members * own, LANES)
        center = block - jnp.mean(block, axis=0, keepdims=True)
        spread = jnp.mean(center * center, axis=0, keepdims=True)
        normed = (center * lax.rsqrt(spread + EPS) * gain_ref[...]).astype(jnp.bfloat16)
        projected = jnp.dot(w_t_ref[...], normed, preferred_element_type=jnp.float32)
        lanes = slice(group * LANES, (group + 1) * LANES)
        update[lanes, :] = (gate_ref[:, lanes] * projected).T.astype(jnp.bfloat16)
        step, last = divmod((group + 1) * steps, groups)
        if last == 0:
            done = slice((step - 1) * (groups // steps) * LANES, (group + 1) * LANES)
            leaving += start_copies(sems.at[step - 1], (update.at[done, :], update_hbm.at[done, :]))
    for copy in leaving:
        copy.wait()


def in_hbm(value):
    return pltpu.with_memory_space_constraint(value, pltpu.HBM)


def on_device(shares, halves, pair, tile_mask, chain_ids, gain_in, w_proj, gain_mid, w_out):
    rows, cols, width = pair.shape
    hidden = w_out.shape[0]
    peers = shares // PARTS
    own = hidden // (peers * halves)
    positions = rows * cols
    groups = positions // LANES
    lines = groups * own
    cycles = groups // cycle_of(cols)[1]
    params = pltpu.CompilerParams(vmem_limit_bytes=VMEM_BYTES)
    tokens = chain_ids.shape[0]
    message = jax.ShapeDtypeStruct((peers * halves, 2 * lines, LANES), jnp.bfloat16)
    message, normed, w_gate, gate, w_out_t, gain = pl.pallas_call(
        functools.partial(project_kernel, rows, cols),
        out_shape=(
            message,
            jax.ShapeDtypeStruct((width, positions), jnp.bfloat16),
            jax.ShapeDtypeStruct((width, width), jnp.bfloat16),
            jax.ShapeDtypeStruct((width, positions), jnp.float32),
            jax.ShapeDtypeStruct(w_out.shape[::-1], jnp.bfloat16),
            jax.ShapeDtypeStruct((hidden, LANES), jnp.float32),
        ),
        in_specs=[HBM] * 7,
        out_specs=[VMEM] * 6,
        scratch_shapes=[
            pltpu.SMEM(tile_mask.shape, jnp.int32),
            pltpu.VMEM((1, tokens), jnp.int32),
            pltpu.VMEM((positions, width), jnp.bfloat16),
            pltpu.VMEM((1, width), jnp.float32),
            pltpu.VMEM(w_proj.shape, jnp.bfloat16),
            pltpu.VMEM((1, hidden), jnp.float32),
            pltpu.VMEM(w_out.shape, jnp.bfloat16),
            pltpu.SemaphoreType.DMA((5,)),
        ],
        compiler_params=params,
        name="project",
    )(
        in_hbm(tile_mask),
        in_hbm(chain_ids[None, :]),
        in_hbm(pair.reshape(positions, width)),
        in_hbm(gain_in[None, :]),
        in_hbm(w_proj),
        in_hbm(gain_mid[None, :]),
        in_hbm(w_out),
    )
    message = lax.all_to_all(
        message,
        ("row", "col"),
        split_axis=0,
        concat_axis=0,
        axis_index_groups=[
            list(range(part * peers * halves, (part + 1) * peers * halves))
            for part in range(PARTS)
        ],
        tiled=True,
    )
    chunks = pl.cdiv(cols, LANES)
    depth = peers * rows
    deep = pl.cdiv(depth, LANES) * LANES
    mixed = pl.pallas_call(
        functools.partial(triangle_kernel, own, cols, shares),
        out_shape=jax.ShapeDtypeStruct((halves * shares * lines, LANES), jnp.bfloat16),
        in_specs=[VMEM],
        out_specs=VMEM,
        scratch_shapes=[
            pltpu.VMEM((halves, chunks, depth * 2 * own, LANES), jnp.float32),
            pltpu.VMEM((own, halves * cols, deep), jnp.bfloat16),
            pltpu.VMEM((halves, halves, chunks, cols * own, LANES), jnp.float32),
        ],
        compiler_params=params,
        name="triangle",
    )(message)
    mixed = lax.all_to_all(
        mixed.reshape(halves * shares, lines, LANES),
        ("row", "col"),
        split_axis=0,
        concat_axis=0,
        tiled=True,
    ).reshape(halves * shares * lines, LANES)
    update = pl.pallas_call(
        functools.partial(output_kernel, own, PARTS),
        out_shape=jax.ShapeDtypeStruct((positions, width), jnp.bfloat16),
        in_specs=[VMEM] * 6 + [HBM] * 2,
        out_specs=HBM,
        scratch_shapes=[
            pltpu.VMEM((halves * shares, lines, LANES), jnp.float32),
            pltpu.VMEM((positions, width), jnp.bfloat16),
            pltpu.SemaphoreType.DMA((math.gcd(groups, 3), 1)),
            pltpu.VMEM((width, positions), jnp.float32),
            pltpu.VMEM(w_out.shape[::-1], jnp.bfloat16),
            pltpu.VMEM((hidden, LANES), jnp.float32),
            pltpu.VMEM((1, hidden), jnp.float32),
            pltpu.VMEM(w_out.shape, jnp.bfloat16),
            pltpu.SemaphoreType.DMA((2,)),
        ],
        compiler_params=params,
        name="output",
    )(mixed, gate, gain, w_out_t, normed, w_gate, in_hbm(gain_mid[None, :]), in_hbm(w_out))
    return update.reshape(rows, cols, width)


def solution(mesh):
    in_specs = (P(("grp", "row"), "col", None), P("grp", None), P("grp"), P(), P(), P(), P())
    out_specs = P(("grp", "row"), "col", None)
    return jax.shard_map(
        functools.partial(on_device, mesh.shape["row"], mesh.shape["col"]),
        mesh=mesh,
        in_specs=in_specs,
        out_specs=out_specs,
        check_vma=False,
    )
```

```python
import functools
import math

import jax
import jax.numpy as jnp
from jax import lax
from jax.experimental import pallas as pl
from jax.experimental.pallas import tpu as pltpu
from jax.sharding import PartitionSpec as P

TILE = 96
LANES = 128
EPS = 1e-05
PARTS = 2
VMEM_BYTES = 32 * 1024 * 1024
VMEM = pl.BlockSpec(memory_space=pltpu.VMEM)
HBM = pl.BlockSpec(memory_space=pltpu.HBM)
SMEM = pl.BlockSpec(memory_space=pltpu.SMEM)


def column(row):
    return jnp.broadcast_to(row, (8, row.shape[1])).T[:, :1]


def steps(at, width, count):
    total = jnp.zeros_like(at)
    for edge in range(1, count):
        total += (at >= edge * width).astype(jnp.int32)
    return total


def identity(rows, cols):
    same = lax.broadcasted_iota(jnp.int32, (rows, cols), 0) == lax.broadcasted_iota(jnp.int32, (rows, cols), 1)
    return same.astype(jnp.bfloat16)


def transpose(block, by=None):
    return lax.dot_general(
        identity(block.shape[1], block.shape[1]) if by is None else by,
        block,
        (((1,), (1,)), ((), ())),
        preferred_element_type=jnp.float32,
    )


def keep_of(tile_ref, chain_ref, rows, cols):
    tokens = chain_ref.shape[1]
    tiles = tile_ref.shape[1]
    positions = rows * cols
    at = lax.broadcasted_iota(jnp.int32, (1, positions), 1)
    row = steps(at, cols, rows)
    k = lax.axis_index("row") * rows + row
    i = lax.axis_index("col") * cols + at - row * cols
    token = lax.broadcasted_iota(jnp.int32, (tokens, positions), 0)
    pick = (token == k).astype(jnp.float32) - (token == i).astype(jnp.float32)
    chains = jnp.broadcast_to(chain_ref[...].astype(jnp.bfloat16), (8, tokens))
    apart = jnp.dot(chains, pick.astype(jnp.bfloat16), preferred_element_type=jnp.float32)[:1]
    k_tile = steps(k, TILE, tiles)
    i_tile = steps(i, TILE, tiles)
    tile_vals = jnp.zeros((1, positions), jnp.float32)
    for a in range(tiles):
        for b in range(tiles):
            here = (k_tile == a) & (i_tile == b)
            tile_vals = jnp.where(here, tile_ref[a, b].astype(jnp.float32), tile_vals)
    return jnp.where(apart == 0.0, 1.0, tile_vals)


def cycle_of(cols):
    cycle = math.lcm(cols, LANES)
    return cycle // cols, cycle // LANES


def start_copies(sems, *pairs):
    copies = [pltpu.make_async_copy(src, dst, sems.at[at]) for at, (src, dst) in enumerate(pairs)]
    for copy in copies:
        copy.start()
    return copies


def fetch(sems, *pairs):
    for copy in start_copies(sems, *pairs):
        copy.wait()


def in_first_part():
    return lax.axis_index("row") < lax.axis_size("row") // PARTS


def tail(normed_ref, w_gate_ref, gate_ref, w_out_ref, gain_ref, gain, w_out, copies):
    gate = jnp.dot(w_gate_ref[...], normed_ref[...], preferred_element_type=jnp.float32)
    gate_ref[...] = 0.5 * jnp.tanh(gate) + 0.5
    for copy in copies:
        copy.wait()
    w_out_ref[...] = w_out[...].T
    gain_ref[...] = jnp.broadcast_to(column(gain[...]), gain_ref.shape)


def project_kernel(
    rows, cols, tile_hbm, chain_hbm, pair_hbm, gain_hbm, w_hbm, gain_mid_hbm, w_out_hbm,
    message_ref, normed_ref, w_gate_ref, gate_ref, w_out_ref, gain_mid_ref,
    tile_ref, chain_ref, pair_ref, gain_ref, w_ref, gain_mid, w_out, sems,
):
    hidden = (w_ref.shape[1] - w_ref.shape[0]) // 4
    peers = message_ref.shape[0]
    own = hidden // peers
    groups = cycle_of(cols)[1]
    size = groups * LANES
    cycles = [slice(start, start + size) for start in range(0, rows * cols, size)]
    copies = start_copies(
        sems,
        (chain_hbm, chain_ref),
        (tile_hbm, tile_ref),
        (gain_hbm, gain_ref),
        (pair_hbm, pair_ref),
        (w_hbm, w_ref),
    )

    def late_copies():
        return [
            pltpu.make_async_copy(gain_mid_hbm, gain_mid, sems.at[5]),
            pltpu.make_async_copy(w_out_hbm, w_out, sems.at[6]),
        ]

    @pl.when(in_first_part())
    def _():
        for copy in late_copies():
            copy.start()

    for copy in copies[:3]:
        copy.wait()
    keep = keep_of(tile_ref, chain_ref, rows, cols)
    gain = column(gain_ref[...])
    width = pair_ref.shape[1]
    centering = (identity(width, width).astype(jnp.float32) - 1.0 / width).astype(jnp.bfloat16)
    copies[4].wait()
    w_t = (w_ref[...] * 0.5).T
    w_gate_ref[...] = w_t[4 * hidden :]
    w_t = w_t[: 4 * hidden]
    copies[3].wait()
    for lanes in cycles:
        center = transpose(pair_ref[lanes, :], centering)
        spread = jnp.mean(center * center, axis=0, keepdims=True)
        normed_ref[:, lanes] = (center * lax.rsqrt(spread + EPS) * gain).astype(jnp.bfloat16)
    for cycle, lanes in enumerate(cycles):
        projected = jnp.dot(w_t, normed_ref[:, lanes], preferred_element_type=jnp.float32)
        sides = []
        for side in range(2):
            value = projected[2 * side * hidden : (2 * side + 1) * hidden]
            gate = projected[(2 * side + 1) * hidden : (2 * side + 2) * hidden]
            sides.append(((jnp.tanh(gate) + 1.0) * value * keep[:, lanes]).reshape(peers, own, size))
        both = jnp.concatenate(sides, axis=1).astype(jnp.bfloat16)
        for group in range(groups):
            line = (cycle * groups + group) * 2 * own
            message_ref[:, line : line + 2 * own, :] = both[:, :, group * LANES : (group + 1) * LANES]

    @pl.when(in_first_part())
    def _():
        tail(normed_ref, w_gate_ref, gate_ref, w_out_ref, gain_mid_ref, gain_mid, w_out, late_copies())


def unpack(message_ref, half, halves, spread_ref, own, cols):
    tokens, groups = cycle_of(cols)
    members, lines, _ = message_ref.shape
    peers = members // halves
    lane = lax.broadcasted_iota(jnp.int32, (2 * own, LANES), 1)
    cycles = lines // (2 * groups * own)
    for peer in range(peers):
        for cycle in range(cycles):
            base = cycle * groups
            held = [
                message_ref[
                    peer * halves + half, (base + group) * 2 * own : (base + group + 1) * 2 * own, :
                ].astype(jnp.float32)
                for group in range(groups)
            ]
            for token in range(tokens):
                k = (peer * cycles + cycle) * tokens + token
                for chunk in range(spread_ref.shape[0]):
                    group, off = divmod(token * cols + chunk * LANES, LANES)
                    value = held[group]
                    if off and group + 1 < groups:
                        value = jnp.where(lane >= off, value, held[group + 1])
                    if off:
                        value = pltpu.roll(value, LANES - off, axis=1)
                    spread_ref[chunk, k * 2 * own : (k + 1) * 2 * own, :] = value


def pack(spread_ref, at, own, cols):
    tokens, groups = cycle_of(cols)
    lane = lax.broadcasted_iota(jnp.int32, (own, LANES), 1)
    rolled, lines = {}, []
    for group in range(groups):
        value, here = None, 0
        while here < LANES:
            token, col = divmod(group * LANES + here, cols)
            chunk, there = divmod(col, LANES)
            shift = (here - there) % LANES
            if (token, chunk, shift) not in rolled:
                line = (at * tokens + token) * own
                piece = spread_ref[chunk, line : line + own, :]
                rolled[token, chunk, shift] = pltpu.roll(piece, shift, axis=1) if shift else piece
            piece = rolled[token, chunk, shift]
            value = piece if value is None else jnp.where(lane >= here, piece, value)
            here += min(LANES - here, LANES - there, cols - col)
        lines.append(value)
    return lines


def channel_of(spread_ref, line, stride):
    count = spread_ref.shape[1] // stride
    return jnp.concatenate(
        [spread_ref[chunk, pl.ds(line, count, stride=stride), :] for chunk in range(spread_ref.shape[0])],
        axis=1,
    ).astype(jnp.bfloat16)


def triangle_kernel(own, cols, shares, message_ref, mixed_ref, spread, left_t, mixed):
    halves, chunks = spread.shape[:2]
    width = chunks * LANES
    depth = spread.shape[2] // (2 * own)
    deep = left_t.shape[2]
    one = identity(cols, width)
    padding = [jnp.zeros((deep - depth, width), jnp.bfloat16)] if depth < deep else []
    for half in range(halves):
        unpack(message_ref, half, halves, spread.at[half], own, cols)

    def operand(channel, half):
        return jnp.concatenate([channel_of(spread.at[half], channel, 2 * own)] + padding, axis=0)

    for channel in range(own):
        left = jnp.concatenate([operand(channel, half) for half in range(halves)], axis=0)
        both = lax.dot_general(
            one, left, (((1,), (1,)), ((), ())), preferred_element_type=jnp.float32
        ).astype(jnp.bfloat16)
        for half in range(halves):
            left_t[channel, half * cols : (half + 1) * cols, :] = both[:, half * deep : (half + 1) * deep]
    for channel in range(own):
        right = jnp.concatenate([operand(own + channel, half) for half in range(halves)], axis=1)
        total = jnp.dot(left_t[channel], right, preferred_element_type=jnp.float32)
        for i_half in range(halves):
            for j_half in range(halves):
                for chunk in range(chunks):
                    start = j_half * width + chunk * LANES
                    mixed[i_half, j_half, chunk, pl.ds(channel, cols, stride=own), :] = total[
                        i_half * cols : (i_half + 1) * cols, start : start + LANES
                    ]
    groups = cycle_of(cols)[1]
    each = mixed_ref.shape[0] // shares
    cycles = each // (halves * groups * own)
    for share in range(shares):
        i_half, peer = divmod(share, shares // halves)
        lines = []
        for j_half in range(halves):
            for cycle in range(cycles):
                lines += pack(mixed.at[i_half, j_half], peer * cycles + cycle, own, cols)
        mixed_ref[share * each : (share + 1) * each, :] = jnp.concatenate(lines, axis=0).astype(jnp.bfloat16)


def output_kernel(
    own, parts, mixed_ref, gate_ref, gain_ref, w_t_ref, normed_ref, w_gate_ref, gain_hbm, w_out_hbm, update_hbm,
    mixed, update, sems, gate, w_t, gain_t, gain, w_out, tail_sems,
):
    first = in_first_part()

    @pl.when(first)
    def _():
        finish(own, parts, mixed_ref, gate_ref, gain_ref, w_t_ref, update_hbm, mixed, update, sems)

    @pl.when(jnp.logical_not(first))
    def _():
        copies = start_copies(tail_sems, (gain_hbm, gain), (w_out_hbm, w_out))
        tail(normed_ref, w_gate_ref, gate, w_t, gain_t, gain, w_out, copies)
        finish(own, parts, mixed_ref, gate, gain_t, w_t, update_hbm, mixed, update, sems)


def finish(own, parts, mixed_ref, gate_ref, gain_ref, w_t_ref, update_hbm, mixed, update, sems):
    members, lines, _ = mixed.shape
    members = members // parts
    mixed[...] = mixed_ref[...].astype(jnp.float32).reshape(mixed.shape)
    groups = lines // own
    steps = math.gcd(groups, 3)
    leaving = []
    for group in range(groups):
        sums = mixed[:members, group * own : (group + 1) * own, :]
        for part in range(1, parts):
            sums += mixed[part * members : (part + 1) * members, group * own : (group + 1) * own, :]
        block = sums.reshape(members * own, LANES)
        center = block - jnp.mean(block, axis=0, keepdims=True)
        spread = jnp.mean(center * center, axis=0, keepdims=True)
        normed = (center * lax.rsqrt(spread + EPS) * gain_ref[...]).astype(jnp.bfloat16)
        projected = jnp.dot(w_t_ref[...], normed, preferred_element_type=jnp.float32)
        lanes = slice(group * LANES, (group + 1) * LANES)
        update[lanes, :] = (gate_ref[:, lanes] * projected).T.astype(jnp.bfloat16)
        step, last = divmod((group + 1) * steps, groups)
        if last == 0:
            done = slice((step - 1) * (groups // steps) * LANES, (group + 1) * LANES)
            leaving += start_copies(sems.at[step - 1], (update.at[done, :], update_hbm.at[done, :]))
    for copy in leaving:
        copy.wait()


def in_hbm(value):
    return pltpu.with_memory_space_constraint(value, pltpu.HBM)


def on_device(shares, halves, pair, tile_mask, chain_ids, gain_in, w_proj, gain_mid, w_out):
    rows, cols, width = pair.shape
    hidden = w_out.shape[0]
    peers = shares // PARTS
    own = hidden // (peers * halves)
    positions = rows * cols
    groups = positions // LANES
    lines = groups * own
    cycles = groups // cycle_of(cols)[1]
    params = pltpu.CompilerParams(vmem_limit_bytes=VMEM_BYTES)
    tokens = chain_ids.shape[0]
    message = jax.ShapeDtypeStruct((peers * halves, 2 * lines, LANES), jnp.bfloat16)
    message, normed, w_gate, gate, w_out_t, gain = pl.pallas_call(
        functools.partial(project_kernel, rows, cols),
        out_shape=(
            message,
            jax.ShapeDtypeStruct((width, positions), jnp.bfloat16),
            jax.ShapeDtypeStruct((width, width), jnp.bfloat16),
            jax.ShapeDtypeStruct((width, positions), jnp.float32),
            jax.ShapeDtypeStruct(w_out.shape[::-1], jnp.bfloat16),
            jax.ShapeDtypeStruct((hidden, LANES), jnp.float32),
        ),
        in_specs=[HBM] * 7,
        out_specs=[VMEM] * 6,
        scratch_shapes=[
            pltpu.SMEM(tile_mask.shape, jnp.int32),
            pltpu.VMEM((1, tokens), jnp.int32),
            pltpu.VMEM((positions, width), jnp.bfloat16),
            pltpu.VMEM((1, width), jnp.float32),
            pltpu.VMEM(w_proj.shape, jnp.bfloat16),
            pltpu.VMEM((1, hidden), jnp.float32),
            pltpu.VMEM(w_out.shape, jnp.bfloat16),
            pltpu.SemaphoreType.DMA((7,)),
        ],
        compiler_params=params,
        name="project",
    )(
        in_hbm(tile_mask),
        in_hbm(chain_ids[None, :]),
        in_hbm(pair.reshape(positions, width)),
        in_hbm(gain_in[None, :]),
        in_hbm(w_proj),
        in_hbm(gain_mid[None, :]),
        in_hbm(w_out),
    )
    message = lax.all_to_all(
        message,
        ("row", "col"),
        split_axis=0,
        concat_axis=0,
        axis_index_groups=[
            list(range(part * peers * halves, (part + 1) * peers * halves))
            for part in range(PARTS)
        ],
        tiled=True,
    )
    chunks = pl.cdiv(cols, LANES)
    depth = peers * rows
    deep = pl.cdiv(depth, LANES) * LANES
    mixed = pl.pallas_call(
        functools.partial(triangle_kernel, own, cols, shares),
        out_shape=jax.ShapeDtypeStruct((halves * shares * lines, LANES), jnp.bfloat16),
        in_specs=[VMEM],
        out_specs=VMEM,
        scratch_shapes=[
            pltpu.VMEM((halves, chunks, depth * 2 * own, LANES), jnp.float32),
            pltpu.VMEM((own, halves * cols, deep), jnp.bfloat16),
            pltpu.VMEM((halves, halves, chunks, cols * own, LANES), jnp.float32),
        ],
        compiler_params=params,
        name="triangle",
    )(message)
    mixed = lax.all_to_all(
        mixed.reshape(halves * shares, lines, LANES),
        ("row", "col"),
        split_axis=0,
        concat_axis=0,
        tiled=True,
    ).reshape(halves * shares * lines, LANES)
    update = pl.pallas_call(
        functools.partial(output_kernel, own, PARTS),
        out_shape=jax.ShapeDtypeStruct((positions, width), jnp.bfloat16),
        in_specs=[VMEM] * 6 + [HBM] * 2,
        out_specs=HBM,
        scratch_shapes=[
            pltpu.VMEM((halves * shares, lines, LANES), jnp.float32),
            pltpu.VMEM((positions, width), jnp.bfloat16),
            pltpu.SemaphoreType.DMA((math.gcd(groups, 3), 1)),
            pltpu.VMEM((width, positions), jnp.float32),
            pltpu.VMEM(w_out.shape[::-1], jnp.bfloat16),
            pltpu.VMEM((hidden, LANES), jnp.float32),
            pltpu.VMEM((1, hidden), jnp.float32),
            pltpu.VMEM(w_out.shape, jnp.bfloat16),
            pltpu.SemaphoreType.DMA((2,)),
        ],
        compiler_params=params,
        name="output",
    )(mixed, gate, gain, w_out_t, normed, w_gate, in_hbm(gain_mid[None, :]), in_hbm(w_out))
    return update.reshape(rows, cols, width)


def solution(mesh):
    in_specs = (P(("grp", "row"), "col", None), P("grp", None), P("grp"), P(), P(), P(), P())
    out_specs = P(("grp", "row"), "col", None)
    return jax.shard_map(
        functools.partial(on_device, mesh.shape["row"], mesh.shape["col"]),
        mesh=mesh,
        in_specs=in_specs,
        out_specs=out_specs,
        check_vma=False,
    )
```

```python
import functools
import math

import jax
import jax.numpy as jnp
from jax import lax
from jax.experimental import pallas as pl
from jax.experimental.pallas import tpu as pltpu
from jax.sharding import PartitionSpec as P

TILE = 96
LANES = 128
EPS = 1e-05
PARTS = 2
VMEM_BYTES = 32 * 1024 * 1024
VMEM = pl.BlockSpec(memory_space=pltpu.VMEM)
HBM = pl.BlockSpec(memory_space=pltpu.HBM)
SMEM = pl.BlockSpec(memory_space=pltpu.SMEM)


def column(row):
    return jnp.broadcast_to(row, (8, row.shape[1])).T[:, :1]


def steps(at, width, count):
    total = jnp.zeros_like(at)
    for edge in range(1, count):
        total += (at >= edge * width).astype(jnp.int32)
    return total


def identity(rows, cols):
    same = lax.broadcasted_iota(jnp.int32, (rows, cols), 0) == lax.broadcasted_iota(jnp.int32, (rows, cols), 1)
    return same.astype(jnp.bfloat16)


def transpose(block, by=None):
    return lax.dot_general(
        identity(block.shape[1], block.shape[1]) if by is None else by,
        block,
        (((1,), (1,)), ((), ())),
        preferred_element_type=jnp.float32,
    )


def keep_of(tile_ref, chain_ref, rows, cols):
    tokens = chain_ref.shape[1]
    tiles = tile_ref.shape[1]
    positions = rows * cols
    at = lax.broadcasted_iota(jnp.int32, (1, positions), 1)
    row = steps(at, cols, rows)
    k = lax.axis_index("row") * rows + row
    i = lax.axis_index("col") * cols + at - row * cols
    token = lax.broadcasted_iota(jnp.int32, (tokens, positions), 0)
    pick = (token == k).astype(jnp.float32) - (token == i).astype(jnp.float32)
    chains = jnp.broadcast_to(chain_ref[...].astype(jnp.bfloat16), (8, tokens))
    apart = jnp.dot(chains, pick.astype(jnp.bfloat16), preferred_element_type=jnp.float32)[:1]
    k_tile = steps(k, TILE, tiles)
    i_tile = steps(i, TILE, tiles)
    tile_vals = jnp.zeros((1, positions), jnp.float32)
    for a in range(tiles):
        for b in range(tiles):
            here = (k_tile == a) & (i_tile == b)
            tile_vals = jnp.where(here, tile_ref[a, b].astype(jnp.float32), tile_vals)
    return jnp.where(apart == 0.0, 1.0, tile_vals)


def cycle_of(cols):
    cycle = math.lcm(cols, LANES)
    return cycle // cols, cycle // LANES


def start_copies(sems, *pairs):
    copies = [pltpu.make_async_copy(src, dst, sems.at[at]) for at, (src, dst) in enumerate(pairs)]
    for copy in copies:
        copy.start()
    return copies


def fetch(sems, *pairs):
    for copy in start_copies(sems, *pairs):
        copy.wait()


def in_first_part():
    return lax.axis_index("row") < lax.axis_size("row") // PARTS


def tail(normed_ref, w_gate_ref, gate_ref, w_out_ref, gain_ref, gain, w_out, copies):
    gate = jnp.dot(w_gate_ref[...], normed_ref[...], preferred_element_type=jnp.float32)
    gate_ref[...] = 0.5 * jnp.tanh(gate) + 0.5
    for copy in copies:
        copy.wait()
    w_out_ref[...] = w_out[...].T
    gain_ref[...] = jnp.broadcast_to(column(gain[...]), gain_ref.shape)


def project_kernel(
    rows, cols, tile_hbm, chain_hbm, pair_hbm, gain_hbm, w_hbm, gain_mid_hbm, w_out_hbm,
    message_ref, normed_ref, w_gate_ref, gate_ref, w_out_ref, gain_mid_ref,
    tile_ref, chain_ref, pair_ref, gain_ref, w_ref, gain_mid, w_out, sems,
):
    hidden = (w_ref.shape[1] - w_ref.shape[0]) // 4
    peers = message_ref.shape[0]
    own = hidden // peers
    groups = cycle_of(cols)[1]
    size = groups * LANES
    cycles = [slice(start, start + size) for start in range(0, rows * cols, size)]
    copies = start_copies(
        sems,
        (chain_hbm, chain_ref),
        (tile_hbm, tile_ref),
        (gain_hbm, gain_ref),
        (pair_hbm, pair_ref),
        (w_hbm, w_ref),
    )

    def late_copies():
        return [
            pltpu.make_async_copy(gain_mid_hbm, gain_mid, sems.at[5]),
            pltpu.make_async_copy(w_out_hbm, w_out, sems.at[6]),
        ]

    @pl.when(in_first_part())
    def _():
        for copy in late_copies():
            copy.start()

    for copy in copies[:3]:
        copy.wait()
    keep = keep_of(tile_ref, chain_ref, rows, cols)
    gain = column(gain_ref[...])
    width = pair_ref.shape[1]
    centering = (identity(width, width).astype(jnp.float32) - 1.0 / width).astype(jnp.bfloat16)
    copies[4].wait()
    w_t = (w_ref[...] * 0.5).T
    w_gate_ref[...] = w_t[4 * hidden :]
    w_t = w_t[: 4 * hidden]
    copies[3].wait()
    for lanes in cycles:
        center = transpose(pair_ref[lanes, :], centering)
        spread = jnp.mean(center * center, axis=0, keepdims=True)
        normed_ref[:, lanes] = (center * lax.rsqrt(spread + EPS) * gain).astype(jnp.bfloat16)
    for cycle, lanes in enumerate(cycles):
        projected = jnp.dot(w_t, normed_ref[:, lanes], preferred_element_type=jnp.float32)
        sides = []
        for side in range(2):
            value = projected[2 * side * hidden : (2 * side + 1) * hidden]
            gate = projected[(2 * side + 1) * hidden : (2 * side + 2) * hidden]
            sides.append(((jnp.tanh(gate) + 1.0) * value * keep[:, lanes]).reshape(peers, own, size))
        both = jnp.concatenate(sides, axis=1).astype(jnp.bfloat16)
        for group in range(groups):
            line = (cycle * groups + group) * 2 * own
            message_ref[:, line : line + 2 * own, :] = both[:, :, group * LANES : (group + 1) * LANES]

    @pl.when(in_first_part())
    def _():
        tail(normed_ref, w_gate_ref, gate_ref, w_out_ref, gain_mid_ref, gain_mid, w_out, late_copies())


def unpack(message_ref, half, halves, spread_ref, own, cols, peers):
    tokens, groups = cycle_of(cols)
    members, lines, _ = message_ref.shape
    peers = members // halves
    lane = lax.broadcasted_iota(jnp.int32, (2 * own, LANES), 1)
    cycles = lines // (2 * groups * own)
    for peer in range(peers):
        for cycle in range(cycles):
            base = cycle * groups
            held = [
                message_ref[
                    peer * halves + half, (base + group) * 2 * own : (base + group + 1) * 2 * own, :
                ].astype(jnp.float32)
                for group in range(groups)
            ]
            for token in range(tokens):
                k = (peer * cycles + cycle) * tokens + token
                for chunk in range(spread_ref.shape[0]):
                    group, off = divmod(token * cols + chunk * LANES, LANES)
                    value = held[group]
                    if off and group + 1 < groups:
                        value = jnp.where(lane >= off, value, held[group + 1])
                    if off:
                        value = pltpu.roll(value, LANES - off, axis=1)
                    spread_ref[chunk, k * 2 * own : (k + 1) * 2 * own, :] = value


def pack(spread_ref, at, own, cols):
    tokens, groups = cycle_of(cols)
    lane = lax.broadcasted_iota(jnp.int32, (own, LANES), 1)
    rolled, lines = {}, []
    for group in range(groups):
        value, here = None, 0
        while here < LANES:
            token, col = divmod(group * LANES + here, cols)
            chunk, there = divmod(col, LANES)
            shift = (here - there) % LANES
            if (token, chunk, shift) not in rolled:
                line = (at * tokens + token) * own
                piece = spread_ref[chunk, line : line + own, :]
                rolled[token, chunk, shift] = pltpu.roll(piece, shift, axis=1) if shift else piece
            piece = rolled[token, chunk, shift]
            value = piece if value is None else jnp.where(lane >= here, piece, value)
            here += min(LANES - here, LANES - there, cols - col)
        lines.append(value)
    return lines


def channel_of(spread_ref, line, stride):
    count = spread_ref.shape[1] // stride
    return jnp.concatenate(
        [spread_ref[chunk, pl.ds(line, count, stride=stride), :] for chunk in range(spread_ref.shape[0])],
        axis=1,
    ).astype(jnp.bfloat16)


def triangle_kernel(own, cols, shares, message_ref, mixed_ref, spread, left_t, mixed):
    halves, chunks = spread.shape[:2]
    width = chunks * LANES
    depth = spread.shape[2] // (2 * own)
    deep = left_t.shape[2]
    one = identity(cols, width)
    padding = [jnp.zeros((deep - depth, width), jnp.bfloat16)] if depth < deep else []
    peers = message_ref.shape[0] // halves

    def operand(channel, half):
        return jnp.concatenate([channel_of(spread.at[half], channel, 2 * own)] + padding, axis=0)

    def turn(channel, half):
        left_t[channel, half * cols : (half + 1) * cols, :] = lax.dot_general(
            one, operand(channel, half), (((1,), (1,)), ((), ())), preferred_element_type=jnp.float32
        ).astype(jnp.bfloat16)

    def multiply(channel, i_half):
        right = jnp.concatenate([operand(own + channel, half) for half in range(halves)], axis=1)
        lines = slice(i_half * cols, (i_half + 1) * cols)
        total = jnp.dot(left_t[channel, lines, :], right, preferred_element_type=jnp.float32)
        for j_half in range(halves):
            for chunk in range(chunks):
                start = j_half * width + chunk * LANES
                mixed[i_half, j_half, chunk, pl.ds(channel, cols, stride=own), :] = total[:, start : start + LANES]

    groups = cycle_of(cols)[1]
    each = mixed_ref.shape[0] // shares
    cycles = each // (halves * groups * own)

    def send(share):
        i_half, peer = divmod(share, shares // halves)
        lines = []
        for j_half in range(halves):
            for cycle in range(cycles):
                lines += pack(mixed.at[i_half, j_half], peer * cycles + cycle, own, cols)
        mixed_ref[share * each : (share + 1) * each, :] = jnp.concatenate(lines, axis=0).astype(jnp.bfloat16)

    def between(works, others):
        for at, work in enumerate(works):
            work()
            for other in others[at * len(others) // len(works) : (at + 1) * len(others) // len(works)]:
                other()

    part = functools.partial
    waiting = [part(unpack, message_ref, 0, halves, spread.at[0], own, cols, [peer]) for peer in range(peers)]
    for half in range(halves):
        for work in waiting:
            work()
        waiting = []
        if half + 1 < halves:
            waiting = [
                part(unpack, message_ref, half + 1, halves, spread.at[half + 1], own, cols, [peer])
                for peer in range(peers)
            ]
        between([part(turn, channel, half) for channel in range(own)], waiting)
        waiting = []
    for i_half in range(halves):
        between([part(multiply, channel, i_half) for channel in range(own)], waiting)
        first = i_half * (shares // halves)
        waiting = [part(send, share) for share in range(first, first + shares // halves)]
    for work in waiting:
        work()


def output_kernel(
    own, parts, mixed_ref, gate_ref, gain_ref, w_t_ref, normed_ref, w_gate_ref, gain_hbm, w_out_hbm, update_hbm,
    mixed, update, sems, gate, w_t, gain_t, gain, w_out, tail_sems,
):
    first = in_first_part()

    @pl.when(first)
    def _():
        finish(own, parts, mixed_ref, gate_ref, gain_ref, w_t_ref, update_hbm, mixed, update, sems)

    @pl.when(jnp.logical_not(first))
    def _():
        copies = start_copies(tail_sems, (gain_hbm, gain), (w_out_hbm, w_out))
        tail(normed_ref, w_gate_ref, gate, w_t, gain_t, gain, w_out, copies)
        finish(own, parts, mixed_ref, gate, gain_t, w_t, update_hbm, mixed, update, sems)


def finish(own, parts, mixed_ref, gate_ref, gain_ref, w_t_ref, update_hbm, mixed, update, sems):
    members, lines, _ = mixed.shape
    members = members // parts
    mixed[...] = mixed_ref[...].astype(jnp.float32).reshape(mixed.shape)
    groups = lines // own
    steps = math.gcd(groups, 3)
    leaving = []
    for group in range(groups):
        sums = mixed[:members, group * own : (group + 1) * own, :]
        for part in range(1, parts):
            sums += mixed[part * members : (part + 1) * members, group * own : (group + 1) * own, :]
        block = sums.reshape(members * own, LANES)
        center = block - jnp.mean(block, axis=0, keepdims=True)
        spread = jnp.mean(center * center, axis=0, keepdims=True)
        normed = (center * lax.rsqrt(spread + EPS) * gain_ref[...]).astype(jnp.bfloat16)
        projected = jnp.dot(w_t_ref[...], normed, preferred_element_type=jnp.float32)
        lanes = slice(group * LANES, (group + 1) * LANES)
        update[lanes, :] = (gate_ref[:, lanes] * projected).T.astype(jnp.bfloat16)
        step, last = divmod((group + 1) * steps, groups)
        if last == 0:
            done = slice((step - 1) * (groups // steps) * LANES, (group + 1) * LANES)
            leaving += start_copies(sems.at[step - 1], (update.at[done, :], update_hbm.at[done, :]))
    for copy in leaving:
        copy.wait()


def in_hbm(value):
    return pltpu.with_memory_space_constraint(value, pltpu.HBM)


def on_device(shares, halves, pair, tile_mask, chain_ids, gain_in, w_proj, gain_mid, w_out):
    rows, cols, width = pair.shape
    hidden = w_out.shape[0]
    peers = shares // PARTS
    own = hidden // (peers * halves)
    positions = rows * cols
    groups = positions // LANES
    lines = groups * own
    cycles = groups // cycle_of(cols)[1]
    params = pltpu.CompilerParams(vmem_limit_bytes=VMEM_BYTES)
    tokens = chain_ids.shape[0]
    message = jax.ShapeDtypeStruct((peers * halves, 2 * lines, LANES), jnp.bfloat16)
    message, normed, w_gate, gate, w_out_t, gain = pl.pallas_call(
        functools.partial(project_kernel, rows, cols),
        out_shape=(
            message,
            jax.ShapeDtypeStruct((width, positions), jnp.bfloat16),
            jax.ShapeDtypeStruct((width, width), jnp.bfloat16),
            jax.ShapeDtypeStruct((width, positions), jnp.float32),
            jax.ShapeDtypeStruct(w_out.shape[::-1], jnp.bfloat16),
            jax.ShapeDtypeStruct((hidden, LANES), jnp.float32),
        ),
        in_specs=[HBM] * 7,
        out_specs=[VMEM] * 6,
        scratch_shapes=[
            pltpu.SMEM(tile_mask.shape, jnp.int32),
            pltpu.VMEM((1, tokens), jnp.int32),
            pltpu.VMEM((positions, width), jnp.bfloat16),
            pltpu.VMEM((1, width), jnp.float32),
            pltpu.VMEM(w_proj.shape, jnp.bfloat16),
            pltpu.VMEM((1, hidden), jnp.float32),
            pltpu.VMEM(w_out.shape, jnp.bfloat16),
            pltpu.SemaphoreType.DMA((7,)),
        ],
        compiler_params=params,
        name="project",
    )(
        in_hbm(tile_mask),
        in_hbm(chain_ids[None, :]),
        in_hbm(pair.reshape(positions, width)),
        in_hbm(gain_in[None, :]),
        in_hbm(w_proj),
        in_hbm(gain_mid[None, :]),
        in_hbm(w_out),
    )
    message = lax.all_to_all(
        message,
        ("row", "col"),
        split_axis=0,
        concat_axis=0,
        axis_index_groups=[
            list(range(part * peers * halves, (part + 1) * peers * halves))
            for part in range(PARTS)
        ],
        tiled=True,
    )
    chunks = pl.cdiv(cols, LANES)
    depth = peers * rows
    deep = pl.cdiv(depth, LANES) * LANES
    mixed = pl.pallas_call(
        functools.partial(triangle_kernel, own, cols, shares),
        out_shape=jax.ShapeDtypeStruct((halves * shares * lines, LANES), jnp.bfloat16),
        in_specs=[VMEM],
        out_specs=VMEM,
        scratch_shapes=[
            pltpu.VMEM((halves, chunks, depth * 2 * own, LANES), jnp.float32),
            pltpu.VMEM((own, halves * cols, deep), jnp.bfloat16),
            pltpu.VMEM((halves, halves, chunks, cols * own, LANES), jnp.float32),
        ],
        compiler_params=params,
        name="triangle",
    )(message)
    mixed = lax.all_to_all(
        mixed.reshape(halves * shares, lines, LANES),
        ("row", "col"),
        split_axis=0,
        concat_axis=0,
        tiled=True,
    ).reshape(halves * shares * lines, LANES)
    update = pl.pallas_call(
        functools.partial(output_kernel, own, PARTS),
        out_shape=jax.ShapeDtypeStruct((positions, width), jnp.bfloat16),
        in_specs=[VMEM] * 6 + [HBM] * 2,
        out_specs=HBM,
        scratch_shapes=[
            pltpu.VMEM((halves * shares, lines, LANES), jnp.float32),
            pltpu.VMEM((positions, width), jnp.bfloat16),
            pltpu.SemaphoreType.DMA((math.gcd(groups, 3), 1)),
            pltpu.VMEM((width, positions), jnp.float32),
            pltpu.VMEM(w_out.shape[::-1], jnp.bfloat16),
            pltpu.VMEM((hidden, LANES), jnp.float32),
            pltpu.VMEM((1, hidden), jnp.float32),
            pltpu.VMEM(w_out.shape, jnp.bfloat16),
            pltpu.SemaphoreType.DMA((2,)),
        ],
        compiler_params=params,
        name="output",
    )(mixed, gate, gain, w_out_t, normed, w_gate, in_hbm(gain_mid[None, :]), in_hbm(w_out))
    return update.reshape(rows, cols, width)


def solution(mesh):
    in_specs = (P(("grp", "row"), "col", None), P("grp", None), P("grp"), P(), P(), P(), P())
    out_specs = P(("grp", "row"), "col", None)
    return jax.shard_map(
        functools.partial(on_device, mesh.shape["row"], mesh.shape["col"]),
        mesh=mesh,
        in_specs=in_specs,
        out_specs=out_specs,
        check_vma=False,
    )
```

```python
import functools
import math

import jax
import jax.numpy as jnp
from jax import lax
from jax.experimental import pallas as pl
from jax.experimental.pallas import tpu as pltpu
from jax.sharding import PartitionSpec as P

TILE = 96
LANES = 128
EPS = 1e-05
PARTS = 2
VMEM_BYTES = 32 * 1024 * 1024
VMEM = pl.BlockSpec(memory_space=pltpu.VMEM)
HBM = pl.BlockSpec(memory_space=pltpu.HBM)
SMEM = pl.BlockSpec(memory_space=pltpu.SMEM)


def column(row):
    return jnp.broadcast_to(row, (8, row.shape[1])).T[:, :1]


def steps(at, width, count):
    total = jnp.zeros_like(at)
    for edge in range(1, count):
        total += (at >= edge * width).astype(jnp.int32)
    return total


def identity(rows, cols):
    same = lax.broadcasted_iota(jnp.int32, (rows, cols), 0) == lax.broadcasted_iota(jnp.int32, (rows, cols), 1)
    return same.astype(jnp.bfloat16)


def transpose(block):
    return lax.dot_general(
        identity(block.shape[1], block.shape[1]),
        block,
        (((1,), (1,)), ((), ())),
        preferred_element_type=jnp.float32,
    )


def keep_of(tile_ref, chain_ref, rows, cols):
    tokens = chain_ref.shape[1]
    tiles = tile_ref.shape[1]
    positions = rows * cols
    at = lax.broadcasted_iota(jnp.int32, (1, positions), 1)
    row = steps(at, cols, rows)
    k = lax.axis_index("row") * rows + row
    i = lax.axis_index("col") * cols + at - row * cols
    token = lax.broadcasted_iota(jnp.int32, (tokens, positions), 0)
    pick = (token == k).astype(jnp.float32) - (token == i).astype(jnp.float32)
    chains = jnp.broadcast_to(chain_ref[...].astype(jnp.bfloat16), (8, tokens))
    apart = jnp.dot(chains, pick.astype(jnp.bfloat16), preferred_element_type=jnp.float32)[:1]
    k_tile = steps(k, TILE, tiles)
    i_tile = steps(i, TILE, tiles)
    tile_vals = jnp.zeros((1, positions), jnp.float32)
    for a in range(tiles):
        for b in range(tiles):
            here = (k_tile == a) & (i_tile == b)
            tile_vals = jnp.where(here, tile_ref[a, b].astype(jnp.float32), tile_vals)
    return jnp.where(apart == 0.0, 1.0, tile_vals)


def cycle_of(cols):
    cycle = math.lcm(cols, LANES)
    return cycle // cols, cycle // LANES


def start_copies(sems, *pairs):
    copies = [pltpu.make_async_copy(src, dst, sems.at[at]) for at, (src, dst) in enumerate(pairs)]
    for copy in copies:
        copy.start()
    return copies


def fetch(sems, *pairs):
    for copy in start_copies(sems, *pairs):
        copy.wait()


def in_first_part():
    return lax.axis_index("row") < lax.axis_size("row") // PARTS


def tail(normed_ref, w_gate_ref, gain_hbm, w_out_hbm, gate_ref, w_out_ref, gain_ref, gain, w_out, sems):
    copies = start_copies(sems, (gain_hbm, gain), (w_out_hbm, w_out))
    gate = jnp.dot(w_gate_ref[...], normed_ref[...], preferred_element_type=jnp.float32)
    gate_ref[...] = 0.5 * jnp.tanh(gate) + 0.5
    for copy in copies:
        copy.wait()
    w_out_ref[...] = w_out[...].T
    gain_ref[...] = jnp.broadcast_to(column(gain[...]), gain_ref.shape)


def project_kernel(
    rows, cols, tile_hbm, chain_hbm, pair_hbm, gain_hbm, w_hbm, gain_mid_hbm, w_out_hbm,
    message_ref, normed_ref, w_gate_ref, gate_ref, w_out_ref, gain_mid_ref,
    tile_ref, chain_ref, pair_ref, gain_ref, w_ref, gain_mid, w_out, sems,
):
    hidden = (w_ref.shape[1] - w_ref.shape[0]) // 4
    peers = message_ref.shape[0]
    own = hidden // peers
    groups = cycle_of(cols)[1]
    size = groups * LANES
    cycles = [slice(start, start + size) for start in range(0, rows * cols, size)]
    copies = start_copies(
        sems,
        (chain_hbm, chain_ref),
        (tile_hbm, tile_ref),
        (pair_hbm, pair_ref),
        (w_hbm, w_ref),
        (gain_hbm, gain_ref),
    )
    for copy in copies[:2]:
        copy.wait()
    keep = keep_of(tile_ref, chain_ref, rows, cols)
    copies[3].wait()
    w_t = (w_ref[...] * 0.5).T
    w_gate_ref[...] = w_t[4 * hidden :]
    w_t = w_t[: 4 * hidden]
    copies[4].wait()
    gain = column(gain_ref[...])
    copies[2].wait()
    for lanes in cycles:
        block = transpose(pair_ref[lanes, :])
        center = block - jnp.mean(block, axis=0, keepdims=True)
        spread = jnp.mean(center * center, axis=0, keepdims=True)
        normed_ref[:, lanes] = (center * lax.rsqrt(spread + EPS) * gain).astype(jnp.bfloat16)
    for cycle, lanes in enumerate(cycles):
        projected = jnp.dot(w_t, normed_ref[:, lanes], preferred_element_type=jnp.float32)
        sides = []
        for side in range(2):
            value = projected[2 * side * hidden : (2 * side + 1) * hidden]
            gate = projected[(2 * side + 1) * hidden : (2 * side + 2) * hidden]
            sides.append(((jnp.tanh(gate) + 1.0) * value * keep[:, lanes]).reshape(peers, own, size))
        both = jnp.concatenate(sides, axis=1).astype(jnp.bfloat16)
        for group in range(groups):
            line = (cycle * groups + group) * 2 * own
            message_ref[:, line : line + 2 * own, :] = both[:, :, group * LANES : (group + 1) * LANES]

    @pl.when(in_first_part())
    def _():
        tail(normed_ref, w_gate_ref, gain_mid_hbm, w_out_hbm, gate_ref, w_out_ref, gain_mid_ref, gain_mid, w_out, sems)


def unpack(message_ref, half, halves, spread_ref, own, cols):
    tokens, groups = cycle_of(cols)
    members, lines, _ = message_ref.shape
    peers = members // halves
    lane = lax.broadcasted_iota(jnp.int32, (2 * own, LANES), 1)
    cycles = lines // (2 * groups * own)
    for peer in range(peers):
        for cycle in range(cycles):
            base = cycle * groups
            held = [
                message_ref[
                    peer * halves + half, (base + group) * 2 * own : (base + group + 1) * 2 * own, :
                ].astype(jnp.float32)
                for group in range(groups)
            ]
            for token in range(tokens):
                k = (peer * cycles + cycle) * tokens + token
                for chunk in range(spread_ref.shape[0]):
                    group, off = divmod(token * cols + chunk * LANES, LANES)
                    value = held[group]
                    if off and group + 1 < groups:
                        value = jnp.where(lane >= off, value, held[group + 1])
                    if off:
                        value = pltpu.roll(value, LANES - off, axis=1)
                    spread_ref[chunk, k * 2 * own : (k + 1) * 2 * own, :] = value


def pack(spread_ref, at, own, cols):
    tokens, groups = cycle_of(cols)
    lane = lax.broadcasted_iota(jnp.int32, (own, LANES), 1)
    rolled, lines = {}, []
    for group in range(groups):
        value, here = None, 0
        while here < LANES:
            token, col = divmod(group * LANES + here, cols)
            chunk, there = divmod(col, LANES)
            shift = (here - there) % LANES
            if (token, chunk, shift) not in rolled:
                line = (at * tokens + token) * own
                piece = spread_ref[chunk, line : line + own, :]
                rolled[token, chunk, shift] = pltpu.roll(piece, shift, axis=1) if shift else piece
            piece = rolled[token, chunk, shift]
            value = piece if value is None else jnp.where(lane >= here, piece, value)
            here += min(LANES - here, LANES - there, cols - col)
        lines.append(value)
    return lines


def channel_of(spread_ref, line, stride):
    count = spread_ref.shape[1] // stride
    return jnp.concatenate(
        [spread_ref[chunk, pl.ds(line, count, stride=stride), :] for chunk in range(spread_ref.shape[0])],
        axis=1,
    ).astype(jnp.bfloat16)


def triangle_kernel(own, cols, shares, message_ref, mixed_ref, spread, left_t, mixed):
    halves, chunks = spread.shape[:2]
    width = chunks * LANES
    depth = spread.shape[2] // (2 * own)
    deep = left_t.shape[2]
    one = identity(cols, width)
    padding = [jnp.zeros((deep - depth, width), jnp.bfloat16)] if depth < deep else []
    for half in range(halves):
        unpack(message_ref, half, halves, spread.at[half], own, cols)

    def operand(channel, half):
        return jnp.concatenate([channel_of(spread.at[half], channel, 2 * own)] + padding, axis=0)

    for channel in range(own):
        left = jnp.concatenate([operand(channel, half) for half in range(halves)], axis=0)
        both = lax.dot_general(
            one, left, (((1,), (1,)), ((), ())), preferred_element_type=jnp.float32
        ).astype(jnp.bfloat16)
        for half in range(halves):
            left_t[channel, half * cols : (half + 1) * cols, :] = both[:, half * deep : (half + 1) * deep]
    for channel in range(own):
        right = jnp.concatenate([operand(own + channel, half) for half in range(halves)], axis=1)
        total = jnp.dot(left_t[channel], right, preferred_element_type=jnp.float32)
        for i_half in range(halves):
            for j_half in range(halves):
                for chunk in range(chunks):
                    start = j_half * width + chunk * LANES
                    mixed[i_half, j_half, chunk, pl.ds(channel, cols, stride=own), :] = total[
                        i_half * cols : (i_half + 1) * cols, start : start + LANES
                    ]
    groups = cycle_of(cols)[1]
    each = mixed_ref.shape[0] // shares
    cycles = each // (halves * groups * own)
    for share in range(shares):
        i_half, peer = divmod(share, shares // halves)
        lines = []
        for j_half in range(halves):
            for cycle in range(cycles):
                lines += pack(mixed.at[i_half, j_half], peer * cycles + cycle, own, cols)
        mixed_ref[share * each : (share + 1) * each, :] = jnp.concatenate(lines, axis=0).astype(jnp.bfloat16)


def output_kernel(
    own, parts, mixed_ref, gate_ref, gain_ref, w_t_ref, normed_ref, w_gate_ref, gain_hbm, w_out_hbm, update_hbm,
    mixed, update, sems, gate, w_t, gain_t, gain, w_out, tail_sems,
):
    first = in_first_part()

    @pl.when(first)
    def _():
        finish(own, parts, mixed_ref, gate_ref, gain_ref, w_t_ref, update_hbm, mixed, update, sems)

    @pl.when(jnp.logical_not(first))
    def _():
        tail(normed_ref, w_gate_ref, gain_hbm, w_out_hbm, gate, w_t, gain_t, gain, w_out, tail_sems)
        finish(own, parts, mixed_ref, gate, gain_t, w_t, update_hbm, mixed, update, sems)


def finish(own, parts, mixed_ref, gate_ref, gain_ref, w_t_ref, update_hbm, mixed, update, sems):
    members, lines, _ = mixed.shape
    members = members // parts
    mixed[...] = mixed_ref[...].astype(jnp.float32).reshape(mixed.shape)
    groups = lines // own
    steps = math.gcd(groups, 3)
    leaving = []
    for group in range(groups):
        sums = mixed[:members, group * own : (group + 1) * own, :]
        for part in range(1, parts):
            sums += mixed[part * members : (part + 1) * members, group * own : (group + 1) * own, :]
        block = sums.reshape(members * own, LANES)
        center = block - jnp.mean(block, axis=0, keepdims=True)
        spread = jnp.mean(center * center, axis=0, keepdims=True)
        normed = (center * lax.rsqrt(spread + EPS) * gain_ref[...]).astype(jnp.bfloat16)
        projected = jnp.dot(w_t_ref[...], normed, preferred_element_type=jnp.float32)
        lanes = slice(group * LANES, (group + 1) * LANES)
        update[lanes, :] = (gate_ref[:, lanes] * projected).T.astype(jnp.bfloat16)
        step, last = divmod((group + 1) * steps, groups)
        if last == 0:
            done = slice((step - 1) * (groups // steps) * LANES, (group + 1) * LANES)
            leaving += start_copies(sems.at[step - 1], (update.at[done, :], update_hbm.at[done, :]))
    for copy in leaving:
        copy.wait()


def in_hbm(value):
    return pltpu.with_memory_space_constraint(value, pltpu.HBM)


def on_device(shares, halves, pair, tile_mask, chain_ids, gain_in, w_proj, gain_mid, w_out):
    rows, cols, width = pair.shape
    hidden = w_out.shape[0]
    peers = shares // PARTS
    own = hidden // (peers * halves)
    positions = rows * cols
    groups = positions // LANES
    lines = groups * own
    cycles = groups // cycle_of(cols)[1]
    params = pltpu.CompilerParams(vmem_limit_bytes=VMEM_BYTES)
    tokens = chain_ids.shape[0]
    message = jax.ShapeDtypeStruct((peers * halves, 2 * lines, LANES), jnp.bfloat16)
    message, normed, w_gate, gate, w_out_t, gain = pl.pallas_call(
        functools.partial(project_kernel, rows, cols),
        out_shape=(
            message,
            jax.ShapeDtypeStruct((width, positions), jnp.bfloat16),
            jax.ShapeDtypeStruct((width, width), jnp.bfloat16),
            jax.ShapeDtypeStruct((width, positions), jnp.float32),
            jax.ShapeDtypeStruct(w_out.shape[::-1], jnp.bfloat16),
            jax.ShapeDtypeStruct((hidden, LANES), jnp.float32),
        ),
        in_specs=[HBM] * 7,
        out_specs=[VMEM] * 6,
        scratch_shapes=[
            pltpu.SMEM(tile_mask.shape, jnp.int32),
            pltpu.VMEM((1, tokens), jnp.int32),
            pltpu.VMEM((positions, width), jnp.bfloat16),
            pltpu.VMEM((1, width), jnp.float32),
            pltpu.VMEM(w_proj.shape, jnp.bfloat16),
            pltpu.VMEM((1, hidden), jnp.float32),
            pltpu.VMEM(w_out.shape, jnp.bfloat16),
            pltpu.SemaphoreType.DMA((5,)),
        ],
        compiler_params=params,
        name="project",
    )(
        in_hbm(tile_mask),
        in_hbm(chain_ids[None, :]),
        in_hbm(pair.reshape(positions, width)),
        in_hbm(gain_in[None, :]),
        in_hbm(w_proj),
        in_hbm(gain_mid[None, :]),
        in_hbm(w_out),
    )
    message = lax.all_to_all(
        message,
        ("row", "col"),
        split_axis=0,
        concat_axis=0,
        axis_index_groups=[
            list(range(part * peers * halves, (part + 1) * peers * halves))
            for part in range(PARTS)
        ],
        tiled=True,
    )
    chunks = pl.cdiv(cols, LANES)
    depth = peers * rows
    deep = pl.cdiv(depth, LANES) * LANES
    mixed = pl.pallas_call(
        functools.partial(triangle_kernel, own, cols, shares),
        out_shape=jax.ShapeDtypeStruct((halves * shares * lines, LANES), jnp.bfloat16),
        in_specs=[VMEM],
        out_specs=VMEM,
        scratch_shapes=[
            pltpu.VMEM((halves, chunks, depth * 2 * own, LANES), jnp.float32),
            pltpu.VMEM((own, halves * cols, deep), jnp.bfloat16),
            pltpu.VMEM((halves, halves, chunks, cols * own, LANES), jnp.float32),
        ],
        compiler_params=params,
        name="triangle",
    )(message)
    mixed = lax.all_to_all(
        mixed.reshape(halves * shares, lines, LANES),
        ("row", "col"),
        split_axis=0,
        concat_axis=0,
        tiled=True,
    ).reshape(halves * shares * lines, LANES)
    update = pl.pallas_call(
        functools.partial(output_kernel, own, PARTS),
        out_shape=jax.ShapeDtypeStruct((positions, width), jnp.bfloat16),
        in_specs=[VMEM] * 6 + [HBM] * 2,
        out_specs=HBM,
        scratch_shapes=[
            pltpu.VMEM((halves * shares, lines, LANES), jnp.float32),
            pltpu.VMEM((positions, width), jnp.bfloat16),
            pltpu.SemaphoreType.DMA((math.gcd(groups, 3), 1)),
            pltpu.VMEM((width, positions), jnp.float32),
            pltpu.VMEM(w_out.shape[::-1], jnp.bfloat16),
            pltpu.VMEM((hidden, LANES), jnp.float32),
            pltpu.VMEM((1, hidden), jnp.float32),
            pltpu.VMEM(w_out.shape, jnp.bfloat16),
            pltpu.SemaphoreType.DMA((2,)),
        ],
        compiler_params=params,
        name="output",
    )(mixed, gate, gain, w_out_t, normed, w_gate, in_hbm(gain_mid[None, :]), in_hbm(w_out))
    return update.reshape(rows, cols, width)


def solution(mesh):
    in_specs = (P(("grp", "row"), "col", None), P("grp", None), P("grp"), P(), P(), P(), P())
    out_specs = P(("grp", "row"), "col", None)
    return jax.shard_map(
        functools.partial(on_device, mesh.shape["row"], mesh.shape["col"]),
        mesh=mesh,
        in_specs=in_specs,
        out_specs=out_specs,
        check_vma=False,
    )
```

```python
import functools
import math

import jax
import jax.numpy as jnp
from jax import lax
from jax.experimental import pallas as pl
from jax.experimental.pallas import tpu as pltpu
from jax.sharding import PartitionSpec as P

TILE = 96
LANES = 128
EPS = 1e-05
PARTS = 2
VMEM_BYTES = 32 * 1024 * 1024
VMEM = pl.BlockSpec(memory_space=pltpu.VMEM)
HBM = pl.BlockSpec(memory_space=pltpu.HBM)
SMEM = pl.BlockSpec(memory_space=pltpu.SMEM)


def column(row):
    return jnp.broadcast_to(row, (8, row.shape[1])).T[:, :1]


def steps(at, width, count):
    total = jnp.zeros_like(at)
    for edge in range(1, count):
        total += (at >= edge * width).astype(jnp.int32)
    return total


def identity(rows, cols):
    same = lax.broadcasted_iota(jnp.int32, (rows, cols), 0) == lax.broadcasted_iota(jnp.int32, (rows, cols), 1)
    return same.astype(jnp.bfloat16)


def transpose(block):
    return lax.dot_general(
        identity(block.shape[1], block.shape[1]),
        block,
        (((1,), (1,)), ((), ())),
        preferred_element_type=jnp.float32,
    )


def keep_of(tile_ref, chain_ref, rows, cols):
    tokens = chain_ref.shape[1]
    tiles = tile_ref.shape[1]
    positions = rows * cols
    at = lax.broadcasted_iota(jnp.int32, (1, positions), 1)
    row = steps(at, cols, rows)
    k = lax.axis_index("row") * rows + row
    i = lax.axis_index("col") * cols + at - row * cols
    token = lax.broadcasted_iota(jnp.int32, (tokens, positions), 0)
    pick = (token == k).astype(jnp.float32) - (token == i).astype(jnp.float32)
    chains = jnp.broadcast_to(chain_ref[...].astype(jnp.bfloat16), (8, tokens))
    apart = jnp.dot(chains, pick.astype(jnp.bfloat16), preferred_element_type=jnp.float32)[:1]
    k_tile = steps(k, TILE, tiles)
    i_tile = steps(i, TILE, tiles)
    tile_vals = jnp.zeros((1, positions), jnp.float32)
    for a in range(tiles):
        for b in range(tiles):
            here = (k_tile == a) & (i_tile == b)
            tile_vals = jnp.where(here, tile_ref[a, b].astype(jnp.float32), tile_vals)
    return jnp.where(apart == 0.0, 1.0, tile_vals)


def cycle_of(cols):
    cycle = math.lcm(cols, LANES)
    return cycle // cols, cycle // LANES


def start_copies(sems, *pairs):
    copies = [pltpu.make_async_copy(src, dst, sems.at[at]) for at, (src, dst) in enumerate(pairs)]
    for copy in copies:
        copy.start()
    return copies


def fetch(sems, *pairs):
    for copy in start_copies(sems, *pairs):
        copy.wait()


def in_first_part():
    return lax.axis_index("row") < lax.axis_size("row") // PARTS


def tail(normed_ref, w_gate_ref, gain_hbm, w_out_hbm, gate_ref, w_out_ref, gain_ref, gain, w_out, sems):
    copies = start_copies(sems, (gain_hbm, gain), (w_out_hbm, w_out))
    gate = jnp.dot(w_gate_ref[...], normed_ref[...], preferred_element_type=jnp.float32)
    gate_ref[...] = 0.5 * jnp.tanh(gate) + 0.5
    for copy in copies:
        copy.wait()
    w_out_ref[...] = w_out[...].T
    gain_ref[...] = jnp.broadcast_to(column(gain[...]), gain_ref.shape)


def project_kernel(
    rows, cols, tile_hbm, chain_hbm, pair_hbm, gain_hbm, w_hbm, gain_mid_hbm, w_out_hbm,
    message_ref, normed_ref, w_gate_ref, gate_ref, w_out_ref, gain_mid_ref,
    tile_ref, chain_ref, pair_ref, gain_ref, w_ref, gain_mid, w_out, sems,
):
    hidden = (w_ref.shape[1] - w_ref.shape[0]) // 4
    peers = message_ref.shape[0]
    own = hidden // peers
    groups = cycle_of(cols)[1]
    size = groups * LANES
    cycles = [slice(start, start + size) for start in range(0, rows * cols, size)]
    copies = start_copies(
        sems,
        (chain_hbm, chain_ref),
        (tile_hbm, tile_ref),
        (gain_hbm, gain_ref),
        (pair_hbm, pair_ref),
        (w_hbm, w_ref),
    )
    for copy in copies[:3]:
        copy.wait()
    keep = keep_of(tile_ref, chain_ref, rows, cols)
    gain = column(gain_ref[...])
    copies[4].wait()
    w_t = (w_ref[...] * 0.5).T
    w_gate_ref[...] = w_t[4 * hidden :]
    w_t = w_t[: 4 * hidden]
    copies[3].wait()
    for lanes in cycles:
        block = transpose(pair_ref[lanes, :])
        center = block - jnp.mean(block, axis=0, keepdims=True)
        spread = jnp.mean(center * center, axis=0, keepdims=True)
        normed_ref[:, lanes] = (center * lax.rsqrt(spread + EPS) * gain).astype(jnp.bfloat16)
    for cycle, lanes in enumerate(cycles):
        projected = jnp.dot(w_t, normed_ref[:, lanes], preferred_element_type=jnp.float32)
        sides = []
        for side in range(2):
            value = projected[2 * side * hidden : (2 * side + 1) * hidden]
            gate = projected[(2 * side + 1) * hidden : (2 * side + 2) * hidden]
            sides.append(((jnp.tanh(gate) + 1.0) * value * keep[:, lanes]).reshape(peers, own, size))
        both = jnp.concatenate(sides, axis=1).astype(jnp.bfloat16)
        for group in range(groups):
            line = (cycle * groups + group) * 2 * own
            message_ref[:, line : line + 2 * own, :] = both[:, :, group * LANES : (group + 1) * LANES]

    @pl.when(in_first_part())
    def _():
        tail(normed_ref, w_gate_ref, gain_mid_hbm, w_out_hbm, gate_ref, w_out_ref, gain_mid_ref, gain_mid, w_out, sems)


def unpack(message_ref, half, halves, spread_ref, own, cols):
    tokens, groups = cycle_of(cols)
    members, lines, _ = message_ref.shape
    peers = members // halves
    lane = lax.broadcasted_iota(jnp.int32, (2 * own, LANES), 1)
    cycles = lines // (2 * groups * own)
    for peer in range(peers):
        for cycle in range(cycles):
            base = cycle * groups
            held = [
                message_ref[
                    peer * halves + half, (base + group) * 2 * own : (base + group + 1) * 2 * own, :
                ].astype(jnp.float32)
                for group in range(groups)
            ]
            for token in range(tokens):
                k = (peer * cycles + cycle) * tokens + token
                for chunk in range(spread_ref.shape[0]):
                    group, off = divmod(token * cols + chunk * LANES, LANES)
                    value = held[group]
                    if off and group + 1 < groups:
                        value = jnp.where(lane >= off, value, held[group + 1])
                    if off:
                        value = pltpu.roll(value, LANES - off, axis=1)
                    spread_ref[chunk, k * 2 * own : (k + 1) * 2 * own, :] = value


def pack(spread_ref, at, own, cols):
    tokens, groups = cycle_of(cols)
    lane = lax.broadcasted_iota(jnp.int32, (own, LANES), 1)
    rolled, lines = {}, []
    for group in range(groups):
        value, here = None, 0
        while here < LANES:
            token, col = divmod(group * LANES + here, cols)
            chunk, there = divmod(col, LANES)
            shift = (here - there) % LANES
            if (token, chunk, shift) not in rolled:
                line = (at * tokens + token) * own
                piece = spread_ref[chunk, line : line + own, :]
                rolled[token, chunk, shift] = pltpu.roll(piece, shift, axis=1) if shift else piece
            piece = rolled[token, chunk, shift]
            value = piece if value is None else jnp.where(lane >= here, piece, value)
            here += min(LANES - here, LANES - there, cols - col)
        lines.append(value)
    return lines


def channel_of(spread_ref, line, stride):
    count = spread_ref.shape[1] // stride
    return jnp.concatenate(
        [spread_ref[chunk, pl.ds(line, count, stride=stride), :] for chunk in range(spread_ref.shape[0])],
        axis=1,
    ).astype(jnp.bfloat16)


def triangle_kernel(own, cols, shares, message_ref, mixed_ref, spread, left_t, mixed):
    halves, chunks = spread.shape[:2]
    width = chunks * LANES
    depth = spread.shape[2] // (2 * own)
    deep = left_t.shape[2]
    one = identity(cols, width)
    padding = [jnp.zeros((deep - depth, width), jnp.bfloat16)] if depth < deep else []
    for half in range(halves):
        unpack(message_ref, half, halves, spread.at[half], own, cols)

    def operand(channel, half):
        return jnp.concatenate([channel_of(spread.at[half], channel, 2 * own)] + padding, axis=0)

    for channel in range(own):
        left = jnp.concatenate([operand(channel, half) for half in range(halves)], axis=0)
        both = lax.dot_general(
            one, left, (((1,), (1,)), ((), ())), preferred_element_type=jnp.float32
        ).astype(jnp.bfloat16)
        for half in range(halves):
            left_t[channel, half * cols : (half + 1) * cols, :] = both[:, half * deep : (half + 1) * deep]
    for channel in range(own):
        right = jnp.concatenate([operand(own + channel, half) for half in range(halves)], axis=1)
        total = jnp.dot(left_t[channel], right, preferred_element_type=jnp.float32)
        for i_half in range(halves):
            for j_half in range(halves):
                for chunk in range(chunks):
                    start = j_half * width + chunk * LANES
                    mixed[i_half, j_half, chunk, pl.ds(channel, cols, stride=own), :] = total[
                        i_half * cols : (i_half + 1) * cols, start : start + LANES
                    ]
    groups = cycle_of(cols)[1]
    each = mixed_ref.shape[0] // shares
    cycles = each // (halves * groups * own)
    for share in range(shares):
        i_half, peer = divmod(share, shares // halves)
        lines = []
        for j_half in range(halves):
            for cycle in range(cycles):
                lines += pack(mixed.at[i_half, j_half], peer * cycles + cycle, own, cols)
        mixed_ref[share * each : (share + 1) * each, :] = jnp.concatenate(lines, axis=0).astype(jnp.bfloat16)


def output_kernel(
    own, parts, mixed_ref, gate_ref, gain_ref, w_t_ref, normed_ref, w_gate_ref, gain_hbm, w_out_hbm, update_hbm,
    mixed, update, sems, gate, w_t, gain_t, gain, w_out, tail_sems,
):
    first = in_first_part()

    @pl.when(first)
    def _():
        finish(own, parts, mixed_ref, gate_ref, gain_ref, w_t_ref, update_hbm, mixed, update, sems)

    @pl.when(jnp.logical_not(first))
    def _():
        tail(normed_ref, w_gate_ref, gain_hbm, w_out_hbm, gate, w_t, gain_t, gain, w_out, tail_sems)
        finish(own, parts, mixed_ref, gate, gain_t, w_t, update_hbm, mixed, update, sems)


def finish(own, parts, mixed_ref, gate_ref, gain_ref, w_t_ref, update_hbm, mixed, update, sems):
    members, lines, _ = mixed.shape
    members = members // parts
    mixed[...] = mixed_ref[...].astype(jnp.float32).reshape(mixed.shape)
    groups = lines // own
    ends = [groups // 2, groups - 1, groups]
    leaving = []
    for group in range(groups):
        sums = mixed[:members, group * own : (group + 1) * own, :]
        for part in range(1, parts):
            sums += mixed[part * members : (part + 1) * members, group * own : (group + 1) * own, :]
        block = sums.reshape(members * own, LANES)
        center = block - jnp.mean(block, axis=0, keepdims=True)
        spread = jnp.mean(center * center, axis=0, keepdims=True)
        normed = (center * lax.rsqrt(spread + EPS) * gain_ref[...]).astype(jnp.bfloat16)
        projected = jnp.dot(w_t_ref[...], normed, preferred_element_type=jnp.float32)
        lanes = slice(group * LANES, (group + 1) * LANES)
        update[lanes, :] = (gate_ref[:, lanes] * projected).T.astype(jnp.bfloat16)
        if group + 1 in ends:
            step = ends.index(group + 1)
            done = slice(([0] + ends)[step] * LANES, (group + 1) * LANES)
            leaving += start_copies(sems.at[step], (update.at[done, :], update_hbm.at[done, :]))
    for copy in leaving:
        copy.wait()


def in_hbm(value):
    return pltpu.with_memory_space_constraint(value, pltpu.HBM)


def on_device(shares, halves, pair, tile_mask, chain_ids, gain_in, w_proj, gain_mid, w_out):
    rows, cols, width = pair.shape
    hidden = w_out.shape[0]
    peers = shares // PARTS
    own = hidden // (peers * halves)
    positions = rows * cols
    groups = positions // LANES
    lines = groups * own
    cycles = groups // cycle_of(cols)[1]
    params = pltpu.CompilerParams(vmem_limit_bytes=VMEM_BYTES)
    tokens = chain_ids.shape[0]
    message = jax.ShapeDtypeStruct((peers * halves, 2 * lines, LANES), jnp.bfloat16)
    message, normed, w_gate, gate, w_out_t, gain = pl.pallas_call(
        functools.partial(project_kernel, rows, cols),
        out_shape=(
            message,
            jax.ShapeDtypeStruct((width, positions), jnp.bfloat16),
            jax.ShapeDtypeStruct((width, width), jnp.bfloat16),
            jax.ShapeDtypeStruct((width, positions), jnp.float32),
            jax.ShapeDtypeStruct(w_out.shape[::-1], jnp.bfloat16),
            jax.ShapeDtypeStruct((hidden, LANES), jnp.float32),
        ),
        in_specs=[HBM] * 7,
        out_specs=[VMEM] * 6,
        scratch_shapes=[
            pltpu.SMEM(tile_mask.shape, jnp.int32),
            pltpu.VMEM((1, tokens), jnp.int32),
            pltpu.VMEM((positions, width), jnp.bfloat16),
            pltpu.VMEM((1, width), jnp.float32),
            pltpu.VMEM(w_proj.shape, jnp.bfloat16),
            pltpu.VMEM((1, hidden), jnp.float32),
            pltpu.VMEM(w_out.shape, jnp.bfloat16),
            pltpu.SemaphoreType.DMA((5,)),
        ],
        compiler_params=params,
        name="project",
    )(
        in_hbm(tile_mask),
        in_hbm(chain_ids[None, :]),
        in_hbm(pair.reshape(positions, width)),
        in_hbm(gain_in[None, :]),
        in_hbm(w_proj),
        in_hbm(gain_mid[None, :]),
        in_hbm(w_out),
    )
    message = lax.all_to_all(
        message,
        ("row", "col"),
        split_axis=0,
        concat_axis=0,
        axis_index_groups=[
            list(range(part * peers * halves, (part + 1) * peers * halves))
            for part in range(PARTS)
        ],
        tiled=True,
    )
    chunks = pl.cdiv(cols, LANES)
    depth = peers * rows
    deep = pl.cdiv(depth, LANES) * LANES
    mixed = pl.pallas_call(
        functools.partial(triangle_kernel, own, cols, shares),
        out_shape=jax.ShapeDtypeStruct((halves * shares * lines, LANES), jnp.bfloat16),
        in_specs=[VMEM],
        out_specs=VMEM,
        scratch_shapes=[
            pltpu.VMEM((halves, chunks, depth * 2 * own, LANES), jnp.float32),
            pltpu.VMEM((own, halves * cols, deep), jnp.bfloat16),
            pltpu.VMEM((halves, halves, chunks, cols * own, LANES), jnp.float32),
        ],
        compiler_params=params,
        name="triangle",
    )(message)
    mixed = lax.all_to_all(
        mixed.reshape(halves * shares, lines, LANES),
        ("row", "col"),
        split_axis=0,
        concat_axis=0,
        tiled=True,
    ).reshape(halves * shares * lines, LANES)
    update = pl.pallas_call(
        functools.partial(output_kernel, own, PARTS),
        out_shape=jax.ShapeDtypeStruct((positions, width), jnp.bfloat16),
        in_specs=[VMEM] * 6 + [HBM] * 2,
        out_specs=HBM,
        scratch_shapes=[
            pltpu.VMEM((halves * shares, lines, LANES), jnp.float32),
            pltpu.VMEM((positions, width), jnp.bfloat16),
            pltpu.SemaphoreType.DMA((3, 1)),
            pltpu.VMEM((width, positions), jnp.float32),
            pltpu.VMEM(w_out.shape[::-1], jnp.bfloat16),
            pltpu.VMEM((hidden, LANES), jnp.float32),
            pltpu.VMEM((1, hidden), jnp.float32),
            pltpu.VMEM(w_out.shape, jnp.bfloat16),
            pltpu.SemaphoreType.DMA((2,)),
        ],
        compiler_params=params,
        name="output",
    )(mixed, gate, gain, w_out_t, normed, w_gate, in_hbm(gain_mid[None, :]), in_hbm(w_out))
    return update.reshape(rows, cols, width)


def solution(mesh):
    in_specs = (P(("grp", "row"), "col", None), P("grp", None), P("grp"), P(), P(), P(), P())
    out_specs = P(("grp", "row"), "col", None)
    return jax.shard_map(
        functools.partial(on_device, mesh.shape["row"], mesh.shape["col"]),
        mesh=mesh,
        in_specs=in_specs,
        out_specs=out_specs,
        check_vma=False,
    )
```

```python
import functools
import math

import jax
import jax.numpy as jnp
from jax import lax
from jax.experimental import pallas as pl
from jax.experimental.pallas import tpu as pltpu
from jax.sharding import PartitionSpec as P

TILE = 96
LANES = 128
EPS = 1e-05
PARTS = 2
VMEM_BYTES = 32 * 1024 * 1024
VMEM = pl.BlockSpec(memory_space=pltpu.VMEM)
HBM = pl.BlockSpec(memory_space=pltpu.HBM)
SMEM = pl.BlockSpec(memory_space=pltpu.SMEM)


def column(row):
    return jnp.broadcast_to(row, (8, row.shape[1])).T[:, :1]


def steps(at, width, count):
    total = jnp.zeros_like(at)
    for edge in range(1, count):
        total += (at >= edge * width).astype(jnp.int32)
    return total


def identity(rows, cols):
    same = lax.broadcasted_iota(jnp.int32, (rows, cols), 0) == lax.broadcasted_iota(jnp.int32, (rows, cols), 1)
    return same.astype(jnp.bfloat16)


def transpose(block):
    return lax.dot_general(
        identity(block.shape[1], block.shape[1]),
        block,
        (((1,), (1,)), ((), ())),
        preferred_element_type=jnp.float32,
    )


def keep_of(tile_ref, chain_ref, rows, cols):
    tokens = chain_ref.shape[1]
    tiles = tile_ref.shape[1]
    positions = rows * cols
    at = lax.broadcasted_iota(jnp.int32, (1, positions), 1)
    row = steps(at, cols, rows)
    k = lax.axis_index("row") * rows + row
    i = lax.axis_index("col") * cols + at - row * cols
    token = lax.broadcasted_iota(jnp.int32, (tokens, positions), 0)
    pick = (token == k).astype(jnp.float32) - (token == i).astype(jnp.float32)
    chains = jnp.broadcast_to(chain_ref[...].astype(jnp.bfloat16), (8, tokens))
    apart = jnp.dot(chains, pick.astype(jnp.bfloat16), preferred_element_type=jnp.float32)[:1]
    k_tile = steps(k, TILE, tiles)
    i_tile = steps(i, TILE, tiles)
    tile_vals = jnp.zeros((1, positions), jnp.float32)
    for a in range(tiles):
        for b in range(tiles):
            here = (k_tile == a) & (i_tile == b)
            tile_vals = jnp.where(here, tile_ref[a, b].astype(jnp.float32), tile_vals)
    return jnp.where(apart == 0.0, 1.0, tile_vals)


def cycle_of(cols):
    cycle = math.lcm(cols, LANES)
    return cycle // cols, cycle // LANES


def start_copies(sems, *pairs):
    copies = [pltpu.make_async_copy(src, dst, sems.at[at]) for at, (src, dst) in enumerate(pairs)]
    for copy in copies:
        copy.start()
    return copies


def fetch(sems, *pairs):
    for copy in start_copies(sems, *pairs):
        copy.wait()


def in_first_part():
    return lax.axis_index("row") < lax.axis_size("row") // PARTS


def tail(normed_ref, w_gate_ref, gain_hbm, w_out_hbm, gate_ref, w_out_ref, gain_ref, gain, w_out, sems):
    copies = start_copies(sems, (gain_hbm, gain), (w_out_hbm, w_out))
    gate = jnp.dot(w_gate_ref[...], normed_ref[...], preferred_element_type=jnp.float32)
    gate_ref[...] = 0.5 * jnp.tanh(gate) + 0.5
    for copy in copies:
        copy.wait()
    w_out_ref[...] = w_out[...].T
    gain_ref[...] = jnp.broadcast_to(column(gain[...]), gain_ref.shape)


def project_kernel(
    rows, cols, tile_hbm, chain_hbm, pair_hbm, gain_hbm, w_hbm, gain_mid_hbm, w_out_hbm,
    message_ref, normed_ref, w_gate_ref, gate_ref, w_out_ref, gain_mid_ref,
    tile_ref, chain_ref, pair_ref, gain_ref, w_ref, gain_mid, w_out, sems,
):
    hidden = (w_ref.shape[1] - w_ref.shape[0]) // 4
    peers = message_ref.shape[0]
    own = hidden // peers
    groups = cycle_of(cols)[1]
    size = groups * LANES
    cycles = [slice(start, start + size) for start in range(0, rows * cols, size)]
    copies = start_copies(
        sems,
        (chain_hbm, chain_ref),
        (tile_hbm, tile_ref),
        (gain_hbm, gain_ref),
        (pair_hbm, pair_ref),
        (w_hbm, w_ref),
    )
    for copy in copies[:3]:
        copy.wait()
    keep = keep_of(tile_ref, chain_ref, rows, cols)
    gain = column(gain_ref[...])
    copies[4].wait()
    w_t = (w_ref[...] * 0.5).T
    w_gate_ref[...] = w_t[4 * hidden :]
    w_t = w_t[: 4 * hidden]
    copies[3].wait()
    for lanes in cycles:
        block = transpose(pair_ref[lanes, :])
        center = block - jnp.mean(block, axis=0, keepdims=True)
        spread = jnp.mean(center * center, axis=0, keepdims=True)
        normed_ref[:, lanes] = (center * lax.rsqrt(spread + EPS) * gain).astype(jnp.bfloat16)
    for cycle, lanes in enumerate(cycles):
        projected = jnp.dot(w_t, normed_ref[:, lanes], preferred_element_type=jnp.float32)
        sides = []
        for side in range(2):
            value = projected[2 * side * hidden : (2 * side + 1) * hidden]
            gate = projected[(2 * side + 1) * hidden : (2 * side + 2) * hidden]
            sides.append(((jnp.tanh(gate) + 1.0) * value * keep[:, lanes]).reshape(peers, own, size))
        both = jnp.concatenate(sides, axis=1).astype(jnp.bfloat16)
        for group in range(groups):
            line = (cycle * groups + group) * 2 * own
            message_ref[:, line : line + 2 * own, :] = both[:, :, group * LANES : (group + 1) * LANES]

    @pl.when(in_first_part())
    def _():
        tail(normed_ref, w_gate_ref, gain_mid_hbm, w_out_hbm, gate_ref, w_out_ref, gain_mid_ref, gain_mid, w_out, sems)


def unpack(message_ref, half, halves, spread_ref, own, cols):
    tokens, groups = cycle_of(cols)
    members, lines, _ = message_ref.shape
    peers = members // halves
    lane = lax.broadcasted_iota(jnp.int32, (2 * own, LANES), 1)
    cycles = lines // (2 * groups * own)
    for peer in range(peers):
        for cycle in range(cycles):
            base = cycle * groups
            held = [
                message_ref[
                    peer * halves + half, (base + group) * 2 * own : (base + group + 1) * 2 * own, :
                ].astype(jnp.float32)
                for group in range(groups)
            ]
            for token in range(tokens):
                k = (peer * cycles + cycle) * tokens + token
                for chunk in range(spread_ref.shape[0]):
                    group, off = divmod(token * cols + chunk * LANES, LANES)
                    value = held[group]
                    if off and group + 1 < groups:
                        value = jnp.where(lane >= off, value, held[group + 1])
                    if off:
                        value = pltpu.roll(value, LANES - off, axis=1)
                    spread_ref[chunk, k * 2 * own : (k + 1) * 2 * own, :] = value


def pack(spread_ref, at, own, cols):
    tokens, groups = cycle_of(cols)
    lane = lax.broadcasted_iota(jnp.int32, (own, LANES), 1)
    rolled, lines = {}, []
    for group in range(groups):
        value, here = None, 0
        while here < LANES:
            token, col = divmod(group * LANES + here, cols)
            chunk, there = divmod(col, LANES)
            shift = (here - there) % LANES
            if (token, chunk, shift) not in rolled:
                line = (at * tokens + token) * own
                piece = spread_ref[chunk, line : line + own, :]
                rolled[token, chunk, shift] = pltpu.roll(piece, shift, axis=1) if shift else piece
            piece = rolled[token, chunk, shift]
            value = piece if value is None else jnp.where(lane >= here, piece, value)
            here += min(LANES - here, LANES - there, cols - col)
        lines.append(value)
    return lines


def channel_of(spread_ref, line, stride):
    count = spread_ref.shape[1] // stride
    return jnp.concatenate(
        [spread_ref[chunk, pl.ds(line, count, stride=stride), :] for chunk in range(spread_ref.shape[0])],
        axis=1,
    ).astype(jnp.bfloat16)


def triangle_kernel(own, cols, shares, message_ref, mixed_ref, spread, left_t, mixed):
    halves, chunks = spread.shape[:2]
    width = chunks * LANES
    depth = spread.shape[2] // (2 * own)
    deep = left_t.shape[2]
    one = identity(cols, width)
    padding = [jnp.zeros((deep - depth, width), jnp.bfloat16)] if depth < deep else []
    for half in range(halves):
        unpack(message_ref, half, halves, spread.at[half], own, cols)

    def operand(channel, half):
        return jnp.concatenate([channel_of(spread.at[half], channel, 2 * own)] + padding, axis=0)

    for pair in range(0, own, 2):
        channels = [(channel, half) for channel in (pair, pair + 1) for half in range(halves)]
        left = jnp.concatenate([operand(channel, half) for channel, half in channels], axis=0)
        both = lax.dot_general(
            one, left, (((1,), (1,)), ((), ())), preferred_element_type=jnp.float32
        ).astype(jnp.bfloat16)
        for at, (channel, half) in enumerate(channels):
            left_t[channel, half * cols : (half + 1) * cols, :] = both[:, at * deep : (at + 1) * deep]
    for channel in range(own):
        right = jnp.concatenate([operand(own + channel, half) for half in range(halves)], axis=1)
        total = jnp.dot(left_t[channel], right, preferred_element_type=jnp.float32)
        for i_half in range(halves):
            for j_half in range(halves):
                for chunk in range(chunks):
                    start = j_half * width + chunk * LANES
                    mixed[i_half, j_half, chunk, pl.ds(channel, cols, stride=own), :] = total[
                        i_half * cols : (i_half + 1) * cols, start : start + LANES
                    ]
    groups = cycle_of(cols)[1]
    each = mixed_ref.shape[0] // shares
    cycles = each // (halves * groups * own)
    for share in range(shares):
        i_half, peer = divmod(share, shares // halves)
        lines = []
        for j_half in range(halves):
            for cycle in range(cycles):
                lines += pack(mixed.at[i_half, j_half], peer * cycles + cycle, own, cols)
        mixed_ref[share * each : (share + 1) * each, :] = jnp.concatenate(lines, axis=0).astype(jnp.bfloat16)


def output_kernel(
    own, parts, mixed_ref, gate_ref, gain_ref, w_t_ref, normed_ref, w_gate_ref, gain_hbm, w_out_hbm, update_hbm,
    mixed, update, sems, gate, w_t, gain_t, gain, w_out, tail_sems,
):
    first = in_first_part()

    @pl.when(first)
    def _():
        finish(own, parts, mixed_ref, gate_ref, gain_ref, w_t_ref, update_hbm, mixed, update, sems)

    @pl.when(jnp.logical_not(first))
    def _():
        tail(normed_ref, w_gate_ref, gain_hbm, w_out_hbm, gate, w_t, gain_t, gain, w_out, tail_sems)
        finish(own, parts, mixed_ref, gate, gain_t, w_t, update_hbm, mixed, update, sems)


def finish(own, parts, mixed_ref, gate_ref, gain_ref, w_t_ref, update_hbm, mixed, update, sems):
    members, lines, _ = mixed.shape
    members = members // parts
    mixed[...] = mixed_ref[...].astype(jnp.float32).reshape(mixed.shape)
    groups = lines // own
    steps = math.gcd(groups, 3)
    leaving = []
    for group in range(groups):
        sums = mixed[:members, group * own : (group + 1) * own, :]
        for part in range(1, parts):
            sums += mixed[part * members : (part + 1) * members, group * own : (group + 1) * own, :]
        block = sums.reshape(members * own, LANES)
        center = block - jnp.mean(block, axis=0, keepdims=True)
        spread = jnp.mean(center * center, axis=0, keepdims=True)
        normed = (center * lax.rsqrt(spread + EPS) * gain_ref[...]).astype(jnp.bfloat16)
        projected = jnp.dot(w_t_ref[...], normed, preferred_element_type=jnp.float32)
        lanes = slice(group * LANES, (group + 1) * LANES)
        update[lanes, :] = (gate_ref[:, lanes] * projected).T.astype(jnp.bfloat16)
        step, last = divmod((group + 1) * steps, groups)
        if last == 0:
            done = slice((step - 1) * (groups // steps) * LANES, (group + 1) * LANES)
            leaving += start_copies(sems.at[step - 1], (update.at[done, :], update_hbm.at[done, :]))
    for copy in leaving:
        copy.wait()


def in_hbm(value):
    return pltpu.with_memory_space_constraint(value, pltpu.HBM)


def on_device(shares, halves, pair, tile_mask, chain_ids, gain_in, w_proj, gain_mid, w_out):
    rows, cols, width = pair.shape
    hidden = w_out.shape[0]
    peers = shares // PARTS
    own = hidden // (peers * halves)
    positions = rows * cols
    groups = positions // LANES
    lines = groups * own
    cycles = groups // cycle_of(cols)[1]
    params = pltpu.CompilerParams(vmem_limit_bytes=VMEM_BYTES)
    tokens = chain_ids.shape[0]
    message = jax.ShapeDtypeStruct((peers * halves, 2 * lines, LANES), jnp.bfloat16)
    message, normed, w_gate, gate, w_out_t, gain = pl.pallas_call(
        functools.partial(project_kernel, rows, cols),
        out_shape=(
            message,
            jax.ShapeDtypeStruct((width, positions), jnp.bfloat16),
            jax.ShapeDtypeStruct((width, width), jnp.bfloat16),
            jax.ShapeDtypeStruct((width, positions), jnp.float32),
            jax.ShapeDtypeStruct(w_out.shape[::-1], jnp.bfloat16),
            jax.ShapeDtypeStruct((hidden, LANES), jnp.float32),
        ),
        in_specs=[HBM] * 7,
        out_specs=[VMEM] * 6,
        scratch_shapes=[
            pltpu.SMEM(tile_mask.shape, jnp.int32),
            pltpu.VMEM((1, tokens), jnp.int32),
            pltpu.VMEM((positions, width), jnp.bfloat16),
            pltpu.VMEM((1, width), jnp.float32),
            pltpu.VMEM(w_proj.shape, jnp.bfloat16),
            pltpu.VMEM((1, hidden), jnp.float32),
            pltpu.VMEM(w_out.shape, jnp.bfloat16),
            pltpu.SemaphoreType.DMA((5,)),
        ],
        compiler_params=params,
        name="project",
    )(
        in_hbm(tile_mask),
        in_hbm(chain_ids[None, :]),
        in_hbm(pair.reshape(positions, width)),
        in_hbm(gain_in[None, :]),
        in_hbm(w_proj),
        in_hbm(gain_mid[None, :]),
        in_hbm(w_out),
    )
    message = lax.all_to_all(
        message,
        ("row", "col"),
        split_axis=0,
        concat_axis=0,
        axis_index_groups=[
            list(range(part * peers * halves, (part + 1) * peers * halves))
            for part in range(PARTS)
        ],
        tiled=True,
    )
    chunks = pl.cdiv(cols, LANES)
    depth = peers * rows
    deep = pl.cdiv(depth, LANES) * LANES
    mixed = pl.pallas_call(
        functools.partial(triangle_kernel, own, cols, shares),
        out_shape=jax.ShapeDtypeStruct((halves * shares * lines, LANES), jnp.bfloat16),
        in_specs=[VMEM],
        out_specs=VMEM,
        scratch_shapes=[
            pltpu.VMEM((halves, chunks, depth * 2 * own, LANES), jnp.float32),
            pltpu.VMEM((own, halves * cols, deep), jnp.bfloat16),
            pltpu.VMEM((halves, halves, chunks, cols * own, LANES), jnp.float32),
        ],
        compiler_params=params,
        name="triangle",
    )(message)
    mixed = lax.all_to_all(
        mixed.reshape(halves * shares, lines, LANES),
        ("row", "col"),
        split_axis=0,
        concat_axis=0,
        tiled=True,
    ).reshape(halves * shares * lines, LANES)
    update = pl.pallas_call(
        functools.partial(output_kernel, own, PARTS),
        out_shape=jax.ShapeDtypeStruct((positions, width), jnp.bfloat16),
        in_specs=[VMEM] * 6 + [HBM] * 2,
        out_specs=HBM,
        scratch_shapes=[
            pltpu.VMEM((halves * shares, lines, LANES), jnp.float32),
            pltpu.VMEM((positions, width), jnp.bfloat16),
            pltpu.SemaphoreType.DMA((math.gcd(groups, 3), 1)),
            pltpu.VMEM((width, positions), jnp.float32),
            pltpu.VMEM(w_out.shape[::-1], jnp.bfloat16),
            pltpu.VMEM((hidden, LANES), jnp.float32),
            pltpu.VMEM((1, hidden), jnp.float32),
            pltpu.VMEM(w_out.shape, jnp.bfloat16),
            pltpu.SemaphoreType.DMA((2,)),
        ],
        compiler_params=params,
        name="output",
    )(mixed, gate, gain, w_out_t, normed, w_gate, in_hbm(gain_mid[None, :]), in_hbm(w_out))
    return update.reshape(rows, cols, width)


def solution(mesh):
    in_specs = (P(("grp", "row"), "col", None), P("grp", None), P("grp"), P(), P(), P(), P())
    out_specs = P(("grp", "row"), "col", None)
    return jax.shard_map(
        functools.partial(on_device, mesh.shape["row"], mesh.shape["col"]),
        mesh=mesh,
        in_specs=in_specs,
        out_specs=out_specs,
        check_vma=False,
    )
```
